32 devices in a mesh: depth: 4 (over y, x), rows: 8 (over z, core).
Axes of the slice: x: 2, y: 2, z: 4, core: 2. Of those that a mesh axis runs over, the one named last changes fastest.
Arguments:
- incident: bfloat16 [3, 2, 256, 1024], P(None, None, 'rows'), may hold values from -6 to 6
- row_taps: bfloat16 [4, 3, 2, 33], P('depth'), may hold values from -0.75 to 0.75
- col_taps: bfloat16 [4, 3, 2, 127], P('depth'), may hold values from -0.375 to 0.375
- hogel_light: float32 [4, 3, 256, 1024], P('depth', None, 'rows'), may hold values from -6 to 6
- silhouette: int32 [4, 256, 64], P('depth', 'rows'), may hold values from 0 to 16
- fill_counts: int32 [4, 16], P('depth', 'rows'), may hold values from 1 to 64, 640 in all within a row
- hogel_index: int32 [4, 16, 64], P('depth', 'rows'), may hold values from 0 to 63, each once within a row
Outputs:
- layer_fields: bfloat16 [4, 3, 2, 256, 1024], P('depth', None, None, 'rows')
The draws below stay inside these ranges and needn't reach their ends.
Inputs may be any that keep to these rules, and one draw needn't show every extreme that they name: Each entry is the count of one hogel row, at most 64; for each layer l, the sum of fill_counts[l, g] over all 16 hogel rows g is 640. `hogel_index`: each list names every position of its hogel row once.
All inputs are finite; a program needn't handle non-finite values. No bound on the sum of `fill_counts` on one device may be relied on, other than what follows from the above.
Results may differ from the reference program's by a relative error of at most 0.006.
Values may be sent and summed in bfloat16 or wider, within the bound.
No kernel may reach another device: no remote copies, remote signals or barrier semaphores. Data moves between devices by JAX's collectives and lax.ppermute only.
A program may use at most 64 MiB of HBM per device.

```python
import math
import jax
import jax.numpy as jnp
import numpy as np
from jax import lax

HS = 16
KR = 16
KC = 63
COLORS = 3
ROWS_DEV = 32
COLS = 1024
LAYERS = 4
ROWS = 256
HROWS = 16
NH = 64
FILLED = 640
N_DEPTH = 4
N_ROWS = 8


def touch_ends(array, own_key, smallest, high):
    spot = [jax.random.randint(jax.random.fold_in(own_key, axis), (), 0, length) for axis, length in enumerate(array.shape)]
    longest = array.shape.index(max(array.shape))
    beside = spot[:longest] + [(spot[longest] + 1) % array.shape[longest]] + spot[longest + 1:]
    return array.at[tuple(spot)].set(smallest).at[tuple(beside)].set(high)


def block_scale(own_key, shape, cuts, least, top_value):
    factor_of, own = 1.0, jax.random.fold_in(own_key, 6)
    for axis_at, blocks in cuts:
        draws = jnp.exp(jax.random.uniform(jax.random.fold_in(own, axis_at), (blocks,), jnp.float32, least / len(cuts), top_value / len(cuts)))
        factor_of = factor_of * jnp.repeat(draws, shape[axis_at] // blocks).reshape([-1 if axis == axis_at else 1 for axis in range(len(shape))])
    return factor_of


def length_profile(number_of, total, bound, skew):
    portions = [(1 << 20) // math.isqrt(rank ** skew) + 1 for rank in range(2, number_of + 1)]
    surplus, holding = total - bound - (number_of - 1), [1] * (number_of - 1)
    while surplus > 0:
        movable = [i for i in range(number_of - 1) if holding[i] < bound]
        whole, left = sum([portions[i] for i in movable]), surplus
        for i in movable:
            extra = min(bound - holding[i], max(1, left * portions[i] // whole), surplus)
            holding[i] = holding[i] + extra
            surplus = surplus - extra
    return np.array([bound] + holding)


def ragged(stream_key, amount, total, most, slope):
    if amount == 2:
        one = jax.random.randint(stream_key, (), max(1, total - most), min(most, total - 1) + 1)
        return jnp.stack([one, total - one])
    sizes = jnp.asarray(length_profile(amount, total, most, slope), jnp.int32)
    twos = (amount - 1) // 2
    source_of, sink = sizes[1:1 + 2 * twos:2], sizes[2:2 + 2 * twos:2]
    room = jnp.minimum(source_of - 1, most - sink)
    passed = jax.random.randint(jax.random.fold_in(stream_key, 1), (twos,), 0, 1 << 20) % (room + 1)
    sizes = sizes.at[1:1 + 2 * twos:2].set(source_of - passed).at[2:2 + 2 * twos:2].set(sink + passed)
    return sizes[jax.random.permutation(jax.random.fold_in(stream_key, 2), amount)]


def gaussian(key, dims, width, most, split=(), held_as=jnp.bfloat16):
    gain = block_scale(key, dims, split, -0.22, 0.18) if split else 1.0
    result = jax.random.normal(key, dims, jnp.float32) * width * gain
    return jnp.minimum(jnp.maximum(result, -most), most).astype(held_as)


def setup_inputs(seed: int = 0) -> dict:
    key_of = jax.random.split(jax.random.key(seed), 8)
    return {
        "incident": gaussian(key_of[0], (COLORS, 2, ROWS, COLS), 1.0, 6.0, ((2, 8),)),
        "row_taps": gaussian(key_of[1], (LAYERS, COLORS, 2, 2 * KR + 1), (4 * KR + 2) ** -0.5, 0.75, ((0, 4),)),
        "col_taps": gaussian(key_of[2], (LAYERS, COLORS, 2, 2 * KC + 1), (4 * KC + 2) ** -0.5, 0.375, ((0, 4),)),
        "hogel_light": gaussian(key_of[3], (LAYERS, COLORS, ROWS, COLS), 1.0, 6.0, ((0, 4), (2, 8)), jnp.float32),
        "silhouette": touch_ends(jax.random.randint(key_of[4], (LAYERS, ROWS, NH), 0, HS + 1), jax.random.fold_in(key_of[4], 1), 0, HS).astype(jnp.int32),
        "fill_counts": jax.vmap(lambda own: ragged(own, HROWS, FILLED, NH, 2))(jax.random.split(key_of[5], LAYERS)).reshape((LAYERS, HROWS)).astype(jnp.int32),
        "hogel_index": jax.vmap(lambda own: jax.random.permutation(own, NH))(jax.random.split(key_of[6], LAYERS * HROWS)).reshape((LAYERS, HROWS, NH)).astype(jnp.int32),
    }


def dft_tables(size_now):
    counter = jnp.arange(size_now, dtype=jnp.int32)
    product = counter[:, None] * counter[None, :] % size_now
    angles = product.astype(jnp.float32) * (2.0 * math.pi / size_now)
    return (jnp.cos(angles) / math.sqrt(size_now), jnp.sin(angles) / math.sqrt(size_now))

def row_matrix(taps, height, reach):
    width_ext = height + 2 * reach
    offsets = jnp.arange(width_ext, dtype=jnp.int32)[None, :] - jnp.arange(height, dtype=jnp.int32)[:, None]
    inside = (offsets >= 0) & (offsets <= 2 * reach)
    picked = jnp.take(taps, jnp.clip(offsets, 0, 2 * reach), axis=1)
    banded = jnp.where(inside[None], picked, jnp.zeros_like(picked))
    upper = jnp.concatenate([banded[0], -banded[1]], axis=1)
    lower = jnp.concatenate([banded[1], banded[0]], axis=1)
    return jnp.concatenate([upper, lower], axis=0)

def column_matrix(taps, reach):
    source = (jnp.arange(3, dtype=jnp.int32)[:, None, None] - 1) * 128 + jnp.arange(128, dtype=jnp.int32)[None, :, None]
    offsets = source - jnp.arange(128, dtype=jnp.int32)[None, None, :]
    inside = jnp.abs(offsets) <= reach
    picked = jnp.take(taps, jnp.clip(offsets + reach, 0, 2 * reach), axis=1)
    blocks = jnp.where(inside[None], picked, jnp.zeros_like(picked))
    real_rows = blocks[0].reshape(384, 128)
    imag_rows = blocks[1].reshape(384, 128)
    upper = jnp.concatenate([real_rows, imag_rows], axis=1)
    lower = jnp.concatenate([-imag_rows, real_rows], axis=1)
    return jnp.concatenate([upper, lower], axis=0)

def apply_columns(rowed, col_mats):
    colour_count, _, height, col_count = rowed.shape
    tile_count = col_count // 128
    padded = jnp.pad(rowed, ((0, 0), (0, 0), (0, 0), (128, 128)))
    pieces = [padded[..., tile_shift * 128:tile_shift * 128 + col_count].reshape(colour_count, 2, height, tile_count, 128) for tile_shift in range(3)]
    stacked = jnp.stack(pieces, axis=2)
    windows = stacked.transpose(0, 3, 4, 1, 2, 5).reshape(colour_count, height * tile_count, 768)
    mixed_cols = jnp.einsum('kna,kab->knb', windows.astype(jnp.float32), col_mats.astype(jnp.float32))
    return mixed_cols.reshape(colour_count, height, tile_count, 2, 128).transpose(0, 3, 1, 2, 4).reshape(colour_count, 2, height, col_count)

def live_tiles(counts, index_list):
    positions = index_list.shape[1]
    slots = jnp.arange(positions, dtype=jnp.int32)
    named = (index_list[:, :, None] == slots[None, None, :]) & (slots[None, :, None] < counts[:, None, None])
    return jnp.any(named, axis=1)

def transparency(edges, hogel_size):
    expanded = jnp.repeat(edges, hogel_size, axis=1)
    within = jnp.arange(expanded.shape[1], dtype=jnp.int32) % hogel_size
    return (within[None, :] < expanded).astype(jnp.float32)

def stereo_field(light, live, hogel_size):
    colour_count, height, col_count = light.shape
    live_pix = jnp.repeat(jnp.repeat(live, hogel_size, axis=0), hogel_size, axis=1).astype(jnp.float32)
    masked = light * live_pix[None]
    cos_tab, sin_tab = dft_tables(hogel_size)
    left_mat = jnp.concatenate([cos_tab, -sin_tab], axis=0)
    groups = height // hogel_size
    blocked = masked.reshape(colour_count, groups, hogel_size, col_count)
    left_out = jnp.einsum('ah,kghc->kgac', left_mat, blocked, precision=lax.Precision.HIGHEST)
    tile_count = col_count // 128
    arranged = left_out.reshape(colour_count, groups, 2, hogel_size, tile_count, 128).transpose(0, 1, 3, 4, 2, 5).reshape(-1, 256)
    per_block = 128 // hogel_size
    cos_big = jnp.kron(jnp.eye(per_block, dtype=jnp.float32), cos_tab)
    sin_big = jnp.kron(jnp.eye(per_block, dtype=jnp.float32), sin_tab)
    right_mat = jnp.concatenate([jnp.concatenate([cos_big, -sin_big], axis=1), jnp.concatenate([sin_big, cos_big], axis=1)], axis=0)
    result_tiles = jnp.dot(arranged, right_mat, precision=lax.Precision.HIGHEST)
    return result_tiles.reshape(colour_count, groups, hogel_size, tile_count, 2, 128).transpose(0, 4, 1, 2, 3, 5).reshape(colour_count, 2, height, col_count)

def reference(incident, row_taps, col_taps, hogel_light, silhouette, fill_counts, hogel_index):
    field_in = incident
    outputs = []
    band_rows = ROWS_DEV + 2 * KR
    starts = (jnp.arange(N_ROWS, dtype=jnp.int32) * ROWS_DEV)[:, None] + jnp.arange(band_rows, dtype=jnp.int32)[None, :]
    for layer_now in range(N_DEPTH):
        row_mats = jnp.stack([row_matrix(row_taps[layer_now, colour], ROWS_DEV, KR) for colour in range(COLORS)])
        col_mats = jnp.stack([column_matrix(col_taps[layer_now, colour], KC) for colour in range(COLORS)])
        padded = jnp.pad(field_in, ((0, 0), (0, 0), (KR, KR), (0, 0)))
        windows = padded[:, :, starts, :]
        windows = windows.transpose(0, 2, 1, 3, 4).reshape(COLORS, N_ROWS, 2 * band_rows, COLS)
        rowed = jnp.einsum('kab,knbc->knac', row_mats.astype(jnp.float32), windows.astype(jnp.float32))
        rowed = rowed.astype(jnp.bfloat16).reshape(COLORS, N_ROWS, 2, ROWS_DEV, COLS).transpose(0, 2, 1, 3, 4).reshape(COLORS, 2, ROWS, COLS)
        columned = apply_columns(rowed, col_mats)
        clear = transparency(silhouette[layer_now], HS)
        live = live_tiles(fill_counts[layer_now], hogel_index[layer_now])
        stereo = stereo_field(hogel_light[layer_now], live, HS)
        field_in = (clear[None, None] * columned + stereo).astype(jnp.bfloat16)
        outputs.append(field_in)
    return jnp.stack(outputs)
```

```python
import math

import jax
import jax.numpy as jnp
import numpy as np
from jax import lax
from jax.experimental import pallas as pl
from jax.experimental.pallas import tpu as pltpu
from jax.sharding import PartitionSpec as P

HS = 16
KR = 16
KC = 63
COLORS = 3
LAYERS = 4
BAND = 32
COLS = 1024
NH = COLS // HS
LANES = 128
TILES = COLS // LANES
HALO_W = COLS + LANES
FULL_W = COLS + 2 * LANES
NEAR = 2 * BAND + KR
FAR = KR
VMEM_LIMIT = 48 * 1024 * 1024


def split_table(table):
    high = table.astype(jnp.bfloat16)
    low = (table - high.astype(np.float64)).astype(jnp.bfloat16)
    return high, low


def dft_pair():
    counter = np.arange(HS)
    angles = (counter[:, None] * counter[None, :] % HS) * (2.0 * math.pi / HS)
    return np.cos(angles) / math.sqrt(HS), np.sin(angles) / math.sqrt(HS)


def left_table(height):
    cos_tab, sin_tab = dft_pair()
    eye = np.eye(height // HS)
    full = np.concatenate([np.kron(eye, cos_tab), np.kron(eye, -sin_tab)], axis=0)
    return np.concatenate(split_table(full), axis=1)


def right_table():
    cos_tab, sin_tab = dft_pair()
    eye = np.eye(LANES // HS)
    cos_big, sin_big = np.kron(eye, cos_tab), np.kron(eye, sin_tab)
    full = np.concatenate(
        [
            np.concatenate([cos_big, -sin_big], axis=1),
            np.concatenate([sin_big, cos_big], axis=1),
        ],
        axis=0,
    )
    return np.concatenate(split_table(full), axis=0)


def layer_height(layer):
    return BAND + 2 * KR * (LAYERS - 1 - layer)


def spread_matrix():
    tile = lax.broadcasted_iota(jnp.int32, (NH, COLS), 0)
    column = lax.broadcasted_iota(jnp.int32, (NH, COLS), 1)
    return jnp.where(column // HS == tile, 1.0, 0.0).astype(jnp.bfloat16)


def pack_kernel(light, edges, counts, listed, row_taps, col_taps, out, taps):
    slot = lax.broadcasted_iota(jnp.int32, (NH, NH), 0)
    place = lax.broadcasted_iota(jnp.int32, (NH, NH), 1)
    rows = []
    for group in range(BAND // HS):
        listing = jnp.broadcast_to(listed[0, group : group + 1, :], (NH, NH))
        column = jnp.sum(jnp.where(slot == place, listing, 0), axis=1, keepdims=True)
        named = (column == place) & (slot < counts[0, group])
        live = jnp.max(jnp.where(named, 1.0, 0.0), axis=0, keepdims=True)
        rows.append(jnp.broadcast_to(live, (HS, NH)))
    live_rows = jnp.concatenate(rows, axis=0).astype(jnp.bfloat16)
    live_pix = jnp.dot(live_rows, spread_matrix(), preferred_element_type=jnp.float32)
    edge_tile = jnp.concatenate(
        [edges[0].astype(jnp.float32), jnp.zeros((BAND, LANES - NH), jnp.float32)], axis=1
    ).astype(jnp.bfloat16)
    for colour in range(COLORS):
        out[colour, :, :COLS] = (light[0, colour] * live_pix).astype(jnp.bfloat16)
        out[colour, :, COLS:HALO_W] = edge_tile
        taps[...] = jnp.zeros_like(taps)
        taps[0:2, : 2 * KC + 1] = col_taps[0, colour].astype(jnp.float32)
        taps[2:4, : 2 * KR + 1] = row_taps[0, colour].astype(jnp.float32)
        out[colour, :, HALO_W:] = taps[...].astype(jnp.bfloat16)
    for spare in range(COLORS, LAYERS):
        out[spare] = jnp.zeros((BAND, FULL_W), jnp.bfloat16)


def halo_kernel(own, incident, up_near, down_near, up_far, down_far):
    for near in (up_near, down_near):
        near[0:BAND] = own[0, :, :HALO_W]
        near[BAND : 2 * BAND] = own[1, :, :HALO_W]
        near[NEAR : NEAR + BAND, :COLS] = incident[0]
        near[NEAR + BAND :, :COLS] = incident[1]
    up_near[2 * BAND : NEAR] = own[2, BAND - KR :, :HALO_W]
    down_near[2 * BAND : NEAR] = own[2, :KR, :HALO_W]
    up_far[0:FAR] = own[0, BAND - KR :, :HALO_W]
    down_far[0:FAR] = own[0, :KR, :HALO_W]
    for far in (up_far, down_far):
        far[FAR : FAR + BAND, :COLS] = incident[0]
        far[FAR + BAND :, :COLS] = incident[1]


def chain_kernel(
    own, incident, low_near, high_near, low_far, high_far, right_tab, *rest
):
    left_tabs, (out, field) = rest[:LAYERS], rest[LAYERS:]
    spread = spread_matrix()
    within = (lax.broadcasted_iota(jnp.int32, (1, COLS), 1) % HS).astype(jnp.float32)
    extended = []
    for part in range(2):
        near = slice(NEAR + part * BAND, NEAR + (part + 1) * BAND)
        far = slice(FAR + part * BAND, FAR + (part + 1) * BAND)
        pieces = [
            low_far[far, :COLS],
            low_near[near, :COLS],
            incident[part],
            high_near[near, :COLS],
            high_far[far, :COLS],
        ]
        extended.append(jnp.concatenate(pieces, axis=0))
    for layer in range(LAYERS):
        height = layer_height(layer)
        before = height + 2 * KR
        if layer == 0:
            pieces = [low_far[0:FAR], low_near[0:BAND], own[0, :, :HALO_W], high_near[0:BAND], high_far[0:FAR]]
        elif layer == 1:
            band = slice(BAND, 2 * BAND)
            pieces = [low_near[band], own[1, :, :HALO_W], high_near[band]]
        elif layer == 2:
            band = slice(2 * BAND, NEAR)
            pieces = [low_near[band], own[2, :, :HALO_W], high_near[band]]
        else:
            pieces = [own[3, :, :HALO_W]]
        packed = jnp.concatenate(pieces, axis=0) if len(pieces) > 1 else pieces[0]
        light = packed[:, :COLS]
        edge_pix = jnp.dot(packed[:, COLS : COLS + NH], spread, preferred_element_type=jnp.float32)
        clear = jnp.where(within < edge_pix, 1.0, 0.0)

        taps = own[layer, 0:16, HALO_W:].astype(jnp.float32)
        blank = jnp.zeros((1, LANES), jnp.float32)

        def banded(line, count, shift):
            base = jnp.concatenate([taps[line : line + 1], blank], axis=1)
            base = jnp.broadcast_to(base, (count, 2 * LANES))
            return pltpu.roll(base, shift, 1, stride=1, stride_axis=0)

        row_re = banded(2, height, 0)[:, :before]
        row_im = banded(3, height, 0)[:, :before]
        from_re = jnp.concatenate([row_re, row_im], axis=0).astype(jnp.bfloat16)
        from_im = jnp.concatenate([-row_im, row_re], axis=0).astype(jnp.bfloat16)
        col_re = banded(0, LANES, 1)
        col_im = banded(1, LANES, 1)
        col_mat = jnp.concatenate(
            [
                jnp.concatenate([col_re, -col_im], axis=1),
                jnp.concatenate([col_im, col_re], axis=1),
            ],
            axis=0,
        ).astype(jnp.bfloat16)

        if layer == 0:
            u_re, u_im = extended
        else:
            u_re, u_im = field[0, :before], field[1, :before]
        rowed = jnp.dot(from_re, u_re, preferred_element_type=jnp.float32)
        rowed = rowed + jnp.dot(from_im, u_im, preferred_element_type=jnp.float32)
        rowed = jnp.concatenate([rowed, jnp.zeros((2 * height, LANES), jnp.float32)], axis=1)
        rowed = pltpu.roll(rowed, LANES // 2, 1).astype(jnp.bfloat16)
        windows = jnp.concatenate(
            [
                jnp.concatenate(
                    [
                        rowed[:height, tile * LANES : (tile + 2) * LANES],
                        rowed[height:, tile * LANES : (tile + 2) * LANES],
                    ],
                    axis=1,
                )
                for tile in range(TILES)
            ],
            axis=0,
        )
        columned = lax.dot_general(
            windows, col_mat, (((1,), (1,)), ((), ())), preferred_element_type=jnp.float32
        )

        left = jnp.dot(
            left_tabs[layer][...],
            jnp.concatenate([light, light], axis=0),
            preferred_element_type=jnp.float32,
        ).astype(jnp.bfloat16)
        arranged = jnp.concatenate(
            [
                jnp.concatenate(
                    [
                        left[:height, tile * LANES : (tile + 1) * LANES],
                        left[height:, tile * LANES : (tile + 1) * LANES],
                    ],
                    axis=1,
                )
                for tile in range(TILES)
            ],
            axis=0,
        )
        stereo = jnp.dot(
            jnp.concatenate([arranged, arranged], axis=1),
            right_tab[...],
            preferred_element_type=jnp.float32,
        )
        for tile in range(TILES):
            span = slice(tile * height, (tile + 1) * height)
            lanes = slice(tile * LANES, (tile + 1) * LANES)
            for part in range(2):
                side = slice(part * LANES, (part + 1) * LANES)
                value = clear[:, lanes] * columned[span, side] + stereo[span, side]
                field[part, :height, lanes] = value.astype(jnp.bfloat16)
        start = (height - BAND) // 2
        for part in range(2):
            out[layer, part] = field[part, start : start + BAND]


def shifted(value, axis, by):
    count = lax.axis_size(axis)
    pairs = [(i, i + by) for i in range(count) if 0 <= i + by < count]
    return lax.ppermute(value, axis, pairs)


def params():
    return pltpu.CompilerParams(vmem_limit_bytes=VMEM_LIMIT)


def body(incident, row_taps, col_taps, hogel_light, silhouette, fill_counts, hogel_index):
    vmem = pl.BlockSpec(memory_space=pltpu.VMEM)
    smem = pl.BlockSpec(memory_space=pltpu.SMEM)
    bf16 = jnp.bfloat16
    payload = pl.pallas_call(
        pack_kernel,
        out_shape=jax.ShapeDtypeStruct((LAYERS, BAND, FULL_W), bf16),
        in_specs=[vmem, vmem, smem, vmem, vmem, vmem],
        out_specs=vmem,
        scratch_shapes=[pltpu.VMEM((BAND, LANES), jnp.float32)],
        compiler_params=params(),
        cost_estimate=pl.CostEstimate(flops=10**7, bytes_accessed=10**6, transcendentals=0),
    )(hogel_light, silhouette, fill_counts, hogel_index, row_taps, col_taps)
    own = lax.all_to_all(payload, "depth", 0, 0, tiled=True)
    colour = jnp.minimum(lax.axis_index("depth"), COLORS - 1)
    mine = lax.dynamic_index_in_dim(incident, colour, 0, keepdims=False)
    near = jax.ShapeDtypeStruct((NEAR + 2 * BAND, HALO_W), bf16)
    far = jax.ShapeDtypeStruct((FAR + 2 * BAND, HALO_W), bf16)
    up_near, down_near, up_far, down_far = pl.pallas_call(
        halo_kernel,
        out_shape=(near, near, far, far),
        in_specs=[vmem, vmem],
        out_specs=(vmem,) * 4,
        compiler_params=params(),
        cost_estimate=pl.CostEstimate(flops=0, bytes_accessed=2 * 10**6, transcendentals=0),
    )(own, mine)
    low_near = shifted(up_near, "rows", 1)
    high_near = shifted(down_near, "rows", -1)
    low_far = shifted(up_far, "rows", 2)
    high_far = shifted(down_far, "rows", -2)
    tables = [jnp.asarray(right_table())]
    tables += [jnp.asarray(left_table(layer_height(layer))) for layer in range(LAYERS)]
    result = pl.pallas_call(
        chain_kernel,
        out_shape=jax.ShapeDtypeStruct((LAYERS, 2, BAND, COLS), bf16),
        in_specs=[vmem] * (6 + len(tables)),
        out_specs=vmem,
        scratch_shapes=[pltpu.VMEM((2, layer_height(0), COLS), bf16)],
        compiler_params=params(),
        cost_estimate=pl.CostEstimate(flops=3 * 10**9, bytes_accessed=3 * 10**6, transcendentals=0),
    )(own, mine, low_near, high_near, low_far, high_far, *tables)
    gathered = lax.all_to_all(result, "depth", 0, 0, tiled=True)
    return gathered[None, :COLORS]


def solution(mesh):
    placed = (
        P(None, None, "rows", None),
        P("depth", None, None, None),
        P("depth", None, None, None),
        P("depth", None, "rows", None),
        P("depth", "rows", None),
        P("depth", "rows"),
        P("depth", "rows", None),
    )
    return jax.shard_map(
        body,
        mesh=mesh,
        in_specs=placed,
        out_specs=P("depth", None, None, "rows", None),
        check_vma=False,
    )
```

```python
import math

import jax
import jax.numpy as jnp
import numpy as np
from jax import lax
from jax.experimental import pallas as pl
from jax.experimental.pallas import tpu as pltpu
from jax.sharding import PartitionSpec as P

HS = 16
KR = 16
KC = 63
COLORS = 3
LAYERS = 4
BAND = 32
COLS = 1024
NH = COLS // HS
LANES = 128
TILES = COLS // LANES
HALO_W = COLS + LANES
HALF = LANES // 2
FULL_W = COLS + 2 * LANES
NEAR = 2 * BAND + KR
FAR = KR
VMEM_LIMIT = 48 * 1024 * 1024


def split_table(table):
    high = table.astype(jnp.bfloat16)
    low = (table - high.astype(np.float64)).astype(jnp.bfloat16)
    return high, low


def dft_pair():
    counter = np.arange(HS)
    angles = (counter[:, None] * counter[None, :] % HS) * (2.0 * math.pi / HS)
    return np.cos(angles) / math.sqrt(HS), np.sin(angles) / math.sqrt(HS)


def left_table():
    cos_tab, sin_tab = dft_pair()
    eye = np.eye(LANES // HS)
    full = np.concatenate([np.kron(eye, cos_tab), np.kron(eye, -sin_tab)], axis=0)
    return np.concatenate(split_table(full), axis=1)


def right_table():
    cos_tab, sin_tab = dft_pair()
    eye = np.eye(LANES // HS)
    cos_big, sin_big = np.kron(eye, cos_tab), np.kron(eye, sin_tab)
    full = np.concatenate(
        [
            np.concatenate([cos_big, -sin_big], axis=1),
            np.concatenate([sin_big, cos_big], axis=1),
        ],
        axis=0,
    )
    return np.concatenate(split_table(full), axis=0)


def layer_height(layer):
    return BAND + 2 * KR * (LAYERS - 1 - layer)


def block_height(layer):
    height = layer_height(layer)
    return height // 2 if 2 * (height + 2 * KR) > 2 * LANES else height


def spread_matrix():
    tile = lax.broadcasted_iota(jnp.int32, (NH, COLS), 0)
    column = lax.broadcasted_iota(jnp.int32, (NH, COLS), 1)
    return jnp.where(column // HS == tile, 1.0, 0.0).astype(jnp.bfloat16)


def pack_kernel(light, edges, counts, listed, row_taps, col_taps, out, *scratch):
    held, sems, taps = scratch[:6], scratch[6], scratch[7]
    sources = (listed, counts, edges, row_taps, col_taps, light)
    copies = [
        pltpu.make_async_copy(source, target, sems.at[place])
        for place, (source, target) in enumerate(zip(sources, held))
    ]
    for copy in reversed(copies):
        copy.start()
    listed, counts, edges, row_taps, col_taps, light = held
    spread = spread_matrix()
    slot = lax.broadcasted_iota(jnp.int32, (NH, NH), 0)
    place = lax.broadcasted_iota(jnp.int32, (NH, NH), 1)
    for copy in copies[:5]:
        copy.wait()
    rows = []
    for group in range(BAND // HS):
        listing = jnp.broadcast_to(listed[0, group : group + 1, :], (NH, NH))
        column = jnp.sum(jnp.where(slot == place, listing, 0), axis=1, keepdims=True)
        named = (column == place) & (slot < counts[0, group])
        live = jnp.max(jnp.where(named, 1.0, 0.0), axis=0, keepdims=True)
        rows.append(jnp.broadcast_to(live, (HS, NH)))
    live_rows = jnp.concatenate(rows, axis=0).astype(jnp.bfloat16)
    live_pix = jnp.dot(live_rows, spread, preferred_element_type=jnp.float32)
    edge_tile = jnp.concatenate(
        [edges[0].astype(jnp.float32), jnp.zeros((BAND, LANES - NH), jnp.float32)], axis=1
    ).astype(jnp.bfloat16)
    for colour in range(COLORS):
        out[colour, :, COLS:HALO_W] = edge_tile
        taps[...] = jnp.zeros_like(taps)
        taps[0:2, : 2 * KC + 1] = col_taps[0, colour].astype(jnp.float32)
        taps[2:4, : 2 * KR + 1] = row_taps[0, colour].astype(jnp.float32)
        out[colour, :, HALO_W:] = taps[...].astype(jnp.bfloat16)
    for spare in range(COLORS, LAYERS):
        out[spare] = jnp.zeros((BAND, FULL_W), jnp.bfloat16)
    copies[5].wait()
    for colour in range(COLORS):
        out[colour, :, :COLS] = (light[0, colour] * live_pix).astype(jnp.bfloat16)


def halo_kernel(own, incident, in_chip, cross, far_even, far_odd):
    band = lax.axis_index("rows")
    core = band % 2
    odd = (band // 2) % 2
    last = BAND - KR
    for near, start in ((in_chip, (1 - core) * last), (cross, core * last)):
        near[0:BAND] = own[0, :, :HALO_W]
        near[BAND : 2 * BAND] = own[1, :, :HALO_W]
        near[2 * BAND : NEAR] = own[2, pl.ds(pl.multiple_of(start, KR), KR), :HALO_W]
        near[NEAR : NEAR + BAND, :COLS] = incident[0]
        near[NEAR + BAND :, :COLS] = incident[1]
    for far, start in ((far_even, (1 - odd) * last), (far_odd, odd * last)):
        far[0:FAR] = own[0, pl.ds(pl.multiple_of(start, KR), KR), :HALO_W]
        far[FAR : FAR + BAND, :COLS] = incident[0]
        far[FAR + BAND :, :COLS] = incident[1]


def tiles_below(value, height):
    return jnp.concatenate(
        [
            jnp.concatenate(
                [
                    value[:height, tile * LANES : (tile + 1) * LANES],
                    value[height:, tile * LANES : (tile + 1) * LANES],
                ],
                axis=1,
            )
            for tile in range(TILES)
        ],
        axis=0,
    )


def stereo_tiles(light, left_tab, right_tab):
    height = light.shape[0]
    rows = jnp.concatenate([left_tab[:height], left_tab[LANES : LANES + height]], axis=0)
    left = jnp.dot(rows[:, :height], light, preferred_element_type=jnp.float32)
    low = rows[:, LANES : LANES + height]
    left = left + jnp.dot(low, light, preferred_element_type=jnp.float32)
    arranged = tiles_below(left.astype(jnp.bfloat16), height)
    out = jnp.dot(arranged, right_tab[: 2 * LANES], preferred_element_type=jnp.float32)
    return out + jnp.dot(arranged, right_tab[2 * LANES :], preferred_element_type=jnp.float32)


def banded(line, count, shift):
    base = jnp.concatenate([line, jnp.zeros((1, LANES), jnp.float32)], axis=1)
    base = jnp.broadcast_to(base, (count, 2 * LANES))
    return pltpu.roll(base, shift, 1, stride=1, stride_axis=0)


def prepare_kernel(own, left_tab, right_tab, col_mats, stereo, *row_mats):
    for layer in range(LAYERS):
        taps = own[layer, 0:16, HALO_W:].astype(jnp.float32)
        row_re, row_im = taps[2:3], taps[3:4]
        height = block_height(layer)
        before = height + 2 * KR
        upper = banded(row_re, height, 0) - banded(row_im, height, before)
        lower = banded(row_im, height, 0) + banded(row_re, height, before)
        row_mats[layer][...] = jnp.concatenate([upper, lower], axis=0).astype(jnp.bfloat16)
        col_re = banded(taps[0:1], LANES, 1)
        col_im = banded(taps[1:2], LANES, 1)
        upper = jnp.concatenate([col_re, -col_im], axis=1)
        lower = jnp.concatenate([col_im, col_re], axis=1)
        col_mats[layer] = jnp.concatenate([upper, lower], axis=0).astype(jnp.bfloat16)
    light = jnp.concatenate([own[layer, :, :COLS] for layer in range(LAYERS)], axis=0)
    tiles = stereo_tiles(light, left_tab, right_tab)
    for tile in range(TILES):
        for part in range(2):
            block = tiles[
                tile * LANES : (tile + 1) * LANES, part * LANES : (part + 1) * LANES
            ]
            stereo[part, :, tile * LANES : (tile + 1) * LANES] = block


def chain_kernel(
    own, incident, in_chip, cross, far_even, far_odd, left_tab, right_tab, col_mats, stereo, *rest
):
    row_mats, (out, field, low_near, high_near, low_far, high_far) = rest[:LAYERS], rest[LAYERS:]
    band = lax.axis_index("rows")
    even_core = band % 2 == 0
    even_chip = (band // 2) % 2 == 0
    low_near[...] = jnp.where(even_core, cross[...], in_chip[...])
    high_near[...] = jnp.where(even_core, in_chip[...], cross[...])
    low_far[...] = jnp.where(even_chip, far_odd[...], far_even[...])
    high_far[...] = jnp.where(even_chip, far_even[...], far_odd[...])

    pieces = [
        low_far[0:FAR],
        low_near[0:BAND],
        high_near[0:BAND],
        high_far[0:FAR],
        low_near[BAND : 2 * BAND],
        high_near[BAND : 2 * BAND],
        low_near[2 * BAND : NEAR],
        high_near[2 * BAND : NEAR],
    ]
    halo = jnp.concatenate(pieces, axis=0)
    count = halo.shape[0] // 2
    halves = [
        stereo_tiles(halo[half * count : (half + 1) * count, :COLS], left_tab, right_tab)
        for half in range(2)
    ]
    edges = jnp.concatenate(
        [halo[:, COLS : COLS + NH]]
        + [own[layer, :, COLS : COLS + NH] for layer in range(LAYERS)],
        axis=0,
    )
    edge_pix = jnp.dot(edges, spread_matrix(), preferred_element_type=jnp.float32)
    within = (lax.broadcasted_iota(jnp.int32, (1, COLS), 1) % HS).astype(jnp.float32)
    clear_all = jnp.where(within < edge_pix, 1.0, 0.0)

    extended = []
    for part in range(2):
        near = slice(NEAR + part * BAND, NEAR + (part + 1) * BAND)
        far = slice(FAR + part * BAND, FAR + (part + 1) * BAND)
        pieces = [
            low_far[far, :COLS],
            low_near[near, :COLS],
            incident[part],
            high_near[near, :COLS],
            high_far[far, :COLS],
        ]
        extended.append(jnp.concatenate(pieces, axis=0))
    below = (0, 2 * (BAND + FAR), 2 * (BAND + FAR) + 2 * BAND, 0)
    sides = (BAND + FAR, BAND, KR, 0)
    for layer in range(LAYERS):
        height = layer_height(layer)
        before = height + 2 * KR
        side = sides[layer]
        if layer == 0:
            u_re, u_im = extended
        else:
            u_re, u_im = field[0, :before], field[1, :before]
        block = block_height(layer)
        reach = block + 2 * KR
        parts = []
        for start in range(0, height, block):
            stacked = jnp.concatenate(
                [u_re[start : start + reach], u_im[start : start + reach]], axis=0
            )
            parts.append(
                jnp.dot(
                    row_mats[layer][:, : 2 * reach], stacked, preferred_element_type=jnp.float32
                )
            )
        rowed = jnp.concatenate(
            [part[:block] for part in parts] + [part[block:] for part in parts], axis=0
        )
        rowed = jnp.concatenate([rowed, jnp.zeros((2 * height, LANES), jnp.float32)], axis=1)
        rowed = pltpu.roll(rowed, HALF, 1).astype(jnp.bfloat16)
        windows = jnp.concatenate(
            [
                jnp.concatenate(
                    [
                        rowed[:height, tile * LANES : (tile + 2) * LANES],
                        rowed[height:, tile * LANES : (tile + 2) * LANES],
                    ],
                    axis=1,
                )
                for tile in range(TILES)
            ],
            axis=0,
        )
        columned = lax.dot_general(
            windows,
            col_mats[layer],
            (((1,), (1,)), ((), ())),
            preferred_element_type=jnp.float32,
        )

        def halo_rows(first, length, tile, part):
            half, inner = divmod(first, count)
            found = []
            while length > 0:
                take = min(length, count - inner)
                row = tile * count + inner
                found.append(
                    halves[half][row : row + take, part * LANES : (part + 1) * LANES]
                )
                half, inner, length = half + 1, 0, length - take
            return found

        own_clear = clear_all[2 * count + layer * BAND : 2 * count + (layer + 1) * BAND]
        low = below[layer]
        clear = jnp.concatenate(
            ([clear_all[low : low + side]] if side else [])
            + [own_clear]
            + ([clear_all[low + side : low + 2 * side]] if side else []),
            axis=0,
        )
        for tile in range(TILES):
            span = slice(tile * height, (tile + 1) * height)
            lanes = slice(tile * LANES, (tile + 1) * LANES)
            for part in range(2):
                pieces = [stereo[part, layer * BAND : (layer + 1) * BAND, lanes]]
                if side:
                    pieces = (
                        halo_rows(low, side, tile, part)
                        + pieces
                        + halo_rows(low + side, side, tile, part)
                    )
                added = jnp.concatenate(pieces, axis=0)
                value = columned[span, part * LANES : (part + 1) * LANES]
                value = clear[:, lanes] * value + added
                field[part, :height, lanes] = value.astype(jnp.bfloat16)
        for part in range(2):
            out[layer, part] = field[part, side : side + BAND]


def exchanged(value, axis, by, phase):
    count = lax.axis_size(axis)
    lower = [i for i in range(count - by) if (i // by) % 2 == phase]
    pairs = [(i, i + by) for i in lower] + [(i + by, i) for i in lower]
    return lax.ppermute(value, axis, pairs)


def call(kernel, out_shape, in_specs, scratch=(), flops=0, moved=10**6):
    vmem = pl.BlockSpec(memory_space=pltpu.VMEM)
    many = isinstance(out_shape, (tuple, list))
    return pl.pallas_call(
        kernel,
        out_shape=out_shape,
        in_specs=in_specs,
        out_specs=(vmem,) * len(out_shape) if many else vmem,
        scratch_shapes=scratch,
        compiler_params=pltpu.CompilerParams(vmem_limit_bytes=VMEM_LIMIT),
        cost_estimate=pl.CostEstimate(flops=flops, bytes_accessed=moved, transcendentals=0),
    )


def body(incident, row_taps, col_taps, hogel_light, silhouette, fill_counts, hogel_index):
    vmem = pl.BlockSpec(memory_space=pltpu.VMEM)
    hbm = pl.BlockSpec(memory_space=pltpu.HBM)
    bf16, f32 = jnp.bfloat16, jnp.float32
    shaped = jax.ShapeDtypeStruct
    held = [
        pltpu.VMEM(hogel_index.shape, jnp.int32),
        pltpu.SMEM(fill_counts.shape, jnp.int32),
        pltpu.VMEM(silhouette.shape, jnp.int32),
        pltpu.VMEM(row_taps.shape, bf16),
        pltpu.VMEM(col_taps.shape, bf16),
        pltpu.VMEM(hogel_light.shape, f32),
    ]
    payload = call(
        pack_kernel,
        shaped((LAYERS, BAND, FULL_W), bf16),
        [hbm] * 6,
        held + [pltpu.SemaphoreType.DMA((6,)), pltpu.VMEM((BAND, LANES), f32)],
        flops=10**7,
    )(hogel_light, silhouette, fill_counts, hogel_index, row_taps, col_taps)
    own = lax.all_to_all(payload, "depth", 0, 0, tiled=True)
    colour = jnp.minimum(lax.axis_index("depth"), COLORS - 1)
    mine = lax.dynamic_index_in_dim(incident, colour, 0, keepdims=False)
    near = shaped((NEAR + 2 * BAND, HALO_W), bf16)
    far = shaped((FAR + 2 * BAND, HALO_W), bf16)
    in_chip, cross, far_even, far_odd = call(halo_kernel, (near, near, far, far), [vmem] * 2)(
        own, mine
    )
    cross = exchanged(cross, "rows", 1, 1)
    far_even = exchanged(far_even, "rows", 2, 0)
    far_odd = exchanged(far_odd, "rows", 2, 1)
    in_chip = exchanged(in_chip, "rows", 1, 0)
    tables = [jnp.asarray(left_table()), jnp.asarray(right_table())]
    made = call(
        prepare_kernel,
        [shaped((LAYERS, 2 * LANES, 4 * LANES), bf16), shaped((2, LANES, COLS), f32)]
        + [shaped((2 * block_height(layer), 2 * LANES), bf16) for layer in range(LAYERS)],
        [vmem] * 3,
        flops=3 * 10**8,
        moved=3 * 10**6,
    )(own, *tables)
    result = call(
        chain_kernel,
        shaped((LAYERS, 2, BAND, COLS), bf16),
        [vmem] * (8 + len(made)),
        [pltpu.VMEM((2, layer_height(0), COLS), bf16)]
        + [pltpu.VMEM(near.shape, bf16)] * 2
        + [pltpu.VMEM(far.shape, bf16)] * 2,
        flops=3 * 10**9,
        moved=3 * 10**6,
    )(own, mine, in_chip, cross, far_even, far_odd, *tables, *made)
    gathered = lax.all_to_all(result, "depth", 0, 0, tiled=True)
    return gathered[None, :COLORS]


def solution(mesh):
    placed = (
        P(None, None, "rows", None),
        P("depth", None, None, None),
        P("depth", None, None, None),
        P("depth", None, "rows", None),
        P("depth", "rows", None),
        P("depth", "rows"),
        P("depth", "rows", None),
    )
    return jax.shard_map(
        body,
        mesh=mesh,
        in_specs=placed,
        out_specs=P("depth", None, None, "rows", None),
        check_vma=False,
    )
```

```python
import math

import jax
import jax.numpy as jnp
import numpy as np
from jax import lax
from jax.experimental import pallas as pl
from jax.experimental.pallas import tpu as pltpu
from jax.sharding import PartitionSpec as P

HS = 16
KR = 16
KC = 63
COLORS = 3
LAYERS = 4
BAND = 32
COLS = 1024
NH = COLS // HS
LANES = 128
TILES = COLS // LANES
HALO_W = COLS + LANES
HALF = LANES // 2
FULL_W = COLS + 2 * LANES
NEAR = 2 * BAND + KR
FAR = KR
VMEM_LIMIT = 48 * 1024 * 1024
PACK_LIMIT = 63 * 1024 * 1024


def split_table(table):
    high = table.astype(jnp.bfloat16)
    low = (table - high.astype(np.float64)).astype(jnp.bfloat16)
    return high, low


def dft_pair():
    counter = np.arange(HS)
    angles = (counter[:, None] * counter[None, :] % HS) * (2.0 * math.pi / HS)
    return np.cos(angles) / math.sqrt(HS), np.sin(angles) / math.sqrt(HS)


def left_table(height):
    cos_tab, sin_tab = dft_pair()
    eye = np.eye(height // HS)
    full = np.concatenate([np.kron(eye, cos_tab), np.kron(eye, -sin_tab)], axis=0)
    return np.concatenate(split_table(full), axis=1)


def right_table():
    cos_tab, sin_tab = dft_pair()
    eye = np.eye(LANES // HS)
    cos_big, sin_big = np.kron(eye, cos_tab), np.kron(eye, sin_tab)
    full = np.concatenate(
        [
            np.concatenate([cos_big, -sin_big], axis=1),
            np.concatenate([sin_big, cos_big], axis=1),
        ],
        axis=0,
    )
    return full.astype(jnp.bfloat16)


def layer_height(layer):
    return BAND + 2 * KR * (LAYERS - 1 - layer)


def block_height(layer):
    height = layer_height(layer)
    return height // 2 if 2 * (height + 2 * KR) > 2 * LANES else height


def spread_matrix():
    tile = lax.broadcasted_iota(jnp.int32, (NH, COLS), 0)
    column = lax.broadcasted_iota(jnp.int32, (NH, COLS), 1)
    return jnp.where(column // HS == tile, 1.0, 0.0).astype(jnp.bfloat16)


def pack_kernel(light, edges, counts, listed, row_taps, col_taps, out, *scratch):
    held, sems, taps = scratch[:6], scratch[6], scratch[7]
    sources = (listed, counts, edges, row_taps, col_taps, light)
    copies = [
        pltpu.make_async_copy(source, target, sems.at[place])
        for place, (source, target) in enumerate(zip(sources, held))
    ]
    for copy in reversed(copies):
        copy.start()
    listed, counts, edges, row_taps, col_taps, light = held
    spread = spread_matrix()
    slot = lax.broadcasted_iota(jnp.int32, (NH, NH), 0)
    place = lax.broadcasted_iota(jnp.int32, (NH, NH), 1)
    for copy in copies[:5]:
        copy.wait()
    rows = []
    for group in range(BAND // HS):
        listing = jnp.broadcast_to(listed[0, group : group + 1, :], (NH, NH))
        column = jnp.sum(jnp.where(slot == place, listing, 0), axis=1, keepdims=True)
        named = (column == place) & (slot < counts[0, group])
        live = jnp.max(jnp.where(named, 1.0, 0.0), axis=0, keepdims=True)
        rows.append(jnp.broadcast_to(live, (HS, NH)))
    live_rows = jnp.concatenate(rows, axis=0).astype(jnp.bfloat16)
    live_pix = jnp.dot(live_rows, spread, preferred_element_type=jnp.float32)
    edge_tile = jnp.concatenate(
        [edges[0].astype(jnp.float32), jnp.zeros((BAND, LANES - NH), jnp.float32)], axis=1
    ).astype(jnp.bfloat16)
    for colour in range(COLORS):
        out[colour, :, COLS:HALO_W] = edge_tile
        taps[...] = jnp.zeros_like(taps)
        taps[0:2, : 2 * KC + 1] = col_taps[0, colour].astype(jnp.float32)
        taps[2:4, : 2 * KR + 1] = row_taps[0, colour].astype(jnp.float32)
        out[colour, :, HALO_W:] = taps[...].astype(jnp.bfloat16)
    for spare in range(COLORS, LAYERS):
        out[spare] = jnp.zeros((BAND, FULL_W), jnp.bfloat16)
    copies[5].wait()
    for colour in range(COLORS):
        out[colour, :, :COLS] = (light[0, colour] * live_pix).astype(jnp.bfloat16)


def halo_kernel(own, in_chip, cross, far_even, far_odd):
    band = lax.axis_index("rows")
    core = band % 2
    odd = (band // 2) % 2
    last = BAND - KR
    for near, start in ((in_chip, (1 - core) * last), (cross, core * last)):
        near[0:BAND] = own[0, :, :HALO_W]
        near[BAND : 2 * BAND] = own[1, :, :HALO_W]
        near[2 * BAND : NEAR] = own[2, pl.ds(pl.multiple_of(start, KR), KR), :HALO_W]
    for far, start in ((far_even, (1 - odd) * last), (far_odd, odd * last)):
        far[...] = own[0, pl.ds(pl.multiple_of(start, KR), KR), :HALO_W]


def ordered(in_chip, cross, far_even, far_odd):
    band = lax.axis_index("rows")
    even_core = band % 2 == 0
    even_chip = (band // 2) % 2 == 0
    in_chip, cross = in_chip[...], cross[...]
    far_even, far_odd = far_even[...], far_odd[...]
    return (
        jnp.where(even_core, cross, in_chip),
        jnp.where(even_core, in_chip, cross),
        jnp.where(even_chip, far_odd, far_even),
        jnp.where(even_chip, far_even, far_odd),
    )


def tiles_below(value, height):
    return jnp.concatenate(
        [
            jnp.concatenate(
                [
                    value[:height, tile * LANES : (tile + 1) * LANES],
                    value[height:, tile * LANES : (tile + 1) * LANES],
                ],
                axis=1,
            )
            for tile in range(TILES)
        ],
        axis=0,
    )


def stereo_tiles(blocks, left_tab, right_tab):
    arranged = []
    for light in blocks:
        doubled = jnp.concatenate([light, light], axis=0)
        left = jnp.dot(left_tab[...], doubled, preferred_element_type=jnp.float32)
        arranged.append(tiles_below(left.astype(jnp.bfloat16), light.shape[0]))
    arranged = jnp.concatenate(arranged, axis=0) if len(arranged) > 1 else arranged[0]
    return jnp.dot(arranged, right_tab[...], preferred_element_type=jnp.float32)


def clear_pixels(edges):
    edge_pix = jnp.dot(edges, spread_matrix(), preferred_element_type=jnp.float32)
    within = (lax.broadcasted_iota(jnp.int32, (1, COLS), 1) % HS).astype(jnp.float32)
    return jnp.where(within < edge_pix, 1.0, 0.0)


def banded(line, count, shift):
    base = jnp.concatenate([line, jnp.zeros((1, LANES), jnp.float32)], axis=1)
    base = jnp.broadcast_to(base, (count, 2 * LANES))
    return pltpu.roll(base, shift, 1, stride=1, stride_axis=0)


def filters(taps, layer):
    row_re, row_im = taps[2:3], taps[3:4]
    height = block_height(layer)
    before = height + 2 * KR
    upper = banded(row_re, height, 0) - banded(row_im, height, before)
    lower = banded(row_im, height, 0) + banded(row_re, height, before)
    row_mat = jnp.concatenate([upper, lower], axis=0).astype(jnp.bfloat16)
    col_re = banded(taps[0:1], LANES, 1)
    col_im = banded(taps[1:2], LANES, 1)
    upper = jnp.concatenate([col_re, -col_im], axis=1)
    lower = jnp.concatenate([col_im, col_re], axis=1)
    col_mat = jnp.concatenate([upper, lower], axis=0).astype(jnp.bfloat16)
    return row_mat, col_mat


def propagated(u_re, u_im, row_mat, col_mat, layer):
    height = layer_height(layer)
    block = block_height(layer)
    reach = block + 2 * KR
    parts = []
    for start in range(0, height, block):
        stacked = jnp.concatenate(
            [u_re[start : start + reach], u_im[start : start + reach]], axis=0
        )
        parts.append(
            jnp.dot(row_mat[:, : 2 * reach], stacked, preferred_element_type=jnp.float32)
        )
    rowed = jnp.concatenate(
        [part[:block] for part in parts] + [part[block:] for part in parts], axis=0
    )
    rowed = jnp.concatenate([rowed, jnp.zeros((2 * height, LANES), jnp.float32)], axis=1)
    rowed = pltpu.roll(rowed, HALF, 1).astype(jnp.bfloat16)
    windows = jnp.concatenate(
        [
            jnp.concatenate(
                [
                    rowed[:height, tile * LANES : (tile + 2) * LANES],
                    rowed[height:, tile * LANES : (tile + 2) * LANES],
                ],
                axis=1,
            )
            for tile in range(TILES)
        ],
        axis=0,
    )
    return lax.dot_general(
        windows, col_mat, (((1,), (1,)), ((), ())), preferred_element_type=jnp.float32
    )


def prepare_kernel(
    own, incident, in_chip, cross, far_even, far_odd, left_tab, right_tab,
    first, stereo, clear, col_mats, *row_mats
):
    low_near, high_near, low_far, high_far = ordered(in_chip, cross, far_even, far_odd)
    extended = []
    for part in range(2):
        pieces = [low_far, low_near, incident[...], high_near, high_far]
        pieces = [piece[part * BAND : (part + 1) * BAND] for piece in pieces]
        extended.append(jnp.concatenate(pieces, axis=0))
    row_mat, col_mat = filters(own[0, 0:16, HALO_W:].astype(jnp.float32), 0)
    first[...] = propagated(extended[0], extended[1], row_mat, col_mat, 0)
    for layer in range(1, LAYERS):
        row_mat, col_mat = filters(own[layer, 0:16, HALO_W:].astype(jnp.float32), layer)
        row_mats[layer - 1][...] = row_mat
        col_mats[layer - 1] = col_mat
    packed = jnp.concatenate([own[layer, :, :HALO_W] for layer in range(LAYERS)], axis=0)
    clear[...] = clear_pixels(packed[:, COLS : COLS + NH])
    tiles = stereo_tiles([packed[:, :COLS]], left_tab, right_tab)
    for tile in range(TILES):
        for part in range(2):
            block = tiles[
                tile * LANES : (tile + 1) * LANES, part * LANES : (part + 1) * LANES
            ]
            stereo[part, :, tile * LANES : (tile + 1) * LANES] = block


def chain_kernel(
    in_chip, cross, far_even, far_odd, left_tab, right_tab, first, stereo, clear, col_mats, *rest
):
    row_mats, (out, field) = rest[: LAYERS - 1], rest[LAYERS - 1 :]
    low_near, high_near, low_far, high_far = ordered(in_chip, cross, far_even, far_odd)
    pieces = [
        low_far,
        low_near[0:BAND],
        high_near[0:BAND],
        high_far,
        low_near[BAND : 2 * BAND],
        high_near[BAND : 2 * BAND],
        low_near[2 * BAND : NEAR],
        high_near[2 * BAND : NEAR],
    ]
    halo = jnp.concatenate(pieces, axis=0)
    half = halo.shape[0] // 2
    halo_tiles = stereo_tiles(
        [halo[:half, :COLS], halo[half:, :COLS]], left_tab, right_tab
    )
    halo_clear = clear_pixels(halo[:, COLS : COLS + NH])
    begins = (0, half, half + 2 * BAND, 0)
    sides = (BAND + FAR, BAND, KR, 0)
    for layer in range(LAYERS):
        height = layer_height(layer)
        before = height + 2 * KR
        low, side = begins[layer], sides[layer]
        if layer == 0:
            columned = first
        else:
            columned = propagated(
                field[0, :before], field[1, :before], row_mats[layer - 1], col_mats[layer - 1], layer
            )
        band = slice(layer * BAND, (layer + 1) * BAND)
        pieces = [clear[band]]
        if side:
            pieces = [halo_clear[low : low + side], clear[band], halo_clear[low + side : low + 2 * side]]
        passing = jnp.concatenate(pieces, axis=0)
        for tile in range(TILES):
            span = slice(tile * height, (tile + 1) * height)
            lanes = slice(tile * LANES, (tile + 1) * LANES)
            row = (low // half * TILES + tile) * half + low % half
            for part in range(2):
                within = slice(part * LANES, (part + 1) * LANES)
                pieces = [stereo[part, band, lanes]]
                if side:
                    pieces = [
                        halo_tiles[row : row + side, within],
                        stereo[part, band, lanes],
                        halo_tiles[row + side : row + 2 * side, within],
                    ]
                added = jnp.concatenate(pieces, axis=0)
                value = passing[:, lanes] * columned[span, within] + added
                field[part, :height, lanes] = value.astype(jnp.bfloat16)
        for part in range(2):
            out[layer, part] = field[part, side : side + BAND]


def exchanged(value, axis, by, phase):
    count = lax.axis_size(axis)
    lower = [i for i in range(count - by) if (i // by) % 2 == phase]
    pairs = [(i, i + by) for i in lower] + [(i + by, i) for i in lower]
    return lax.ppermute(value, axis, pairs)


def neighbours(sent):
    in_chip, cross, far_even, far_odd = sent
    cross = exchanged(cross, "rows", 1, 1)
    far_even = exchanged(far_even, "rows", 2, 0)
    far_odd = exchanged(far_odd, "rows", 2, 1)
    in_chip = exchanged(in_chip, "rows", 1, 0)
    return in_chip, cross, far_even, far_odd


def call(kernel, out_shape, in_specs, scratch=(), flops=0, moved=10**6, limit=VMEM_LIMIT):
    vmem = pl.BlockSpec(memory_space=pltpu.VMEM)
    many = isinstance(out_shape, (tuple, list))
    return pl.pallas_call(
        kernel,
        out_shape=out_shape,
        in_specs=in_specs,
        out_specs=(vmem,) * len(out_shape) if many else vmem,
        scratch_shapes=scratch,
        compiler_params=pltpu.CompilerParams(vmem_limit_bytes=limit),
        cost_estimate=pl.CostEstimate(flops=flops, bytes_accessed=moved, transcendentals=0),
    )


def body(incident, row_taps, col_taps, hogel_light, silhouette, fill_counts, hogel_index):
    vmem = pl.BlockSpec(memory_space=pltpu.VMEM)
    hbm = pl.BlockSpec(memory_space=pltpu.HBM)
    bf16, f32 = jnp.bfloat16, jnp.float32
    shaped = jax.ShapeDtypeStruct
    held = [
        pltpu.VMEM(hogel_index.shape, jnp.int32),
        pltpu.SMEM(fill_counts.shape, jnp.int32),
        pltpu.VMEM(silhouette.shape, jnp.int32),
        pltpu.VMEM(row_taps.shape, bf16),
        pltpu.VMEM(col_taps.shape, bf16),
        pltpu.VMEM(hogel_light.shape, f32),
    ]
    payload = call(
        pack_kernel,
        shaped((LAYERS, BAND, FULL_W), bf16),
        [hbm] * 6,
        held + [pltpu.SemaphoreType.DMA((6,)), pltpu.VMEM((BAND, LANES), f32)],
        flops=10**7,
        limit=PACK_LIMIT,
    )(hogel_light, silhouette, fill_counts, hogel_index, row_taps, col_taps)
    colour = jnp.minimum(lax.axis_index("depth"), COLORS - 1)
    mine = lax.dynamic_index_in_dim(incident, colour, 0, keepdims=False)
    mine = mine.reshape(2 * BAND, COLS)
    payload, mine = lax.optimization_barrier((payload, mine))
    own = lax.all_to_all(payload, "depth", 0, 0, tiled=True)
    arrived = neighbours((mine,) * 4)
    near = shaped((NEAR, HALO_W), bf16)
    far = shaped((FAR, HALO_W), bf16)
    halos = neighbours(call(halo_kernel, (near, near, far, far), [vmem])(own))
    right_tab = jnp.asarray(right_table())
    made = call(
        prepare_kernel,
        [
            shaped((TILES * layer_height(0), 2 * LANES), f32),
            shaped((2, LANES, COLS), f32),
            shaped((LANES, COLS), f32),
            shaped((LAYERS - 1, 2 * LANES, 4 * LANES), bf16),
        ]
        + [shaped((2 * block_height(layer), 2 * LANES), bf16) for layer in range(1, LAYERS)],
        [vmem] * 8,
        flops=10**9,
        moved=3 * 10**6,
    )(own, mine, *arrived, jnp.asarray(left_table(LANES)), right_tab)
    halo_rows = NEAR + FAR
    result = call(
        chain_kernel,
        shaped((LAYERS, 2, BAND, COLS), bf16),
        [vmem] * (6 + len(made)),
        [pltpu.VMEM((2, layer_height(0), COLS), bf16)],
        flops=2 * 10**9,
        moved=3 * 10**6,
    )(*halos, jnp.asarray(left_table(halo_rows)), right_tab, *made)
    gathered = lax.all_to_all(result, "depth", 0, 0, tiled=True)
    return gathered[None, :COLORS]


def solution(mesh):
    placed = (
        P(None, None, "rows", None),
        P("depth", None, None, None),
        P("depth", None, None, None),
        P("depth", None, "rows", None),
        P("depth", "rows", None),
        P("depth", "rows"),
        P("depth", "rows", None),
    )
    return jax.shard_map(
        body,
        mesh=mesh,
        in_specs=placed,
        out_specs=P("depth", None, None, "rows", None),
        check_vma=False,
    )
```

```python
import math

import jax
import jax.numpy as jnp
import numpy as np
from jax import lax
from jax.experimental import pallas as pl
from jax.experimental.pallas import tpu as pltpu
from jax.sharding import PartitionSpec as P

HS = 16
KR = 16
KC = 63
COLORS = 3
LAYERS = 4
BAND = 32
COLS = 1024
NH = COLS // HS
LANES = 128
TILES = COLS // LANES
HALO_W = COLS + LANES
HALF = LANES // 2
FULL_W = COLS + 2 * LANES
NEAR = 2 * BAND + KR
FAR = KR
VMEM_LIMIT = 48 * 1024 * 1024
PACK_LIMIT = 63 * 1024 * 1024


def split_table(table):
    high = table.astype(jnp.bfloat16)
    low = (table - high.astype(np.float64)).astype(jnp.bfloat16)
    return high, low


def dft_pair():
    counter = np.arange(HS)
    angles = (counter[:, None] * counter[None, :] % HS) * (2.0 * math.pi / HS)
    return np.cos(angles) / math.sqrt(HS), np.sin(angles) / math.sqrt(HS)


def left_table(height):
    cos_tab, sin_tab = dft_pair()
    eye = np.eye(height // HS)
    full = np.concatenate([np.kron(eye, cos_tab), np.kron(eye, -sin_tab)], axis=0)
    return np.concatenate(split_table(full), axis=1)


def right_table():
    cos_tab, sin_tab = dft_pair()
    eye = np.eye(LANES // HS)
    cos_big, sin_big = np.kron(eye, cos_tab), np.kron(eye, sin_tab)
    full = np.concatenate(
        [
            np.concatenate([cos_big, -sin_big], axis=1),
            np.concatenate([sin_big, cos_big], axis=1),
        ],
        axis=0,
    )
    return full.astype(jnp.bfloat16)


def layer_height(layer):
    return BAND + 2 * KR * (LAYERS - 1 - layer)


def block_height(layer):
    height = layer_height(layer)
    return height // 2 if 2 * (height + 2 * KR) > 2 * LANES else height


def spread_matrix():
    tile = lax.broadcasted_iota(jnp.int32, (NH, COLS), 0)
    column = lax.broadcasted_iota(jnp.int32, (NH, COLS), 1)
    return jnp.where(column // HS == tile, 1.0, 0.0).astype(jnp.bfloat16)


def own_colour():
    return jnp.maximum(lax.axis_index("depth") - (LAYERS - COLORS), 0)


def pack_kernel(light, edges, counts, listed, row_taps, col_taps, incident, out, mine, *scratch):
    held, sems, taps = scratch[:6], scratch[6], scratch[7]
    picked = pltpu.make_async_copy(incident.at[own_colour()], mine, sems.at[6])
    sources = (listed, counts, edges, row_taps, col_taps, light)
    copies = [
        pltpu.make_async_copy(source, target, sems.at[place])
        for place, (source, target) in enumerate(zip(sources, held))
    ]
    for copy in reversed(copies):
        copy.start()
    picked.start()
    listed, counts, edges, row_taps, col_taps, light = held
    spread = spread_matrix()
    slot = lax.broadcasted_iota(jnp.int32, (NH, NH), 0)
    place = lax.broadcasted_iota(jnp.int32, (NH, NH), 1)
    for copy in copies[:5]:
        copy.wait()
    rows = []
    for group in range(BAND // HS):
        listing = jnp.broadcast_to(listed[0, group : group + 1, :], (NH, NH))
        column = jnp.sum(jnp.where(slot == place, listing, 0), axis=1, keepdims=True)
        named = (column == place) & (slot < counts[0, group])
        live = jnp.max(jnp.where(named, 1.0, 0.0), axis=0, keepdims=True)
        rows.append(jnp.broadcast_to(live, (HS, NH)))
    live_rows = jnp.concatenate(rows, axis=0).astype(jnp.bfloat16)
    live_pix = jnp.dot(live_rows, spread, preferred_element_type=jnp.float32)
    edge_tile = jnp.concatenate(
        [edges[0].astype(jnp.float32), jnp.zeros((BAND, LANES - NH), jnp.float32)], axis=1
    ).astype(jnp.bfloat16)
    for colour in range(COLORS):
        chunk = colour + LAYERS - COLORS
        out[chunk, :, COLS:HALO_W] = edge_tile
        taps[...] = jnp.zeros_like(taps)
        taps[0:2, : 2 * KC + 1] = col_taps[0, colour].astype(jnp.float32)
        taps[2:4, : 2 * KR + 1] = row_taps[0, colour].astype(jnp.float32)
        out[chunk, :, HALO_W:] = taps[...].astype(jnp.bfloat16)
    for spare in range(LAYERS - COLORS):
        out[spare] = jnp.zeros((BAND, FULL_W), jnp.bfloat16)
    copies[5].wait()
    for colour in range(COLORS):
        chunk = colour + LAYERS - COLORS
        out[chunk, :, :COLS] = (light[0, colour] * live_pix).astype(jnp.bfloat16)
    picked.wait()


def halo_kernel(own, incident, beyond, in_chip, cross, far_even, far_odd):
    band = lax.axis_index("rows")
    core = band % 2
    odd = (band // 2) % 2
    last = BAND - KR
    for near, start in ((in_chip, (1 - core) * last), (cross, core * last)):
        near[0:BAND] = own[0, :, :HALO_W]
        near[BAND : 2 * BAND] = own[1, :, :HALO_W]
        near[2 * BAND : NEAR] = own[2, pl.ds(pl.multiple_of(start, KR), KR), :HALO_W]
    in_chip[NEAR : NEAR + BAND, :COLS] = incident[0]
    in_chip[NEAR + BAND : NEAR + 2 * BAND, :COLS] = incident[1]
    in_chip[NEAR + 2 * BAND :, :COLS] = beyond[...]
    for far, start in ((far_even, (1 - odd) * last), (far_odd, odd * last)):
        far[...] = own[0, pl.ds(pl.multiple_of(start, KR), KR), :HALO_W]


def ordered(in_chip, cross, far_even, far_odd):
    band = lax.axis_index("rows")
    even_core = band % 2 == 0
    even_chip = (band // 2) % 2 == 0
    in_chip, cross = in_chip[:NEAR], cross[...]
    far_even, far_odd = far_even[...], far_odd[...]
    return (
        jnp.where(even_core, cross, in_chip),
        jnp.where(even_core, in_chip, cross),
        jnp.where(even_chip, far_odd, far_even),
        jnp.where(even_chip, far_even, far_odd),
    )


def tiles_below(value, height):
    return jnp.concatenate(
        [
            jnp.concatenate(
                [
                    value[:height, tile * LANES : (tile + 1) * LANES],
                    value[height:, tile * LANES : (tile + 1) * LANES],
                ],
                axis=1,
            )
            for tile in range(TILES)
        ],
        axis=0,
    )


def stereo_tiles(blocks, left_tab, right_tab):
    arranged = []
    for light in blocks:
        doubled = jnp.concatenate([light, light], axis=0)
        left = jnp.dot(left_tab[...], doubled, preferred_element_type=jnp.float32)
        arranged.append(tiles_below(left.astype(jnp.bfloat16), light.shape[0]))
    arranged = jnp.concatenate(arranged, axis=0) if len(arranged) > 1 else arranged[0]
    return jnp.dot(arranged, right_tab[...], preferred_element_type=jnp.float32)


def clear_pixels(edges):
    edge_pix = jnp.dot(edges, spread_matrix(), preferred_element_type=jnp.float32)
    within = (lax.broadcasted_iota(jnp.int32, (1, COLS), 1) % HS).astype(jnp.float32)
    return jnp.where(within < edge_pix, 1.0, 0.0)


def banded(line, count, shift):
    base = jnp.concatenate([line, jnp.zeros((1, LANES), jnp.float32)], axis=1)
    base = jnp.broadcast_to(base, (count, 2 * LANES))
    return pltpu.roll(base, shift, 1, stride=1, stride_axis=0)


def filters(taps, layer):
    row_re, row_im = taps[2:3], taps[3:4]
    height = block_height(layer)
    before = height + 2 * KR
    upper = banded(row_re, height, 0) - banded(row_im, height, before)
    lower = banded(row_im, height, 0) + banded(row_re, height, before)
    row_mat = jnp.concatenate([upper, lower], axis=0).astype(jnp.bfloat16)
    col_re = banded(taps[0:1], LANES, 1)
    col_im = banded(taps[1:2], LANES, 1)
    upper = jnp.concatenate([col_re, -col_im], axis=1)
    lower = jnp.concatenate([col_im, col_re], axis=1)
    col_mat = jnp.concatenate([upper, lower], axis=0).astype(jnp.bfloat16)
    return row_mat, col_mat


def propagated(u_re, u_im, row_mat, col_mat, layer):
    height = layer_height(layer)
    block = block_height(layer)
    reach = block + 2 * KR
    parts = []
    for start in range(0, height, block):
        stacked = jnp.concatenate(
            [u_re[start : start + reach], u_im[start : start + reach]], axis=0
        )
        parts.append(
            jnp.dot(row_mat[:, : 2 * reach], stacked, preferred_element_type=jnp.float32)
        )
    rowed = jnp.concatenate(
        [part[:block] for part in parts] + [part[block:] for part in parts], axis=0
    )
    rowed = jnp.concatenate([rowed, jnp.zeros((2 * height, LANES), jnp.float32)], axis=1)
    rowed = pltpu.roll(rowed, HALF, 1).astype(jnp.bfloat16)
    windows = jnp.concatenate(
        [
            jnp.concatenate(
                [
                    rowed[:height, tile * LANES : (tile + 2) * LANES],
                    rowed[height:, tile * LANES : (tile + 2) * LANES],
                ],
                axis=1,
            )
            for tile in range(TILES)
        ],
        axis=0,
    )
    return lax.dot_general(
        windows, col_mat, (((1,), (1,)), ((), ())), preferred_element_type=jnp.float32
    )


def prepare_kernel(
    own, incident, in_chip, cross, far, left_tab, right_tab,
    first, stereo, clear, col_mats, *row_mats
):
    even_core = lax.axis_index("rows") % 2 == 0
    cross, far = cross[...], far[...]
    partner = in_chip[NEAR : NEAR + 2 * BAND, :COLS]
    beyond = in_chip[NEAR + 2 * BAND :, :COLS]
    sides = (
        jnp.where(even_core, far, beyond),
        jnp.where(even_core, cross, partner),
        jnp.where(even_core, partner, cross),
        jnp.where(even_core, beyond, far),
    )
    extended = []
    for part in range(2):
        low_far, low_near, high_near, high_far = (
            side[part * BAND : (part + 1) * BAND] for side in sides
        )
        pieces = [low_far, low_near, incident[part], high_near, high_far]
        extended.append(jnp.concatenate(pieces, axis=0))
    row_mat, col_mat = filters(own[0, 0:16, HALO_W:].astype(jnp.float32), 0)
    first[...] = propagated(extended[0], extended[1], row_mat, col_mat, 0)
    for layer in range(1, LAYERS):
        row_mat, col_mat = filters(own[layer, 0:16, HALO_W:].astype(jnp.float32), layer)
        row_mats[layer - 1][...] = row_mat
        col_mats[layer - 1] = col_mat
    packed = jnp.concatenate([own[layer, :, :HALO_W] for layer in range(LAYERS)], axis=0)
    clear[...] = clear_pixels(packed[:, COLS : COLS + NH])
    tiles = stereo_tiles([packed[:, :COLS]], left_tab, right_tab)
    for tile in range(TILES):
        for part in range(2):
            block = tiles[
                tile * LANES : (tile + 1) * LANES, part * LANES : (part + 1) * LANES
            ]
            stereo[part, :, tile * LANES : (tile + 1) * LANES] = block


def chain_kernel(
    in_chip, cross, far_even, far_odd, left_tab, right_tab, first, stereo, clear, col_mats, *rest
):
    row_mats, outs, field = rest[: LAYERS - 1], rest[LAYERS - 1 : -1], rest[-1]
    depth = lax.axis_index("depth")
    low_near, high_near, low_far, high_far = ordered(in_chip, cross, far_even, far_odd)
    pieces = [
        low_far,
        low_near[0:BAND],
        high_near[0:BAND],
        high_far,
        low_near[BAND : 2 * BAND],
        high_near[BAND : 2 * BAND],
        low_near[2 * BAND : NEAR],
        high_near[2 * BAND : NEAR],
    ]
    halo = jnp.concatenate(pieces, axis=0)
    half = halo.shape[0] // 2
    halo_tiles = stereo_tiles(
        [halo[:half, :COLS], halo[half:, :COLS]], left_tab, right_tab
    )
    halo_clear = clear_pixels(halo[:, COLS : COLS + NH])
    begins = (0, half, half + 2 * BAND, 0)
    sides = (BAND + FAR, BAND, KR, 0)
    for layer in range(LAYERS):
        height = layer_height(layer)
        before = height + 2 * KR
        low, side = begins[layer], sides[layer]
        if layer == 0:
            columned = first
        else:
            columned = propagated(
                field[0, :before], field[1, :before], row_mats[layer - 1], col_mats[layer - 1], layer
            )
        band = slice(layer * BAND, (layer + 1) * BAND)
        pieces = [clear[band]]
        if side:
            pieces = [halo_clear[low : low + side], clear[band], halo_clear[low + side : low + 2 * side]]
        passing = jnp.concatenate(pieces, axis=0)
        for tile in range(TILES):
            span = slice(tile * height, (tile + 1) * height)
            lanes = slice(tile * LANES, (tile + 1) * LANES)
            row = (low // half * TILES + tile) * half + low % half
            for part in range(2):
                within = slice(part * LANES, (part + 1) * LANES)
                pieces = [stereo[part, band, lanes]]
                if side:
                    pieces = [
                        halo_tiles[row : row + side, within],
                        stereo[part, band, lanes],
                        halo_tiles[row + side : row + 2 * side, within],
                    ]
                added = jnp.concatenate(pieces, axis=0)
                value = passing[:, lanes] * columned[span, within] + added
                field[part, :height, lanes] = value.astype(jnp.bfloat16)
        for hop, out in enumerate(outs):

            @pl.when((depth + hop) % LAYERS == layer)
            def keep(out=out, side=side):
                for part in range(2):
                    out[part] = field[part, side : side + BAND]


def home_kernel(*refs):
    arrived, out, sems = refs[:LAYERS], refs[LAYERS], refs[LAYERS + 1]
    depth = lax.axis_index("depth")
    for colour in range(COLORS):
        source = colour + LAYERS - COLORS
        for hop in range(LAYERS):

            @pl.when((source + hop) % LAYERS == depth)
            def begin(hop=hop, colour=colour):
                pltpu.make_async_copy(arrived[hop], out.at[0, colour], sems.at[colour]).start()

    for colour in range(COLORS):
        pltpu.make_async_copy(arrived[0], out.at[0, colour], sems.at[colour]).wait()


def exchanged(value, axis, by, phase):
    count = lax.axis_size(axis)
    lower = [i for i in range(count - by) if (i // by) % 2 == phase]
    pairs = [(i, i + by) for i in lower] + [(i + by, i) for i in lower]
    return lax.ppermute(value, axis, pairs)


def far_incident(value):
    count = lax.axis_size("rows")
    pairs = [(i, i + 2) for i in range(0, count - 2, 2)]
    pairs += [(i, i - 2) for i in range(3, count, 2)]
    return lax.ppermute(value, "rows", pairs)


def sent_home(value, hop):
    first = LAYERS - COLORS
    pairs = [(i, (i + hop) % LAYERS) for i in range(first, LAYERS)]
    return lax.ppermute(value, "depth", pairs)


def neighbours(sent):
    in_chip, cross, far_even, far_odd = sent
    in_chip = exchanged(in_chip, "rows", 1, 0)
    cross = exchanged(cross, "rows", 1, 1)
    far_even = exchanged(far_even, "rows", 2, 0)
    far_odd = exchanged(far_odd, "rows", 2, 1)
    return in_chip, cross, far_even, far_odd


def call(
    kernel, out_shape, in_specs, scratch=(), flops=0, moved=10**6, limit=VMEM_LIMIT,
    out_space=pltpu.VMEM,
):
    vmem = pl.BlockSpec(memory_space=out_space)
    many = isinstance(out_shape, (tuple, list))
    return pl.pallas_call(
        kernel,
        out_shape=out_shape,
        in_specs=in_specs,
        out_specs=(vmem,) * len(out_shape) if many else vmem,
        scratch_shapes=scratch,
        compiler_params=pltpu.CompilerParams(vmem_limit_bytes=limit),
        cost_estimate=pl.CostEstimate(flops=flops, bytes_accessed=moved, transcendentals=0),
    )


def body(incident, row_taps, col_taps, hogel_light, silhouette, fill_counts, hogel_index):
    vmem = pl.BlockSpec(memory_space=pltpu.VMEM)
    hbm = pl.BlockSpec(memory_space=pltpu.HBM)
    bf16, f32 = jnp.bfloat16, jnp.float32
    shaped = jax.ShapeDtypeStruct
    held = [
        pltpu.VMEM(hogel_index.shape, jnp.int32),
        pltpu.SMEM(fill_counts.shape, jnp.int32),
        pltpu.VMEM(silhouette.shape, jnp.int32),
        pltpu.VMEM(row_taps.shape, bf16),
        pltpu.VMEM(col_taps.shape, bf16),
        pltpu.VMEM(hogel_light.shape, f32),
    ]
    payload, mine = call(
        pack_kernel,
        (shaped((LAYERS, BAND, FULL_W), bf16), shaped(incident.shape[1:], bf16)),
        [hbm] * 7,
        held + [pltpu.SemaphoreType.DMA((7,)), pltpu.VMEM((BAND, LANES), f32)],
        flops=10**7,
        limit=PACK_LIMIT,
    )(hogel_light, silhouette, fill_counts, hogel_index, row_taps, col_taps, incident)
    flat = mine.reshape(2 * BAND, COLS)
    own = lax.all_to_all(payload, "depth", 0, 0, tiled=True)
    cross_in = exchanged(flat, "rows", 1, 1)
    far_in = far_incident(flat)
    chip = shaped((NEAR + 4 * BAND, HALO_W), bf16)
    near = shaped((NEAR, HALO_W), bf16)
    far = shaped((FAR, HALO_W), bf16)
    halos = neighbours(call(halo_kernel, (chip, near, far, far), [vmem] * 3)(own, mine, cross_in))
    right_tab = jnp.asarray(right_table())
    made = call(
        prepare_kernel,
        [
            shaped((TILES * layer_height(0), 2 * LANES), f32),
            shaped((2, LANES, COLS), f32),
            shaped((LANES, COLS), f32),
            shaped((LAYERS - 1, 2 * LANES, 4 * LANES), bf16),
        ]
        + [shaped((2 * block_height(layer), 2 * LANES), bf16) for layer in range(1, LAYERS)],
        [vmem] * 7,
        flops=10**9,
        moved=3 * 10**6,
    )(own, mine, halos[0], cross_in, far_in, jnp.asarray(left_table(LANES)), right_tab)
    halo_rows = NEAR + FAR
    results = call(
        chain_kernel,
        [shaped((2, BAND, COLS), bf16)] * LAYERS,
        [vmem] * (6 + len(made)),
        [pltpu.VMEM((2, layer_height(0), COLS), bf16)],
        flops=2 * 10**9,
        moved=3 * 10**6,
    )(*halos, jnp.asarray(left_table(halo_rows)), right_tab, *made)
    arrived = [results[0]] + [sent_home(results[hop], hop) for hop in (2, 1, 3)]
    arrived = [arrived[0], arrived[2], arrived[1], arrived[3]]
    return call(
        home_kernel,
        shaped((1, COLORS, 2, BAND, COLS), bf16),
        [vmem] * LAYERS,
        [pltpu.SemaphoreType.DMA((COLORS,))],
        out_space=pltpu.HBM,
    )(*arrived)


def solution(mesh):
    placed = (
        P(None, None, "rows", None),
        P("depth", None, None, None),
        P("depth", None, None, None),
        P("depth", None, "rows", None),
        P("depth", "rows", None),
        P("depth", "rows"),
        P("depth", "rows", None),
    )
    return jax.shard_map(
        body,
        mesh=mesh,
        in_specs=placed,
        out_specs=P("depth", None, None, "rows", None),
        check_vma=False,
    )
```

```python
import math

import jax
import jax.numpy as jnp
import numpy as np
from jax import lax
from jax.experimental import pallas as pl
from jax.experimental.pallas import tpu as pltpu
from jax.sharding import PartitionSpec as P

HS = 16
KR = 16
KC = 63
COLORS = 3
LAYERS = 4
BAND = 32
COLS = 1024
NH = COLS // HS
LANES = 128
TILES = COLS // LANES
HALO_W = COLS + LANES
HALF = LANES // 2
FULL_W = COLS + 2 * LANES
NEAR = 2 * BAND + KR
FAR = KR
VMEM_LIMIT = 48 * 1024 * 1024
PACK_LIMIT = 63 * 1024 * 1024


def split_table(table):
    high = table.astype(jnp.bfloat16)
    low = (table - high.astype(np.float64)).astype(jnp.bfloat16)
    return high, low


def dft_pair():
    counter = np.arange(HS)
    angles = (counter[:, None] * counter[None, :] % HS) * (2.0 * math.pi / HS)
    return np.cos(angles) / math.sqrt(HS), np.sin(angles) / math.sqrt(HS)


def left_table(height):
    cos_tab, sin_tab = dft_pair()
    eye = np.eye(height // HS)
    full = np.concatenate([np.kron(eye, cos_tab), np.kron(eye, -sin_tab)], axis=0)
    return np.concatenate(split_table(full), axis=1)


def right_table():
    cos_tab, sin_tab = dft_pair()
    eye = np.eye(LANES // HS)
    cos_big, sin_big = np.kron(eye, cos_tab), np.kron(eye, sin_tab)
    full = np.concatenate(
        [
            np.concatenate([cos_big, -sin_big], axis=1),
            np.concatenate([sin_big, cos_big], axis=1),
        ],
        axis=0,
    )
    return full.astype(jnp.bfloat16)


def layer_height(layer):
    return BAND + 2 * KR * (LAYERS - 1 - layer)


def block_height(layer):
    height = layer_height(layer)
    return height // 2 if 2 * (height + 2 * KR) > 2 * LANES else height


def spread_matrix():
    tile = lax.broadcasted_iota(jnp.int32, (NH, COLS), 0)
    column = lax.broadcasted_iota(jnp.int32, (NH, COLS), 1)
    return jnp.where(column // HS == tile, 1.0, 0.0).astype(jnp.bfloat16)


def own_colour():
    return jnp.maximum(lax.axis_index("depth") - (LAYERS - COLORS), 0)


def pack_kernel(light, edges, counts, listed, row_taps, col_taps, incident, out, mine, *scratch):
    held, sems, taps = scratch[:6], scratch[6], scratch[7]
    picked = pltpu.make_async_copy(incident.at[own_colour()], mine, sems.at[6])
    sources = (listed, counts, edges, row_taps, col_taps, light)
    copies = [
        pltpu.make_async_copy(source, target, sems.at[place])
        for place, (source, target) in enumerate(zip(sources, held))
    ]
    for copy in reversed(copies):
        copy.start()
    picked.start()
    listed, counts, edges, row_taps, col_taps, light = held
    spread = spread_matrix()
    slot = lax.broadcasted_iota(jnp.int32, (NH, NH), 0)
    place = lax.broadcasted_iota(jnp.int32, (NH, NH), 1)
    for copy in copies[:5]:
        copy.wait()
    rows = []
    for group in range(BAND // HS):
        listing = jnp.broadcast_to(listed[0, group : group + 1, :], (NH, NH))
        column = jnp.sum(jnp.where(slot == place, listing, 0), axis=1, keepdims=True)
        named = (column == place) & (slot < counts[0, group])
        live = jnp.max(jnp.where(named, 1.0, 0.0), axis=0, keepdims=True)
        rows.append(jnp.broadcast_to(live, (HS, NH)))
    live_rows = jnp.concatenate(rows, axis=0).astype(jnp.bfloat16)
    live_pix = jnp.dot(live_rows, spread, preferred_element_type=jnp.float32)
    edge_tile = jnp.concatenate(
        [edges[0].astype(jnp.float32), jnp.zeros((BAND, LANES - NH), jnp.float32)], axis=1
    ).astype(jnp.bfloat16)
    for colour in range(COLORS):
        chunk = colour + LAYERS - COLORS
        out[chunk, :, COLS:HALO_W] = edge_tile
        taps[...] = jnp.zeros_like(taps)
        taps[0:2, : 2 * KC + 1] = col_taps[0, colour].astype(jnp.float32)
        taps[2:4, : 2 * KR + 1] = row_taps[0, colour].astype(jnp.float32)
        out[chunk, :, HALO_W:] = taps[...].astype(jnp.bfloat16)
    for spare in range(LAYERS - COLORS):
        out[spare] = jnp.zeros((BAND, FULL_W), jnp.bfloat16)
    copies[5].wait()
    for colour in range(COLORS):
        chunk = colour + LAYERS - COLORS
        out[chunk, :, :COLS] = (light[0, colour] * live_pix).astype(jnp.bfloat16)
    picked.wait()


def halo_kernel(own, incident, beyond, distant, in_chip, cross, far_even, far_odd):
    band = lax.axis_index("rows")
    core = band % 2
    odd = (band // 2) % 2
    last = BAND - KR
    for near, start in ((in_chip, (1 - core) * last), (cross, core * last)):
        near[0:BAND] = own[0, :, :HALO_W]
        near[BAND : 2 * BAND] = own[1, :, :HALO_W]
        near[2 * BAND : NEAR] = own[2, pl.ds(pl.multiple_of(start, KR), KR), :HALO_W]
    in_chip[NEAR : NEAR + BAND, :COLS] = incident[0]
    in_chip[NEAR + BAND : NEAR + 2 * BAND, :COLS] = incident[1]
    in_chip[NEAR + 2 * BAND :, :COLS] = beyond[...]
    for far, start in ((far_even, (1 - odd) * last), (far_odd, odd * last)):
        far[...] = own[0, pl.ds(pl.multiple_of(start, KR), KR), :HALO_W]


def ordered(in_chip, cross, far_even, far_odd):
    band = lax.axis_index("rows")
    even_core = band % 2 == 0
    even_chip = (band // 2) % 2 == 0
    in_chip, cross = in_chip[:NEAR], cross[...]
    far_even, far_odd = far_even[...], far_odd[...]
    return (
        jnp.where(even_core, cross, in_chip),
        jnp.where(even_core, in_chip, cross),
        jnp.where(even_chip, far_odd, far_even),
        jnp.where(even_chip, far_even, far_odd),
    )


def tiles_below(value, height):
    return jnp.concatenate(
        [
            jnp.concatenate(
                [
                    value[:height, tile * LANES : (tile + 1) * LANES],
                    value[height:, tile * LANES : (tile + 1) * LANES],
                ],
                axis=1,
            )
            for tile in range(TILES)
        ],
        axis=0,
    )


def stereo_tiles(blocks, left_tab, right_tab):
    arranged = []
    for light in blocks:
        doubled = jnp.concatenate([light, light], axis=0)
        left = jnp.dot(left_tab[...], doubled, preferred_element_type=jnp.float32)
        arranged.append(tiles_below(left.astype(jnp.bfloat16), light.shape[0]))
    arranged = jnp.concatenate(arranged, axis=0) if len(arranged) > 1 else arranged[0]
    return jnp.dot(arranged, right_tab[...], preferred_element_type=jnp.float32)


def clear_pixels(edges):
    edge_pix = jnp.dot(edges, spread_matrix(), preferred_element_type=jnp.float32)
    within = (lax.broadcasted_iota(jnp.int32, (1, COLS), 1) % HS).astype(jnp.float32)
    return jnp.where(within < edge_pix, 1.0, 0.0)


def banded(line, count, shift):
    base = jnp.concatenate([line, jnp.zeros((1, LANES), jnp.float32)], axis=1)
    base = jnp.broadcast_to(base, (count, 2 * LANES))
    return pltpu.roll(base, shift, 1, stride=1, stride_axis=0)


def filters(taps, layer):
    row_re, row_im = taps[2:3], taps[3:4]
    height = block_height(layer)
    before = height + 2 * KR
    upper = banded(row_re, height, 0) - banded(row_im, height, before)
    lower = banded(row_im, height, 0) + banded(row_re, height, before)
    row_mat = jnp.concatenate([upper, lower], axis=0).astype(jnp.bfloat16)
    col_re = banded(taps[0:1], LANES, 1)
    col_im = banded(taps[1:2], LANES, 1)
    upper = jnp.concatenate([col_re, -col_im], axis=1)
    lower = jnp.concatenate([col_im, col_re], axis=1)
    col_mat = jnp.concatenate([upper, lower], axis=0).astype(jnp.bfloat16)
    return row_mat, col_mat


def propagated(u_re, u_im, row_mat, col_mat, layer):
    height = layer_height(layer)
    block = block_height(layer)
    reach = block + 2 * KR
    parts = []
    for start in range(0, height, block):
        stacked = jnp.concatenate(
            [u_re[start : start + reach], u_im[start : start + reach]], axis=0
        )
        parts.append(
            jnp.dot(row_mat[:, : 2 * reach], stacked, preferred_element_type=jnp.float32)
        )
    rowed = jnp.concatenate(
        [part[:block] for part in parts] + [part[block:] for part in parts], axis=0
    )
    rowed = jnp.concatenate([rowed, jnp.zeros((2 * height, LANES), jnp.float32)], axis=1)
    rowed = pltpu.roll(rowed, HALF, 1).astype(jnp.bfloat16)
    windows = jnp.concatenate(
        [
            jnp.concatenate(
                [
                    rowed[:height, tile * LANES : (tile + 2) * LANES],
                    rowed[height:, tile * LANES : (tile + 2) * LANES],
                ],
                axis=1,
            )
            for tile in range(TILES)
        ],
        axis=0,
    )
    return lax.dot_general(
        windows, col_mat, (((1,), (1,)), ((), ())), preferred_element_type=jnp.float32
    )


def prepare_kernel(
    own, incident, in_chip, cross, far, left_tab, right_tab,
    first, stereo, clear, col_mats, *row_mats
):
    even_core = lax.axis_index("rows") % 2 == 0
    cross, far = cross[...], far[...]
    partner = in_chip[NEAR : NEAR + 2 * BAND, :COLS]
    beyond = in_chip[NEAR + 2 * BAND :, :COLS]
    sides = (
        jnp.where(even_core, far, beyond),
        jnp.where(even_core, cross, partner),
        jnp.where(even_core, partner, cross),
        jnp.where(even_core, beyond, far),
    )
    extended = []
    for part in range(2):
        low_far, low_near, high_near, high_far = (
            side[part * BAND : (part + 1) * BAND] for side in sides
        )
        pieces = [low_far, low_near, incident[part], high_near, high_far]
        extended.append(jnp.concatenate(pieces, axis=0))
    row_mat, col_mat = filters(own[0, 0:16, HALO_W:].astype(jnp.float32), 0)
    first[...] = propagated(extended[0], extended[1], row_mat, col_mat, 0)
    for layer in range(1, LAYERS):
        row_mat, col_mat = filters(own[layer, 0:16, HALO_W:].astype(jnp.float32), layer)
        row_mats[layer - 1][...] = row_mat
        col_mats[layer - 1] = col_mat
    packed = jnp.concatenate([own[layer, :, :HALO_W] for layer in range(LAYERS)], axis=0)
    clear[...] = clear_pixels(packed[:, COLS : COLS + NH])
    tiles = stereo_tiles([packed[:, :COLS]], left_tab, right_tab)
    for tile in range(TILES):
        for part in range(2):
            block = tiles[
                tile * LANES : (tile + 1) * LANES, part * LANES : (part + 1) * LANES
            ]
            stereo[part, :, tile * LANES : (tile + 1) * LANES] = block


def chain_kernel(
    in_chip, cross, far_even, far_odd, left_tab, right_tab, first, stereo, clear, col_mats, *rest
):
    row_mats, (out, field) = rest[: LAYERS - 1], rest[LAYERS - 1 :]
    low_near, high_near, low_far, high_far = ordered(in_chip, cross, far_even, far_odd)
    pieces = [
        low_far,
        low_near[0:BAND],
        high_near[0:BAND],
        high_far,
        low_near[BAND : 2 * BAND],
        high_near[BAND : 2 * BAND],
        low_near[2 * BAND : NEAR],
        high_near[2 * BAND : NEAR],
    ]
    halo = jnp.concatenate(pieces, axis=0)
    half = halo.shape[0] // 2
    halo_tiles = stereo_tiles(
        [halo[:half, :COLS], halo[half:, :COLS]], left_tab, right_tab
    )
    halo_clear = clear_pixels(halo[:, COLS : COLS + NH])
    begins = (0, half, half + 2 * BAND, 0)
    sides = (BAND + FAR, BAND, KR, 0)
    for layer in range(LAYERS):
        height = layer_height(layer)
        before = height + 2 * KR
        low, side = begins[layer], sides[layer]
        if layer == 0:
            columned = first
        else:
            columned = propagated(
                field[0, :before], field[1, :before], row_mats[layer - 1], col_mats[layer - 1], layer
            )
        band = slice(layer * BAND, (layer + 1) * BAND)
        pieces = [clear[band]]
        if side:
            pieces = [halo_clear[low : low + side], clear[band], halo_clear[low + side : low + 2 * side]]
        passing = jnp.concatenate(pieces, axis=0)
        for tile in range(TILES):
            span = slice(tile * height, (tile + 1) * height)
            lanes = slice(tile * LANES, (tile + 1) * LANES)
            row = (low // half * TILES + tile) * half + low % half
            for part in range(2):
                within = slice(part * LANES, (part + 1) * LANES)
                pieces = [stereo[part, band, lanes]]
                if side:
                    pieces = [
                        halo_tiles[row : row + side, within],
                        stereo[part, band, lanes],
                        halo_tiles[row + side : row + 2 * side, within],
                    ]
                added = jnp.concatenate(pieces, axis=0)
                value = passing[:, lanes] * columned[span, within] + added
                field[part, :height, lanes] = value.astype(jnp.bfloat16)
        for part in range(2):
            out[layer, part] = field[part, side : side + BAND]


def exchanged(value, axis, by, phase):
    count = lax.axis_size(axis)
    lower = [i for i in range(count - by) if (i // by) % 2 == phase]
    pairs = [(i, i + by) for i in lower] + [(i + by, i) for i in lower]
    return lax.ppermute(value, axis, pairs)


def far_incident(value):
    count = lax.axis_size("rows")
    pairs = [(i, i + 2) for i in range(0, count - 2, 2)]
    pairs += [(i, i - 2) for i in range(3, count, 2)]
    return lax.ppermute(value, "rows", pairs)


def neighbours(sent):
    in_chip, cross, far_even, far_odd = sent
    in_chip = exchanged(in_chip, "rows", 1, 0)
    cross = exchanged(cross, "rows", 1, 1)
    far_even = exchanged(far_even, "rows", 2, 0)
    far_odd = exchanged(far_odd, "rows", 2, 1)
    return in_chip, cross, far_even, far_odd


def call(kernel, out_shape, in_specs, scratch=(), flops=0, moved=10**6, limit=VMEM_LIMIT):
    vmem = pl.BlockSpec(memory_space=pltpu.VMEM)
    many = isinstance(out_shape, (tuple, list))
    return pl.pallas_call(
        kernel,
        out_shape=out_shape,
        in_specs=in_specs,
        out_specs=(vmem,) * len(out_shape) if many else vmem,
        scratch_shapes=scratch,
        compiler_params=pltpu.CompilerParams(vmem_limit_bytes=limit),
        cost_estimate=pl.CostEstimate(flops=flops, bytes_accessed=moved, transcendentals=0),
    )


def body(incident, row_taps, col_taps, hogel_light, silhouette, fill_counts, hogel_index):
    vmem = pl.BlockSpec(memory_space=pltpu.VMEM)
    hbm = pl.BlockSpec(memory_space=pltpu.HBM)
    bf16, f32 = jnp.bfloat16, jnp.float32
    shaped = jax.ShapeDtypeStruct
    held = [
        pltpu.VMEM(hogel_index.shape, jnp.int32),
        pltpu.SMEM(fill_counts.shape, jnp.int32),
        pltpu.VMEM(silhouette.shape, jnp.int32),
        pltpu.VMEM(row_taps.shape, bf16),
        pltpu.VMEM(col_taps.shape, bf16),
        pltpu.VMEM(hogel_light.shape, f32),
    ]
    payload, mine = call(
        pack_kernel,
        (shaped((LAYERS, BAND, FULL_W), bf16), shaped(incident.shape[1:], bf16)),
        [hbm] * 7,
        held + [pltpu.SemaphoreType.DMA((7,)), pltpu.VMEM((BAND, LANES), f32)],
        flops=10**7,
        limit=PACK_LIMIT,
    )(hogel_light, silhouette, fill_counts, hogel_index, row_taps, col_taps, incident)
    flat = mine.reshape(2 * BAND, COLS)
    own = lax.all_to_all(payload, "depth", 0, 0, tiled=True)
    cross_in = exchanged(flat, "rows", 1, 1)
    far_in = far_incident(flat)
    chip = shaped((NEAR + 4 * BAND, HALO_W), bf16)
    near = shaped((NEAR, HALO_W), bf16)
    far = shaped((FAR, HALO_W), bf16)
    halos = neighbours(
        call(halo_kernel, (chip, near, far, far), [vmem] * 4)(own, mine, cross_in, far_in)
    )
    right_tab = jnp.asarray(right_table())
    made = call(
        prepare_kernel,
        [
            shaped((TILES * layer_height(0), 2 * LANES), f32),
            shaped((2, LANES, COLS), f32),
            shaped((LANES, COLS), f32),
            shaped((LAYERS - 1, 2 * LANES, 4 * LANES), bf16),
        ]
        + [shaped((2 * block_height(layer), 2 * LANES), bf16) for layer in range(1, LAYERS)],
        [vmem] * 7,
        flops=10**9,
        moved=3 * 10**6,
    )(own, mine, halos[0], cross_in, far_in, jnp.asarray(left_table(LANES)), right_tab)
    halo_rows = NEAR + FAR
    result = call(
        chain_kernel,
        shaped((LAYERS, 2, BAND, COLS), bf16),
        [vmem] * (6 + len(made)),
        [pltpu.VMEM((2, layer_height(0), COLS), bf16)],
        flops=2 * 10**9,
        moved=3 * 10**6,
    )(*halos, jnp.asarray(left_table(halo_rows)), right_tab, *made)
    gathered = lax.all_to_all(result, "depth", 0, 0, tiled=True)
    return gathered[None, LAYERS - COLORS :]


def solution(mesh):
    placed = (
        P(None, None, "rows", None),
        P("depth", None, None, None),
        P("depth", None, None, None),
        P("depth", None, "rows", None),
        P("depth", "rows", None),
        P("depth", "rows"),
        P("depth", "rows", None),
    )
    return jax.shard_map(
        body,
        mesh=mesh,
        in_specs=placed,
        out_specs=P("depth", None, None, "rows", None),
        check_vma=False,
    )
```

```python
import math

import jax
import jax.numpy as jnp
import numpy as np
from jax import lax
from jax.experimental import pallas as pl
from jax.experimental.pallas import tpu as pltpu
from jax.sharding import PartitionSpec as P

HS = 16
KR = 16
KC = 63
COLORS = 3
LAYERS = 4
BAND = 32
COLS = 1024
NH = COLS // HS
LANES = 128
TILES = COLS // LANES
HALO_W = COLS + LANES
HALF = LANES // 2
FULL_W = COLS + 2 * LANES
NEAR = 2 * BAND + KR
FAR = KR
VMEM_LIMIT = 48 * 1024 * 1024
PACK_LIMIT = 63 * 1024 * 1024


def split_table(table):
    high = table.astype(jnp.bfloat16)
    low = (table - high.astype(np.float64)).astype(jnp.bfloat16)
    return high, low


def dft_pair():
    counter = np.arange(HS)
    angles = (counter[:, None] * counter[None, :] % HS) * (2.0 * math.pi / HS)
    return np.cos(angles) / math.sqrt(HS), np.sin(angles) / math.sqrt(HS)


def left_table(height):
    cos_tab, sin_tab = dft_pair()
    eye = np.eye(height // HS)
    full = np.concatenate([np.kron(eye, cos_tab), np.kron(eye, -sin_tab)], axis=0)
    return np.concatenate(split_table(full), axis=1)


def right_table():
    cos_tab, sin_tab = dft_pair()
    eye = np.eye(LANES // HS)
    cos_big, sin_big = np.kron(eye, cos_tab), np.kron(eye, sin_tab)
    full = np.concatenate(
        [
            np.concatenate([cos_big, -sin_big], axis=1),
            np.concatenate([sin_big, cos_big], axis=1),
        ],
        axis=0,
    )
    return full.astype(jnp.bfloat16)


def layer_height(layer):
    return BAND + 2 * KR * (LAYERS - 1 - layer)


def block_height(layer):
    height = layer_height(layer)
    return height // 2 if 2 * (height + 2 * KR) > 2 * LANES else height


def spread_matrix():
    tile = lax.broadcasted_iota(jnp.int32, (NH, COLS), 0)
    column = lax.broadcasted_iota(jnp.int32, (NH, COLS), 1)
    return jnp.where(column // HS == tile, 1.0, 0.0).astype(jnp.bfloat16)


def own_colour():
    return jnp.maximum(lax.axis_index("depth") - (LAYERS - COLORS), 0)


def pack_kernel(light, edges, counts, listed, row_taps, col_taps, incident, out, mine, *scratch):
    held, sems, taps = scratch[:6], scratch[6], scratch[7]
    picked = pltpu.make_async_copy(incident.at[own_colour()], mine, sems.at[6])
    sources = (listed, counts, edges, row_taps, col_taps, light)
    copies = [
        pltpu.make_async_copy(source, target, sems.at[place])
        for place, (source, target) in enumerate(zip(sources, held))
    ]
    for copy in reversed(copies):
        copy.start()
    picked.start()
    listed, counts, edges, row_taps, col_taps, light = held
    spread = spread_matrix()
    slot = lax.broadcasted_iota(jnp.int32, (NH, NH), 0)
    place = lax.broadcasted_iota(jnp.int32, (NH, NH), 1)
    for copy in copies[:5]:
        copy.wait()
    rows = []
    for group in range(BAND // HS):
        listing = jnp.broadcast_to(listed[0, group : group + 1, :], (NH, NH))
        column = jnp.sum(jnp.where(slot == place, listing, 0), axis=1, keepdims=True)
        named = (column == place) & (slot < counts[0, group])
        live = jnp.max(jnp.where(named, 1.0, 0.0), axis=0, keepdims=True)
        rows.append(jnp.broadcast_to(live, (HS, NH)))
    live_rows = jnp.concatenate(rows, axis=0).astype(jnp.bfloat16)
    live_pix = jnp.dot(live_rows, spread, preferred_element_type=jnp.float32)
    edge_tile = jnp.concatenate(
        [edges[0].astype(jnp.float32), jnp.zeros((BAND, LANES - NH), jnp.float32)], axis=1
    ).astype(jnp.bfloat16)
    for colour in range(COLORS):
        chunk = colour + LAYERS - COLORS
        out[chunk, :, COLS:HALO_W] = edge_tile
        taps[...] = jnp.zeros_like(taps)
        taps[0:2, : 2 * KC + 1] = col_taps[0, colour].astype(jnp.float32)
        taps[2:4, : 2 * KR + 1] = row_taps[0, colour].astype(jnp.float32)
        out[chunk, :, HALO_W:] = taps[...].astype(jnp.bfloat16)
    for spare in range(LAYERS - COLORS):
        out[spare] = jnp.zeros((BAND, FULL_W), jnp.bfloat16)
    copies[5].wait()
    for colour in range(COLORS):
        chunk = colour + LAYERS - COLORS
        out[chunk, :, :COLS] = (light[0, colour] * live_pix).astype(jnp.bfloat16)
    picked.wait()


def halo_kernel(own, incident, in_chip, cross, far_even, far_odd):
    band = lax.axis_index("rows")
    core = band % 2
    odd = (band // 2) % 2
    last = BAND - KR
    for near, start in ((in_chip, (1 - core) * last), (cross, core * last)):
        near[0:BAND] = own[0, :, :HALO_W]
        near[BAND : 2 * BAND] = own[1, :, :HALO_W]
        near[2 * BAND : NEAR] = own[2, pl.ds(pl.multiple_of(start, KR), KR), :HALO_W]
    in_chip[NEAR : NEAR + BAND, :COLS] = incident[0]
    in_chip[NEAR + BAND :, :COLS] = incident[1]
    for far, start in ((far_even, (1 - odd) * last), (far_odd, odd * last)):
        far[...] = own[0, pl.ds(pl.multiple_of(start, KR), KR), :HALO_W]


def ordered(in_chip, cross, far_even, far_odd):
    band = lax.axis_index("rows")
    even_core = band % 2 == 0
    even_chip = (band // 2) % 2 == 0
    in_chip, cross = in_chip[...], cross[...]
    far_even, far_odd = far_even[...], far_odd[...]
    return (
        jnp.where(even_core, cross, in_chip),
        jnp.where(even_core, in_chip, cross),
        jnp.where(even_chip, far_odd, far_even),
        jnp.where(even_chip, far_even, far_odd),
    )


def tiles_below(value, height):
    return jnp.concatenate(
        [
            jnp.concatenate(
                [
                    value[:height, tile * LANES : (tile + 1) * LANES],
                    value[height:, tile * LANES : (tile + 1) * LANES],
                ],
                axis=1,
            )
            for tile in range(TILES)
        ],
        axis=0,
    )


def stereo_tiles(blocks, left_tab, right_tab):
    arranged = []
    for light in blocks:
        doubled = jnp.concatenate([light, light], axis=0)
        left = jnp.dot(left_tab[...], doubled, preferred_element_type=jnp.float32)
        arranged.append(tiles_below(left.astype(jnp.bfloat16), light.shape[0]))
    arranged = jnp.concatenate(arranged, axis=0) if len(arranged) > 1 else arranged[0]
    return jnp.dot(arranged, right_tab[...], preferred_element_type=jnp.float32)


def clear_pixels(edges):
    edge_pix = jnp.dot(edges, spread_matrix(), preferred_element_type=jnp.float32)
    within = (lax.broadcasted_iota(jnp.int32, (1, COLS), 1) % HS).astype(jnp.float32)
    return jnp.where(within < edge_pix, 1.0, 0.0)


def banded(line, count, shift):
    base = jnp.concatenate([line, jnp.zeros((1, LANES), jnp.float32)], axis=1)
    base = jnp.broadcast_to(base, (count, 2 * LANES))
    return pltpu.roll(base, shift, 1, stride=1, stride_axis=0)


def filters(taps, layer):
    row_re, row_im = taps[2:3], taps[3:4]
    height = block_height(layer)
    before = height + 2 * KR
    upper = banded(row_re, height, 0) - banded(row_im, height, before)
    lower = banded(row_im, height, 0) + banded(row_re, height, before)
    row_mat = jnp.concatenate([upper, lower], axis=0).astype(jnp.bfloat16)
    col_re = banded(taps[0:1], LANES, 1)
    col_im = banded(taps[1:2], LANES, 1)
    upper = jnp.concatenate([col_re, -col_im], axis=1)
    lower = jnp.concatenate([col_im, col_re], axis=1)
    col_mat = jnp.concatenate([upper, lower], axis=0).astype(jnp.bfloat16)
    return row_mat, col_mat


def propagated(u_re, u_im, row_mat, col_mat, layer):
    height = layer_height(layer)
    block = block_height(layer)
    reach = block + 2 * KR
    parts = []
    for start in range(0, height, block):
        stacked = jnp.concatenate(
            [u_re[start : start + reach], u_im[start : start + reach]], axis=0
        )
        parts.append(
            jnp.dot(row_mat[:, : 2 * reach], stacked, preferred_element_type=jnp.float32)
        )
    rowed = jnp.concatenate(
        [part[:block] for part in parts] + [part[block:] for part in parts], axis=0
    )
    rowed = jnp.concatenate([rowed, jnp.zeros((2 * height, LANES), jnp.float32)], axis=1)
    rowed = pltpu.roll(rowed, HALF, 1).astype(jnp.bfloat16)
    windows = jnp.concatenate(
        [
            jnp.concatenate(
                [
                    rowed[:height, tile * LANES : (tile + 2) * LANES],
                    rowed[height:, tile * LANES : (tile + 2) * LANES],
                ],
                axis=1,
            )
            for tile in range(TILES)
        ],
        axis=0,
    )
    return lax.dot_general(
        windows, col_mat, (((1,), (1,)), ((), ())), preferred_element_type=jnp.float32
    )


def prepare_kernel(
    own, incident, in_chip, cross, far_even, far_odd, left_tab, right_tab,
    first, stereo, clear, col_mats, *row_mats
):
    sides = ordered(in_chip[NEAR:, :COLS], cross, far_even, far_odd)
    extended = []
    for part in range(2):
        low_near, high_near, low_far, high_far = (
            side[part * BAND : (part + 1) * BAND] for side in sides
        )
        pieces = [low_far, low_near, incident[part], high_near, high_far]
        extended.append(jnp.concatenate(pieces, axis=0))
    row_mat, col_mat = filters(own[0, 0:16, HALO_W:].astype(jnp.float32), 0)
    first[...] = propagated(extended[0], extended[1], row_mat, col_mat, 0)
    for layer in range(1, LAYERS):
        row_mat, col_mat = filters(own[layer, 0:16, HALO_W:].astype(jnp.float32), layer)
        row_mats[layer - 1][...] = row_mat
        col_mats[layer - 1] = col_mat
    packed = jnp.concatenate([own[layer, :, :HALO_W] for layer in range(LAYERS)], axis=0)
    clear[...] = clear_pixels(packed[:, COLS : COLS + NH])
    tiles = stereo_tiles([packed[:, :COLS]], left_tab, right_tab)
    for tile in range(TILES):
        for part in range(2):
            block = tiles[
                tile * LANES : (tile + 1) * LANES, part * LANES : (part + 1) * LANES
            ]
            stereo[part, :, tile * LANES : (tile + 1) * LANES] = block


def chain_kernel(
    in_chip, cross, far_even, far_odd, left_tab, right_tab, first, stereo, clear, col_mats, *rest
):
    row_mats, (out, field) = rest[: LAYERS - 1], rest[LAYERS - 1 :]
    low_near, high_near, low_far, high_far = ordered(in_chip[:NEAR], cross, far_even, far_odd)
    pieces = [
        low_far,
        low_near[0:BAND],
        high_near[0:BAND],
        high_far,
        low_near[BAND : 2 * BAND],
        high_near[BAND : 2 * BAND],
        low_near[2 * BAND : NEAR],
        high_near[2 * BAND : NEAR],
    ]
    halo = jnp.concatenate(pieces, axis=0)
    half = halo.shape[0] // 2
    halo_tiles = stereo_tiles(
        [halo[:half, :COLS], halo[half:, :COLS]], left_tab, right_tab
    )
    halo_clear = clear_pixels(halo[:, COLS : COLS + NH])
    begins = (0, half, half + 2 * BAND, 0)
    sides = (BAND + FAR, BAND, KR, 0)
    for layer in range(LAYERS):
        height = layer_height(layer)
        before = height + 2 * KR
        low, side = begins[layer], sides[layer]
        if layer == 0:
            columned = first
        else:
            columned = propagated(
                field[0, :before], field[1, :before], row_mats[layer - 1], col_mats[layer - 1], layer
            )
        band = slice(layer * BAND, (layer + 1) * BAND)
        pieces = [clear[band]]
        if side:
            pieces = [halo_clear[low : low + side], clear[band], halo_clear[low + side : low + 2 * side]]
        passing = jnp.concatenate(pieces, axis=0)
        for tile in range(TILES):
            span = slice(tile * height, (tile + 1) * height)
            lanes = slice(tile * LANES, (tile + 1) * LANES)
            row = (low // half * TILES + tile) * half + low % half
            for part in range(2):
                within = slice(part * LANES, (part + 1) * LANES)
                pieces = [stereo[part, band, lanes]]
                if side:
                    pieces = [
                        halo_tiles[row : row + side, within],
                        stereo[part, band, lanes],
                        halo_tiles[row + side : row + 2 * side, within],
                    ]
                added = jnp.concatenate(pieces, axis=0)
                value = passing[:, lanes] * columned[span, within] + added
                field[part, :height, lanes] = value.astype(jnp.bfloat16)
        for part in range(2):
            out[layer, part] = field[part, side : side + BAND]


def exchanged(value, axis, by, phase):
    count = lax.axis_size(axis)
    lower = [i for i in range(count - by) if (i // by) % 2 == phase]
    pairs = [(i, i + by) for i in lower] + [(i + by, i) for i in lower]
    return lax.ppermute(value, axis, pairs)


def neighbours(sent):
    in_chip, cross, far_even, far_odd = sent
    in_chip = exchanged(in_chip, "rows", 1, 0)
    cross = exchanged(cross, "rows", 1, 1)
    far_even = exchanged(far_even, "rows", 2, 0)
    far_odd = exchanged(far_odd, "rows", 2, 1)
    return in_chip, cross, far_even, far_odd


def call(kernel, out_shape, in_specs, scratch=(), flops=0, moved=10**6, limit=VMEM_LIMIT):
    vmem = pl.BlockSpec(memory_space=pltpu.VMEM)
    many = isinstance(out_shape, (tuple, list))
    return pl.pallas_call(
        kernel,
        out_shape=out_shape,
        in_specs=in_specs,
        out_specs=(vmem,) * len(out_shape) if many else vmem,
        scratch_shapes=scratch,
        compiler_params=pltpu.CompilerParams(vmem_limit_bytes=limit),
        cost_estimate=pl.CostEstimate(flops=flops, bytes_accessed=moved, transcendentals=0),
    )


def body(incident, row_taps, col_taps, hogel_light, silhouette, fill_counts, hogel_index):
    vmem = pl.BlockSpec(memory_space=pltpu.VMEM)
    hbm = pl.BlockSpec(memory_space=pltpu.HBM)
    bf16, f32 = jnp.bfloat16, jnp.float32
    shaped = jax.ShapeDtypeStruct
    held = [
        pltpu.VMEM(hogel_index.shape, jnp.int32),
        pltpu.SMEM(fill_counts.shape, jnp.int32),
        pltpu.VMEM(silhouette.shape, jnp.int32),
        pltpu.VMEM(row_taps.shape, bf16),
        pltpu.VMEM(col_taps.shape, bf16),
        pltpu.VMEM(hogel_light.shape, f32),
    ]
    payload, mine = call(
        pack_kernel,
        (shaped((LAYERS, BAND, FULL_W), bf16), shaped(incident.shape[1:], bf16)),
        [hbm] * 7,
        held + [pltpu.SemaphoreType.DMA((7,)), pltpu.VMEM((BAND, LANES), f32)],
        flops=10**7,
        limit=PACK_LIMIT,
    )(hogel_light, silhouette, fill_counts, hogel_index, row_taps, col_taps, incident)
    flat = mine.reshape(2 * BAND, COLS)
    own = lax.all_to_all(payload, "depth", 0, 0, tiled=True)
    cross_in = exchanged(flat, "rows", 1, 1)
    far_in = [exchanged(flat, "rows", 2, phase) for phase in range(2)]
    chip = shaped((NEAR + 2 * BAND, HALO_W), bf16)
    near = shaped((NEAR, HALO_W), bf16)
    far = shaped((FAR, HALO_W), bf16)
    halos = neighbours(call(halo_kernel, (chip, near, far, far), [vmem] * 2)(own, mine))
    right_tab = jnp.asarray(right_table())
    made = call(
        prepare_kernel,
        [
            shaped((TILES * layer_height(0), 2 * LANES), f32),
            shaped((2, LANES, COLS), f32),
            shaped((LANES, COLS), f32),
            shaped((LAYERS - 1, 2 * LANES, 4 * LANES), bf16),
        ]
        + [shaped((2 * block_height(layer), 2 * LANES), bf16) for layer in range(1, LAYERS)],
        [vmem] * 8,
        flops=10**9,
        moved=3 * 10**6,
    )(own, mine, halos[0], cross_in, *far_in, jnp.asarray(left_table(LANES)), right_tab)
    halo_rows = NEAR + FAR
    result = call(
        chain_kernel,
        shaped((LAYERS, 2, BAND, COLS), bf16),
        [vmem] * (6 + len(made)),
        [pltpu.VMEM((2, layer_height(0), COLS), bf16)],
        flops=2 * 10**9,
        moved=3 * 10**6,
    )(*halos, jnp.asarray(left_table(halo_rows)), right_tab, *made)
    gathered = lax.all_to_all(result, "depth", 0, 0, tiled=True)
    return gathered[None, LAYERS - COLORS :]


def solution(mesh):
    placed = (
        P(None, None, "rows", None),
        P("depth", None, None, None),
        P("depth", None, None, None),
        P("depth", None, "rows", None),
        P("depth", "rows", None),
        P("depth", "rows"),
        P("depth", "rows", None),
    )
    return jax.shard_map(
        body,
        mesh=mesh,
        in_specs=placed,
        out_specs=P("depth", None, None, "rows", None),
        check_vma=False,
    )
```

```python
import math

import jax
import jax.numpy as jnp
import numpy as np
from jax import lax
from jax.experimental import pallas as pl
from jax.experimental.pallas import tpu as pltpu
from jax.sharding import PartitionSpec as P

HS = 16
KR = 16
KC = 63
COLORS = 3
LAYERS = 4
BAND = 32
COLS = 1024
NH = COLS // HS
LANES = 128
TILES = COLS // LANES
HALO_W = COLS + LANES
HALF = LANES // 2
FULL_W = COLS + 2 * LANES
NEAR = 2 * BAND + KR
FAR = KR
VMEM_LIMIT = 48 * 1024 * 1024
PACK_LIMIT = 63 * 1024 * 1024


def split_table(table):
    high = table.astype(jnp.bfloat16)
    low = (table - high.astype(np.float64)).astype(jnp.bfloat16)
    return high, low


def dft_pair():
    counter = np.arange(HS)
    angles = (counter[:, None] * counter[None, :] % HS) * (2.0 * math.pi / HS)
    return np.cos(angles) / math.sqrt(HS), np.sin(angles) / math.sqrt(HS)


def left_table(height):
    cos_tab, sin_tab = dft_pair()
    eye = np.eye(height // HS)
    full = np.concatenate([np.kron(eye, cos_tab), np.kron(eye, -sin_tab)], axis=0)
    return np.concatenate(split_table(full), axis=1)


def right_table():
    cos_tab, sin_tab = dft_pair()
    eye = np.eye(LANES // HS)
    cos_big, sin_big = np.kron(eye, cos_tab), np.kron(eye, sin_tab)
    full = np.concatenate(
        [
            np.concatenate([cos_big, -sin_big], axis=1),
            np.concatenate([sin_big, cos_big], axis=1),
        ],
        axis=0,
    )
    return full.astype(jnp.bfloat16)


def layer_height(layer):
    return BAND + 2 * KR * (LAYERS - 1 - layer)


def block_height(layer):
    height = layer_height(layer)
    return height // 2 if 2 * (height + 2 * KR) > 2 * LANES else height


def spread_matrix():
    tile = lax.broadcasted_iota(jnp.int32, (NH, COLS), 0)
    column = lax.broadcasted_iota(jnp.int32, (NH, COLS), 1)
    return jnp.where(column // HS == tile, 1.0, 0.0).astype(jnp.bfloat16)


def own_colour():
    return jnp.maximum(lax.axis_index("depth") - (LAYERS - COLORS), 0)


def pack_kernel(light, edges, counts, listed, row_taps, col_taps, incident, out, mine, *scratch):
    held, sems, taps = scratch[:6], scratch[6], scratch[7]
    picked = pltpu.make_async_copy(incident.at[own_colour()], mine, sems.at[6])
    sources = (listed, counts, edges, row_taps, col_taps, light)
    copies = [
        pltpu.make_async_copy(source, target, sems.at[place])
        for place, (source, target) in enumerate(zip(sources, held))
    ]
    for copy in reversed(copies):
        copy.start()
    picked.start()
    listed, counts, edges, row_taps, col_taps, light = held
    spread = spread_matrix()
    slot = lax.broadcasted_iota(jnp.int32, (NH, NH), 0)
    place = lax.broadcasted_iota(jnp.int32, (NH, NH), 1)
    for copy in copies[:5]:
        copy.wait()
    rows = []
    for group in range(BAND // HS):
        listing = jnp.broadcast_to(listed[0, group : group + 1, :], (NH, NH))
        column = jnp.sum(jnp.where(slot == place, listing, 0), axis=1, keepdims=True)
        named = (column == place) & (slot < counts[0, group])
        live = jnp.max(jnp.where(named, 1.0, 0.0), axis=0, keepdims=True)
        rows.append(jnp.broadcast_to(live, (HS, NH)))
    live_rows = jnp.concatenate(rows, axis=0).astype(jnp.bfloat16)
    live_pix = jnp.dot(live_rows, spread, preferred_element_type=jnp.float32)
    edge_tile = jnp.concatenate(
        [edges[0].astype(jnp.float32), jnp.zeros((BAND, LANES - NH), jnp.float32)], axis=1
    ).astype(jnp.bfloat16)
    for colour in range(COLORS):
        chunk = colour + LAYERS - COLORS
        out[chunk, :, COLS:HALO_W] = edge_tile
        taps[...] = jnp.zeros_like(taps)
        taps[0:2, : 2 * KC + 1] = col_taps[0, colour].astype(jnp.float32)
        taps[2:4, : 2 * KR + 1] = row_taps[0, colour].astype(jnp.float32)
        out[chunk, :, HALO_W:] = taps[...].astype(jnp.bfloat16)
    for spare in range(LAYERS - COLORS):
        out[spare] = jnp.zeros((BAND, FULL_W), jnp.bfloat16)
    copies[5].wait()
    for colour in range(COLORS):
        chunk = colour + LAYERS - COLORS
        out[chunk, :, :COLS] = (light[0, colour] * live_pix).astype(jnp.bfloat16)
    picked.wait()


def halo_kernel(own, incident, *rest):
    in_chip, cross, far_even, far_odd = rest[-4:]
    band = lax.axis_index("rows")
    core = band % 2
    odd = (band // 2) % 2
    last = BAND - KR
    for near, start in ((in_chip, (1 - core) * last), (cross, core * last)):
        near[0:BAND] = own[0, :, :HALO_W]
        near[BAND : 2 * BAND] = own[1, :, :HALO_W]
        near[2 * BAND : NEAR] = own[2, pl.ds(pl.multiple_of(start, KR), KR), :HALO_W]
    in_chip[NEAR : NEAR + BAND, :COLS] = incident[0]
    in_chip[NEAR + BAND :, :COLS] = incident[1]
    for far, start in ((far_even, (1 - odd) * last), (far_odd, odd * last)):
        far[...] = own[0, pl.ds(pl.multiple_of(start, KR), KR), :HALO_W]


def ordered(in_chip, cross, far_even, far_odd):
    band = lax.axis_index("rows")
    even_core = band % 2 == 0
    even_chip = (band // 2) % 2 == 0
    in_chip, cross = in_chip[...], cross[...]
    far_even, far_odd = far_even[...], far_odd[...]
    return (
        jnp.where(even_core, cross, in_chip),
        jnp.where(even_core, in_chip, cross),
        jnp.where(even_chip, far_odd, far_even),
        jnp.where(even_chip, far_even, far_odd),
    )


def tiles_below(value, height):
    return jnp.concatenate(
        [
            jnp.concatenate(
                [
                    value[:height, tile * LANES : (tile + 1) * LANES],
                    value[height:, tile * LANES : (tile + 1) * LANES],
                ],
                axis=1,
            )
            for tile in range(TILES)
        ],
        axis=0,
    )


def stereo_tiles(blocks, left_tab, right_tab):
    arranged = []
    for light in blocks:
        doubled = jnp.concatenate([light, light], axis=0)
        left = jnp.dot(left_tab[...], doubled, preferred_element_type=jnp.float32)
        arranged.append(tiles_below(left.astype(jnp.bfloat16), light.shape[0]))
    arranged = jnp.concatenate(arranged, axis=0) if len(arranged) > 1 else arranged[0]
    return jnp.dot(arranged, right_tab[...], preferred_element_type=jnp.float32)


def clear_pixels(edges):
    edge_pix = jnp.dot(edges, spread_matrix(), preferred_element_type=jnp.float32)
    within = (lax.broadcasted_iota(jnp.int32, (1, COLS), 1) % HS).astype(jnp.float32)
    return jnp.where(within < edge_pix, 1.0, 0.0)


def banded(line, count, shift):
    base = jnp.concatenate([line, jnp.zeros((1, LANES), jnp.float32)], axis=1)
    base = jnp.broadcast_to(base, (count, 2 * LANES))
    return pltpu.roll(base, shift, 1, stride=1, stride_axis=0)


def filters(taps, layer):
    row_re, row_im = taps[2:3], taps[3:4]
    height = block_height(layer)
    before = height + 2 * KR
    upper = banded(row_re, height, 0) - banded(row_im, height, before)
    lower = banded(row_im, height, 0) + banded(row_re, height, before)
    row_mat = jnp.concatenate([upper, lower], axis=0).astype(jnp.bfloat16)
    col_re = banded(taps[0:1], LANES, 1)
    col_im = banded(taps[1:2], LANES, 1)
    upper = jnp.concatenate([col_re, -col_im], axis=1)
    lower = jnp.concatenate([col_im, col_re], axis=1)
    col_mat = jnp.concatenate([upper, lower], axis=0).astype(jnp.bfloat16)
    return row_mat, col_mat


def propagated(u_re, u_im, row_mat, col_mat, layer):
    height = layer_height(layer)
    block = block_height(layer)
    reach = block + 2 * KR
    parts = []
    for start in range(0, height, block):
        stacked = jnp.concatenate(
            [u_re[start : start + reach], u_im[start : start + reach]], axis=0
        )
        parts.append(
            jnp.dot(row_mat[:, : 2 * reach], stacked, preferred_element_type=jnp.float32)
        )
    rowed = jnp.concatenate(
        [part[:block] for part in parts] + [part[block:] for part in parts], axis=0
    )
    rowed = jnp.concatenate([rowed, jnp.zeros((2 * height, LANES), jnp.float32)], axis=1)
    rowed = pltpu.roll(rowed, HALF, 1).astype(jnp.bfloat16)
    windows = jnp.concatenate(
        [
            jnp.concatenate(
                [
                    rowed[:height, tile * LANES : (tile + 2) * LANES],
                    rowed[height:, tile * LANES : (tile + 2) * LANES],
                ],
                axis=1,
            )
            for tile in range(TILES)
        ],
        axis=0,
    )
    return lax.dot_general(
        windows, col_mat, (((1,), (1,)), ((), ())), preferred_element_type=jnp.float32
    )


def prepare_kernel(
    own, incident, in_chip, cross, far_even, far_odd, left_tab, right_tab,
    first, stereo, clear, col_mats, *row_mats
):
    sides = ordered(in_chip[NEAR:, :COLS], cross, far_even, far_odd)
    extended = []
    for part in range(2):
        low_near, high_near, low_far, high_far = (
            side[part * BAND : (part + 1) * BAND] for side in sides
        )
        pieces = [low_far, low_near, incident[part], high_near, high_far]
        extended.append(jnp.concatenate(pieces, axis=0))
    row_mat, col_mat = filters(own[0, 0:16, HALO_W:].astype(jnp.float32), 0)
    first[...] = propagated(extended[0], extended[1], row_mat, col_mat, 0)
    for layer in range(1, LAYERS):
        row_mat, col_mat = filters(own[layer, 0:16, HALO_W:].astype(jnp.float32), layer)
        row_mats[layer - 1][...] = row_mat
        col_mats[layer - 1] = col_mat
    packed = jnp.concatenate([own[layer, :, :HALO_W] for layer in range(LAYERS)], axis=0)
    clear[...] = clear_pixels(packed[:, COLS : COLS + NH])
    tiles = stereo_tiles([packed[:, :COLS]], left_tab, right_tab)
    for tile in range(TILES):
        for part in range(2):
            block = tiles[
                tile * LANES : (tile + 1) * LANES, part * LANES : (part + 1) * LANES
            ]
            stereo[part, :, tile * LANES : (tile + 1) * LANES] = block


def chain_kernel(
    in_chip, cross, far_even, far_odd, left_tab, right_tab, first, stereo, clear, col_mats, *rest
):
    row_mats, (out, field) = rest[: LAYERS - 1], rest[LAYERS - 1 :]
    low_near, high_near, low_far, high_far = ordered(in_chip[:NEAR], cross, far_even, far_odd)
    pieces = [
        low_far,
        low_near[0:BAND],
        high_near[0:BAND],
        high_far,
        low_near[BAND : 2 * BAND],
        high_near[BAND : 2 * BAND],
        low_near[2 * BAND : NEAR],
        high_near[2 * BAND : NEAR],
    ]
    halo = jnp.concatenate(pieces, axis=0)
    half = halo.shape[0] // 2
    halo_tiles = stereo_tiles(
        [halo[:half, :COLS], halo[half:, :COLS]], left_tab, right_tab
    )
    halo_clear = clear_pixels(halo[:, COLS : COLS + NH])
    begins = (0, half, half + 2 * BAND, 0)
    sides = (BAND + FAR, BAND, KR, 0)
    for layer in range(LAYERS):
        height = layer_height(layer)
        before = height + 2 * KR
        low, side = begins[layer], sides[layer]
        if layer == 0:
            columned = first
        else:
            columned = propagated(
                field[0, :before], field[1, :before], row_mats[layer - 1], col_mats[layer - 1], layer
            )
        band = slice(layer * BAND, (layer + 1) * BAND)
        pieces = [clear[band]]
        if side:
            pieces = [halo_clear[low : low + side], clear[band], halo_clear[low + side : low + 2 * side]]
        passing = jnp.concatenate(pieces, axis=0)
        for tile in range(TILES):
            span = slice(tile * height, (tile + 1) * height)
            lanes = slice(tile * LANES, (tile + 1) * LANES)
            row = (low // half * TILES + tile) * half + low % half
            for part in range(2):
                within = slice(part * LANES, (part + 1) * LANES)
                pieces = [stereo[part, band, lanes]]
                if side:
                    pieces = [
                        halo_tiles[row : row + side, within],
                        stereo[part, band, lanes],
                        halo_tiles[row + side : row + 2 * side, within],
                    ]
                added = jnp.concatenate(pieces, axis=0)
                value = passing[:, lanes] * columned[span, within] + added
                field[part, :height, lanes] = value.astype(jnp.bfloat16)
        for part in range(2):
            out[layer, part] = field[part, side : side + BAND]


def exchanged(value, axis, by, phase):
    count = lax.axis_size(axis)
    lower = [i for i in range(count - by) if (i // by) % 2 == phase]
    pairs = [(i, i + by) for i in lower] + [(i + by, i) for i in lower]
    return lax.ppermute(value, axis, pairs)


def neighbours(sent):
    in_chip, cross, far_even, far_odd = sent
    in_chip = exchanged(in_chip, "rows", 1, 0)
    cross = exchanged(cross, "rows", 1, 1)
    far_even = exchanged(far_even, "rows", 2, 0)
    far_odd = exchanged(far_odd, "rows", 2, 1)
    return in_chip, cross, far_even, far_odd


def call(kernel, out_shape, in_specs, scratch=(), flops=0, moved=10**6, limit=VMEM_LIMIT):
    vmem = pl.BlockSpec(memory_space=pltpu.VMEM)
    many = isinstance(out_shape, (tuple, list))
    return pl.pallas_call(
        kernel,
        out_shape=out_shape,
        in_specs=in_specs,
        out_specs=(vmem,) * len(out_shape) if many else vmem,
        scratch_shapes=scratch,
        compiler_params=pltpu.CompilerParams(vmem_limit_bytes=limit),
        cost_estimate=pl.CostEstimate(flops=flops, bytes_accessed=moved, transcendentals=0),
    )


def body(incident, row_taps, col_taps, hogel_light, silhouette, fill_counts, hogel_index):
    vmem = pl.BlockSpec(memory_space=pltpu.VMEM)
    hbm = pl.BlockSpec(memory_space=pltpu.HBM)
    bf16, f32 = jnp.bfloat16, jnp.float32
    shaped = jax.ShapeDtypeStruct
    held = [
        pltpu.VMEM(hogel_index.shape, jnp.int32),
        pltpu.SMEM(fill_counts.shape, jnp.int32),
        pltpu.VMEM(silhouette.shape, jnp.int32),
        pltpu.VMEM(row_taps.shape, bf16),
        pltpu.VMEM(col_taps.shape, bf16),
        pltpu.VMEM(hogel_light.shape, f32),
    ]
    payload, mine = call(
        pack_kernel,
        (shaped((LAYERS, BAND, FULL_W), bf16), shaped(incident.shape[1:], bf16)),
        [hbm] * 7,
        held + [pltpu.SemaphoreType.DMA((7,)), pltpu.VMEM((BAND, LANES), f32)],
        flops=10**7,
        limit=PACK_LIMIT,
    )(hogel_light, silhouette, fill_counts, hogel_index, row_taps, col_taps, incident)
    flat = mine.reshape(2 * BAND, COLS)
    own = lax.all_to_all(payload, "depth", 0, 0, tiled=True)
    cross_in = exchanged(flat, "rows", 1, 1)
    far_in = [exchanged(flat, "rows", 2, phase) for phase in range(2)]
    chip = shaped((NEAR + 2 * BAND, HALO_W), bf16)
    near = shaped((NEAR, HALO_W), bf16)
    far = shaped((FAR, HALO_W), bf16)
    halos = neighbours(
        call(halo_kernel, (chip, near, far, far), [vmem] * 5)(own, mine, cross_in, *far_in)
    )
    right_tab = jnp.asarray(right_table())
    made = call(
        prepare_kernel,
        [
            shaped((TILES * layer_height(0), 2 * LANES), f32),
            shaped((2, LANES, COLS), f32),
            shaped((LANES, COLS), f32),
            shaped((LAYERS - 1, 2 * LANES, 4 * LANES), bf16),
        ]
        + [shaped((2 * block_height(layer), 2 * LANES), bf16) for layer in range(1, LAYERS)],
        [vmem] * 8,
        flops=10**9,
        moved=3 * 10**6,
    )(own, mine, halos[0], cross_in, *far_in, jnp.asarray(left_table(LANES)), right_tab)
    halo_rows = NEAR + FAR
    result = call(
        chain_kernel,
        shaped((LAYERS, 2, BAND, COLS), bf16),
        [vmem] * (6 + len(made)),
        [pltpu.VMEM((2, layer_height(0), COLS), bf16)],
        flops=2 * 10**9,
        moved=3 * 10**6,
    )(*halos, jnp.asarray(left_table(halo_rows)), right_tab, *made)
    gathered = lax.all_to_all(result, "depth", 0, 0, tiled=True)
    return gathered[None, LAYERS - COLORS :]


def solution(mesh):
    placed = (
        P(None, None, "rows", None),
        P("depth", None, None, None),
        P("depth", None, None, None),
        P("depth", None, "rows", None),
        P("depth", "rows", None),
        P("depth", "rows"),
        P("depth", "rows", None),
    )
    return jax.shard_map(
        body,
        mesh=mesh,
        in_specs=placed,
        out_specs=P("depth", None, None, "rows", None),
        check_vma=False,
    )
```

```python
import math

import jax
import jax.numpy as jnp
import numpy as np
from jax import lax
from jax.experimental import pallas as pl
from jax.experimental.pallas import tpu as pltpu
from jax.sharding import PartitionSpec as P

HS = 16
KR = 16
KC = 63
COLORS = 3
LAYERS = 4
BAND = 32
COLS = 1024
NH = COLS // HS
LANES = 128
TILES = COLS // LANES
HALO_W = COLS + LANES
HALF = LANES // 2
FULL_W = COLS + 2 * LANES
NEAR = 2 * BAND + KR
FAR = KR
VMEM_LIMIT = 48 * 1024 * 1024
PACK_LIMIT = 63 * 1024 * 1024


def split_table(table):
    high = table.astype(jnp.bfloat16)
    low = (table - high.astype(np.float64)).astype(jnp.bfloat16)
    return high, low


def dft_pair():
    counter = np.arange(HS)
    angles = (counter[:, None] * counter[None, :] % HS) * (2.0 * math.pi / HS)
    return np.cos(angles) / math.sqrt(HS), np.sin(angles) / math.sqrt(HS)


def left_table(height):
    cos_tab, sin_tab = dft_pair()
    eye = np.eye(height // HS)
    full = np.concatenate([np.kron(eye, cos_tab), np.kron(eye, -sin_tab)], axis=0)
    return np.concatenate(split_table(full), axis=1)


def right_table():
    cos_tab, sin_tab = dft_pair()
    eye = np.eye(LANES // HS)
    cos_big, sin_big = np.kron(eye, cos_tab), np.kron(eye, sin_tab)
    full = np.concatenate(
        [
            np.concatenate([cos_big, -sin_big], axis=1),
            np.concatenate([sin_big, cos_big], axis=1),
        ],
        axis=0,
    )
    return full.astype(jnp.bfloat16)


def layer_height(layer):
    return BAND + 2 * KR * (LAYERS - 1 - layer)


def block_height(layer):
    height = layer_height(layer)
    return height // 2 if 2 * (height + 2 * KR) > 2 * LANES else height


def spread_matrix():
    tile = lax.broadcasted_iota(jnp.int32, (NH, COLS), 0)
    column = lax.broadcasted_iota(jnp.int32, (NH, COLS), 1)
    return jnp.where(column // HS == tile, 1.0, 0.0).astype(jnp.bfloat16)


def own_colour():
    return jnp.minimum(lax.axis_index("depth"), COLORS - 1)


def pack_kernel(light, edges, counts, listed, row_taps, col_taps, incident, out, mine, *scratch):
    held, sems, taps = scratch[:6], scratch[6], scratch[7]
    picked = pltpu.make_async_copy(incident.at[own_colour()], mine, sems.at[6])
    sources = (listed, counts, edges, row_taps, col_taps, light)
    copies = [
        pltpu.make_async_copy(source, target, sems.at[place])
        for place, (source, target) in enumerate(zip(sources, held))
    ]
    for copy in reversed(copies):
        copy.start()
    picked.start()
    listed, counts, edges, row_taps, col_taps, light = held
    spread = spread_matrix()
    slot = lax.broadcasted_iota(jnp.int32, (NH, NH), 0)
    place = lax.broadcasted_iota(jnp.int32, (NH, NH), 1)
    for copy in copies[:5]:
        copy.wait()
    rows = []
    for group in range(BAND // HS):
        listing = jnp.broadcast_to(listed[0, group : group + 1, :], (NH, NH))
        column = jnp.sum(jnp.where(slot == place, listing, 0), axis=1, keepdims=True)
        named = (column == place) & (slot < counts[0, group])
        live = jnp.max(jnp.where(named, 1.0, 0.0), axis=0, keepdims=True)
        rows.append(jnp.broadcast_to(live, (HS, NH)))
    live_rows = jnp.concatenate(rows, axis=0).astype(jnp.bfloat16)
    live_pix = jnp.dot(live_rows, spread, preferred_element_type=jnp.float32)
    edge_tile = jnp.concatenate(
        [edges[0].astype(jnp.float32), jnp.zeros((BAND, LANES - NH), jnp.float32)], axis=1
    ).astype(jnp.bfloat16)
    for colour in range(COLORS):
        out[colour, :, COLS:HALO_W] = edge_tile
        taps[...] = jnp.zeros_like(taps)
        taps[0:2, : 2 * KC + 1] = col_taps[0, colour].astype(jnp.float32)
        taps[2:4, : 2 * KR + 1] = row_taps[0, colour].astype(jnp.float32)
        out[colour, :, HALO_W:] = taps[...].astype(jnp.bfloat16)
    for spare in range(COLORS, LAYERS):
        out[spare] = jnp.zeros((BAND, FULL_W), jnp.bfloat16)
    copies[5].wait()
    for colour in range(COLORS):
        out[colour, :, :COLS] = (light[0, colour] * live_pix).astype(jnp.bfloat16)
    picked.wait()


def halo_kernel(own, in_chip, cross, far_even, far_odd):
    band = lax.axis_index("rows")
    core = band % 2
    odd = (band // 2) % 2
    last = BAND - KR
    for near, start in ((in_chip, (1 - core) * last), (cross, core * last)):
        near[0:BAND] = own[0, :, :HALO_W]
        near[BAND : 2 * BAND] = own[1, :, :HALO_W]
        near[2 * BAND : NEAR] = own[2, pl.ds(pl.multiple_of(start, KR), KR), :HALO_W]
    for far, start in ((far_even, (1 - odd) * last), (far_odd, odd * last)):
        far[...] = own[0, pl.ds(pl.multiple_of(start, KR), KR), :HALO_W]


def ordered(in_chip, cross, far_even, far_odd):
    band = lax.axis_index("rows")
    even_core = band % 2 == 0
    even_chip = (band // 2) % 2 == 0
    in_chip, cross = in_chip[...], cross[...]
    far_even, far_odd = far_even[...], far_odd[...]
    return (
        jnp.where(even_core, cross, in_chip),
        jnp.where(even_core, in_chip, cross),
        jnp.where(even_chip, far_odd, far_even),
        jnp.where(even_chip, far_even, far_odd),
    )


def tiles_below(value, height):
    return jnp.concatenate(
        [
            jnp.concatenate(
                [
                    value[:height, tile * LANES : (tile + 1) * LANES],
                    value[height:, tile * LANES : (tile + 1) * LANES],
                ],
                axis=1,
            )
            for tile in range(TILES)
        ],
        axis=0,
    )


def stereo_tiles(blocks, left_tab, right_tab):
    arranged = []
    for light in blocks:
        doubled = jnp.concatenate([light, light], axis=0)
        left = jnp.dot(left_tab[...], doubled, preferred_element_type=jnp.float32)
        arranged.append(tiles_below(left.astype(jnp.bfloat16), light.shape[0]))
    arranged = jnp.concatenate(arranged, axis=0) if len(arranged) > 1 else arranged[0]
    return jnp.dot(arranged, right_tab[...], preferred_element_type=jnp.float32)


def clear_pixels(edges):
    edge_pix = jnp.dot(edges, spread_matrix(), preferred_element_type=jnp.float32)
    within = (lax.broadcasted_iota(jnp.int32, (1, COLS), 1) % HS).astype(jnp.float32)
    return jnp.where(within < edge_pix, 1.0, 0.0)


def banded(line, count, shift):
    base = jnp.concatenate([line, jnp.zeros((1, LANES), jnp.float32)], axis=1)
    base = jnp.broadcast_to(base, (count, 2 * LANES))
    return pltpu.roll(base, shift, 1, stride=1, stride_axis=0)


def filters(taps, layer):
    row_re, row_im = taps[2:3], taps[3:4]
    height = block_height(layer)
    before = height + 2 * KR
    upper = banded(row_re, height, 0) - banded(row_im, height, before)
    lower = banded(row_im, height, 0) + banded(row_re, height, before)
    row_mat = jnp.concatenate([upper, lower], axis=0).astype(jnp.bfloat16)
    col_re = banded(taps[0:1], LANES, 1)
    col_im = banded(taps[1:2], LANES, 1)
    upper = jnp.concatenate([col_re, -col_im], axis=1)
    lower = jnp.concatenate([col_im, col_re], axis=1)
    col_mat = jnp.concatenate([upper, lower], axis=0).astype(jnp.bfloat16)
    return row_mat, col_mat


def propagated(u_re, u_im, row_mat, col_mat, layer):
    height = layer_height(layer)
    block = block_height(layer)
    reach = block + 2 * KR
    parts = []
    for start in range(0, height, block):
        stacked = jnp.concatenate(
            [u_re[start : start + reach], u_im[start : start + reach]], axis=0
        )
        parts.append(
            jnp.dot(row_mat[:, : 2 * reach], stacked, preferred_element_type=jnp.float32)
        )
    rowed = jnp.concatenate(
        [part[:block] for part in parts] + [part[block:] for part in parts], axis=0
    )
    rowed = jnp.concatenate([rowed, jnp.zeros((2 * height, LANES), jnp.float32)], axis=1)
    rowed = pltpu.roll(rowed, HALF, 1).astype(jnp.bfloat16)
    windows = jnp.concatenate(
        [
            jnp.concatenate(
                [
                    rowed[:height, tile * LANES : (tile + 2) * LANES],
                    rowed[height:, tile * LANES : (tile + 2) * LANES],
                ],
                axis=1,
            )
            for tile in range(TILES)
        ],
        axis=0,
    )
    return lax.dot_general(
        windows, col_mat, (((1,), (1,)), ((), ())), preferred_element_type=jnp.float32
    )


def prepare_kernel(
    own, incident, in_chip, cross, far_even, far_odd, left_tab, right_tab,
    first, stereo, clear, col_mats, *row_mats
):
    low_near, high_near, low_far, high_far = ordered(in_chip, cross, far_even, far_odd)
    extended = []
    for part in range(2):
        pieces = [low_far, low_near, incident[...], high_near, high_far]
        pieces = [piece[part * BAND : (part + 1) * BAND] for piece in pieces]
        extended.append(jnp.concatenate(pieces, axis=0))
    row_mat, col_mat = filters(own[0, 0:16, HALO_W:].astype(jnp.float32), 0)
    first[...] = propagated(extended[0], extended[1], row_mat, col_mat, 0)
    for layer in range(1, LAYERS):
        row_mat, col_mat = filters(own[layer, 0:16, HALO_W:].astype(jnp.float32), layer)
        row_mats[layer - 1][...] = row_mat
        col_mats[layer - 1] = col_mat
    packed = jnp.concatenate([own[layer, :, :HALO_W] for layer in range(LAYERS)], axis=0)
    clear[...] = clear_pixels(packed[:, COLS : COLS + NH])
    tiles = stereo_tiles([packed[:, :COLS]], left_tab, right_tab)
    for tile in range(TILES):
        for part in range(2):
            block = tiles[
                tile * LANES : (tile + 1) * LANES, part * LANES : (part + 1) * LANES
            ]
            stereo[part, :, tile * LANES : (tile + 1) * LANES] = block


def chain_kernel(
    in_chip, cross, far_even, far_odd, left_tab, right_tab, first, stereo, clear, col_mats, *rest
):
    row_mats, (out, field) = rest[: LAYERS - 1], rest[LAYERS - 1 :]
    low_near, high_near, low_far, high_far = ordered(in_chip, cross, far_even, far_odd)
    pieces = [
        low_far,
        low_near[0:BAND],
        high_near[0:BAND],
        high_far,
        low_near[BAND : 2 * BAND],
        high_near[BAND : 2 * BAND],
        low_near[2 * BAND : NEAR],
        high_near[2 * BAND : NEAR],
    ]
    halo = jnp.concatenate(pieces, axis=0)
    half = halo.shape[0] // 2
    halo_tiles = stereo_tiles(
        [halo[:half, :COLS], halo[half:, :COLS]], left_tab, right_tab
    )
    halo_clear = clear_pixels(halo[:, COLS : COLS + NH])
    begins = (0, half, half + 2 * BAND, 0)
    sides = (BAND + FAR, BAND, KR, 0)
    for layer in range(LAYERS):
        height = layer_height(layer)
        before = height + 2 * KR
        low, side = begins[layer], sides[layer]
        if layer == 0:
            columned = first
        else:
            columned = propagated(
                field[0, :before], field[1, :before], row_mats[layer - 1], col_mats[layer - 1], layer
            )
        band = slice(layer * BAND, (layer + 1) * BAND)
        pieces = [clear[band]]
        if side:
            pieces = [halo_clear[low : low + side], clear[band], halo_clear[low + side : low + 2 * side]]
        passing = jnp.concatenate(pieces, axis=0)
        for tile in range(TILES):
            span = slice(tile * height, (tile + 1) * height)
            lanes = slice(tile * LANES, (tile + 1) * LANES)
            row = (low // half * TILES + tile) * half + low % half
            for part in range(2):
                within = slice(part * LANES, (part + 1) * LANES)
                pieces = [stereo[part, band, lanes]]
                if side:
                    pieces = [
                        halo_tiles[row : row + side, within],
                        stereo[part, band, lanes],
                        halo_tiles[row + side : row + 2 * side, within],
                    ]
                added = jnp.concatenate(pieces, axis=0)
                value = passing[:, lanes] * columned[span, within] + added
                field[part, :height, lanes] = value.astype(jnp.bfloat16)
        for part in range(2):
            out[layer, part] = field[part, side : side + BAND]


def exchanged(value, axis, by, phase):
    count = lax.axis_size(axis)
    lower = [i for i in range(count - by) if (i // by) % 2 == phase]
    pairs = [(i, i + by) for i in lower] + [(i + by, i) for i in lower]
    return lax.ppermute(value, axis, pairs)


def neighbours(sent):
    in_chip, cross, far_even, far_odd = sent
    cross = exchanged(cross, "rows", 1, 1)
    far_even = exchanged(far_even, "rows", 2, 0)
    far_odd = exchanged(far_odd, "rows", 2, 1)
    in_chip = exchanged(in_chip, "rows", 1, 0)
    return in_chip, cross, far_even, far_odd


def call(kernel, out_shape, in_specs, scratch=(), flops=0, moved=10**6, limit=VMEM_LIMIT):
    vmem = pl.BlockSpec(memory_space=pltpu.VMEM)
    many = isinstance(out_shape, (tuple, list))
    return pl.pallas_call(
        kernel,
        out_shape=out_shape,
        in_specs=in_specs,
        out_specs=(vmem,) * len(out_shape) if many else vmem,
        scratch_shapes=scratch,
        compiler_params=pltpu.CompilerParams(vmem_limit_bytes=limit),
        cost_estimate=pl.CostEstimate(flops=flops, bytes_accessed=moved, transcendentals=0),
    )


def body(incident, row_taps, col_taps, hogel_light, silhouette, fill_counts, hogel_index):
    vmem = pl.BlockSpec(memory_space=pltpu.VMEM)
    hbm = pl.BlockSpec(memory_space=pltpu.HBM)
    bf16, f32 = jnp.bfloat16, jnp.float32
    shaped = jax.ShapeDtypeStruct
    held = [
        pltpu.VMEM(hogel_index.shape, jnp.int32),
        pltpu.SMEM(fill_counts.shape, jnp.int32),
        pltpu.VMEM(silhouette.shape, jnp.int32),
        pltpu.VMEM(row_taps.shape, bf16),
        pltpu.VMEM(col_taps.shape, bf16),
        pltpu.VMEM(hogel_light.shape, f32),
    ]
    payload, mine = call(
        pack_kernel,
        (shaped((LAYERS, BAND, FULL_W), bf16), shaped(incident.shape[1:], bf16)),
        [hbm] * 7,
        held + [pltpu.SemaphoreType.DMA((7,)), pltpu.VMEM((BAND, LANES), f32)],
        flops=10**7,
        limit=PACK_LIMIT,
    )(hogel_light, silhouette, fill_counts, hogel_index, row_taps, col_taps, incident)
    mine = mine.reshape(2 * BAND, COLS)
    own = lax.all_to_all(payload, "depth", 0, 0, tiled=True)
    arrived = neighbours((mine,) * 4)
    near = shaped((NEAR, HALO_W), bf16)
    far = shaped((FAR, HALO_W), bf16)
    halos = neighbours(call(halo_kernel, (near, near, far, far), [vmem])(own))
    right_tab = jnp.asarray(right_table())
    made = call(
        prepare_kernel,
        [
            shaped((TILES * layer_height(0), 2 * LANES), f32),
            shaped((2, LANES, COLS), f32),
            shaped((LANES, COLS), f32),
            shaped((LAYERS - 1, 2 * LANES, 4 * LANES), bf16),
        ]
        + [shaped((2 * block_height(layer), 2 * LANES), bf16) for layer in range(1, LAYERS)],
        [vmem] * 8,
        flops=10**9,
        moved=3 * 10**6,
    )(own, mine, *arrived, jnp.asarray(left_table(LANES)), right_tab)
    halo_rows = NEAR + FAR
    result = call(
        chain_kernel,
        shaped((LAYERS, 2, BAND, COLS), bf16),
        [vmem] * (6 + len(made)),
        [pltpu.VMEM((2, layer_height(0), COLS), bf16)],
        flops=2 * 10**9,
        moved=3 * 10**6,
    )(*halos, jnp.asarray(left_table(halo_rows)), right_tab, *made)
    gathered = lax.all_to_all(result, "depth", 0, 0, tiled=True)
    return gathered[None, :COLORS]


def solution(mesh):
    placed = (
        P(None, None, "rows", None),
        P("depth", None, None, None),
        P("depth", None, None, None),
        P("depth", None, "rows", None),
        P("depth", "rows", None),
        P("depth", "rows"),
        P("depth", "rows", None),
    )
    return jax.shard_map(
        body,
        mesh=mesh,
        in_specs=placed,
        out_specs=P("depth", None, None, "rows", None),
        check_vma=False,
    )
```

```python
import math

import jax
import jax.numpy as jnp
import numpy as np
from jax import lax
from jax.experimental import pallas as pl
from jax.experimental.pallas import tpu as pltpu
from jax.sharding import PartitionSpec as P

HS = 16
KR = 16
KC = 63
COLORS = 3
LAYERS = 4
BAND = 32
COLS = 1024
NH = COLS // HS
LANES = 128
TILES = COLS // LANES
HALO_W = COLS + LANES
HALF = LANES // 2
FULL_W = COLS + 2 * LANES
NEAR = 2 * BAND + KR
FAR = KR
REACH = 5
VMEM_LIMIT = 48 * 1024 * 1024
PACK_LIMIT = 63 * 1024 * 1024


def split_table(table):
    high = table.astype(jnp.bfloat16)
    low = (table - high.astype(np.float64)).astype(jnp.bfloat16)
    return high, low


def dft_pair():
    counter = np.arange(HS)
    angles = (counter[:, None] * counter[None, :] % HS) * (2.0 * math.pi / HS)
    return np.cos(angles) / math.sqrt(HS), np.sin(angles) / math.sqrt(HS)


def left_table(height):
    cos_tab, sin_tab = dft_pair()
    eye = np.eye(height // HS)
    full = np.concatenate([np.kron(eye, cos_tab), np.kron(eye, -sin_tab)], axis=0)
    return np.concatenate(split_table(full), axis=1)


def right_table():
    cos_tab, sin_tab = dft_pair()
    eye = np.eye(LANES // HS)
    cos_big, sin_big = np.kron(eye, cos_tab), np.kron(eye, sin_tab)
    full = np.concatenate(
        [
            np.concatenate([cos_big, -sin_big], axis=1),
            np.concatenate([sin_big, cos_big], axis=1),
        ],
        axis=0,
    )
    return full.astype(jnp.bfloat16)


def layer_height(layer):
    return BAND + 2 * KR * (LAYERS - 1 - layer)


def block_height(layer):
    height = layer_height(layer)
    return height // 2 if 2 * (height + 2 * KR) > 2 * LANES else height


def spread_matrix():
    tile = lax.broadcasted_iota(jnp.int32, (NH, COLS), 0)
    column = lax.broadcasted_iota(jnp.int32, (NH, COLS), 1)
    return jnp.where(column // HS == tile, 1.0, 0.0).astype(jnp.bfloat16)


def own_colour():
    return jnp.minimum(lax.axis_index("depth"), COLORS - 1)


def pack_kernel(light, edges, counts, listed, row_taps, col_taps, incident, out, mine, *scratch):
    held, sems, taps = scratch[:6], scratch[6], scratch[7]
    picked = pltpu.make_async_copy(incident.at[own_colour()], mine, sems.at[6])
    sources = (listed, counts, edges, row_taps, col_taps, light)
    copies = [
        pltpu.make_async_copy(source, target, sems.at[place])
        for place, (source, target) in enumerate(zip(sources, held))
    ]
    for copy in reversed(copies):
        copy.start()
    picked.start()
    listed, counts, edges, row_taps, col_taps, light = held
    spread = spread_matrix()
    slot = lax.broadcasted_iota(jnp.int32, (NH, NH), 0)
    place = lax.broadcasted_iota(jnp.int32, (NH, NH), 1)
    for copy in copies[:5]:
        copy.wait()
    rows = []
    for group in range(BAND // HS):
        listing = jnp.broadcast_to(listed[0, group : group + 1, :], (NH, NH))
        column = jnp.sum(jnp.where(slot == place, listing, 0), axis=1, keepdims=True)
        named = (column == place) & (slot < counts[0, group])
        live = jnp.max(jnp.where(named, 1.0, 0.0), axis=0, keepdims=True)
        rows.append(jnp.broadcast_to(live, (HS, NH)))
    live_rows = jnp.concatenate(rows, axis=0).astype(jnp.bfloat16)
    live_pix = jnp.dot(live_rows, spread, preferred_element_type=jnp.float32)
    edge_tile = jnp.concatenate(
        [edges[0].astype(jnp.float32), jnp.zeros((BAND, LANES - NH), jnp.float32)], axis=1
    ).astype(jnp.bfloat16)
    for colour in range(COLORS):
        out[colour, :, COLS:HALO_W] = edge_tile
        taps[...] = jnp.zeros_like(taps)
        taps[0:2, : 2 * KC + 1] = col_taps[0, colour].astype(jnp.float32)
        taps[2:4, : 2 * KR + 1] = row_taps[0, colour].astype(jnp.float32)
        out[colour, :, HALO_W:] = taps[...].astype(jnp.bfloat16)
    for spare in range(COLORS, LAYERS):
        out[spare] = jnp.zeros((BAND, FULL_W), jnp.bfloat16)
    copies[5].wait()
    for colour in range(COLORS):
        out[colour, :, :COLS] = (light[0, colour] * live_pix).astype(jnp.bfloat16)
    picked.wait()


def halo_kernel(own, in_chip, cross, far_even, far_odd):
    band = lax.axis_index("rows")
    core = band % 2
    odd = (band // 2) % 2
    last = BAND - KR
    for near, start in ((in_chip, (1 - core) * last), (cross, core * last)):
        near[0:BAND] = own[0, :, :HALO_W]
        near[BAND : 2 * BAND] = own[1, :, :HALO_W]
        near[2 * BAND : NEAR] = own[2, pl.ds(pl.multiple_of(start, KR), KR), :HALO_W]
    for far, start in ((far_even, (1 - odd) * last), (far_odd, odd * last)):
        far[...] = own[0, pl.ds(pl.multiple_of(start, KR), KR), :HALO_W]


def ordered(in_chip, cross, far_even, far_odd):
    band = lax.axis_index("rows")
    even_core = band % 2 == 0
    even_chip = (band // 2) % 2 == 0
    in_chip, cross = in_chip[...], cross[...]
    far_even, far_odd = far_even[...], far_odd[...]
    return (
        jnp.where(even_core, cross, in_chip),
        jnp.where(even_core, in_chip, cross),
        jnp.where(even_chip, far_odd, far_even),
        jnp.where(even_chip, far_even, far_odd),
    )


def tiles_below(value, height):
    return jnp.concatenate(
        [
            jnp.concatenate(
                [
                    value[:height, tile * LANES : (tile + 1) * LANES],
                    value[height:, tile * LANES : (tile + 1) * LANES],
                ],
                axis=1,
            )
            for tile in range(TILES)
        ],
        axis=0,
    )


def stereo_tiles(blocks, left_tab, right_tab):
    arranged = []
    for light in blocks:
        doubled = jnp.concatenate([light, light], axis=0)
        left = jnp.dot(left_tab[...], doubled, preferred_element_type=jnp.float32)
        arranged.append(tiles_below(left.astype(jnp.bfloat16), light.shape[0]))
    arranged = jnp.concatenate(arranged, axis=0) if len(arranged) > 1 else arranged[0]
    return jnp.dot(arranged, right_tab[...], preferred_element_type=jnp.float32)


def clear_pixels(edges):
    edge_pix = jnp.dot(edges, spread_matrix(), preferred_element_type=jnp.float32)
    within = (lax.broadcasted_iota(jnp.int32, (1, COLS), 1) % HS).astype(jnp.float32)
    return jnp.where(within < edge_pix, 1.0, 0.0)


def banded(line, count, shift):
    base = jnp.concatenate([line, jnp.zeros((1, LANES), jnp.float32)], axis=1)
    base = jnp.broadcast_to(base, (count, 2 * LANES))
    return pltpu.roll(base, shift, 1, stride=1, stride_axis=0)


def filters(taps, layer):
    row_re, row_im = taps[2:3], taps[3:4]
    height = block_height(layer)
    before = height + 2 * KR
    upper = banded(row_re, height, 0) - banded(row_im, height, before)
    lower = banded(row_im, height, 0) + banded(row_re, height, before)
    row_mat = jnp.concatenate([upper, lower], axis=0).astype(jnp.bfloat16)
    col_re = banded(taps[0:1], LANES, 1)
    col_im = banded(taps[1:2], LANES, 1)
    upper = jnp.concatenate([col_re, -col_im], axis=1)
    lower = jnp.concatenate([col_im, col_re], axis=1)
    col_mat = jnp.concatenate([upper, lower], axis=0).astype(jnp.bfloat16)
    return row_mat, col_mat


def propagated(u_re, u_im, row_mat, col_mat, layer):
    height = layer_height(layer)
    block = block_height(layer)
    reach = block + 2 * KR
    parts = []
    for start in range(0, height, block):
        stacked = jnp.concatenate(
            [u_re[start : start + reach], u_im[start : start + reach]], axis=0
        )
        parts.append(
            jnp.dot(row_mat[:, : 2 * reach], stacked, preferred_element_type=jnp.float32)
        )
    rowed = jnp.concatenate(
        [part[:block] for part in parts] + [part[block:] for part in parts], axis=0
    )
    rowed = jnp.concatenate([rowed, jnp.zeros((2 * height, LANES), jnp.float32)], axis=1)
    rowed = pltpu.roll(rowed, HALF, 1).astype(jnp.bfloat16)
    windows = jnp.concatenate(
        [
            jnp.concatenate(
                [
                    rowed[:height, tile * LANES : (tile + 2) * LANES],
                    rowed[height:, tile * LANES : (tile + 2) * LANES],
                ],
                axis=1,
            )
            for tile in range(TILES)
        ],
        axis=0,
    )
    return lax.dot_general(
        windows, col_mat, (((1,), (1,)), ((), ())), preferred_element_type=jnp.float32
    )


def prepare_kernel(
    own, bands, left_tab, right_tab, first, stereo, clear, col_mats, *rest
):
    row_mats, (near, sems) = rest[:-2], rest[-2:]
    here = lax.axis_index("rows")
    count = lax.axis_size("rows")
    for place in range(REACH):
        band = here + place - REACH // 2
        inside = (band >= 0) & (band < count)

        @pl.when(inside)
        def fetch(place=place, band=band):
            pltpu.make_async_copy(bands.at[band], near.at[place], sems.at[place]).start()

        @pl.when(jnp.logical_not(inside))
        def blank(place=place):
            near[place] = jnp.zeros((2 * BAND, COLS), jnp.bfloat16)

    for layer in range(1, LAYERS):
        row_mat, col_mat = filters(own[layer, 0:16, HALO_W:].astype(jnp.float32), layer)
        row_mats[layer - 1][...] = row_mat
        col_mats[layer - 1] = col_mat
    packed = jnp.concatenate([own[layer, :, :HALO_W] for layer in range(LAYERS)], axis=0)
    clear[...] = clear_pixels(packed[:, COLS : COLS + NH])
    tiles = stereo_tiles([packed[:, :COLS]], left_tab, right_tab)
    for tile in range(TILES):
        for part in range(2):
            block = tiles[
                tile * LANES : (tile + 1) * LANES, part * LANES : (part + 1) * LANES
            ]
            stereo[part, :, tile * LANES : (tile + 1) * LANES] = block
    for place in range(REACH):
        band = here + place - REACH // 2

        @pl.when((band >= 0) & (band < count))
        def arrive(place=place, band=band):
            pltpu.make_async_copy(bands.at[band], near.at[place], sems.at[place]).wait()

    extended = [
        jnp.concatenate(
            [near[place, part * BAND : (part + 1) * BAND] for place in range(REACH)], axis=0
        )
        for part in range(2)
    ]
    row_mat, col_mat = filters(own[0, 0:16, HALO_W:].astype(jnp.float32), 0)
    first[...] = propagated(extended[0], extended[1], row_mat, col_mat, 0)


def chain_kernel(
    in_chip, cross, far_even, far_odd, left_tab, right_tab, first, stereo, clear, col_mats, *rest
):
    row_mats, (out, field) = rest[: LAYERS - 1], rest[LAYERS - 1 :]
    low_near, high_near, low_far, high_far = ordered(in_chip, cross, far_even, far_odd)
    pieces = [
        low_far,
        low_near[0:BAND],
        high_near[0:BAND],
        high_far,
        low_near[BAND : 2 * BAND],
        high_near[BAND : 2 * BAND],
        low_near[2 * BAND : NEAR],
        high_near[2 * BAND : NEAR],
    ]
    halo = jnp.concatenate(pieces, axis=0)
    half = halo.shape[0] // 2
    halo_tiles = stereo_tiles(
        [halo[:half, :COLS], halo[half:, :COLS]], left_tab, right_tab
    )
    halo_clear = clear_pixels(halo[:, COLS : COLS + NH])
    begins = (0, half, half + 2 * BAND, 0)
    sides = (BAND + FAR, BAND, KR, 0)
    for layer in range(LAYERS):
        height = layer_height(layer)
        before = height + 2 * KR
        low, side = begins[layer], sides[layer]
        if layer == 0:
            columned = first
        else:
            columned = propagated(
                field[0, :before], field[1, :before], row_mats[layer - 1], col_mats[layer - 1], layer
            )
        band = slice(layer * BAND, (layer + 1) * BAND)
        pieces = [clear[band]]
        if side:
            pieces = [halo_clear[low : low + side], clear[band], halo_clear[low + side : low + 2 * side]]
        passing = jnp.concatenate(pieces, axis=0)
        for tile in range(TILES):
            span = slice(tile * height, (tile + 1) * height)
            lanes = slice(tile * LANES, (tile + 1) * LANES)
            row = (low // half * TILES + tile) * half + low % half
            for part in range(2):
                within = slice(part * LANES, (part + 1) * LANES)
                pieces = [stereo[part, band, lanes]]
                if side:
                    pieces = [
                        halo_tiles[row : row + side, within],
                        stereo[part, band, lanes],
                        halo_tiles[row + side : row + 2 * side, within],
                    ]
                added = jnp.concatenate(pieces, axis=0)
                value = passing[:, lanes] * columned[span, within] + added
                field[part, :height, lanes] = value.astype(jnp.bfloat16)
        for part in range(2):
            out[layer, part] = field[part, side : side + BAND]


def exchanged(value, axis, by, phase):
    count = lax.axis_size(axis)
    lower = [i for i in range(count - by) if (i // by) % 2 == phase]
    pairs = [(i, i + by) for i in lower] + [(i + by, i) for i in lower]
    return lax.ppermute(value, axis, pairs)


def neighbours(sent):
    in_chip, cross, far_even, far_odd = sent
    cross = exchanged(cross, "rows", 1, 1)
    far_even = exchanged(far_even, "rows", 2, 0)
    far_odd = exchanged(far_odd, "rows", 2, 1)
    in_chip = exchanged(in_chip, "rows", 1, 0)
    return in_chip, cross, far_even, far_odd


def call(kernel, out_shape, in_specs, scratch=(), flops=0, moved=10**6, limit=VMEM_LIMIT):
    vmem = pl.BlockSpec(memory_space=pltpu.VMEM)
    many = isinstance(out_shape, (tuple, list))
    return pl.pallas_call(
        kernel,
        out_shape=out_shape,
        in_specs=in_specs,
        out_specs=(vmem,) * len(out_shape) if many else vmem,
        scratch_shapes=scratch,
        compiler_params=pltpu.CompilerParams(vmem_limit_bytes=limit),
        cost_estimate=pl.CostEstimate(flops=flops, bytes_accessed=moved, transcendentals=0),
    )


def body(incident, row_taps, col_taps, hogel_light, silhouette, fill_counts, hogel_index):
    vmem = pl.BlockSpec(memory_space=pltpu.VMEM)
    hbm = pl.BlockSpec(memory_space=pltpu.HBM)
    bf16, f32 = jnp.bfloat16, jnp.float32
    shaped = jax.ShapeDtypeStruct
    held = [
        pltpu.VMEM(hogel_index.shape, jnp.int32),
        pltpu.SMEM(fill_counts.shape, jnp.int32),
        pltpu.VMEM(silhouette.shape, jnp.int32),
        pltpu.VMEM(row_taps.shape, bf16),
        pltpu.VMEM(col_taps.shape, bf16),
        pltpu.VMEM(hogel_light.shape, f32),
    ]
    payload, mine = call(
        pack_kernel,
        (shaped((LAYERS, BAND, FULL_W), bf16), shaped(incident.shape[1:], bf16)),
        [hbm] * 7,
        held + [pltpu.SemaphoreType.DMA((7,)), pltpu.VMEM((BAND, LANES), f32)],
        flops=10**7,
        limit=PACK_LIMIT,
    )(hogel_light, silhouette, fill_counts, hogel_index, row_taps, col_taps, incident)
    mine = mine.reshape(2 * BAND, COLS)
    own = lax.all_to_all(payload, "depth", 0, 0, tiled=True)
    bands = lax.all_gather(mine, "rows")
    near = shaped((NEAR, HALO_W), bf16)
    far = shaped((FAR, HALO_W), bf16)
    halos = neighbours(call(halo_kernel, (near, near, far, far), [vmem])(own))
    right_tab = jnp.asarray(right_table())
    made = call(
        prepare_kernel,
        [
            shaped((TILES * layer_height(0), 2 * LANES), f32),
            shaped((2, LANES, COLS), f32),
            shaped((LANES, COLS), f32),
            shaped((LAYERS - 1, 2 * LANES, 4 * LANES), bf16),
        ]
        + [shaped((2 * block_height(layer), 2 * LANES), bf16) for layer in range(1, LAYERS)],
        [vmem, hbm, vmem, vmem],
        [
            pltpu.VMEM((REACH, 2 * BAND, COLS), bf16),
            pltpu.SemaphoreType.DMA((REACH,)),
        ],
        flops=10**9,
        moved=3 * 10**6,
    )(own, bands, jnp.asarray(left_table(LANES)), right_tab)
    halo_rows = NEAR + FAR
    result = call(
        chain_kernel,
        shaped((LAYERS, 2, BAND, COLS), bf16),
        [vmem] * (6 + len(made)),
        [pltpu.VMEM((2, layer_height(0), COLS), bf16)],
        flops=2 * 10**9,
        moved=3 * 10**6,
    )(*halos, jnp.asarray(left_table(halo_rows)), right_tab, *made)
    gathered = lax.all_to_all(result, "depth", 0, 0, tiled=True)
    return gathered[None, :COLORS]


def solution(mesh):
    placed = (
        P(None, None, "rows", None),
        P("depth", None, None, None),
        P("depth", None, None, None),
        P("depth", None, "rows", None),
        P("depth", "rows", None),
        P("depth", "rows"),
        P("depth", "rows", None),
    )
    return jax.shard_map(
        body,
        mesh=mesh,
        in_specs=placed,
        out_specs=P("depth", None, None, "rows", None),
        check_vma=False,
    )
```

```python
import math

import jax
import jax.numpy as jnp
import numpy as np
from jax import lax
from jax.experimental import pallas as pl
from jax.experimental.pallas import tpu as pltpu
from jax.sharding import PartitionSpec as P

HS = 16
KR = 16
KC = 63
COLORS = 3
LAYERS = 4
BAND = 32
COLS = 1024
NH = COLS // HS
LANES = 128
TILES = COLS // LANES
HALO_W = COLS + LANES
HALF = LANES // 2
FULL_W = COLS + 2 * LANES
NEAR = 2 * BAND + KR
FAR = KR
VMEM_LIMIT = 48 * 1024 * 1024
PACK_LIMIT = 63 * 1024 * 1024


def split_table(table):
    high = table.astype(jnp.bfloat16)
    low = (table - high.astype(np.float64)).astype(jnp.bfloat16)
    return high, low


def dft_pair():
    counter = np.arange(HS)
    angles = (counter[:, None] * counter[None, :] % HS) * (2.0 * math.pi / HS)
    return np.cos(angles) / math.sqrt(HS), np.sin(angles) / math.sqrt(HS)


def left_table(height):
    cos_tab, sin_tab = dft_pair()
    eye = np.eye(height // HS)
    full = np.concatenate([np.kron(eye, cos_tab), np.kron(eye, -sin_tab)], axis=0)
    return np.concatenate(split_table(full), axis=1)


def right_table():
    cos_tab, sin_tab = dft_pair()
    eye = np.eye(LANES // HS)
    cos_big, sin_big = np.kron(eye, cos_tab), np.kron(eye, sin_tab)
    full = np.concatenate(
        [
            np.concatenate([cos_big, -sin_big], axis=1),
            np.concatenate([sin_big, cos_big], axis=1),
        ],
        axis=0,
    )
    return full.astype(jnp.bfloat16)


def layer_height(layer):
    return BAND + 2 * KR * (LAYERS - 1 - layer)


def block_height(layer):
    height = layer_height(layer)
    return height // 2 if 2 * (height + 2 * KR) > 2 * LANES else height


def spread_matrix():
    tile = lax.broadcasted_iota(jnp.int32, (NH, COLS), 0)
    column = lax.broadcasted_iota(jnp.int32, (NH, COLS), 1)
    return jnp.where(column // HS == tile, 1.0, 0.0).astype(jnp.bfloat16)


def own_colour():
    return jnp.minimum(lax.axis_index("depth"), COLORS - 1)


def pack_kernel(light, edges, counts, listed, row_taps, col_taps, incident, out, mine, *scratch):
    held, sems, taps = scratch[:6], scratch[6], scratch[7]
    picked = pltpu.make_async_copy(incident.at[own_colour()], mine, sems.at[6])
    sources = (listed, counts, edges, row_taps, col_taps, light)
    copies = [
        pltpu.make_async_copy(source, target, sems.at[place])
        for place, (source, target) in enumerate(zip(sources, held))
    ]
    for copy in reversed(copies):
        copy.start()
    picked.start()
    listed, counts, edges, row_taps, col_taps, light = held
    spread = spread_matrix()
    slot = lax.broadcasted_iota(jnp.int32, (NH, NH), 0)
    place = lax.broadcasted_iota(jnp.int32, (NH, NH), 1)
    for copy in copies[:5]:
        copy.wait()
    rows = []
    for group in range(BAND // HS):
        listing = jnp.broadcast_to(listed[0, group : group + 1, :], (NH, NH))
        column = jnp.sum(jnp.where(slot == place, listing, 0), axis=1, keepdims=True)
        named = (column == place) & (slot < counts[0, group])
        live = jnp.max(jnp.where(named, 1.0, 0.0), axis=0, keepdims=True)
        rows.append(jnp.broadcast_to(live, (HS, NH)))
    live_rows = jnp.concatenate(rows, axis=0).astype(jnp.bfloat16)
    live_pix = jnp.dot(live_rows, spread, preferred_element_type=jnp.float32)
    edge_tile = jnp.concatenate(
        [edges[0].astype(jnp.float32), jnp.zeros((BAND, LANES - NH), jnp.float32)], axis=1
    ).astype(jnp.bfloat16)
    for colour in range(COLORS):
        out[colour, :, COLS:HALO_W] = edge_tile
        taps[...] = jnp.zeros_like(taps)
        taps[0:2, : 2 * KC + 1] = col_taps[0, colour].astype(jnp.float32)
        taps[2:4, : 2 * KR + 1] = row_taps[0, colour].astype(jnp.float32)
        out[colour, :, HALO_W:] = taps[...].astype(jnp.bfloat16)
    for spare in range(COLORS, LAYERS):
        out[spare] = jnp.zeros((BAND, FULL_W), jnp.bfloat16)
    copies[5].wait()
    for colour in range(COLORS):
        out[colour, :, :COLS] = (light[0, colour] * live_pix).astype(jnp.bfloat16)
    picked.wait()


def halo_kernel(own, in_chip, cross, far_even, far_odd):
    band = lax.axis_index("rows")
    core = band % 2
    odd = (band // 2) % 2
    last = BAND - KR
    for near, start in ((in_chip, (1 - core) * last), (cross, core * last)):
        near[0:BAND] = own[0, :, :HALO_W]
        near[BAND : 2 * BAND] = own[1, :, :HALO_W]
        near[2 * BAND : NEAR] = own[2, pl.ds(pl.multiple_of(start, KR), KR), :HALO_W]
    for far, start in ((far_even, (1 - odd) * last), (far_odd, odd * last)):
        far[...] = own[0, pl.ds(pl.multiple_of(start, KR), KR), :HALO_W]


def ordered(in_chip, cross, far_even, far_odd):
    band = lax.axis_index("rows")
    even_core = band % 2 == 0
    even_chip = (band // 2) % 2 == 0
    in_chip, cross = in_chip[...], cross[...]
    far_even, far_odd = far_even[...], far_odd[...]
    return (
        jnp.where(even_core, cross, in_chip),
        jnp.where(even_core, in_chip, cross),
        jnp.where(even_chip, far_odd, far_even),
        jnp.where(even_chip, far_even, far_odd),
    )


def tiles_below(value, height):
    return jnp.concatenate(
        [
            jnp.concatenate(
                [
                    value[:height, tile * LANES : (tile + 1) * LANES],
                    value[height:, tile * LANES : (tile + 1) * LANES],
                ],
                axis=1,
            )
            for tile in range(TILES)
        ],
        axis=0,
    )


def stereo_tiles(blocks, left_tab, right_tab):
    arranged = []
    for light in blocks:
        doubled = jnp.concatenate([light, light], axis=0)
        left = jnp.dot(left_tab[...], doubled, preferred_element_type=jnp.float32)
        arranged.append(tiles_below(left.astype(jnp.bfloat16), light.shape[0]))
    arranged = jnp.concatenate(arranged, axis=0) if len(arranged) > 1 else arranged[0]
    return jnp.dot(arranged, right_tab[...], preferred_element_type=jnp.float32)


def clear_pixels(edges):
    edge_pix = jnp.dot(edges, spread_matrix(), preferred_element_type=jnp.float32)
    within = (lax.broadcasted_iota(jnp.int32, (1, COLS), 1) % HS).astype(jnp.float32)
    return jnp.where(within < edge_pix, 1.0, 0.0)


def banded(line, count, shift):
    base = jnp.concatenate([line, jnp.zeros((1, LANES), jnp.float32)], axis=1)
    base = jnp.broadcast_to(base, (count, 2 * LANES))
    return pltpu.roll(base, shift, 1, stride=1, stride_axis=0)


def filters(taps, layer):
    row_re, row_im = taps[2:3], taps[3:4]
    height = block_height(layer)
    before = height + 2 * KR
    upper = banded(row_re, height, 0) - banded(row_im, height, before)
    lower = banded(row_im, height, 0) + banded(row_re, height, before)
    row_mat = jnp.concatenate([upper, lower], axis=0).astype(jnp.bfloat16)
    col_re = banded(taps[0:1], LANES, 1)
    col_im = banded(taps[1:2], LANES, 1)
    upper = jnp.concatenate([col_re, -col_im], axis=1)
    lower = jnp.concatenate([col_im, col_re], axis=1)
    col_mat = jnp.concatenate([upper, lower], axis=0).astype(jnp.bfloat16)
    return row_mat, col_mat


def propagated(u_re, u_im, row_mat, col_mat, layer):
    height = layer_height(layer)
    block = block_height(layer)
    reach = block + 2 * KR
    parts = []
    for start in range(0, height, block):
        stacked = jnp.concatenate(
            [u_re[start : start + reach], u_im[start : start + reach]], axis=0
        )
        parts.append(
            jnp.dot(row_mat[:, : 2 * reach], stacked, preferred_element_type=jnp.float32)
        )
    rowed = jnp.concatenate(
        [part[:block] for part in parts] + [part[block:] for part in parts], axis=0
    )
    rowed = jnp.concatenate([rowed, jnp.zeros((2 * height, LANES), jnp.float32)], axis=1)
    rowed = pltpu.roll(rowed, HALF, 1).astype(jnp.bfloat16)
    windows = jnp.concatenate(
        [
            jnp.concatenate(
                [
                    rowed[:height, tile * LANES : (tile + 2) * LANES],
                    rowed[height:, tile * LANES : (tile + 2) * LANES],
                ],
                axis=1,
            )
            for tile in range(TILES)
        ],
        axis=0,
    )
    return lax.dot_general(
        windows, col_mat, (((1,), (1,)), ((), ())), preferred_element_type=jnp.float32
    )


def prepare_kernel(
    own, incident, partner, cross, relayed, left_tab, right_tab,
    first, stereo, clear, col_mats, *row_mats
):
    even_core = lax.axis_index("rows") % 2 == 0
    partner, beyond = partner[...], relayed[: 2 * BAND]
    near, distant = cross[: 2 * BAND], cross[2 * BAND :]
    low_far = jnp.where(even_core, distant, beyond)
    low_near = jnp.where(even_core, near, partner)
    high_near = jnp.where(even_core, partner, near)
    high_far = jnp.where(even_core, beyond, distant)
    extended = []
    for part in range(2):
        pieces = [low_far, low_near, incident[...], high_near, high_far]
        pieces = [piece[part * BAND : (part + 1) * BAND] for piece in pieces]
        extended.append(jnp.concatenate(pieces, axis=0))
    row_mat, col_mat = filters(own[0, 0:16, HALO_W:].astype(jnp.float32), 0)
    first[...] = propagated(extended[0], extended[1], row_mat, col_mat, 0)
    for layer in range(1, LAYERS):
        row_mat, col_mat = filters(own[layer, 0:16, HALO_W:].astype(jnp.float32), layer)
        row_mats[layer - 1][...] = row_mat
        col_mats[layer - 1] = col_mat
    packed = jnp.concatenate([own[layer, :, :HALO_W] for layer in range(LAYERS)], axis=0)
    clear[...] = clear_pixels(packed[:, COLS : COLS + NH])
    tiles = stereo_tiles([packed[:, :COLS]], left_tab, right_tab)
    for tile in range(TILES):
        for part in range(2):
            block = tiles[
                tile * LANES : (tile + 1) * LANES, part * LANES : (part + 1) * LANES
            ]
            stereo[part, :, tile * LANES : (tile + 1) * LANES] = block


def chain_kernel(
    in_chip, cross, far_even, far_odd, left_tab, right_tab, first, stereo, clear, col_mats, *rest
):
    row_mats, (out, field) = rest[: LAYERS - 1], rest[LAYERS - 1 :]
    low_near, high_near, low_far, high_far = ordered(in_chip, cross, far_even, far_odd)
    pieces = [
        low_far,
        low_near[0:BAND],
        high_near[0:BAND],
        high_far,
        low_near[BAND : 2 * BAND],
        high_near[BAND : 2 * BAND],
        low_near[2 * BAND : NEAR],
        high_near[2 * BAND : NEAR],
    ]
    halo = jnp.concatenate(pieces, axis=0)
    half = halo.shape[0] // 2
    halo_tiles = stereo_tiles(
        [halo[:half, :COLS], halo[half:, :COLS]], left_tab, right_tab
    )
    halo_clear = clear_pixels(halo[:, COLS : COLS + NH])
    begins = (0, half, half + 2 * BAND, 0)
    sides = (BAND + FAR, BAND, KR, 0)
    for layer in range(LAYERS):
        height = layer_height(layer)
        before = height + 2 * KR
        low, side = begins[layer], sides[layer]
        if layer == 0:
            columned = first
        else:
            columned = propagated(
                field[0, :before], field[1, :before], row_mats[layer - 1], col_mats[layer - 1], layer
            )
        band = slice(layer * BAND, (layer + 1) * BAND)
        pieces = [clear[band]]
        if side:
            pieces = [halo_clear[low : low + side], clear[band], halo_clear[low + side : low + 2 * side]]
        passing = jnp.concatenate(pieces, axis=0)
        for tile in range(TILES):
            span = slice(tile * height, (tile + 1) * height)
            lanes = slice(tile * LANES, (tile + 1) * LANES)
            row = (low // half * TILES + tile) * half + low % half
            for part in range(2):
                within = slice(part * LANES, (part + 1) * LANES)
                pieces = [stereo[part, band, lanes]]
                if side:
                    pieces = [
                        halo_tiles[row : row + side, within],
                        stereo[part, band, lanes],
                        halo_tiles[row + side : row + 2 * side, within],
                    ]
                added = jnp.concatenate(pieces, axis=0)
                value = passing[:, lanes] * columned[span, within] + added
                field[part, :height, lanes] = value.astype(jnp.bfloat16)
        for part in range(2):
            out[layer, part] = field[part, side : side + BAND]


def exchanged(value, axis, by, phase):
    count = lax.axis_size(axis)
    lower = [i for i in range(count - by) if (i // by) % 2 == phase]
    pairs = [(i, i + by) for i in lower] + [(i + by, i) for i in lower]
    return lax.ppermute(value, axis, pairs)


def neighbours(sent):
    in_chip, cross, far_even, far_odd = sent
    cross = exchanged(cross, "rows", 1, 1)
    far_even = exchanged(far_even, "rows", 2, 0)
    far_odd = exchanged(far_odd, "rows", 2, 1)
    in_chip = exchanged(in_chip, "rows", 1, 0)
    return in_chip, cross, far_even, far_odd


def call(kernel, out_shape, in_specs, scratch=(), flops=0, moved=10**6, limit=VMEM_LIMIT):
    vmem = pl.BlockSpec(memory_space=pltpu.VMEM)
    many = isinstance(out_shape, (tuple, list))
    return pl.pallas_call(
        kernel,
        out_shape=out_shape,
        in_specs=in_specs,
        out_specs=(vmem,) * len(out_shape) if many else vmem,
        scratch_shapes=scratch,
        compiler_params=pltpu.CompilerParams(vmem_limit_bytes=limit),
        cost_estimate=pl.CostEstimate(flops=flops, bytes_accessed=moved, transcendentals=0),
    )


def body(incident, row_taps, col_taps, hogel_light, silhouette, fill_counts, hogel_index):
    vmem = pl.BlockSpec(memory_space=pltpu.VMEM)
    hbm = pl.BlockSpec(memory_space=pltpu.HBM)
    bf16, f32 = jnp.bfloat16, jnp.float32
    shaped = jax.ShapeDtypeStruct
    held = [
        pltpu.VMEM(hogel_index.shape, jnp.int32),
        pltpu.SMEM(fill_counts.shape, jnp.int32),
        pltpu.VMEM(silhouette.shape, jnp.int32),
        pltpu.VMEM(row_taps.shape, bf16),
        pltpu.VMEM(col_taps.shape, bf16),
        pltpu.VMEM(hogel_light.shape, f32),
    ]
    payload, mine = call(
        pack_kernel,
        (shaped((LAYERS, BAND, FULL_W), bf16), shaped(incident.shape[1:], bf16)),
        [hbm] * 7,
        held + [pltpu.SemaphoreType.DMA((7,)), pltpu.VMEM((BAND, LANES), f32)],
        flops=10**7,
        limit=PACK_LIMIT,
    )(hogel_light, silhouette, fill_counts, hogel_index, row_taps, col_taps, incident)
    mine = mine.reshape(2 * BAND, COLS)
    own = lax.all_to_all(payload, "depth", 0, 0, tiled=True)
    partner = exchanged(mine, "rows", 1, 0)
    cross = exchanged(jnp.concatenate([mine, partner], axis=0), "rows", 1, 1)
    relayed = exchanged(cross, "rows", 1, 0)
    near = shaped((NEAR, HALO_W), bf16)
    far = shaped((FAR, HALO_W), bf16)
    halos = neighbours(call(halo_kernel, (near, near, far, far), [vmem])(own))
    right_tab = jnp.asarray(right_table())
    made = call(
        prepare_kernel,
        [
            shaped((TILES * layer_height(0), 2 * LANES), f32),
            shaped((2, LANES, COLS), f32),
            shaped((LANES, COLS), f32),
            shaped((LAYERS - 1, 2 * LANES, 4 * LANES), bf16),
        ]
        + [shaped((2 * block_height(layer), 2 * LANES), bf16) for layer in range(1, LAYERS)],
        [vmem] * 7,
        flops=10**9,
        moved=3 * 10**6,
    )(own, mine, partner, cross, relayed, jnp.asarray(left_table(LANES)), right_tab)
    halo_rows = NEAR + FAR
    result = call(
        chain_kernel,
        shaped((LAYERS, 2, BAND, COLS), bf16),
        [vmem] * (6 + len(made)),
        [pltpu.VMEM((2, layer_height(0), COLS), bf16)],
        flops=2 * 10**9,
        moved=3 * 10**6,
    )(*halos, jnp.asarray(left_table(halo_rows)), right_tab, *made)
    gathered = lax.all_to_all(result, "depth", 0, 0, tiled=True)
    return gathered[None, :COLORS]


def solution(mesh):
    placed = (
        P(None, None, "rows", None),
        P("depth", None, None, None),
        P("depth", None, None, None),
        P("depth", None, "rows", None),
        P("depth", "rows", None),
        P("depth", "rows"),
        P("depth", "rows", None),
    )
    return jax.shard_map(
        body,
        mesh=mesh,
        in_specs=placed,
        out_specs=P("depth", None, None, "rows", None),
        check_vma=False,
    )
```

```python
import math

import jax
import jax.numpy as jnp
import numpy as np
from jax import lax
from jax.experimental import pallas as pl
from jax.experimental.pallas import tpu as pltpu
from jax.sharding import PartitionSpec as P

HS = 16
KR = 16
KC = 63
COLORS = 3
LAYERS = 4
BAND = 32
COLS = 1024
NH = COLS // HS
LANES = 128
TILES = COLS // LANES
HALO_W = COLS + LANES
HALF = LANES // 2
FULL_W = COLS + 2 * LANES
NEAR = 2 * BAND + KR
FAR = KR
VMEM_LIMIT = 48 * 1024 * 1024
PACK_LIMIT = 63 * 1024 * 1024


def split_table(table):
    high = table.astype(jnp.bfloat16)
    low = (table - high.astype(np.float64)).astype(jnp.bfloat16)
    return high, low


def dft_pair():
    counter = np.arange(HS)
    angles = (counter[:, None] * counter[None, :] % HS) * (2.0 * math.pi / HS)
    return np.cos(angles) / math.sqrt(HS), np.sin(angles) / math.sqrt(HS)


def left_table(height):
    cos_tab, sin_tab = dft_pair()
    eye = np.eye(height // HS)
    full = np.concatenate([np.kron(eye, cos_tab), np.kron(eye, -sin_tab)], axis=0)
    return np.concatenate(split_table(full), axis=1)


def right_table():
    cos_tab, sin_tab = dft_pair()
    eye = np.eye(LANES // HS)
    cos_big, sin_big = np.kron(eye, cos_tab), np.kron(eye, sin_tab)
    full = np.concatenate(
        [
            np.concatenate([cos_big, -sin_big], axis=1),
            np.concatenate([sin_big, cos_big], axis=1),
        ],
        axis=0,
    )
    return full.astype(jnp.bfloat16)


def layer_height(layer):
    return BAND + 2 * KR * (LAYERS - 1 - layer)


def block_height(layer):
    height = layer_height(layer)
    return height // 2 if 2 * (height + 2 * KR) > 2 * LANES else height


def spread_matrix():
    tile = lax.broadcasted_iota(jnp.int32, (NH, COLS), 0)
    column = lax.broadcasted_iota(jnp.int32, (NH, COLS), 1)
    return jnp.where(column // HS == tile, 1.0, 0.0).astype(jnp.bfloat16)


def own_colour():
    return jnp.minimum(lax.axis_index("depth"), COLORS - 1)


def pack_kernel(light, edges, counts, listed, row_taps, col_taps, incident, out, mine, *scratch):
    held, sems, taps = scratch[:6], scratch[6], scratch[7]
    picked = pltpu.make_async_copy(incident.at[own_colour()], mine, sems.at[6])
    sources = (listed, counts, edges, row_taps, col_taps, light)
    copies = [
        pltpu.make_async_copy(source, target, sems.at[place])
        for place, (source, target) in enumerate(zip(sources, held))
    ]
    for copy in reversed(copies):
        copy.start()
    picked.start()
    listed, counts, edges, row_taps, col_taps, light = held
    spread = spread_matrix()
    slot = lax.broadcasted_iota(jnp.int32, (NH, NH), 0)
    place = lax.broadcasted_iota(jnp.int32, (NH, NH), 1)
    for copy in copies[:5]:
        copy.wait()
    rows = []
    for group in range(BAND // HS):
        listing = jnp.broadcast_to(listed[0, group : group + 1, :], (NH, NH))
        column = jnp.sum(jnp.where(slot == place, listing, 0), axis=1, keepdims=True)
        named = (column == place) & (slot < counts[0, group])
        live = jnp.max(jnp.where(named, 1.0, 0.0), axis=0, keepdims=True)
        rows.append(jnp.broadcast_to(live, (HS, NH)))
    live_rows = jnp.concatenate(rows, axis=0).astype(jnp.bfloat16)
    live_pix = jnp.dot(live_rows, spread, preferred_element_type=jnp.float32)
    edge_tile = jnp.concatenate(
        [edges[0].astype(jnp.float32), jnp.zeros((BAND, LANES - NH), jnp.float32)], axis=1
    ).astype(jnp.bfloat16)
    for colour in range(COLORS):
        out[colour, :, COLS:HALO_W] = edge_tile
        taps[...] = jnp.zeros_like(taps)
        taps[0:2, : 2 * KC + 1] = col_taps[0, colour].astype(jnp.float32)
        taps[2:4, : 2 * KR + 1] = row_taps[0, colour].astype(jnp.float32)
        out[colour, :, HALO_W:] = taps[...].astype(jnp.bfloat16)
    for spare in range(COLORS, LAYERS):
        out[spare] = jnp.zeros((BAND, FULL_W), jnp.bfloat16)
    copies[5].wait()
    for colour in range(COLORS):
        out[colour, :, :COLS] = (light[0, colour] * live_pix).astype(jnp.bfloat16)
    picked.wait()


def halo_kernel(own, in_chip, cross, far_even, far_odd):
    band = lax.axis_index("rows")
    core = band % 2
    odd = (band // 2) % 2
    last = BAND - KR
    for near, start in ((in_chip, (1 - core) * last), (cross, core * last)):
        near[0:BAND] = own[0, :, :HALO_W]
        near[BAND : 2 * BAND] = own[1, :, :HALO_W]
        near[2 * BAND : NEAR] = own[2, pl.ds(pl.multiple_of(start, KR), KR), :HALO_W]
    for far, start in ((far_even, (1 - odd) * last), (far_odd, odd * last)):
        far[...] = own[0, pl.ds(pl.multiple_of(start, KR), KR), :HALO_W]


def ordered(in_chip, cross, far_even, far_odd):
    band = lax.axis_index("rows")
    even_core = band % 2 == 0
    even_chip = (band // 2) % 2 == 0
    in_chip, cross = in_chip[...], cross[...]
    far_even, far_odd = far_even[...], far_odd[...]
    return (
        jnp.where(even_core, cross, in_chip),
        jnp.where(even_core, in_chip, cross),
        jnp.where(even_chip, far_odd, far_even),
        jnp.where(even_chip, far_even, far_odd),
    )


def tiles_below(value, height):
    return jnp.concatenate(
        [
            jnp.concatenate(
                [
                    value[:height, tile * LANES : (tile + 1) * LANES],
                    value[height:, tile * LANES : (tile + 1) * LANES],
                ],
                axis=1,
            )
            for tile in range(TILES)
        ],
        axis=0,
    )


def stereo_tiles(blocks, left_tab, right_tab):
    arranged = []
    for light in blocks:
        doubled = jnp.concatenate([light, light], axis=0)
        left = jnp.dot(left_tab[...], doubled, preferred_element_type=jnp.float32)
        arranged.append(tiles_below(left.astype(jnp.bfloat16), light.shape[0]))
    arranged = jnp.concatenate(arranged, axis=0) if len(arranged) > 1 else arranged[0]
    return jnp.dot(arranged, right_tab[...], preferred_element_type=jnp.float32)


def clear_pixels(edges):
    edge_pix = jnp.dot(edges, spread_matrix(), preferred_element_type=jnp.float32)
    within = (lax.broadcasted_iota(jnp.int32, (1, COLS), 1) % HS).astype(jnp.float32)
    return jnp.where(within < edge_pix, 1.0, 0.0)


def banded(line, count, shift):
    base = jnp.concatenate([line, jnp.zeros((1, LANES), jnp.float32)], axis=1)
    base = jnp.broadcast_to(base, (count, 2 * LANES))
    return pltpu.roll(base, shift, 1, stride=1, stride_axis=0)


def filters(taps, layer):
    row_re, row_im = taps[2:3], taps[3:4]
    height = block_height(layer)
    before = height + 2 * KR
    upper = banded(row_re, height, 0) - banded(row_im, height, before)
    lower = banded(row_im, height, 0) + banded(row_re, height, before)
    row_mat = jnp.concatenate([upper, lower], axis=0).astype(jnp.bfloat16)
    col_re = banded(taps[0:1], LANES, 1)
    col_im = banded(taps[1:2], LANES, 1)
    upper = jnp.concatenate([col_re, -col_im], axis=1)
    lower = jnp.concatenate([col_im, col_re], axis=1)
    col_mat = jnp.concatenate([upper, lower], axis=0).astype(jnp.bfloat16)
    return row_mat, col_mat


def propagated(u_re, u_im, row_mat, col_mat, layer):
    height = layer_height(layer)
    block = block_height(layer)
    reach = block + 2 * KR
    parts = []
    for start in range(0, height, block):
        stacked = jnp.concatenate(
            [u_re[start : start + reach], u_im[start : start + reach]], axis=0
        )
        parts.append(
            jnp.dot(row_mat[:, : 2 * reach], stacked, preferred_element_type=jnp.float32)
        )
    rowed = jnp.concatenate(
        [part[:block] for part in parts] + [part[block:] for part in parts], axis=0
    )
    rowed = jnp.concatenate([rowed, jnp.zeros((2 * height, LANES), jnp.float32)], axis=1)
    rowed = pltpu.roll(rowed, HALF, 1).astype(jnp.bfloat16)
    windows = jnp.concatenate(
        [
            jnp.concatenate(
                [
                    rowed[:height, tile * LANES : (tile + 2) * LANES],
                    rowed[height:, tile * LANES : (tile + 2) * LANES],
                ],
                axis=1,
            )
            for tile in range(TILES)
        ],
        axis=0,
    )
    return lax.dot_general(
        windows, col_mat, (((1,), (1,)), ((), ())), preferred_element_type=jnp.float32
    )


def prepare_kernel(
    own, incident, cross, far_even, far_odd, in_chip, left_tab, right_tab,
    first, stereo, clear, col_mats, *row_mats
):
    low_near, high_near, low_far, high_far = ordered(in_chip, cross, far_even, far_odd)
    extended = []
    for part in range(2):
        pieces = [low_far, low_near, incident[...], high_near, high_far]
        pieces = [piece[part * BAND : (part + 1) * BAND] for piece in pieces]
        extended.append(jnp.concatenate(pieces, axis=0))
    row_mat, col_mat = filters(own[0, 0:16, HALO_W:].astype(jnp.float32), 0)
    first[...] = propagated(extended[0], extended[1], row_mat, col_mat, 0)
    for layer in range(1, LAYERS):
        row_mat, col_mat = filters(own[layer, 0:16, HALO_W:].astype(jnp.float32), layer)
        row_mats[layer - 1][...] = row_mat
        col_mats[layer - 1] = col_mat
    packed = jnp.concatenate([own[layer, :, :HALO_W] for layer in range(LAYERS)], axis=0)
    clear[...] = clear_pixels(packed[:, COLS : COLS + NH])
    tiles = stereo_tiles([packed[:, :COLS]], left_tab, right_tab)
    for tile in range(TILES):
        for part in range(2):
            block = tiles[
                tile * LANES : (tile + 1) * LANES, part * LANES : (part + 1) * LANES
            ]
            stereo[part, :, tile * LANES : (tile + 1) * LANES] = block


def chain_kernel(
    in_chip, cross, far_even, far_odd, left_tab, right_tab, first, stereo, clear, col_mats, *rest
):
    row_mats, (out, field) = rest[: LAYERS - 1], rest[LAYERS - 1 :]
    low_near, high_near, low_far, high_far = ordered(in_chip, cross, far_even, far_odd)
    pieces = [
        low_far,
        low_near[0:BAND],
        high_near[0:BAND],
        high_far,
        low_near[BAND : 2 * BAND],
        high_near[BAND : 2 * BAND],
        low_near[2 * BAND : NEAR],
        high_near[2 * BAND : NEAR],
    ]
    halo = jnp.concatenate(pieces, axis=0)
    half = halo.shape[0] // 2
    halo_tiles = stereo_tiles(
        [halo[:half, :COLS], halo[half:, :COLS]], left_tab, right_tab
    )
    halo_clear = clear_pixels(halo[:, COLS : COLS + NH])
    begins = (0, half, half + 2 * BAND, 0)
    sides = (BAND + FAR, BAND, KR, 0)
    for layer in range(LAYERS):
        height = layer_height(layer)
        before = height + 2 * KR
        low, side = begins[layer], sides[layer]
        if layer == 0:
            columned = first
        else:
            columned = propagated(
                field[0, :before], field[1, :before], row_mats[layer - 1], col_mats[layer - 1], layer
            )
        band = slice(layer * BAND, (layer + 1) * BAND)
        pieces = [clear[band]]
        if side:
            pieces = [halo_clear[low : low + side], clear[band], halo_clear[low + side : low + 2 * side]]
        passing = jnp.concatenate(pieces, axis=0)
        for tile in range(TILES):
            span = slice(tile * height, (tile + 1) * height)
            lanes = slice(tile * LANES, (tile + 1) * LANES)
            row = (low // half * TILES + tile) * half + low % half
            for part in range(2):
                within = slice(part * LANES, (part + 1) * LANES)
                pieces = [stereo[part, band, lanes]]
                if side:
                    pieces = [
                        halo_tiles[row : row + side, within],
                        stereo[part, band, lanes],
                        halo_tiles[row + side : row + 2 * side, within],
                    ]
                added = jnp.concatenate(pieces, axis=0)
                value = passing[:, lanes] * columned[span, within] + added
                field[part, :height, lanes] = value.astype(jnp.bfloat16)
        for part in range(2):
            out[layer, part] = field[part, side : side + BAND]


def exchanged(value, axis, by, phase):
    count = lax.axis_size(axis)
    lower = [i for i in range(count - by) if (i // by) % 2 == phase]
    pairs = [(i, i + by) for i in lower] + [(i + by, i) for i in lower]
    return lax.ppermute(value, axis, pairs)


def neighbours(sent):
    in_chip, cross, far_even, far_odd = sent
    cross = exchanged(cross, "rows", 1, 1)
    far_even = exchanged(far_even, "rows", 2, 0)
    far_odd = exchanged(far_odd, "rows", 2, 1)
    in_chip = exchanged(in_chip, "rows", 1, 0)
    return in_chip, cross, far_even, far_odd


def call(kernel, out_shape, in_specs, scratch=(), flops=0, moved=10**6, limit=VMEM_LIMIT):
    vmem = pl.BlockSpec(memory_space=pltpu.VMEM)
    many = isinstance(out_shape, (tuple, list))
    return pl.pallas_call(
        kernel,
        out_shape=out_shape,
        in_specs=in_specs,
        out_specs=(vmem,) * len(out_shape) if many else vmem,
        scratch_shapes=scratch,
        compiler_params=pltpu.CompilerParams(vmem_limit_bytes=limit),
        cost_estimate=pl.CostEstimate(flops=flops, bytes_accessed=moved, transcendentals=0),
    )


def body(incident, row_taps, col_taps, hogel_light, silhouette, fill_counts, hogel_index):
    vmem = pl.BlockSpec(memory_space=pltpu.VMEM)
    hbm = pl.BlockSpec(memory_space=pltpu.HBM)
    bf16, f32 = jnp.bfloat16, jnp.float32
    shaped = jax.ShapeDtypeStruct
    held = [
        pltpu.VMEM(hogel_index.shape, jnp.int32),
        pltpu.SMEM(fill_counts.shape, jnp.int32),
        pltpu.VMEM(silhouette.shape, jnp.int32),
        pltpu.VMEM(row_taps.shape, bf16),
        pltpu.VMEM(col_taps.shape, bf16),
        pltpu.VMEM(hogel_light.shape, f32),
    ]
    payload, mine = call(
        pack_kernel,
        (shaped((LAYERS, BAND, FULL_W), bf16), shaped(incident.shape[1:], bf16)),
        [hbm] * 7,
        held + [pltpu.SemaphoreType.DMA((7,)), pltpu.VMEM((BAND, LANES), f32)],
        flops=10**7,
        limit=PACK_LIMIT,
    )(hogel_light, silhouette, fill_counts, hogel_index, row_taps, col_taps, incident)
    mine = mine.reshape(2 * BAND, COLS)
    own = lax.all_to_all(payload, "depth", 0, 0, tiled=True)
    in_chip, *arrived = neighbours((mine,) * 4)
    near = shaped((NEAR, HALO_W), bf16)
    far = shaped((FAR, HALO_W), bf16)
    halos = neighbours(call(halo_kernel, (near, near, far, far), [vmem])(own))
    right_tab = jnp.asarray(right_table())
    made = call(
        prepare_kernel,
        [
            shaped((TILES * layer_height(0), 2 * LANES), f32),
            shaped((2, LANES, COLS), f32),
            shaped((LANES, COLS), f32),
            shaped((LAYERS - 1, 2 * LANES, 4 * LANES), bf16),
        ]
        + [shaped((2 * block_height(layer), 2 * LANES), bf16) for layer in range(1, LAYERS)],
        [vmem] * 8,
        flops=10**9,
        moved=3 * 10**6,
    )(own, mine, *arrived, in_chip, jnp.asarray(left_table(LANES)), right_tab)
    halo_rows = NEAR + FAR
    result = call(
        chain_kernel,
        shaped((LAYERS, 2, BAND, COLS), bf16),
        [vmem] * (6 + len(made)),
        [pltpu.VMEM((2, layer_height(0), COLS), bf16)],
        flops=2 * 10**9,
        moved=3 * 10**6,
    )(*halos, jnp.asarray(left_table(halo_rows)), right_tab, *made)
    gathered = lax.all_to_all(result, "depth", 0, 0, tiled=True)
    return gathered[None, :COLORS]


def solution(mesh):
    placed = (
        P(None, None, "rows", None),
        P("depth", None, None, None),
        P("depth", None, None, None),
        P("depth", None, "rows", None),
        P("depth", "rows", None),
        P("depth", "rows"),
        P("depth", "rows", None),
    )
    return jax.shard_map(
        body,
        mesh=mesh,
        in_specs=placed,
        out_specs=P("depth", None, None, "rows", None),
        check_vma=False,
    )
```

```python
import math

import jax
import jax.numpy as jnp
import numpy as np
from jax import lax
from jax.experimental import pallas as pl
from jax.experimental.pallas import tpu as pltpu
from jax.sharding import PartitionSpec as P

HS = 16
KR = 16
KC = 63
COLORS = 3
LAYERS = 4
BAND = 32
COLS = 1024
NH = COLS // HS
LANES = 128
TILES = COLS // LANES
HALO_W = COLS + LANES
HALF = LANES // 2
FULL_W = COLS + 2 * LANES
NEAR = 2 * BAND + KR
FAR = KR
VMEM_LIMIT = 48 * 1024 * 1024
PACK_LIMIT = 63 * 1024 * 1024


def split_table(table):
    high = table.astype(jnp.bfloat16)
    low = (table - high.astype(np.float64)).astype(jnp.bfloat16)
    return high, low


def dft_pair():
    counter = np.arange(HS)
    angles = (counter[:, None] * counter[None, :] % HS) * (2.0 * math.pi / HS)
    return np.cos(angles) / math.sqrt(HS), np.sin(angles) / math.sqrt(HS)


def left_table(height):
    cos_tab, sin_tab = dft_pair()
    eye = np.eye(height // HS)
    full = np.concatenate([np.kron(eye, cos_tab), np.kron(eye, -sin_tab)], axis=0)
    return np.concatenate(split_table(full), axis=1)


def right_table():
    cos_tab, sin_tab = dft_pair()
    eye = np.eye(LANES // HS)
    cos_big, sin_big = np.kron(eye, cos_tab), np.kron(eye, sin_tab)
    full = np.concatenate(
        [
            np.concatenate([cos_big, -sin_big], axis=1),
            np.concatenate([sin_big, cos_big], axis=1),
        ],
        axis=0,
    )
    return full.astype(jnp.bfloat16)


def layer_height(layer):
    return BAND + 2 * KR * (LAYERS - 1 - layer)


def block_height(layer):
    height = layer_height(layer)
    return height // 2 if 2 * (height + 2 * KR) > 2 * LANES else height


def spread_matrix():
    tile = lax.broadcasted_iota(jnp.int32, (NH, COLS), 0)
    column = lax.broadcasted_iota(jnp.int32, (NH, COLS), 1)
    return jnp.where(column // HS == tile, 1.0, 0.0).astype(jnp.bfloat16)


def own_colour():
    return jnp.minimum(lax.axis_index("depth"), COLORS - 1)


def pack_kernel(light, edges, counts, listed, row_taps, col_taps, incident, out, mine, *scratch):
    held, sems, taps = scratch[:6], scratch[6], scratch[7]
    picked = pltpu.make_async_copy(incident.at[own_colour()], mine, sems.at[6])
    sources = (listed, counts, edges, row_taps, col_taps, light)
    copies = [
        pltpu.make_async_copy(source, target, sems.at[place])
        for place, (source, target) in enumerate(zip(sources, held))
    ]
    for copy in reversed(copies):
        copy.start()
    picked.start()
    listed, counts, edges, row_taps, col_taps, light = held
    spread = spread_matrix()
    slot = lax.broadcasted_iota(jnp.int32, (NH, NH), 0)
    place = lax.broadcasted_iota(jnp.int32, (NH, NH), 1)
    for copy in copies[:5]:
        copy.wait()
    rows = []
    for group in range(BAND // HS):
        listing = jnp.broadcast_to(listed[0, group : group + 1, :], (NH, NH))
        column = jnp.sum(jnp.where(slot == place, listing, 0), axis=1, keepdims=True)
        named = (column == place) & (slot < counts[0, group])
        live = jnp.max(jnp.where(named, 1.0, 0.0), axis=0, keepdims=True)
        rows.append(jnp.broadcast_to(live, (HS, NH)))
    live_rows = jnp.concatenate(rows, axis=0).astype(jnp.bfloat16)
    live_pix = jnp.dot(live_rows, spread, preferred_element_type=jnp.float32)
    edge_tile = jnp.concatenate(
        [edges[0].astype(jnp.float32), jnp.zeros((BAND, LANES - NH), jnp.float32)], axis=1
    ).astype(jnp.bfloat16)
    for colour in range(COLORS):
        out[colour, :, COLS:HALO_W] = edge_tile
        taps[...] = jnp.zeros_like(taps)
        taps[0:2, : 2 * KC + 1] = col_taps[0, colour].astype(jnp.float32)
        taps[2:4, : 2 * KR + 1] = row_taps[0, colour].astype(jnp.float32)
        out[colour, :, HALO_W:] = taps[...].astype(jnp.bfloat16)
    for spare in range(COLORS, LAYERS):
        out[spare] = jnp.zeros((BAND, FULL_W), jnp.bfloat16)
    copies[5].wait()
    for colour in range(COLORS):
        out[colour, :, :COLS] = (light[0, colour] * live_pix).astype(jnp.bfloat16)
    picked.wait()


def halo_kernel(own, in_chip, cross, far_even, far_odd):
    band = lax.axis_index("rows")
    core = band % 2
    odd = (band // 2) % 2
    last = BAND - KR
    for near, start in ((in_chip, (1 - core) * last), (cross, core * last)):
        near[0:BAND] = own[0, :, :HALO_W]
        near[BAND : 2 * BAND] = own[1, :, :HALO_W]
        near[2 * BAND : NEAR] = own[2, pl.ds(pl.multiple_of(start, KR), KR), :HALO_W]
    for far, start in ((far_even, (1 - odd) * last), (far_odd, odd * last)):
        far[...] = own[0, pl.ds(pl.multiple_of(start, KR), KR), :HALO_W]


def ordered(in_chip, cross, far_even, far_odd):
    band = lax.axis_index("rows")
    even_core = band % 2 == 0
    even_chip = (band // 2) % 2 == 0
    in_chip, cross = in_chip[...], cross[...]
    far_even, far_odd = far_even[...], far_odd[...]
    return (
        jnp.where(even_core, cross, in_chip),
        jnp.where(even_core, in_chip, cross),
        jnp.where(even_chip, far_odd, far_even),
        jnp.where(even_chip, far_even, far_odd),
    )


def tiles_below(value, height):
    return jnp.concatenate(
        [
            jnp.concatenate(
                [
                    value[:height, tile * LANES : (tile + 1) * LANES],
                    value[height:, tile * LANES : (tile + 1) * LANES],
                ],
                axis=1,
            )
            for tile in range(TILES)
        ],
        axis=0,
    )


def stereo_tiles(blocks, left_tab, right_tab):
    arranged = []
    for light in blocks:
        doubled = jnp.concatenate([light, light], axis=0)
        left = jnp.dot(left_tab[...], doubled, preferred_element_type=jnp.float32)
        arranged.append(tiles_below(left.astype(jnp.bfloat16), light.shape[0]))
    arranged = jnp.concatenate(arranged, axis=0) if len(arranged) > 1 else arranged[0]
    return jnp.dot(arranged, right_tab[...], preferred_element_type=jnp.float32)


def clear_pixels(edges):
    edge_pix = jnp.dot(edges, spread_matrix(), preferred_element_type=jnp.float32)
    within = (lax.broadcasted_iota(jnp.int32, (1, COLS), 1) % HS).astype(jnp.float32)
    return jnp.where(within < edge_pix, 1.0, 0.0)


def banded(line, count, shift):
    base = jnp.concatenate([line, jnp.zeros((1, LANES), jnp.float32)], axis=1)
    base = jnp.broadcast_to(base, (count, 2 * LANES))
    return pltpu.roll(base, shift, 1, stride=1, stride_axis=0)


def filters(taps, layer):
    row_re, row_im = taps[2:3], taps[3:4]
    height = block_height(layer)
    before = height + 2 * KR
    upper = banded(row_re, height, 0) - banded(row_im, height, before)
    lower = banded(row_im, height, 0) + banded(row_re, height, before)
    row_mat = jnp.concatenate([upper, lower], axis=0).astype(jnp.bfloat16)
    col_re = banded(taps[0:1], LANES, 1)
    col_im = banded(taps[1:2], LANES, 1)
    upper = jnp.concatenate([col_re, -col_im], axis=1)
    lower = jnp.concatenate([col_im, col_re], axis=1)
    col_mat = jnp.concatenate([upper, lower], axis=0).astype(jnp.bfloat16)
    return row_mat, col_mat


def propagated(u_re, u_im, row_mat, col_mat, layer):
    height = layer_height(layer)
    block = block_height(layer)
    reach = block + 2 * KR
    parts = []
    for start in range(0, height, block):
        stacked = jnp.concatenate(
            [u_re[start : start + reach], u_im[start : start + reach]], axis=0
        )
        parts.append(
            jnp.dot(row_mat[:, : 2 * reach], stacked, preferred_element_type=jnp.float32)
        )
    rowed = jnp.concatenate(
        [part[:block] for part in parts] + [part[block:] for part in parts], axis=0
    )
    rowed = jnp.concatenate([rowed, jnp.zeros((2 * height, LANES), jnp.float32)], axis=1)
    rowed = pltpu.roll(rowed, HALF, 1).astype(jnp.bfloat16)
    windows = jnp.concatenate(
        [
            jnp.concatenate(
                [
                    rowed[:height, tile * LANES : (tile + 2) * LANES],
                    rowed[height:, tile * LANES : (tile + 2) * LANES],
                ],
                axis=1,
            )
            for tile in range(TILES)
        ],
        axis=0,
    )
    return lax.dot_general(
        windows, col_mat, (((1,), (1,)), ((), ())), preferred_element_type=jnp.float32
    )


def prepare_kernel(
    own, incident, far_odd, far_even, cross, in_chip, left_tab, right_tab,
    first, stereo, clear, col_mats, *row_mats
):
    low_near, high_near, low_far, high_far = ordered(in_chip, cross, far_even, far_odd)
    extended = []
    for part in range(2):
        pieces = [low_far, low_near, incident[...], high_near, high_far]
        pieces = [piece[part * BAND : (part + 1) * BAND] for piece in pieces]
        extended.append(jnp.concatenate(pieces, axis=0))
    row_mat, col_mat = filters(own[0, 0:16, HALO_W:].astype(jnp.float32), 0)
    first[...] = propagated(extended[0], extended[1], row_mat, col_mat, 0)
    for layer in range(1, LAYERS):
        row_mat, col_mat = filters(own[layer, 0:16, HALO_W:].astype(jnp.float32), layer)
        row_mats[layer - 1][...] = row_mat
        col_mats[layer - 1] = col_mat
    packed = jnp.concatenate([own[layer, :, :HALO_W] for layer in range(LAYERS)], axis=0)
    clear[...] = clear_pixels(packed[:, COLS : COLS + NH])
    tiles = stereo_tiles([packed[:, :COLS]], left_tab, right_tab)
    for tile in range(TILES):
        for part in range(2):
            block = tiles[
                tile * LANES : (tile + 1) * LANES, part * LANES : (part + 1) * LANES
            ]
            stereo[part, :, tile * LANES : (tile + 1) * LANES] = block


def chain_kernel(
    in_chip, cross, far_even, far_odd, left_tab, right_tab, first, stereo, clear, col_mats, *rest
):
    row_mats, (out, field) = rest[: LAYERS - 1], rest[LAYERS - 1 :]
    low_near, high_near, low_far, high_far = ordered(in_chip, cross, far_even, far_odd)
    pieces = [
        low_far,
        low_near[0:BAND],
        high_near[0:BAND],
        high_far,
        low_near[BAND : 2 * BAND],
        high_near[BAND : 2 * BAND],
        low_near[2 * BAND : NEAR],
        high_near[2 * BAND : NEAR],
    ]
    halo = jnp.concatenate(pieces, axis=0)
    half = halo.shape[0] // 2
    halo_tiles = stereo_tiles(
        [halo[:half, :COLS], halo[half:, :COLS]], left_tab, right_tab
    )
    halo_clear = clear_pixels(halo[:, COLS : COLS + NH])
    begins = (0, half, half + 2 * BAND, 0)
    sides = (BAND + FAR, BAND, KR, 0)
    for layer in range(LAYERS):
        height = layer_height(layer)
        before = height + 2 * KR
        low, side = begins[layer], sides[layer]
        if layer == 0:
            columned = first
        else:
            columned = propagated(
                field[0, :before], field[1, :before], row_mats[layer - 1], col_mats[layer - 1], layer
            )
        band = slice(layer * BAND, (layer + 1) * BAND)
        pieces = [clear[band]]
        if side:
            pieces = [halo_clear[low : low + side], clear[band], halo_clear[low + side : low + 2 * side]]
        passing = jnp.concatenate(pieces, axis=0)
        for tile in range(TILES):
            span = slice(tile * height, (tile + 1) * height)
            lanes = slice(tile * LANES, (tile + 1) * LANES)
            row = (low // half * TILES + tile) * half + low % half
            for part in range(2):
                within = slice(part * LANES, (part + 1) * LANES)
                pieces = [stereo[part, band, lanes]]
                if side:
                    pieces = [
                        halo_tiles[row : row + side, within],
                        stereo[part, band, lanes],
                        halo_tiles[row + side : row + 2 * side, within],
                    ]
                added = jnp.concatenate(pieces, axis=0)
                value = passing[:, lanes] * columned[span, within] + added
                field[part, :height, lanes] = value.astype(jnp.bfloat16)
        for part in range(2):
            out[layer, part] = field[part, side : side + BAND]


def exchanged(value, axis, by, phase):
    count = lax.axis_size(axis)
    lower = [i for i in range(count - by) if (i // by) % 2 == phase]
    pairs = [(i, i + by) for i in lower] + [(i + by, i) for i in lower]
    return lax.ppermute(value, axis, pairs)


def neighbours(sent):
    in_chip, cross, far_even, far_odd = sent
    far_odd = exchanged(far_odd, "rows", 2, 1)
    far_even = exchanged(far_even, "rows", 2, 0)
    cross = exchanged(cross, "rows", 1, 1)
    in_chip = exchanged(in_chip, "rows", 1, 0)
    return in_chip, cross, far_even, far_odd


def call(kernel, out_shape, in_specs, scratch=(), flops=0, moved=10**6, limit=VMEM_LIMIT):
    vmem = pl.BlockSpec(memory_space=pltpu.VMEM)
    many = isinstance(out_shape, (tuple, list))
    return pl.pallas_call(
        kernel,
        out_shape=out_shape,
        in_specs=in_specs,
        out_specs=(vmem,) * len(out_shape) if many else vmem,
        scratch_shapes=scratch,
        compiler_params=pltpu.CompilerParams(vmem_limit_bytes=limit),
        cost_estimate=pl.CostEstimate(flops=flops, bytes_accessed=moved, transcendentals=0),
    )


def body(incident, row_taps, col_taps, hogel_light, silhouette, fill_counts, hogel_index):
    vmem = pl.BlockSpec(memory_space=pltpu.VMEM)
    hbm = pl.BlockSpec(memory_space=pltpu.HBM)
    bf16, f32 = jnp.bfloat16, jnp.float32
    shaped = jax.ShapeDtypeStruct
    held = [
        pltpu.VMEM(hogel_index.shape, jnp.int32),
        pltpu.SMEM(fill_counts.shape, jnp.int32),
        pltpu.VMEM(silhouette.shape, jnp.int32),
        pltpu.VMEM(row_taps.shape, bf16),
        pltpu.VMEM(col_taps.shape, bf16),
        pltpu.VMEM(hogel_light.shape, f32),
    ]
    payload, mine = call(
        pack_kernel,
        (shaped((LAYERS, BAND, FULL_W), bf16), shaped(incident.shape[1:], bf16)),
        [hbm] * 7,
        held + [pltpu.SemaphoreType.DMA((7,)), pltpu.VMEM((BAND, LANES), f32)],
        flops=10**7,
        limit=PACK_LIMIT,
    )(hogel_light, silhouette, fill_counts, hogel_index, row_taps, col_taps, incident)
    mine = mine.reshape(2 * BAND, COLS)
    own = lax.all_to_all(payload, "depth", 0, 0, tiled=True)
    arrived = neighbours((mine,) * 4)[::-1]
    near = shaped((NEAR, HALO_W), bf16)
    far = shaped((FAR, HALO_W), bf16)
    halos = neighbours(call(halo_kernel, (near, near, far, far), [vmem])(own))
    right_tab = jnp.asarray(right_table())
    made = call(
        prepare_kernel,
        [
            shaped((TILES * layer_height(0), 2 * LANES), f32),
            shaped((2, LANES, COLS), f32),
            shaped((LANES, COLS), f32),
            shaped((LAYERS - 1, 2 * LANES, 4 * LANES), bf16),
        ]
        + [shaped((2 * block_height(layer), 2 * LANES), bf16) for layer in range(1, LAYERS)],
        [vmem] * 8,
        flops=10**9,
        moved=3 * 10**6,
    )(own, mine, *arrived, jnp.asarray(left_table(LANES)), right_tab)
    halo_rows = NEAR + FAR
    result = call(
        chain_kernel,
        shaped((LAYERS, 2, BAND, COLS), bf16),
        [vmem] * (6 + len(made)),
        [pltpu.VMEM((2, layer_height(0), COLS), bf16)],
        flops=2 * 10**9,
        moved=3 * 10**6,
    )(*halos, jnp.asarray(left_table(halo_rows)), right_tab, *made)
    gathered = lax.all_to_all(result, "depth", 0, 0, tiled=True)
    return gathered[None, :COLORS]


def solution(mesh):
    placed = (
        P(None, None, "rows", None),
        P("depth", None, None, None),
        P("depth", None, None, None),
        P("depth", None, "rows", None),
        P("depth", "rows", None),
        P("depth", "rows"),
        P("depth", "rows", None),
    )
    return jax.shard_map(
        body,
        mesh=mesh,
        in_specs=placed,
        out_specs=P("depth", None, None, "rows", None),
        check_vma=False,
    )
```

```python
import math

import jax
import jax.numpy as jnp
import numpy as np
from jax import lax
from jax.experimental import pallas as pl
from jax.experimental.pallas import tpu as pltpu
from jax.sharding import PartitionSpec as P

HS = 16
KR = 16
KC = 63
COLORS = 3
LAYERS = 4
BAND = 32
COLS = 1024
NH = COLS // HS
LANES = 128
TILES = COLS // LANES
HALO_W = COLS + LANES
HALF = LANES // 2
FULL_W = COLS + 2 * LANES
NEAR = 2 * BAND + KR
FAR = KR
VMEM_LIMIT = 48 * 1024 * 1024
PACK_LIMIT = 63 * 1024 * 1024


def split_table(table):
    high = table.astype(jnp.bfloat16)
    low = (table - high.astype(np.float64)).astype(jnp.bfloat16)
    return high, low


def dft_pair():
    counter = np.arange(HS)
    angles = (counter[:, None] * counter[None, :] % HS) * (2.0 * math.pi / HS)
    return np.cos(angles) / math.sqrt(HS), np.sin(angles) / math.sqrt(HS)


def left_table(height):
    cos_tab, sin_tab = dft_pair()
    eye = np.eye(height // HS)
    full = np.concatenate([np.kron(eye, cos_tab), np.kron(eye, -sin_tab)], axis=0)
    return np.concatenate(split_table(full), axis=1)


def right_table():
    cos_tab, sin_tab = dft_pair()
    eye = np.eye(LANES // HS)
    cos_big, sin_big = np.kron(eye, cos_tab), np.kron(eye, sin_tab)
    full = np.concatenate(
        [
            np.concatenate([cos_big, -sin_big], axis=1),
            np.concatenate([sin_big, cos_big], axis=1),
        ],
        axis=0,
    )
    return full.astype(jnp.bfloat16)


def layer_height(layer):
    return BAND + 2 * KR * (LAYERS - 1 - layer)


def block_height(layer):
    height = layer_height(layer)
    return height // 2 if 2 * (height + 2 * KR) > 2 * LANES else height


def spread_matrix():
    tile = lax.broadcasted_iota(jnp.int32, (NH, COLS), 0)
    column = lax.broadcasted_iota(jnp.int32, (NH, COLS), 1)
    return jnp.where(column // HS == tile, 1.0, 0.0).astype(jnp.bfloat16)


def own_colour():
    return jnp.minimum(lax.axis_index("depth"), COLORS - 1)


def pack_kernel(light, edges, counts, listed, row_taps, col_taps, incident, out, mine, *scratch):
    held, sems, taps = scratch[:6], scratch[6], scratch[7]
    picked = pltpu.make_async_copy(incident.at[own_colour()], mine, sems.at[6])
    sources = (listed, counts, edges, row_taps, col_taps, light)
    copies = [
        pltpu.make_async_copy(source, target, sems.at[place])
        for place, (source, target) in enumerate(zip(sources, held))
    ]
    for copy in reversed(copies):
        copy.start()
    picked.start()
    listed, counts, edges, row_taps, col_taps, light = held
    spread = spread_matrix()
    slot = lax.broadcasted_iota(jnp.int32, (NH, NH), 0)
    place = lax.broadcasted_iota(jnp.int32, (NH, NH), 1)
    for copy in copies[:5]:
        copy.wait()
    rows = []
    for group in range(BAND // HS):
        listing = jnp.broadcast_to(listed[0, group : group + 1, :], (NH, NH))
        column = jnp.sum(jnp.where(slot == place, listing, 0), axis=1, keepdims=True)
        named = (column == place) & (slot < counts[0, group])
        live = jnp.max(jnp.where(named, 1.0, 0.0), axis=0, keepdims=True)
        rows.append(jnp.broadcast_to(live, (HS, NH)))
    live_rows = jnp.concatenate(rows, axis=0).astype(jnp.bfloat16)
    live_pix = jnp.dot(live_rows, spread, preferred_element_type=jnp.float32)
    edge_tile = jnp.concatenate(
        [edges[0].astype(jnp.float32), jnp.zeros((BAND, LANES - NH), jnp.float32)], axis=1
    ).astype(jnp.bfloat16)
    for colour in range(COLORS):
        out[colour, :, COLS:HALO_W] = edge_tile
        taps[...] = jnp.zeros_like(taps)
        taps[0:2, : 2 * KC + 1] = col_taps[0, colour].astype(jnp.float32)
        taps[2:4, : 2 * KR + 1] = row_taps[0, colour].astype(jnp.float32)
        out[colour, :, HALO_W:] = taps[...].astype(jnp.bfloat16)
    for spare in range(COLORS, LAYERS):
        out[spare] = jnp.zeros((BAND, FULL_W), jnp.bfloat16)
    copies[5].wait()
    for colour in range(COLORS):
        out[colour, :, :COLS] = (light[0, colour] * live_pix).astype(jnp.bfloat16)
    picked.wait()


def halo_kernel(own, in_chip, cross, far_even, far_odd):
    band = lax.axis_index("rows")
    core = band % 2
    odd = (band // 2) % 2
    last = BAND - KR
    for near, start in ((in_chip, (1 - core) * last), (cross, core * last)):
        near[0:BAND] = own[0, :, :HALO_W]
        near[BAND : 2 * BAND] = own[1, :, :HALO_W]
        near[2 * BAND : NEAR] = own[2, pl.ds(pl.multiple_of(start, KR), KR), :HALO_W]
    for far, start in ((far_even, (1 - odd) * last), (far_odd, odd * last)):
        far[...] = own[0, pl.ds(pl.multiple_of(start, KR), KR), :HALO_W]


def ordered(in_chip, cross, far_even, far_odd):
    band = lax.axis_index("rows")
    even_core = band % 2 == 0
    even_chip = (band // 2) % 2 == 0
    in_chip, cross = in_chip[...], cross[...]
    far_even, far_odd = far_even[...], far_odd[...]
    return (
        jnp.where(even_core, cross, in_chip),
        jnp.where(even_core, in_chip, cross),
        jnp.where(even_chip, far_odd, far_even),
        jnp.where(even_chip, far_even, far_odd),
    )


def tiles_below(value, height):
    return jnp.concatenate(
        [
            jnp.concatenate(
                [
                    value[:height, tile * LANES : (tile + 1) * LANES],
                    value[height:, tile * LANES : (tile + 1) * LANES],
                ],
                axis=1,
            )
            for tile in range(TILES)
        ],
        axis=0,
    )


def stereo_tiles(blocks, left_tab, right_tab):
    arranged = []
    for light in blocks:
        doubled = jnp.concatenate([light, light], axis=0)
        left = jnp.dot(left_tab[...], doubled, preferred_element_type=jnp.float32)
        arranged.append(tiles_below(left.astype(jnp.bfloat16), light.shape[0]))
    arranged = jnp.concatenate(arranged, axis=0) if len(arranged) > 1 else arranged[0]
    return jnp.dot(arranged, right_tab[...], preferred_element_type=jnp.float32)


def clear_pixels(edges):
    edge_pix = jnp.dot(edges, spread_matrix(), preferred_element_type=jnp.float32)
    within = (lax.broadcasted_iota(jnp.int32, (1, COLS), 1) % HS).astype(jnp.float32)
    return jnp.where(within < edge_pix, 1.0, 0.0)


def banded(line, count, shift):
    base = jnp.concatenate([line, jnp.zeros((1, LANES), jnp.float32)], axis=1)
    base = jnp.broadcast_to(base, (count, 2 * LANES))
    return pltpu.roll(base, shift, 1, stride=1, stride_axis=0)


def filters(taps, layer):
    row_re, row_im = taps[2:3], taps[3:4]
    height = block_height(layer)
    before = height + 2 * KR
    upper = banded(row_re, height, 0) - banded(row_im, height, before)
    lower = banded(row_im, height, 0) + banded(row_re, height, before)
    row_mat = jnp.concatenate([upper, lower], axis=0).astype(jnp.bfloat16)
    col_re = banded(taps[0:1], LANES, 1)
    col_im = banded(taps[1:2], LANES, 1)
    upper = jnp.concatenate([col_re, -col_im], axis=1)
    lower = jnp.concatenate([col_im, col_re], axis=1)
    col_mat = jnp.concatenate([upper, lower], axis=0).astype(jnp.bfloat16)
    return row_mat, col_mat


def propagated(u_re, u_im, row_mat, col_mat, layer):
    height = layer_height(layer)
    block = block_height(layer)
    reach = block + 2 * KR
    parts = []
    for start in range(0, height, block):
        stacked = jnp.concatenate(
            [u_re[start : start + reach], u_im[start : start + reach]], axis=0
        )
        parts.append(
            jnp.dot(row_mat[:, : 2 * reach], stacked, preferred_element_type=jnp.float32)
        )
    rowed = jnp.concatenate(
        [part[:block] for part in parts] + [part[block:] for part in parts], axis=0
    )
    rowed = jnp.concatenate([rowed, jnp.zeros((2 * height, LANES), jnp.float32)], axis=1)
    rowed = pltpu.roll(rowed, HALF, 1).astype(jnp.bfloat16)
    windows = jnp.concatenate(
        [
            jnp.concatenate(
                [
                    rowed[:height, tile * LANES : (tile + 2) * LANES],
                    rowed[height:, tile * LANES : (tile + 2) * LANES],
                ],
                axis=1,
            )
            for tile in range(TILES)
        ],
        axis=0,
    )
    return lax.dot_general(
        windows, col_mat, (((1,), (1,)), ((), ())), preferred_element_type=jnp.float32
    )


def prepare_kernel(
    own, incident, in_chip, cross, far_even, far_odd, left_tab, right_tab,
    first, stereo, clear, col_mats, *row_mats
):
    low_near, high_near, low_far, high_far = ordered(in_chip, cross, far_even, far_odd)
    extended = []
    for part in range(2):
        pieces = [low_far, low_near, incident[...], high_near, high_far]
        pieces = [piece[part * BAND : (part + 1) * BAND] for piece in pieces]
        extended.append(jnp.concatenate(pieces, axis=0))
    row_mat, col_mat = filters(own[0, 0:16, HALO_W:].astype(jnp.float32), 0)
    first[...] = propagated(extended[0], extended[1], row_mat, col_mat, 0)
    for layer in range(1, LAYERS):
        row_mat, col_mat = filters(own[layer, 0:16, HALO_W:].astype(jnp.float32), layer)
        row_mats[layer - 1][...] = row_mat
        col_mats[layer - 1] = col_mat
    packed = jnp.concatenate([own[layer, :, :HALO_W] for layer in range(LAYERS)], axis=0)
    clear[...] = clear_pixels(packed[:, COLS : COLS + NH])
    tiles = stereo_tiles([packed[:, :COLS]], left_tab, right_tab)
    for tile in range(TILES):
        for part in range(2):
            block = tiles[
                tile * LANES : (tile + 1) * LANES, part * LANES : (part + 1) * LANES
            ]
            stereo[part, :, tile * LANES : (tile + 1) * LANES] = block


def chain_kernel(
    in_chip, cross, far_even, far_odd, left_tab, right_tab, first, stereo, clear, col_mats, *rest
):
    row_mats, outs, field = rest[: LAYERS - 1], rest[LAYERS - 1 : -1], rest[-1]
    depth = lax.axis_index("depth")
    low_near, high_near, low_far, high_far = ordered(in_chip, cross, far_even, far_odd)
    pieces = [
        low_far,
        low_near[0:BAND],
        high_near[0:BAND],
        high_far,
        low_near[BAND : 2 * BAND],
        high_near[BAND : 2 * BAND],
        low_near[2 * BAND : NEAR],
        high_near[2 * BAND : NEAR],
    ]
    halo = jnp.concatenate(pieces, axis=0)
    half = halo.shape[0] // 2
    halo_tiles = stereo_tiles(
        [halo[:half, :COLS], halo[half:, :COLS]], left_tab, right_tab
    )
    halo_clear = clear_pixels(halo[:, COLS : COLS + NH])
    begins = (0, half, half + 2 * BAND, 0)
    sides = (BAND + FAR, BAND, KR, 0)
    for layer in range(LAYERS):
        height = layer_height(layer)
        before = height + 2 * KR
        low, side = begins[layer], sides[layer]
        if layer == 0:
            columned = first
        else:
            columned = propagated(
                field[0, :before], field[1, :before], row_mats[layer - 1], col_mats[layer - 1], layer
            )
        band = slice(layer * BAND, (layer + 1) * BAND)
        pieces = [clear[band]]
        if side:
            pieces = [halo_clear[low : low + side], clear[band], halo_clear[low + side : low + 2 * side]]
        passing = jnp.concatenate(pieces, axis=0)
        for tile in range(TILES):
            span = slice(tile * height, (tile + 1) * height)
            lanes = slice(tile * LANES, (tile + 1) * LANES)
            row = (low // half * TILES + tile) * half + low % half
            for part in range(2):
                within = slice(part * LANES, (part + 1) * LANES)
                pieces = [stereo[part, band, lanes]]
                if side:
                    pieces = [
                        halo_tiles[row : row + side, within],
                        stereo[part, band, lanes],
                        halo_tiles[row + side : row + 2 * side, within],
                    ]
                added = jnp.concatenate(pieces, axis=0)
                value = passing[:, lanes] * columned[span, within] + added
                field[part, :height, lanes] = value.astype(jnp.bfloat16)
        for hop, out in enumerate(outs):

            @pl.when((depth ^ hop) == layer)
            def keep(out=out, side=side):
                for part in range(2):
                    out[part] = field[part, side : side + BAND]


def home_kernel(*refs):
    arrived, out, sems = refs[:LAYERS], refs[LAYERS], refs[LAYERS + 1]
    depth = lax.axis_index("depth")
    for colour in range(COLORS):
        for hop in range(LAYERS):

            @pl.when((depth ^ hop) == colour)
            def begin(hop=hop, colour=colour):
                pltpu.make_async_copy(arrived[hop], out.at[0, colour], sems.at[colour]).start()

    for colour in range(COLORS):
        pltpu.make_async_copy(arrived[0], out.at[0, colour], sems.at[colour]).wait()


def sent_home(value, hop):
    return lax.ppermute(value, "depth", [(i, i ^ hop) for i in range(COLORS)])


def exchanged(value, axis, by, phase):
    count = lax.axis_size(axis)
    lower = [i for i in range(count - by) if (i // by) % 2 == phase]
    pairs = [(i, i + by) for i in lower] + [(i + by, i) for i in lower]
    return lax.ppermute(value, axis, pairs)


def neighbours(sent):
    in_chip, cross, far_even, far_odd = sent
    cross = exchanged(cross, "rows", 1, 1)
    far_even = exchanged(far_even, "rows", 2, 0)
    far_odd = exchanged(far_odd, "rows", 2, 1)
    in_chip = exchanged(in_chip, "rows", 1, 0)
    return in_chip, cross, far_even, far_odd


def call(
    kernel, out_shape, in_specs, scratch=(), flops=0, moved=10**6, limit=VMEM_LIMIT,
    out_space=pltpu.VMEM,
):
    vmem = pl.BlockSpec(memory_space=out_space)
    many = isinstance(out_shape, (tuple, list))
    return pl.pallas_call(
        kernel,
        out_shape=out_shape,
        in_specs=in_specs,
        out_specs=(vmem,) * len(out_shape) if many else vmem,
        scratch_shapes=scratch,
        compiler_params=pltpu.CompilerParams(vmem_limit_bytes=limit),
        cost_estimate=pl.CostEstimate(flops=flops, bytes_accessed=moved, transcendentals=0),
    )


def body(incident, row_taps, col_taps, hogel_light, silhouette, fill_counts, hogel_index):
    vmem = pl.BlockSpec(memory_space=pltpu.VMEM)
    hbm = pl.BlockSpec(memory_space=pltpu.HBM)
    bf16, f32 = jnp.bfloat16, jnp.float32
    shaped = jax.ShapeDtypeStruct
    held = [
        pltpu.VMEM(hogel_index.shape, jnp.int32),
        pltpu.SMEM(fill_counts.shape, jnp.int32),
        pltpu.VMEM(silhouette.shape, jnp.int32),
        pltpu.VMEM(row_taps.shape, bf16),
        pltpu.VMEM(col_taps.shape, bf16),
        pltpu.VMEM(hogel_light.shape, f32),
    ]
    payload, mine = call(
        pack_kernel,
        (shaped((LAYERS, BAND, FULL_W), bf16), shaped(incident.shape[1:], bf16)),
        [hbm] * 7,
        held + [pltpu.SemaphoreType.DMA((7,)), pltpu.VMEM((BAND, LANES), f32)],
        flops=10**7,
        limit=PACK_LIMIT,
    )(hogel_light, silhouette, fill_counts, hogel_index, row_taps, col_taps, incident)
    mine = mine.reshape(2 * BAND, COLS)
    own = lax.all_to_all(payload, "depth", 0, 0, tiled=True)
    arrived = neighbours((mine,) * 4)
    near = shaped((NEAR, HALO_W), bf16)
    far = shaped((FAR, HALO_W), bf16)
    halos = neighbours(call(halo_kernel, (near, near, far, far), [vmem])(own))
    right_tab = jnp.asarray(right_table())
    made = call(
        prepare_kernel,
        [
            shaped((TILES * layer_height(0), 2 * LANES), f32),
            shaped((2, LANES, COLS), f32),
            shaped((LANES, COLS), f32),
            shaped((LAYERS - 1, 2 * LANES, 4 * LANES), bf16),
        ]
        + [shaped((2 * block_height(layer), 2 * LANES), bf16) for layer in range(1, LAYERS)],
        [vmem] * 8,
        flops=10**9,
        moved=3 * 10**6,
    )(own, mine, *arrived, jnp.asarray(left_table(LANES)), right_tab)
    halo_rows = NEAR + FAR
    results = call(
        chain_kernel,
        [shaped((2, BAND, COLS), bf16)] * LAYERS,
        [vmem] * (6 + len(made)),
        [pltpu.VMEM((2, layer_height(0), COLS), bf16)],
        flops=2 * 10**9,
        moved=3 * 10**6,
    )(*halos, jnp.asarray(left_table(halo_rows)), right_tab, *made)
    diagonal = sent_home(results[3], 3)
    along_x = sent_home(results[1], 1)
    along_y = sent_home(results[2], 2)
    return call(
        home_kernel,
        shaped((1, COLORS, 2, BAND, COLS), bf16),
        [vmem] * LAYERS,
        [pltpu.SemaphoreType.DMA((COLORS,))],
        out_space=pltpu.HBM,
    )(results[0], along_x, along_y, diagonal)


def solution(mesh):
    placed = (
        P(None, None, "rows", None),
        P("depth", None, None, None),
        P("depth", None, None, None),
        P("depth", None, "rows", None),
        P("depth", "rows", None),
        P("depth", "rows"),
        P("depth", "rows", None),
    )
    return jax.shard_map(
        body,
        mesh=mesh,
        in_specs=placed,
        out_specs=P("depth", None, None, "rows", None),
        check_vma=False,
    )
```

```python
import math

import jax
import jax.numpy as jnp
import numpy as np
from jax import lax
from jax.experimental import pallas as pl
from jax.experimental.pallas import tpu as pltpu
from jax.sharding import PartitionSpec as P

HS = 16
KR = 16
KC = 63
COLORS = 3
LAYERS = 4
BAND = 32
COLS = 1024
NH = COLS // HS
LANES = 128
TILES = COLS // LANES
HALO_W = COLS + LANES
HALF = LANES // 2
FULL_W = COLS + 2 * LANES
NEAR = 2 * BAND + KR
FAR = KR
VMEM_LIMIT = 48 * 1024 * 1024
PACK_LIMIT = 63 * 1024 * 1024


def split_table(table):
    high = table.astype(jnp.bfloat16)
    low = (table - high.astype(np.float64)).astype(jnp.bfloat16)
    return high, low


def dft_pair():
    counter = np.arange(HS)
    angles = (counter[:, None] * counter[None, :] % HS) * (2.0 * math.pi / HS)
    return np.cos(angles) / math.sqrt(HS), np.sin(angles) / math.sqrt(HS)


def left_table(height):
    cos_tab, sin_tab = dft_pair()
    eye = np.eye(height // HS)
    full = np.concatenate([np.kron(eye, cos_tab), np.kron(eye, -sin_tab)], axis=0)
    return np.concatenate(split_table(full), axis=1)


def right_table():
    cos_tab, sin_tab = dft_pair()
    eye = np.eye(LANES // HS)
    cos_big, sin_big = np.kron(eye, cos_tab), np.kron(eye, sin_tab)
    full = np.concatenate(
        [
            np.concatenate([cos_big, -sin_big], axis=1),
            np.concatenate([sin_big, cos_big], axis=1),
        ],
        axis=0,
    )
    return full.astype(jnp.bfloat16)


def layer_height(layer):
    return BAND + 2 * KR * (LAYERS - 1 - layer)


def block_height(layer):
    height = layer_height(layer)
    return height // 2 if 2 * (height + 2 * KR) > 2 * LANES else height


def spread_matrix():
    tile = lax.broadcasted_iota(jnp.int32, (NH, COLS), 0)
    column = lax.broadcasted_iota(jnp.int32, (NH, COLS), 1)
    return jnp.where(column // HS == tile, 1.0, 0.0).astype(jnp.bfloat16)


def own_colour():
    return jnp.minimum(lax.axis_index("depth"), COLORS - 1)


def pack_kernel(light, edges, counts, listed, row_taps, col_taps, incident, out, mine, *scratch):
    held, sems, taps = scratch[:6], scratch[6], scratch[7]
    picked = pltpu.make_async_copy(incident.at[own_colour()], mine, sems.at[6])
    sources = (listed, counts, edges, row_taps, col_taps, light)
    copies = [
        pltpu.make_async_copy(source, target, sems.at[place])
        for place, (source, target) in enumerate(zip(sources, held))
    ]
    for copy in reversed(copies):
        copy.start()
    picked.start()
    listed, counts, edges, row_taps, col_taps, light = held
    spread = spread_matrix()
    slot = lax.broadcasted_iota(jnp.int32, (NH, NH), 0)
    place = lax.broadcasted_iota(jnp.int32, (NH, NH), 1)
    for copy in copies[:5]:
        copy.wait()
    rows = []
    for group in range(BAND // HS):
        listing = jnp.broadcast_to(listed[0, group : group + 1, :], (NH, NH))
        column = jnp.sum(jnp.where(slot == place, listing, 0), axis=1, keepdims=True)
        named = (column == place) & (slot < counts[0, group])
        live = jnp.max(jnp.where(named, 1.0, 0.0), axis=0, keepdims=True)
        rows.append(jnp.broadcast_to(live, (HS, NH)))
    live_rows = jnp.concatenate(rows, axis=0).astype(jnp.bfloat16)
    live_pix = jnp.dot(live_rows, spread, preferred_element_type=jnp.float32)
    edge_tile = jnp.concatenate(
        [edges[0].astype(jnp.float32), jnp.zeros((BAND, LANES - NH), jnp.float32)], axis=1
    ).astype(jnp.bfloat16)
    for colour in range(COLORS):
        out[colour, :, COLS:HALO_W] = edge_tile
        taps[...] = jnp.zeros_like(taps)
        taps[0:2, : 2 * KC + 1] = col_taps[0, colour].astype(jnp.float32)
        taps[2:4, : 2 * KR + 1] = row_taps[0, colour].astype(jnp.float32)
        out[colour, :, HALO_W:] = taps[...].astype(jnp.bfloat16)
    for spare in range(COLORS, LAYERS):
        out[spare] = jnp.zeros((BAND, FULL_W), jnp.bfloat16)
    copies[5].wait()
    for colour in range(COLORS):
        out[colour, :, :COLS] = (light[0, colour] * live_pix).astype(jnp.bfloat16)
    picked.wait()


def halo_kernel(own, in_chip, cross, far_even, far_odd):
    band = lax.axis_index("rows")
    core = band % 2
    odd = (band // 2) % 2
    last = BAND - KR
    for near, start in ((in_chip, (1 - core) * last), (cross, core * last)):
        near[0:BAND] = own[0, :, :HALO_W]
        near[BAND : 2 * BAND] = own[1, :, :HALO_W]
        near[2 * BAND : NEAR] = own[2, pl.ds(pl.multiple_of(start, KR), KR), :HALO_W]
    for far, start in ((far_even, (1 - odd) * last), (far_odd, odd * last)):
        far[...] = own[0, pl.ds(pl.multiple_of(start, KR), KR), :HALO_W]


def near_sides(in_chip, cross):
    even_core = lax.axis_index("rows") % 2 == 0
    in_chip, cross = in_chip[...], cross[...]
    return jnp.where(even_core, cross, in_chip), jnp.where(even_core, in_chip, cross)


def far_sides(far_even, far_odd):
    even_chip = (lax.axis_index("rows") // 2) % 2 == 0
    far_even, far_odd = far_even[...], far_odd[...]
    return jnp.where(even_chip, far_odd, far_even), jnp.where(even_chip, far_even, far_odd)


def tiles_below(value, height):
    return jnp.concatenate(
        [
            jnp.concatenate(
                [
                    value[:height, tile * LANES : (tile + 1) * LANES],
                    value[height:, tile * LANES : (tile + 1) * LANES],
                ],
                axis=1,
            )
            for tile in range(TILES)
        ],
        axis=0,
    )


def stereo_tiles(blocks, left_tab, right_tab):
    arranged = []
    for light in blocks:
        doubled = jnp.concatenate([light, light], axis=0)
        left = jnp.dot(left_tab[...], doubled, preferred_element_type=jnp.float32)
        arranged.append(tiles_below(left.astype(jnp.bfloat16), light.shape[0]))
    arranged = jnp.concatenate(arranged, axis=0) if len(arranged) > 1 else arranged[0]
    return jnp.dot(arranged, right_tab[...], preferred_element_type=jnp.float32)


def clear_pixels(edges):
    edge_pix = jnp.dot(edges, spread_matrix(), preferred_element_type=jnp.float32)
    within = (lax.broadcasted_iota(jnp.int32, (1, COLS), 1) % HS).astype(jnp.float32)
    return jnp.where(within < edge_pix, 1.0, 0.0)


def banded(line, count, shift):
    base = jnp.concatenate([line, jnp.zeros((1, LANES), jnp.float32)], axis=1)
    base = jnp.broadcast_to(base, (count, 2 * LANES))
    return pltpu.roll(base, shift, 1, stride=1, stride_axis=0)


def filters(taps, layer):
    row_re, row_im = taps[2:3], taps[3:4]
    height = block_height(layer)
    before = height + 2 * KR
    upper = banded(row_re, height, 0) - banded(row_im, height, before)
    lower = banded(row_im, height, 0) + banded(row_re, height, before)
    row_mat = jnp.concatenate([upper, lower], axis=0).astype(jnp.bfloat16)
    col_re = banded(taps[0:1], LANES, 1)
    col_im = banded(taps[1:2], LANES, 1)
    upper = jnp.concatenate([col_re, -col_im], axis=1)
    lower = jnp.concatenate([col_im, col_re], axis=1)
    col_mat = jnp.concatenate([upper, lower], axis=0).astype(jnp.bfloat16)
    return row_mat, col_mat


def propagated(u_re, u_im, row_mat, col_mat, layer):
    height = layer_height(layer)
    block = block_height(layer)
    reach = block + 2 * KR
    parts = []
    for start in range(0, height, block):
        stacked = jnp.concatenate(
            [u_re[start : start + reach], u_im[start : start + reach]], axis=0
        )
        parts.append(
            jnp.dot(row_mat[:, : 2 * reach], stacked, preferred_element_type=jnp.float32)
        )
    rowed = jnp.concatenate(
        [part[:block] for part in parts] + [part[block:] for part in parts], axis=0
    )
    rowed = jnp.concatenate([rowed, jnp.zeros((2 * height, LANES), jnp.float32)], axis=1)
    rowed = pltpu.roll(rowed, HALF, 1).astype(jnp.bfloat16)
    windows = jnp.concatenate(
        [
            jnp.concatenate(
                [
                    rowed[:height, tile * LANES : (tile + 2) * LANES],
                    rowed[height:, tile * LANES : (tile + 2) * LANES],
                ],
                axis=1,
            )
            for tile in range(TILES)
        ],
        axis=0,
    )
    return lax.dot_general(
        windows, col_mat, (((1,), (1,)), ((), ())), preferred_element_type=jnp.float32
    )


def prepare_kernel(
    own, incident, in_chip, cross, far_even, far_odd, light_in_chip, light_cross,
    left_tab, near_tab, right_tab,
    first, stereo, clear, near_tiles, near_clear, col_mats, *row_mats
):
    low_near, high_near = near_sides(in_chip, cross)
    low_far, high_far = far_sides(far_even, far_odd)
    extended = []
    for part in range(2):
        pieces = [low_far, low_near, incident[...], high_near, high_far]
        pieces = [piece[part * BAND : (part + 1) * BAND] for piece in pieces]
        extended.append(jnp.concatenate(pieces, axis=0))
    row_mat, col_mat = filters(own[0, 0:16, HALO_W:].astype(jnp.float32), 0)
    first[...] = propagated(extended[0], extended[1], row_mat, col_mat, 0)
    for layer in range(1, LAYERS):
        row_mat, col_mat = filters(own[layer, 0:16, HALO_W:].astype(jnp.float32), layer)
        row_mats[layer - 1][...] = row_mat
        col_mats[layer - 1] = col_mat
    packed = jnp.concatenate([own[layer, :, :HALO_W] for layer in range(LAYERS)], axis=0)
    clear[...] = clear_pixels(packed[:, COLS : COLS + NH])
    tiles = stereo_tiles([packed[:, :COLS]], left_tab, right_tab)
    for tile in range(TILES):
        for part in range(2):
            block = tiles[
                tile * LANES : (tile + 1) * LANES, part * LANES : (part + 1) * LANES
            ]
            stereo[part, :, tile * LANES : (tile + 1) * LANES] = block
    low, high = near_sides(light_in_chip, light_cross)
    blocks = [
        jnp.concatenate([low[0:BAND], high[0:BAND], low[2 * BAND :]], axis=0),
        jnp.concatenate(
            [low[BAND : 2 * BAND], high[BAND : 2 * BAND], high[2 * BAND :]], axis=0
        ),
    ]
    near_tiles[...] = stereo_tiles([block[:, :COLS] for block in blocks], near_tab, right_tab)
    edges = jnp.concatenate([block[:, COLS : COLS + NH] for block in blocks], axis=0)
    near_clear[...] = clear_pixels(edges)


def chain_kernel(
    far_even, far_odd, left_tab, right_tab,
    first, stereo, clear, near_tiles, near_clear, col_mats, *rest
):
    row_mats, (out, field) = rest[: LAYERS - 1], rest[LAYERS - 1 :]
    far = jnp.concatenate(far_sides(far_even, far_odd), axis=0)
    far_tiles = stereo_tiles([far[:, :COLS]], left_tab, right_tab)
    far_clear = clear_pixels(far[:, COLS : COLS + NH])

    spots = (
        ((0, BAND), (BAND, BAND)),
        ((NEAR, BAND), (NEAR + BAND, BAND)),
        ((2 * BAND, KR), (NEAR + 2 * BAND, KR)),
        None,
    )
    for layer in range(LAYERS):
        height = layer_height(layer)
        before = height + 2 * KR
        side = (height - BAND) // 2
        if layer == 0:
            columned = first
        else:
            columned = propagated(
                field[0, :before], field[1, :before], row_mats[layer - 1], col_mats[layer - 1], layer
            )
        band = slice(layer * BAND, (layer + 1) * BAND)
        pieces = [clear[band]]
        if side:
            (low, count), (high, _) = spots[layer]
            pieces = [near_clear[low : low + count], clear[band], near_clear[high : high + count]]
        if layer == 0:
            pieces = [far_clear[:FAR]] + pieces + [far_clear[FAR:]]
        passing = jnp.concatenate(pieces, axis=0)
        for tile in range(TILES):
            span = slice(tile * height, (tile + 1) * height)
            lanes = slice(tile * LANES, (tile + 1) * LANES)
            for part in range(2):
                within = slice(part * LANES, (part + 1) * LANES)
                pieces = [stereo[part, band, lanes]]
                if side:
                    rows = [
                        (start // NEAR * TILES + tile) * NEAR + start % NEAR for start in (low, high)
                    ]
                    pieces = [
                        near_tiles[rows[0] : rows[0] + count, within],
                        stereo[part, band, lanes],
                        near_tiles[rows[1] : rows[1] + count, within],
                    ]
                if layer == 0:
                    row = tile * 2 * FAR
                    pieces = (
                        [far_tiles[row : row + FAR, within]]
                        + pieces
                        + [far_tiles[row + FAR : row + 2 * FAR, within]]
                    )
                added = jnp.concatenate(pieces, axis=0)
                value = passing[:, lanes] * columned[span, within] + added
                field[part, :height, lanes] = value.astype(jnp.bfloat16)
        for part in range(2):
            out[layer, part] = field[part, side : side + BAND]


def exchanged(value, axis, by, phase):
    count = lax.axis_size(axis)
    lower = [i for i in range(count - by) if (i // by) % 2 == phase]
    pairs = [(i, i + by) for i in lower] + [(i + by, i) for i in lower]
    return lax.ppermute(value, axis, pairs)


def neighbours(sent):
    in_chip, cross, far_even, far_odd = sent
    cross = exchanged(cross, "rows", 1, 1)
    far_even = exchanged(far_even, "rows", 2, 0)
    far_odd = exchanged(far_odd, "rows", 2, 1)
    in_chip = exchanged(in_chip, "rows", 1, 0)
    return in_chip, cross, far_even, far_odd


def call(kernel, out_shape, in_specs, scratch=(), flops=0, moved=10**6, limit=VMEM_LIMIT):
    vmem = pl.BlockSpec(memory_space=pltpu.VMEM)
    many = isinstance(out_shape, (tuple, list))
    return pl.pallas_call(
        kernel,
        out_shape=out_shape,
        in_specs=in_specs,
        out_specs=(vmem,) * len(out_shape) if many else vmem,
        scratch_shapes=scratch,
        compiler_params=pltpu.CompilerParams(vmem_limit_bytes=limit),
        cost_estimate=pl.CostEstimate(flops=flops, bytes_accessed=moved, transcendentals=0),
    )


def body(incident, row_taps, col_taps, hogel_light, silhouette, fill_counts, hogel_index):
    vmem = pl.BlockSpec(memory_space=pltpu.VMEM)
    hbm = pl.BlockSpec(memory_space=pltpu.HBM)
    bf16, f32 = jnp.bfloat16, jnp.float32
    shaped = jax.ShapeDtypeStruct
    held = [
        pltpu.VMEM(hogel_index.shape, jnp.int32),
        pltpu.SMEM(fill_counts.shape, jnp.int32),
        pltpu.VMEM(silhouette.shape, jnp.int32),
        pltpu.VMEM(row_taps.shape, bf16),
        pltpu.VMEM(col_taps.shape, bf16),
        pltpu.VMEM(hogel_light.shape, f32),
    ]
    payload, mine = call(
        pack_kernel,
        (shaped((LAYERS, BAND, FULL_W), bf16), shaped(incident.shape[1:], bf16)),
        [hbm] * 7,
        held + [pltpu.SemaphoreType.DMA((7,)), pltpu.VMEM((BAND, LANES), f32)],
        flops=10**7,
        limit=PACK_LIMIT,
    )(hogel_light, silhouette, fill_counts, hogel_index, row_taps, col_taps, incident)
    mine = mine.reshape(2 * BAND, COLS)
    own = lax.all_to_all(payload, "depth", 0, 0, tiled=True)
    arrived = neighbours((mine,) * 4)
    near = shaped((NEAR, HALO_W), bf16)
    far = shaped((FAR, HALO_W), bf16)
    halos = neighbours(call(halo_kernel, (near, near, far, far), [vmem])(own))
    right_tab = jnp.asarray(right_table())
    made = call(
        prepare_kernel,
        [
            shaped((TILES * layer_height(0), 2 * LANES), f32),
            shaped((2, LANES, COLS), f32),
            shaped((LANES, COLS), f32),
            shaped((2 * NEAR * TILES, 2 * LANES), f32),
            shaped((2 * NEAR, COLS), f32),
            shaped((LAYERS - 1, 2 * LANES, 4 * LANES), bf16),
        ]
        + [shaped((2 * block_height(layer), 2 * LANES), bf16) for layer in range(1, LAYERS)],
        [vmem] * 11,
        flops=10**9,
        moved=3 * 10**6,
    )(
        own,
        mine,
        *arrived,
        *halos[:2],
        jnp.asarray(left_table(LANES)),
        jnp.asarray(left_table(NEAR)),
        right_tab,
    )
    result = call(
        chain_kernel,
        shaped((LAYERS, 2, BAND, COLS), bf16),
        [vmem] * (4 + len(made)),
        [pltpu.VMEM((2, layer_height(0), COLS), bf16)],
        flops=2 * 10**9,
        moved=3 * 10**6,
    )(*halos[2:], jnp.asarray(left_table(2 * FAR)), right_tab, *made)
    gathered = lax.all_to_all(result, "depth", 0, 0, tiled=True)
    return gathered[None, :COLORS]


def solution(mesh):
    placed = (
        P(None, None, "rows", None),
        P("depth", None, None, None),
        P("depth", None, None, None),
        P("depth", None, "rows", None),
        P("depth", "rows", None),
        P("depth", "rows"),
        P("depth", "rows", None),
    )
    return jax.shard_map(
        body,
        mesh=mesh,
        in_specs=placed,
        out_specs=P("depth", None, None, "rows", None),
        check_vma=False,
    )
```

```python
import math

import jax
import jax.numpy as jnp
import numpy as np
from jax import lax
from jax.experimental import pallas as pl
from jax.experimental.pallas import tpu as pltpu
from jax.sharding import PartitionSpec as P

HS = 16
KR = 16
KC = 63
COLORS = 3
LAYERS = 4
BAND = 32
COLS = 1024
NH = COLS // HS
LANES = 128
TILES = COLS // LANES
HALO_W = COLS + LANES
HALF = LANES // 2
FULL_W = COLS + 2 * LANES
NEAR = 2 * BAND + KR
FAR = KR
VMEM_LIMIT = 48 * 1024 * 1024
PACK_LIMIT = 63 * 1024 * 1024


def split_table(table):
    high = table.astype(jnp.bfloat16)
    low = (table - high.astype(np.float64)).astype(jnp.bfloat16)
    return high, low


def dft_pair():
    counter = np.arange(HS)
    angles = (counter[:, None] * counter[None, :] % HS) * (2.0 * math.pi / HS)
    return np.cos(angles) / math.sqrt(HS), np.sin(angles) / math.sqrt(HS)


def left_table(height):
    cos_tab, sin_tab = dft_pair()
    eye = np.eye(height // HS)
    full = np.concatenate([np.kron(eye, cos_tab), np.kron(eye, -sin_tab)], axis=0)
    return np.concatenate(split_table(full), axis=1)


def right_table():
    cos_tab, sin_tab = dft_pair()
    eye = np.eye(LANES // HS)
    cos_big, sin_big = np.kron(eye, cos_tab), np.kron(eye, sin_tab)
    full = np.concatenate(
        [
            np.concatenate([cos_big, -sin_big], axis=1),
            np.concatenate([sin_big, cos_big], axis=1),
        ],
        axis=0,
    )
    return full.astype(jnp.bfloat16)


def layer_height(layer):
    return BAND + 2 * KR * (LAYERS - 1 - layer)


def block_height(layer):
    height = layer_height(layer)
    return height // 2 if 2 * (height + 2 * KR) > 2 * LANES else height


def spread_matrix():
    tile = lax.broadcasted_iota(jnp.int32, (NH, COLS), 0)
    column = lax.broadcasted_iota(jnp.int32, (NH, COLS), 1)
    return jnp.where(column // HS == tile, 1.0, 0.0).astype(jnp.bfloat16)


def own_colour():
    return jnp.minimum(lax.axis_index("depth"), COLORS - 1)


def pack_kernel(light, edges, counts, listed, row_taps, col_taps, incident, out, mine, *scratch):
    held, sems, taps = scratch[:6], scratch[6], scratch[7]
    picked = pltpu.make_async_copy(incident.at[own_colour()], mine, sems.at[6])
    sources = (listed, counts, edges, row_taps, col_taps, light)
    copies = [
        pltpu.make_async_copy(source, target, sems.at[place])
        for place, (source, target) in enumerate(zip(sources, held))
    ]
    for copy in reversed(copies):
        copy.start()
    picked.start()
    listed, counts, edges, row_taps, col_taps, light = held
    spread = spread_matrix()
    slot = lax.broadcasted_iota(jnp.int32, (NH, NH), 0)
    place = lax.broadcasted_iota(jnp.int32, (NH, NH), 1)
    for copy in copies[:5]:
        copy.wait()
    rows = []
    for group in range(BAND // HS):
        listing = jnp.broadcast_to(listed[0, group : group + 1, :], (NH, NH))
        column = jnp.sum(jnp.where(slot == place, listing, 0), axis=1, keepdims=True)
        named = (column == place) & (slot < counts[0, group])
        live = jnp.max(jnp.where(named, 1.0, 0.0), axis=0, keepdims=True)
        rows.append(jnp.broadcast_to(live, (HS, NH)))
    live_rows = jnp.concatenate(rows, axis=0).astype(jnp.bfloat16)
    live_pix = jnp.dot(live_rows, spread, preferred_element_type=jnp.float32)
    edge_tile = jnp.concatenate(
        [edges[0].astype(jnp.float32), jnp.zeros((BAND, LANES - NH), jnp.float32)], axis=1
    ).astype(jnp.bfloat16)
    for colour in range(COLORS):
        out[colour, :, COLS:HALO_W] = edge_tile
        taps[...] = jnp.zeros_like(taps)
        taps[0:2, : 2 * KC + 1] = col_taps[0, colour].astype(jnp.float32)
        taps[2:4, : 2 * KR + 1] = row_taps[0, colour].astype(jnp.float32)
        out[colour, :, HALO_W:] = taps[...].astype(jnp.bfloat16)
    for spare in range(COLORS, LAYERS):
        out[spare] = jnp.zeros((BAND, FULL_W), jnp.bfloat16)
    copies[5].wait()
    for colour in range(COLORS):
        out[colour, :, :COLS] = (light[0, colour] * live_pix).astype(jnp.bfloat16)
    picked.wait()


def halo_kernel(own, in_chip, cross, far_even, far_odd):
    band = lax.axis_index("rows")
    core = band % 2
    odd = (band // 2) % 2
    last = BAND - KR
    for near, start in ((in_chip, (1 - core) * last), (cross, core * last)):
        near[0:BAND] = own[0, :, :HALO_W]
        near[BAND : 2 * BAND] = own[1, :, :HALO_W]
        near[2 * BAND : NEAR] = own[2, pl.ds(pl.multiple_of(start, KR), KR), :HALO_W]
    for far, start in ((far_even, (1 - odd) * last), (far_odd, odd * last)):
        far[...] = own[0, pl.ds(pl.multiple_of(start, KR), KR), :HALO_W]


def ordered(in_chip, cross, far_even, far_odd):
    band = lax.axis_index("rows")
    count = lax.axis_size("rows")
    even_core = band % 2 == 0
    even_chip = (band // 2) % 2 == 0

    def received(value, by, phase):
        lower = (band // by) % 2 == phase
        paired = jnp.where(lower, band + by < count, band >= by)
        value = value[...]
        return jnp.where(paired, value, jnp.zeros_like(value))

    in_chip, cross = received(in_chip, 1, 0), received(cross, 1, 1)
    far_even, far_odd = received(far_even, 2, 0), received(far_odd, 2, 1)
    return (
        jnp.where(even_core, cross, in_chip),
        jnp.where(even_core, in_chip, cross),
        jnp.where(even_chip, far_odd, far_even),
        jnp.where(even_chip, far_even, far_odd),
    )


def tiles_below(value, height):
    return jnp.concatenate(
        [
            jnp.concatenate(
                [
                    value[:height, tile * LANES : (tile + 1) * LANES],
                    value[height:, tile * LANES : (tile + 1) * LANES],
                ],
                axis=1,
            )
            for tile in range(TILES)
        ],
        axis=0,
    )


def stereo_tiles(blocks, left_tab, right_tab):
    arranged = []
    for light in blocks:
        doubled = jnp.concatenate([light, light], axis=0)
        left = jnp.dot(left_tab[...], doubled, preferred_element_type=jnp.float32)
        arranged.append(tiles_below(left.astype(jnp.bfloat16), light.shape[0]))
    arranged = jnp.concatenate(arranged, axis=0) if len(arranged) > 1 else arranged[0]
    return jnp.dot(arranged, right_tab[...], preferred_element_type=jnp.float32)


def clear_pixels(edges):
    edge_pix = jnp.dot(edges, spread_matrix(), preferred_element_type=jnp.float32)
    within = (lax.broadcasted_iota(jnp.int32, (1, COLS), 1) % HS).astype(jnp.float32)
    return jnp.where(within < edge_pix, 1.0, 0.0)


def banded(line, count, shift):
    base = jnp.concatenate([line, jnp.zeros((1, LANES), jnp.float32)], axis=1)
    base = jnp.broadcast_to(base, (count, 2 * LANES))
    return pltpu.roll(base, shift, 1, stride=1, stride_axis=0)


def filters(taps, layer):
    row_re, row_im = taps[2:3], taps[3:4]
    height = block_height(layer)
    before = height + 2 * KR
    upper = banded(row_re, height, 0) - banded(row_im, height, before)
    lower = banded(row_im, height, 0) + banded(row_re, height, before)
    row_mat = jnp.concatenate([upper, lower], axis=0).astype(jnp.bfloat16)
    col_re = banded(taps[0:1], LANES, 1)
    col_im = banded(taps[1:2], LANES, 1)
    upper = jnp.concatenate([col_re, -col_im], axis=1)
    lower = jnp.concatenate([col_im, col_re], axis=1)
    col_mat = jnp.concatenate([upper, lower], axis=0).astype(jnp.bfloat16)
    return row_mat, col_mat


def propagated(u_re, u_im, row_mat, col_mat, layer):
    height = layer_height(layer)
    block = block_height(layer)
    reach = block + 2 * KR
    parts = []
    for start in range(0, height, block):
        stacked = jnp.concatenate(
            [u_re[start : start + reach], u_im[start : start + reach]], axis=0
        )
        parts.append(
            jnp.dot(row_mat[:, : 2 * reach], stacked, preferred_element_type=jnp.float32)
        )
    rowed = jnp.concatenate(
        [part[:block] for part in parts] + [part[block:] for part in parts], axis=0
    )
    rowed = jnp.concatenate([rowed, jnp.zeros((2 * height, LANES), jnp.float32)], axis=1)
    rowed = pltpu.roll(rowed, HALF, 1).astype(jnp.bfloat16)
    windows = jnp.concatenate(
        [
            jnp.concatenate(
                [
                    rowed[:height, tile * LANES : (tile + 2) * LANES],
                    rowed[height:, tile * LANES : (tile + 2) * LANES],
                ],
                axis=1,
            )
            for tile in range(TILES)
        ],
        axis=0,
    )
    return lax.dot_general(
        windows, col_mat, (((1,), (1,)), ((), ())), preferred_element_type=jnp.float32
    )


def prepare_kernel(
    own, incident, in_chip, cross, far_even, far_odd, left_tab, right_tab,
    first, stereo, clear, col_mats, *row_mats
):
    low_near, high_near, low_far, high_far = ordered(in_chip, cross, far_even, far_odd)
    extended = []
    for part in range(2):
        pieces = [low_far, low_near, incident[...], high_near, high_far]
        pieces = [piece[part * BAND : (part + 1) * BAND] for piece in pieces]
        extended.append(jnp.concatenate(pieces, axis=0))
    row_mat, col_mat = filters(own[0, 0:16, HALO_W:].astype(jnp.float32), 0)
    first[...] = propagated(extended[0], extended[1], row_mat, col_mat, 0)
    for layer in range(1, LAYERS):
        row_mat, col_mat = filters(own[layer, 0:16, HALO_W:].astype(jnp.float32), layer)
        row_mats[layer - 1][...] = row_mat
        col_mats[layer - 1] = col_mat
    packed = jnp.concatenate([own[layer, :, :HALO_W] for layer in range(LAYERS)], axis=0)
    clear[...] = clear_pixels(packed[:, COLS : COLS + NH])
    tiles = stereo_tiles([packed[:, :COLS]], left_tab, right_tab)
    for tile in range(TILES):
        for part in range(2):
            block = tiles[
                tile * LANES : (tile + 1) * LANES, part * LANES : (part + 1) * LANES
            ]
            stereo[part, :, tile * LANES : (tile + 1) * LANES] = block


def chain_kernel(
    in_chip, cross, far_even, far_odd, left_tab, right_tab, first, stereo, clear, col_mats, *rest
):
    row_mats, (out, field) = rest[: LAYERS - 1], rest[LAYERS - 1 :]
    low_near, high_near, low_far, high_far = ordered(in_chip, cross, far_even, far_odd)
    pieces = [
        low_far,
        low_near[0:BAND],
        high_near[0:BAND],
        high_far,
        low_near[BAND : 2 * BAND],
        high_near[BAND : 2 * BAND],
        low_near[2 * BAND : NEAR],
        high_near[2 * BAND : NEAR],
    ]
    halo = jnp.concatenate(pieces, axis=0)
    half = halo.shape[0] // 2
    halo_tiles = stereo_tiles(
        [halo[:half, :COLS], halo[half:, :COLS]], left_tab, right_tab
    )
    halo_clear = clear_pixels(halo[:, COLS : COLS + NH])
    begins = (0, half, half + 2 * BAND, 0)
    sides = (BAND + FAR, BAND, KR, 0)
    for layer in range(LAYERS):
        height = layer_height(layer)
        before = height + 2 * KR
        low, side = begins[layer], sides[layer]
        if layer == 0:
            columned = first
        else:
            columned = propagated(
                field[0, :before], field[1, :before], row_mats[layer - 1], col_mats[layer - 1], layer
            )
        band = slice(layer * BAND, (layer + 1) * BAND)
        pieces = [clear[band]]
        if side:
            pieces = [halo_clear[low : low + side], clear[band], halo_clear[low + side : low + 2 * side]]
        passing = jnp.concatenate(pieces, axis=0)
        for tile in range(TILES):
            span = slice(tile * height, (tile + 1) * height)
            lanes = slice(tile * LANES, (tile + 1) * LANES)
            row = (low // half * TILES + tile) * half + low % half
            for part in range(2):
                within = slice(part * LANES, (part + 1) * LANES)
                pieces = [stereo[part, band, lanes]]
                if side:
                    pieces = [
                        halo_tiles[row : row + side, within],
                        stereo[part, band, lanes],
                        halo_tiles[row + side : row + 2 * side, within],
                    ]
                added = jnp.concatenate(pieces, axis=0)
                value = passing[:, lanes] * columned[span, within] + added
                field[part, :height, lanes] = value.astype(jnp.bfloat16)
        for part in range(2):
            out[layer, part] = field[part, side : side + BAND]


def exchanged(value, axis, by, phase):
    count = lax.axis_size(axis)
    lower = [i for i in range(count - by) if (i // by) % 2 == phase]
    pairs = [(i, i + by) for i in lower] + [(i + by, i) for i in lower]
    paired = {source for source, _ in pairs}
    pairs += [(i, i) for i in range(count) if i not in paired]
    return lax.ppermute(value, axis, pairs)


def neighbours(sent):
    in_chip, cross, far_even, far_odd = sent
    cross = exchanged(cross, "rows", 1, 1)
    far_even = exchanged(far_even, "rows", 2, 0)
    far_odd = exchanged(far_odd, "rows", 2, 1)
    in_chip = exchanged(in_chip, "rows", 1, 0)
    return in_chip, cross, far_even, far_odd


def call(kernel, out_shape, in_specs, scratch=(), flops=0, moved=10**6, limit=VMEM_LIMIT):
    vmem = pl.BlockSpec(memory_space=pltpu.VMEM)
    many = isinstance(out_shape, (tuple, list))
    return pl.pallas_call(
        kernel,
        out_shape=out_shape,
        in_specs=in_specs,
        out_specs=(vmem,) * len(out_shape) if many else vmem,
        scratch_shapes=scratch,
        compiler_params=pltpu.CompilerParams(vmem_limit_bytes=limit),
        cost_estimate=pl.CostEstimate(flops=flops, bytes_accessed=moved, transcendentals=0),
    )


def body(incident, row_taps, col_taps, hogel_light, silhouette, fill_counts, hogel_index):
    vmem = pl.BlockSpec(memory_space=pltpu.VMEM)
    hbm = pl.BlockSpec(memory_space=pltpu.HBM)
    bf16, f32 = jnp.bfloat16, jnp.float32
    shaped = jax.ShapeDtypeStruct
    held = [
        pltpu.VMEM(hogel_index.shape, jnp.int32),
        pltpu.SMEM(fill_counts.shape, jnp.int32),
        pltpu.VMEM(silhouette.shape, jnp.int32),
        pltpu.VMEM(row_taps.shape, bf16),
        pltpu.VMEM(col_taps.shape, bf16),
        pltpu.VMEM(hogel_light.shape, f32),
    ]
    payload, mine = call(
        pack_kernel,
        (shaped((LAYERS, BAND, FULL_W), bf16), shaped(incident.shape[1:], bf16)),
        [hbm] * 7,
        held + [pltpu.SemaphoreType.DMA((7,)), pltpu.VMEM((BAND, LANES), f32)],
        flops=10**7,
        limit=PACK_LIMIT,
    )(hogel_light, silhouette, fill_counts, hogel_index, row_taps, col_taps, incident)
    mine = mine.reshape(2 * BAND, COLS)
    own = lax.all_to_all(payload, "depth", 0, 0, tiled=True)
    arrived = neighbours((mine,) * 4)
    near = shaped((NEAR, HALO_W), bf16)
    far = shaped((FAR, HALO_W), bf16)
    halos = neighbours(call(halo_kernel, (near, near, far, far), [vmem])(own))
    right_tab = jnp.asarray(right_table())
    made = call(
        prepare_kernel,
        [
            shaped((TILES * layer_height(0), 2 * LANES), f32),
            shaped((2, LANES, COLS), f32),
            shaped((LANES, COLS), f32),
            shaped((LAYERS - 1, 2 * LANES, 4 * LANES), bf16),
        ]
        + [shaped((2 * block_height(layer), 2 * LANES), bf16) for layer in range(1, LAYERS)],
        [vmem] * 8,
        flops=10**9,
        moved=3 * 10**6,
    )(own, mine, *arrived, jnp.asarray(left_table(LANES)), right_tab)
    halo_rows = NEAR + FAR
    result = call(
        chain_kernel,
        shaped((LAYERS, 2, BAND, COLS), bf16),
        [vmem] * (6 + len(made)),
        [pltpu.VMEM((2, layer_height(0), COLS), bf16)],
        flops=2 * 10**9,
        moved=3 * 10**6,
    )(*halos, jnp.asarray(left_table(halo_rows)), right_tab, *made)
    gathered = lax.all_to_all(result, "depth", 0, 0, tiled=True)
    return gathered[None, :COLORS]


def solution(mesh):
    placed = (
        P(None, None, "rows", None),
        P("depth", None, None, None),
        P("depth", None, None, None),
        P("depth", None, "rows", None),
        P("depth", "rows", None),
        P("depth", "rows"),
        P("depth", "rows", None),
    )
    return jax.shard_map(
        body,
        mesh=mesh,
        in_specs=placed,
        out_specs=P("depth", None, None, "rows", None),
        check_vma=False,
    )
```

```python
import math

import jax
import jax.numpy as jnp
import numpy as np
from jax import lax
from jax.experimental import pallas as pl
from jax.experimental.pallas import tpu as pltpu
from jax.sharding import PartitionSpec as P

HS = 16
KR = 16
KC = 63
COLORS = 3
LAYERS = 4
BAND = 32
COLS = 1024
NH = COLS // HS
LANES = 128
TILES = COLS // LANES
HALO_W = COLS + LANES
HALF = LANES // 2
FULL_W = COLS + 2 * LANES
NEAR = 2 * BAND + KR
FAR = KR
VMEM_LIMIT = 40 * 1024 * 1024
PACK_LIMIT = 63 * 1024 * 1024


def split_table(table):
    high = table.astype(jnp.bfloat16)
    low = (table - high.astype(np.float64)).astype(jnp.bfloat16)
    return high, low


def dft_pair():
    counter = np.arange(HS)
    angles = (counter[:, None] * counter[None, :] % HS) * (2.0 * math.pi / HS)
    return np.cos(angles) / math.sqrt(HS), np.sin(angles) / math.sqrt(HS)


def left_table(height):
    cos_tab, sin_tab = dft_pair()
    eye = np.eye(height // HS)
    full = np.concatenate([np.kron(eye, cos_tab), np.kron(eye, -sin_tab)], axis=0)
    return np.concatenate(split_table(full), axis=1)


def right_table():
    cos_tab, sin_tab = dft_pair()
    eye = np.eye(LANES // HS)
    cos_big, sin_big = np.kron(eye, cos_tab), np.kron(eye, sin_tab)
    full = np.concatenate(
        [
            np.concatenate([cos_big, -sin_big], axis=1),
            np.concatenate([sin_big, cos_big], axis=1),
        ],
        axis=0,
    )
    return full.astype(jnp.bfloat16)


def layer_height(layer):
    return BAND + 2 * KR * (LAYERS - 1 - layer)


def block_height(layer):
    height = layer_height(layer)
    return height // 2 if 2 * (height + 2 * KR) > 2 * LANES else height


def spread_matrix():
    tile = lax.broadcasted_iota(jnp.int32, (NH, COLS), 0)
    column = lax.broadcasted_iota(jnp.int32, (NH, COLS), 1)
    return jnp.where(column // HS == tile, 1.0, 0.0).astype(jnp.bfloat16)


def own_colour():
    return jnp.minimum(lax.axis_index("depth"), COLORS - 1)


def pack_kernel(light, edges, counts, listed, row_taps, col_taps, incident, out, mine, *scratch):
    held, sems, taps = scratch[:6], scratch[6], scratch[7]
    picked = pltpu.make_async_copy(incident.at[own_colour()], mine, sems.at[6])
    sources = (listed, counts, edges, row_taps, col_taps, light)
    copies = [
        pltpu.make_async_copy(source, target, sems.at[place])
        for place, (source, target) in enumerate(zip(sources, held))
    ]
    for copy in reversed(copies):
        copy.start()
    picked.start()
    listed, counts, edges, row_taps, col_taps, light = held
    spread = spread_matrix()
    slot = lax.broadcasted_iota(jnp.int32, (NH, NH), 0)
    place = lax.broadcasted_iota(jnp.int32, (NH, NH), 1)
    for copy in copies[:5]:
        copy.wait()
    rows = []
    for group in range(BAND // HS):
        listing = jnp.broadcast_to(listed[0, group : group + 1, :], (NH, NH))
        column = jnp.sum(jnp.where(slot == place, listing, 0), axis=1, keepdims=True)
        named = (column == place) & (slot < counts[0, group])
        live = jnp.max(jnp.where(named, 1.0, 0.0), axis=0, keepdims=True)
        rows.append(jnp.broadcast_to(live, (HS, NH)))
    live_rows = jnp.concatenate(rows, axis=0).astype(jnp.bfloat16)
    live_pix = jnp.dot(live_rows, spread, preferred_element_type=jnp.float32)
    edge_tile = jnp.concatenate(
        [edges[0].astype(jnp.float32), jnp.zeros((BAND, LANES - NH), jnp.float32)], axis=1
    ).astype(jnp.bfloat16)
    for colour in range(COLORS):
        out[colour, :, COLS:HALO_W] = edge_tile
        taps[...] = jnp.zeros_like(taps)
        taps[0:2, : 2 * KC + 1] = col_taps[0, colour].astype(jnp.float32)
        taps[2:4, : 2 * KR + 1] = row_taps[0, colour].astype(jnp.float32)
        out[colour, :, HALO_W:] = taps[...].astype(jnp.bfloat16)
    for spare in range(COLORS, LAYERS):
        out[spare] = jnp.zeros((BAND, FULL_W), jnp.bfloat16)
    copies[5].wait()
    for colour in range(COLORS):
        out[colour, :, :COLS] = (light[0, colour] * live_pix).astype(jnp.bfloat16)
    picked.wait()


def halo_kernel(own, in_chip, cross, far_even, far_odd):
    band = lax.axis_index("rows")
    core = band % 2
    odd = (band // 2) % 2
    last = BAND - KR
    for near, start in ((in_chip, (1 - core) * last), (cross, core * last)):
        near[0:BAND] = own[0, :, :HALO_W]
        near[BAND : 2 * BAND] = own[1, :, :HALO_W]
        near[2 * BAND : NEAR] = own[2, pl.ds(pl.multiple_of(start, KR), KR), :HALO_W]
    for far, start in ((far_even, (1 - odd) * last), (far_odd, odd * last)):
        far[...] = own[0, pl.ds(pl.multiple_of(start, KR), KR), :HALO_W]


def near_sides(in_chip, cross):
    even_core = lax.axis_index("rows") % 2 == 0
    in_chip, cross = in_chip[...], cross[...]
    return jnp.where(even_core, cross, in_chip), jnp.where(even_core, in_chip, cross)


def far_sides(far_even, far_odd):
    even_chip = (lax.axis_index("rows") // 2) % 2 == 0
    far_even, far_odd = far_even[...], far_odd[...]
    return jnp.where(even_chip, far_odd, far_even), jnp.where(even_chip, far_even, far_odd)


def tiles_below(value, height):
    return jnp.concatenate(
        [
            jnp.concatenate(
                [
                    value[:height, tile * LANES : (tile + 1) * LANES],
                    value[height:, tile * LANES : (tile + 1) * LANES],
                ],
                axis=1,
            )
            for tile in range(TILES)
        ],
        axis=0,
    )


def stereo_tiles(blocks, left_tab, right_tab):
    arranged = []
    for light in blocks:
        doubled = jnp.concatenate([light, light], axis=0)
        left = jnp.dot(left_tab[...], doubled, preferred_element_type=jnp.float32)
        arranged.append(tiles_below(left.astype(jnp.bfloat16), light.shape[0]))
    arranged = jnp.concatenate(arranged, axis=0) if len(arranged) > 1 else arranged[0]
    return jnp.dot(arranged, right_tab[...], preferred_element_type=jnp.float32)


def clear_pixels(edges):
    edge_pix = jnp.dot(edges, spread_matrix(), preferred_element_type=jnp.float32)
    within = (lax.broadcasted_iota(jnp.int32, (1, COLS), 1) % HS).astype(jnp.float32)
    return jnp.where(within < edge_pix, 1.0, 0.0)


def banded(line, count, shift):
    base = jnp.concatenate([line, jnp.zeros((1, LANES), jnp.float32)], axis=1)
    base = jnp.broadcast_to(base, (count, 2 * LANES))
    return pltpu.roll(base, shift, 1, stride=1, stride_axis=0)


def filters(taps, layer):
    row_re, row_im = taps[2:3], taps[3:4]
    height = block_height(layer)
    before = height + 2 * KR
    upper = banded(row_re, height, 0) - banded(row_im, height, before)
    lower = banded(row_im, height, 0) + banded(row_re, height, before)
    row_mat = jnp.concatenate([upper, lower], axis=0).astype(jnp.bfloat16)
    col_re = banded(taps[0:1], LANES, 1)
    col_im = banded(taps[1:2], LANES, 1)
    upper = jnp.concatenate([col_re, -col_im], axis=1)
    lower = jnp.concatenate([col_im, col_re], axis=1)
    col_mat = jnp.concatenate([upper, lower], axis=0).astype(jnp.bfloat16)
    return row_mat, col_mat


def propagated(u_re, u_im, row_mat, col_mat, layer):
    height = layer_height(layer)
    block = block_height(layer)
    reach = block + 2 * KR
    parts = []
    for start in range(0, height, block):
        stacked = jnp.concatenate(
            [u_re[start : start + reach], u_im[start : start + reach]], axis=0
        )
        parts.append(
            jnp.dot(row_mat[:, : 2 * reach], stacked, preferred_element_type=jnp.float32)
        )
    rowed = jnp.concatenate(
        [part[:block] for part in parts] + [part[block:] for part in parts], axis=0
    )
    rowed = jnp.concatenate([rowed, jnp.zeros((2 * height, LANES), jnp.float32)], axis=1)
    rowed = pltpu.roll(rowed, HALF, 1).astype(jnp.bfloat16)
    windows = jnp.concatenate(
        [
            jnp.concatenate(
                [
                    rowed[:height, tile * LANES : (tile + 2) * LANES],
                    rowed[height:, tile * LANES : (tile + 2) * LANES],
                ],
                axis=1,
            )
            for tile in range(TILES)
        ],
        axis=0,
    )
    return lax.dot_general(
        windows, col_mat, (((1,), (1,)), ((), ())), preferred_element_type=jnp.float32
    )


def prepare_kernel(
    own, incident, in_chip, cross, far_even, far_odd, left_tab, right_tab,
    first, stereo, clear, col_mats, *row_mats
):
    low_near, high_near = near_sides(in_chip, cross)
    low_far, high_far = far_sides(far_even, far_odd)
    extended = []
    for part in range(2):
        pieces = [low_far, low_near, incident[...], high_near, high_far]
        pieces = [piece[part * BAND : (part + 1) * BAND] for piece in pieces]
        extended.append(jnp.concatenate(pieces, axis=0))
    row_mat, col_mat = filters(own[0, 0:16, HALO_W:].astype(jnp.float32), 0)
    first[...] = propagated(extended[0], extended[1], row_mat, col_mat, 0)
    for layer in range(1, LAYERS):
        row_mat, col_mat = filters(own[layer, 0:16, HALO_W:].astype(jnp.float32), layer)
        row_mats[layer - 1][...] = row_mat
        col_mats[layer - 1] = col_mat
    packed = jnp.concatenate([own[layer, :, :HALO_W] for layer in range(LAYERS)], axis=0)
    clear[...] = clear_pixels(packed[:, COLS : COLS + NH])
    tiles = stereo_tiles([packed[:, :COLS]], left_tab, right_tab)
    for tile in range(TILES):
        for part in range(2):
            block = tiles[
                tile * LANES : (tile + 1) * LANES, part * LANES : (part + 1) * LANES
            ]
            stereo[part, :, tile * LANES : (tile + 1) * LANES] = block


def near_kernel(light_in_chip, light_cross, near_tab, right_tab, near_tiles, near_clear):
    low, high = near_sides(light_in_chip, light_cross)
    blocks = [
        jnp.concatenate([low[0:BAND], high[0:BAND], low[2 * BAND :]], axis=0),
        jnp.concatenate(
            [low[BAND : 2 * BAND], high[BAND : 2 * BAND], high[2 * BAND :]], axis=0
        ),
    ]
    near_tiles[...] = stereo_tiles([block[:, :COLS] for block in blocks], near_tab, right_tab)
    edges = jnp.concatenate([block[:, COLS : COLS + NH] for block in blocks], axis=0)
    near_clear[...] = clear_pixels(edges)


def chain_kernel(
    far_even, far_odd, left_tab, right_tab,
    near_tiles, near_clear, first, stereo, clear, col_mats, *rest
):
    row_mats, (out, field) = rest[: LAYERS - 1], rest[LAYERS - 1 :]
    far = jnp.concatenate(far_sides(far_even, far_odd), axis=0)
    far_tiles = stereo_tiles([far[:, :COLS]], left_tab, right_tab)
    far_clear = clear_pixels(far[:, COLS : COLS + NH])

    spots = (
        ((0, BAND), (BAND, BAND)),
        ((NEAR, BAND), (NEAR + BAND, BAND)),
        ((2 * BAND, KR), (NEAR + 2 * BAND, KR)),
        None,
    )
    for layer in range(LAYERS):
        height = layer_height(layer)
        before = height + 2 * KR
        side = (height - BAND) // 2
        if layer == 0:
            columned = first
        else:
            columned = propagated(
                field[0, :before], field[1, :before], row_mats[layer - 1], col_mats[layer - 1], layer
            )
        band = slice(layer * BAND, (layer + 1) * BAND)
        pieces = [clear[band]]
        if side:
            (low, count), (high, _) = spots[layer]
            pieces = [near_clear[low : low + count], clear[band], near_clear[high : high + count]]
        if layer == 0:
            pieces = [far_clear[:FAR]] + pieces + [far_clear[FAR:]]
        passing = jnp.concatenate(pieces, axis=0)
        for tile in range(TILES):
            span = slice(tile * height, (tile + 1) * height)
            lanes = slice(tile * LANES, (tile + 1) * LANES)
            for part in range(2):
                within = slice(part * LANES, (part + 1) * LANES)
                pieces = [stereo[part, band, lanes]]
                if side:
                    rows = [
                        (start // NEAR * TILES + tile) * NEAR + start % NEAR for start in (low, high)
                    ]
                    pieces = [
                        near_tiles[rows[0] : rows[0] + count, within],
                        stereo[part, band, lanes],
                        near_tiles[rows[1] : rows[1] + count, within],
                    ]
                if layer == 0:
                    row = tile * 2 * FAR
                    pieces = (
                        [far_tiles[row : row + FAR, within]]
                        + pieces
                        + [far_tiles[row + FAR : row + 2 * FAR, within]]
                    )
                added = jnp.concatenate(pieces, axis=0)
                value = passing[:, lanes] * columned[span, within] + added
                field[part, :height, lanes] = value.astype(jnp.bfloat16)
        for part in range(2):
            out[layer, part] = field[part, side : side + BAND]


def exchanged(value, axis, by, phase):
    count = lax.axis_size(axis)
    lower = [i for i in range(count - by) if (i // by) % 2 == phase]
    pairs = [(i, i + by) for i in lower] + [(i + by, i) for i in lower]
    return lax.ppermute(value, axis, pairs)


def neighbours(sent):
    in_chip, cross, far_even, far_odd = sent
    cross = exchanged(cross, "rows", 1, 1)
    far_even = exchanged(far_even, "rows", 2, 0)
    far_odd = exchanged(far_odd, "rows", 2, 1)
    in_chip = exchanged(in_chip, "rows", 1, 0)
    return in_chip, cross, far_even, far_odd


def call(kernel, out_shape, in_specs, scratch=(), flops=0, moved=10**6, limit=VMEM_LIMIT):
    vmem = pl.BlockSpec(memory_space=pltpu.VMEM)
    many = isinstance(out_shape, (tuple, list))
    return pl.pallas_call(
        kernel,
        out_shape=out_shape,
        in_specs=in_specs,
        out_specs=(vmem,) * len(out_shape) if many else vmem,
        scratch_shapes=scratch,
        compiler_params=pltpu.CompilerParams(vmem_limit_bytes=limit),
        cost_estimate=pl.CostEstimate(flops=flops, bytes_accessed=moved, transcendentals=0),
    )


def body(incident, row_taps, col_taps, hogel_light, silhouette, fill_counts, hogel_index):
    vmem = pl.BlockSpec(memory_space=pltpu.VMEM)
    hbm = pl.BlockSpec(memory_space=pltpu.HBM)
    bf16, f32 = jnp.bfloat16, jnp.float32
    shaped = jax.ShapeDtypeStruct
    held = [
        pltpu.VMEM(hogel_index.shape, jnp.int32),
        pltpu.SMEM(fill_counts.shape, jnp.int32),
        pltpu.VMEM(silhouette.shape, jnp.int32),
        pltpu.VMEM(row_taps.shape, bf16),
        pltpu.VMEM(col_taps.shape, bf16),
        pltpu.VMEM(hogel_light.shape, f32),
    ]
    payload, mine = call(
        pack_kernel,
        (shaped((LAYERS, BAND, FULL_W), bf16), shaped(incident.shape[1:], bf16)),
        [hbm] * 7,
        held + [pltpu.SemaphoreType.DMA((7,)), pltpu.VMEM((BAND, LANES), f32)],
        flops=10**7,
        limit=PACK_LIMIT,
    )(hogel_light, silhouette, fill_counts, hogel_index, row_taps, col_taps, incident)
    mine = mine.reshape(2 * BAND, COLS)
    own = lax.all_to_all(payload, "depth", 0, 0, tiled=True)
    arrived = neighbours((mine,) * 4)
    near = shaped((NEAR, HALO_W), bf16)
    far = shaped((FAR, HALO_W), bf16)
    halos = neighbours(call(halo_kernel, (near, near, far, far), [vmem])(own))
    right_tab = jnp.asarray(right_table())
    made = call(
        prepare_kernel,
        [
            shaped((TILES * layer_height(0), 2 * LANES), f32),
            shaped((2, LANES, COLS), f32),
            shaped((LANES, COLS), f32),
            shaped((LAYERS - 1, 2 * LANES, 4 * LANES), bf16),
        ]
        + [shaped((2 * block_height(layer), 2 * LANES), bf16) for layer in range(1, LAYERS)],
        [vmem] * 8,
        flops=10**9,
        moved=3 * 10**6,
    )(own, mine, *arrived, jnp.asarray(left_table(LANES)), right_tab)
    near_made = call(
        near_kernel,
        [shaped((2 * NEAR * TILES, 2 * LANES), f32), shaped((2 * NEAR, COLS), f32)],
        [vmem] * 4,
        flops=5 * 10**8,
        moved=2 * 10**6,
    )(*halos[:2], jnp.asarray(left_table(NEAR)), right_tab)
    result = call(
        chain_kernel,
        shaped((LAYERS, 2, BAND, COLS), bf16),
        [vmem] * (6 + len(made)),
        [pltpu.VMEM((2, layer_height(0), COLS), bf16)],
        flops=2 * 10**9,
        moved=3 * 10**6,
    )(*halos[2:], jnp.asarray(left_table(2 * FAR)), right_tab, *near_made, *made)
    gathered = lax.all_to_all(result, "depth", 0, 0, tiled=True)
    return gathered[None, :COLORS]


def solution(mesh):
    placed = (
        P(None, None, "rows", None),
        P("depth", None, None, None),
        P("depth", None, None, None),
        P("depth", None, "rows", None),
        P("depth", "rows", None),
        P("depth", "rows"),
        P("depth", "rows", None),
    )
    return jax.shard_map(
        body,
        mesh=mesh,
        in_specs=placed,
        out_specs=P("depth", None, None, "rows", None),
        check_vma=False,
    )
```

```python
import math

import jax
import jax.numpy as jnp
import numpy as np
from jax import lax
from jax.experimental import pallas as pl
from jax.experimental.pallas import tpu as pltpu
from jax.sharding import PartitionSpec as P

HS = 16
KR = 16
KC = 63
COLORS = 3
LAYERS = 4
BAND = 32
COLS = 1024
NH = COLS // HS
LANES = 128
TILES = COLS // LANES
HALO_W = COLS + LANES
HALF = LANES // 2
FULL_W = COLS + 2 * LANES
NEAR = 2 * BAND + KR
FAR = KR
VMEM_LIMIT = 40 * 1024 * 1024
PACK_LIMIT = 63 * 1024 * 1024


def split_table(table):
    high = table.astype(jnp.bfloat16)
    low = (table - high.astype(np.float64)).astype(jnp.bfloat16)
    return high, low


def dft_pair():
    counter = np.arange(HS)
    angles = (counter[:, None] * counter[None, :] % HS) * (2.0 * math.pi / HS)
    return np.cos(angles) / math.sqrt(HS), np.sin(angles) / math.sqrt(HS)


def left_table(height):
    cos_tab, sin_tab = dft_pair()
    eye = np.eye(height // HS)
    full = np.concatenate([np.kron(eye, cos_tab), np.kron(eye, -sin_tab)], axis=0)
    return np.concatenate(split_table(full), axis=1)


def right_table():
    cos_tab, sin_tab = dft_pair()
    eye = np.eye(LANES // HS)
    cos_big, sin_big = np.kron(eye, cos_tab), np.kron(eye, sin_tab)
    full = np.concatenate(
        [
            np.concatenate([cos_big, -sin_big], axis=1),
            np.concatenate([sin_big, cos_big], axis=1),
        ],
        axis=0,
    )
    return full.astype(jnp.bfloat16)


def layer_height(layer):
    return BAND + 2 * KR * (LAYERS - 1 - layer)


def block_height(layer):
    height = layer_height(layer)
    return height // 2 if 2 * (height + 2 * KR) > 2 * LANES else height


def spread_matrix():
    tile = lax.broadcasted_iota(jnp.int32, (NH, COLS), 0)
    column = lax.broadcasted_iota(jnp.int32, (NH, COLS), 1)
    return jnp.where(column // HS == tile, 1.0, 0.0).astype(jnp.bfloat16)


def own_colour():
    return jnp.minimum(lax.axis_index("depth"), COLORS - 1)


def pack_kernel(light, edges, counts, listed, row_taps, col_taps, incident, out, mine, *scratch):
    held, sems, taps = scratch[:6], scratch[6], scratch[7]
    picked = pltpu.make_async_copy(incident.at[own_colour()], mine, sems.at[6])
    sources = (listed, counts, edges, row_taps, col_taps, light)
    copies = [
        pltpu.make_async_copy(source, target, sems.at[place])
        for place, (source, target) in enumerate(zip(sources, held))
    ]
    for copy in reversed(copies):
        copy.start()
    picked.start()
    listed, counts, edges, row_taps, col_taps, light = held
    spread = spread_matrix()
    slot = lax.broadcasted_iota(jnp.int32, (NH, NH), 0)
    place = lax.broadcasted_iota(jnp.int32, (NH, NH), 1)
    for copy in copies[:5]:
        copy.wait()
    rows = []
    for group in range(BAND // HS):
        listing = jnp.broadcast_to(listed[0, group : group + 1, :], (NH, NH))
        column = jnp.sum(jnp.where(slot == place, listing, 0), axis=1, keepdims=True)
        named = (column == place) & (slot < counts[0, group])
        live = jnp.max(jnp.where(named, 1.0, 0.0), axis=0, keepdims=True)
        rows.append(jnp.broadcast_to(live, (HS, NH)))
    live_rows = jnp.concatenate(rows, axis=0).astype(jnp.bfloat16)
    live_pix = jnp.dot(live_rows, spread, preferred_element_type=jnp.float32)
    edge_tile = jnp.concatenate(
        [edges[0].astype(jnp.float32), jnp.zeros((BAND, LANES - NH), jnp.float32)], axis=1
    ).astype(jnp.bfloat16)
    for colour in range(COLORS):
        out[colour, :, COLS:HALO_W] = edge_tile
        taps[...] = jnp.zeros_like(taps)
        taps[0:2, : 2 * KC + 1] = col_taps[0, colour].astype(jnp.float32)
        taps[2:4, : 2 * KR + 1] = row_taps[0, colour].astype(jnp.float32)
        out[colour, :, HALO_W:] = taps[...].astype(jnp.bfloat16)
    for spare in range(COLORS, LAYERS):
        out[spare] = jnp.zeros((BAND, FULL_W), jnp.bfloat16)
    copies[5].wait()
    for colour in range(COLORS):
        out[colour, :, :COLS] = (light[0, colour] * live_pix).astype(jnp.bfloat16)
    picked.wait()


def halo_kernel(own, in_chip, cross, far_even, far_odd):
    band = lax.axis_index("rows")
    core = band % 2
    odd = (band // 2) % 2
    last = BAND - KR
    for near, start in ((in_chip, (1 - core) * last), (cross, core * last)):
        near[0:BAND] = own[0, :, :HALO_W]
        near[BAND : 2 * BAND] = own[1, :, :HALO_W]
        near[2 * BAND : NEAR] = own[2, pl.ds(pl.multiple_of(start, KR), KR), :HALO_W]
    for far, start in ((far_even, (1 - odd) * last), (far_odd, odd * last)):
        far[...] = own[0, pl.ds(pl.multiple_of(start, KR), KR), :HALO_W]


def near_sides(in_chip, cross):
    even_core = lax.axis_index("rows") % 2 == 0
    in_chip, cross = in_chip[...], cross[...]
    return jnp.where(even_core, cross, in_chip), jnp.where(even_core, in_chip, cross)


def far_sides(far_even, far_odd):
    even_chip = (lax.axis_index("rows") // 2) % 2 == 0
    far_even, far_odd = far_even[...], far_odd[...]
    return jnp.where(even_chip, far_odd, far_even), jnp.where(even_chip, far_even, far_odd)


def tiles_below(value, height):
    return jnp.concatenate(
        [
            jnp.concatenate(
                [
                    value[:height, tile * LANES : (tile + 1) * LANES],
                    value[height:, tile * LANES : (tile + 1) * LANES],
                ],
                axis=1,
            )
            for tile in range(TILES)
        ],
        axis=0,
    )


def stereo_tiles(blocks, left_tab, right_tab):
    arranged = []
    for light in blocks:
        doubled = jnp.concatenate([light, light], axis=0)
        left = jnp.dot(left_tab[...], doubled, preferred_element_type=jnp.float32)
        arranged.append(tiles_below(left.astype(jnp.bfloat16), light.shape[0]))
    arranged = jnp.concatenate(arranged, axis=0) if len(arranged) > 1 else arranged[0]
    return jnp.dot(arranged, right_tab[...], preferred_element_type=jnp.float32)


def clear_pixels(edges):
    edge_pix = jnp.dot(edges, spread_matrix(), preferred_element_type=jnp.float32)
    within = (lax.broadcasted_iota(jnp.int32, (1, COLS), 1) % HS).astype(jnp.float32)
    return jnp.where(within < edge_pix, 1.0, 0.0)


def banded(line, count, shift):
    base = jnp.concatenate([line, jnp.zeros((1, LANES), jnp.float32)], axis=1)
    base = jnp.broadcast_to(base, (count, 2 * LANES))
    return pltpu.roll(base, shift, 1, stride=1, stride_axis=0)


def filters(taps, layer):
    row_re, row_im = taps[2:3], taps[3:4]
    height = block_height(layer)
    before = height + 2 * KR
    upper = banded(row_re, height, 0) - banded(row_im, height, before)
    lower = banded(row_im, height, 0) + banded(row_re, height, before)
    row_mat = jnp.concatenate([upper, lower], axis=0).astype(jnp.bfloat16)
    col_re = banded(taps[0:1], LANES, 1)
    col_im = banded(taps[1:2], LANES, 1)
    upper = jnp.concatenate([col_re, -col_im], axis=1)
    lower = jnp.concatenate([col_im, col_re], axis=1)
    col_mat = jnp.concatenate([upper, lower], axis=0).astype(jnp.bfloat16)
    return row_mat, col_mat


def propagated(u_re, u_im, row_mat, col_mat, layer):
    height = layer_height(layer)
    block = block_height(layer)
    reach = block + 2 * KR
    parts = []
    for start in range(0, height, block):
        stacked = jnp.concatenate(
            [u_re[start : start + reach], u_im[start : start + reach]], axis=0
        )
        parts.append(
            jnp.dot(row_mat[:, : 2 * reach], stacked, preferred_element_type=jnp.float32)
        )
    rowed = jnp.concatenate(
        [part[:block] for part in parts] + [part[block:] for part in parts], axis=0
    )
    rowed = jnp.concatenate([rowed, jnp.zeros((2 * height, LANES), jnp.float32)], axis=1)
    rowed = pltpu.roll(rowed, HALF, 1).astype(jnp.bfloat16)
    windows = jnp.concatenate(
        [
            jnp.concatenate(
                [
                    rowed[:height, tile * LANES : (tile + 2) * LANES],
                    rowed[height:, tile * LANES : (tile + 2) * LANES],
                ],
                axis=1,
            )
            for tile in range(TILES)
        ],
        axis=0,
    )
    return lax.dot_general(
        windows, col_mat, (((1,), (1,)), ((), ())), preferred_element_type=jnp.float32
    )


def prepare_kernel(
    own, incident, in_chip, cross, far_even, far_odd, left_tab, right_tab,
    first, stereo, clear, col_mats, *row_mats
):
    low_near, high_near = near_sides(in_chip, cross)
    low_far, high_far = far_sides(far_even, far_odd)
    colour = own_colour()
    extended = []
    for part in range(2):
        low_rows, near_rows, high_rows, top_rows = (
            side[part * BAND : (part + 1) * BAND]
            for side in (low_far, low_near, high_near, high_far)
        )
        pieces = [low_rows, near_rows, incident[colour, part], high_rows, top_rows]
        extended.append(jnp.concatenate(pieces, axis=0))
    row_mat, col_mat = filters(own[0, 0:16, HALO_W:].astype(jnp.float32), 0)
    first[...] = propagated(extended[0], extended[1], row_mat, col_mat, 0)
    for layer in range(1, LAYERS):
        row_mat, col_mat = filters(own[layer, 0:16, HALO_W:].astype(jnp.float32), layer)
        row_mats[layer - 1][...] = row_mat
        col_mats[layer - 1] = col_mat
    packed = jnp.concatenate([own[layer, :, :HALO_W] for layer in range(LAYERS)], axis=0)
    clear[...] = clear_pixels(packed[:, COLS : COLS + NH])
    tiles = stereo_tiles([packed[:, :COLS]], left_tab, right_tab)
    for tile in range(TILES):
        for part in range(2):
            block = tiles[
                tile * LANES : (tile + 1) * LANES, part * LANES : (part + 1) * LANES
            ]
            stereo[part, :, tile * LANES : (tile + 1) * LANES] = block


def near_kernel(light_in_chip, light_cross, near_tab, right_tab, near_tiles, near_clear):
    low, high = near_sides(light_in_chip, light_cross)
    blocks = [
        jnp.concatenate([low[0:BAND], high[0:BAND], low[2 * BAND :]], axis=0),
        jnp.concatenate(
            [low[BAND : 2 * BAND], high[BAND : 2 * BAND], high[2 * BAND :]], axis=0
        ),
    ]
    near_tiles[...] = stereo_tiles([block[:, :COLS] for block in blocks], near_tab, right_tab)
    edges = jnp.concatenate([block[:, COLS : COLS + NH] for block in blocks], axis=0)
    near_clear[...] = clear_pixels(edges)


def chain_kernel(
    far_even, far_odd, left_tab, right_tab,
    near_tiles, near_clear, first, stereo, clear, col_mats, *rest
):
    row_mats, (out, field) = rest[: LAYERS - 1], rest[LAYERS - 1 :]
    far = jnp.concatenate(far_sides(far_even, far_odd), axis=0)
    far_tiles = stereo_tiles([far[:, :COLS]], left_tab, right_tab)
    far_clear = clear_pixels(far[:, COLS : COLS + NH])

    spots = (
        ((0, BAND), (BAND, BAND)),
        ((NEAR, BAND), (NEAR + BAND, BAND)),
        ((2 * BAND, KR), (NEAR + 2 * BAND, KR)),
        None,
    )
    for layer in range(LAYERS):
        height = layer_height(layer)
        before = height + 2 * KR
        side = (height - BAND) // 2
        if layer == 0:
            columned = first
        else:
            columned = propagated(
                field[0, :before], field[1, :before], row_mats[layer - 1], col_mats[layer - 1], layer
            )
        band = slice(layer * BAND, (layer + 1) * BAND)
        pieces = [clear[band]]
        if side:
            (low, count), (high, _) = spots[layer]
            pieces = [near_clear[low : low + count], clear[band], near_clear[high : high + count]]
        if layer == 0:
            pieces = [far_clear[:FAR]] + pieces + [far_clear[FAR:]]
        passing = jnp.concatenate(pieces, axis=0)
        for tile in range(TILES):
            span = slice(tile * height, (tile + 1) * height)
            lanes = slice(tile * LANES, (tile + 1) * LANES)
            for part in range(2):
                within = slice(part * LANES, (part + 1) * LANES)
                pieces = [stereo[part, band, lanes]]
                if side:
                    rows = [
                        (start // NEAR * TILES + tile) * NEAR + start % NEAR for start in (low, high)
                    ]
                    pieces = [
                        near_tiles[rows[0] : rows[0] + count, within],
                        stereo[part, band, lanes],
                        near_tiles[rows[1] : rows[1] + count, within],
                    ]
                if layer == 0:
                    row = tile * 2 * FAR
                    pieces = (
                        [far_tiles[row : row + FAR, within]]
                        + pieces
                        + [far_tiles[row + FAR : row + 2 * FAR, within]]
                    )
                added = jnp.concatenate(pieces, axis=0)
                value = passing[:, lanes] * columned[span, within] + added
                field[part, :height, lanes] = value.astype(jnp.bfloat16)
        for part in range(2):
            out[layer, part] = field[part, side : side + BAND]


def exchanged(value, axis, by, phase):
    count = lax.axis_size(axis)
    lower = [i for i in range(count - by) if (i // by) % 2 == phase]
    pairs = [(i, i + by) for i in lower] + [(i + by, i) for i in lower]
    return lax.ppermute(value, axis, pairs)


def neighbours(sent):
    in_chip, cross, far_even, far_odd = sent
    cross = exchanged(cross, "rows", 1, 1)
    far_even = exchanged(far_even, "rows", 2, 0)
    far_odd = exchanged(far_odd, "rows", 2, 1)
    in_chip = exchanged(in_chip, "rows", 1, 0)
    return in_chip, cross, far_even, far_odd


def call(kernel, out_shape, in_specs, scratch=(), flops=0, moved=10**6, limit=VMEM_LIMIT):
    vmem = pl.BlockSpec(memory_space=pltpu.VMEM)
    many = isinstance(out_shape, (tuple, list))
    return pl.pallas_call(
        kernel,
        out_shape=out_shape,
        in_specs=in_specs,
        out_specs=(vmem,) * len(out_shape) if many else vmem,
        scratch_shapes=scratch,
        compiler_params=pltpu.CompilerParams(vmem_limit_bytes=limit),
        cost_estimate=pl.CostEstimate(flops=flops, bytes_accessed=moved, transcendentals=0),
    )


def body(incident, row_taps, col_taps, hogel_light, silhouette, fill_counts, hogel_index):
    vmem = pl.BlockSpec(memory_space=pltpu.VMEM)
    hbm = pl.BlockSpec(memory_space=pltpu.HBM)
    bf16, f32 = jnp.bfloat16, jnp.float32
    shaped = jax.ShapeDtypeStruct
    held = [
        pltpu.VMEM(hogel_index.shape, jnp.int32),
        pltpu.SMEM(fill_counts.shape, jnp.int32),
        pltpu.VMEM(silhouette.shape, jnp.int32),
        pltpu.VMEM(row_taps.shape, bf16),
        pltpu.VMEM(col_taps.shape, bf16),
        pltpu.VMEM(hogel_light.shape, f32),
    ]
    payload, mine = call(
        pack_kernel,
        (shaped((LAYERS, BAND, FULL_W), bf16), shaped(incident.shape[1:], bf16)),
        [hbm] * 7,
        held + [pltpu.SemaphoreType.DMA((7,)), pltpu.VMEM((BAND, LANES), f32)],
        flops=10**7,
        limit=PACK_LIMIT,
    )(hogel_light, silhouette, fill_counts, hogel_index, row_taps, col_taps, incident)
    mine = mine.reshape(2 * BAND, COLS)
    own = lax.all_to_all(payload, "depth", 0, 0, tiled=True)
    arrived = neighbours((mine,) * 4)
    near = shaped((NEAR, HALO_W), bf16)
    far = shaped((FAR, HALO_W), bf16)
    halos = neighbours(call(halo_kernel, (near, near, far, far), [vmem])(own))
    right_tab = jnp.asarray(right_table())
    made = call(
        prepare_kernel,
        [
            shaped((TILES * layer_height(0), 2 * LANES), f32),
            shaped((2, LANES, COLS), f32),
            shaped((LANES, COLS), f32),
            shaped((LAYERS - 1, 2 * LANES, 4 * LANES), bf16),
        ]
        + [shaped((2 * block_height(layer), 2 * LANES), bf16) for layer in range(1, LAYERS)],
        [vmem] * 8,
        flops=10**9,
        moved=3 * 10**6,
    )(own, incident, *arrived, jnp.asarray(left_table(LANES)), right_tab)
    near_made = call(
        near_kernel,
        [shaped((2 * NEAR * TILES, 2 * LANES), f32), shaped((2 * NEAR, COLS), f32)],
        [vmem] * 4,
        flops=5 * 10**8,
        moved=2 * 10**6,
    )(*halos[:2], jnp.asarray(left_table(NEAR)), right_tab)
    result = call(
        chain_kernel,
        shaped((LAYERS, 2, BAND, COLS), bf16),
        [vmem] * (6 + len(made)),
        [pltpu.VMEM((2, layer_height(0), COLS), bf16)],
        flops=2 * 10**9,
        moved=3 * 10**6,
    )(*halos[2:], jnp.asarray(left_table(2 * FAR)), right_tab, *near_made, *made)
    gathered = lax.all_to_all(result, "depth", 0, 0, tiled=True)
    return gathered[None, :COLORS]


def solution(mesh):
    placed = (
        P(None, None, "rows", None),
        P("depth", None, None, None),
        P("depth", None, None, None),
        P("depth", None, "rows", None),
        P("depth", "rows", None),
        P("depth", "rows"),
        P("depth", "rows", None),
    )
    return jax.shard_map(
        body,
        mesh=mesh,
        in_specs=placed,
        out_specs=P("depth", None, None, "rows", None),
        check_vma=False,
    )
```

```python
import math

import jax
import jax.numpy as jnp
import numpy as np
from jax import lax
from jax.experimental import pallas as pl
from jax.experimental.pallas import tpu as pltpu
from jax.sharding import PartitionSpec as P

HS = 16
KR = 16
KC = 63
COLORS = 3
LAYERS = 4
BAND = 32
COLS = 1024
NH = COLS // HS
LANES = 128
TILES = COLS // LANES
HALO_W = COLS + LANES
HALF = LANES // 2
NEAR = 2 * BAND + KR
FAR = KR
VMEM_LIMIT = 48 * 1024 * 1024
PACK_LIMIT = 63 * 1024 * 1024


def split_table(table):
    high = table.astype(jnp.bfloat16)
    low = (table - high.astype(np.float64)).astype(jnp.bfloat16)
    return high, low


def dft_pair():
    counter = np.arange(HS)
    angles = (counter[:, None] * counter[None, :] % HS) * (2.0 * math.pi / HS)
    return np.cos(angles) / math.sqrt(HS), np.sin(angles) / math.sqrt(HS)


def left_table(height):
    cos_tab, sin_tab = dft_pair()
    eye = np.eye(height // HS)
    full = np.concatenate([np.kron(eye, cos_tab), np.kron(eye, -sin_tab)], axis=0)
    return np.concatenate(split_table(full), axis=1)


def right_table():
    cos_tab, sin_tab = dft_pair()
    eye = np.eye(LANES // HS)
    cos_big, sin_big = np.kron(eye, cos_tab), np.kron(eye, sin_tab)
    full = np.concatenate(
        [
            np.concatenate([cos_big, -sin_big], axis=1),
            np.concatenate([sin_big, cos_big], axis=1),
        ],
        axis=0,
    )
    return full.astype(jnp.bfloat16)


def layer_height(layer):
    return BAND + 2 * KR * (LAYERS - 1 - layer)


def block_height(layer):
    height = layer_height(layer)
    return height // 2 if 2 * (height + 2 * KR) > 2 * LANES else height


def spread_matrix():
    tile = lax.broadcasted_iota(jnp.int32, (NH, COLS), 0)
    column = lax.broadcasted_iota(jnp.int32, (NH, COLS), 1)
    return jnp.where(column // HS == tile, 1.0, 0.0).astype(jnp.bfloat16)


def own_colour():
    return jnp.minimum(lax.axis_index("depth"), COLORS - 1)


def pack_kernel(light, edges, counts, listed, row_taps, col_taps, incident, out, mine, *scratch):
    held, sems, taps = scratch[:6], scratch[6], scratch[7]
    picked = pltpu.make_async_copy(incident.at[own_colour()], mine, sems.at[6])
    sources = (listed, counts, edges, row_taps, col_taps, light)
    copies = [
        pltpu.make_async_copy(source, target, sems.at[place])
        for place, (source, target) in enumerate(zip(sources, held))
    ]
    for copy in reversed(copies):
        copy.start()
    picked.start()
    listed, counts, edges, row_taps, col_taps, light = held
    spread = spread_matrix()
    slot = lax.broadcasted_iota(jnp.int32, (NH, NH), 0)
    place = lax.broadcasted_iota(jnp.int32, (NH, NH), 1)
    for copy in copies[:5]:
        copy.wait()
    rows = []
    for group in range(BAND // HS):
        listing = jnp.broadcast_to(listed[0, group : group + 1, :], (NH, NH))
        column = jnp.sum(jnp.where(slot == place, listing, 0), axis=1, keepdims=True)
        named = (column == place) & (slot < counts[0, group])
        live = jnp.max(jnp.where(named, 1.0, 0.0), axis=0, keepdims=True)
        rows.append(jnp.broadcast_to(live, (HS, NH)))
    live_rows = jnp.concatenate(rows, axis=0).astype(jnp.bfloat16)
    live_pix = jnp.dot(live_rows, spread, preferred_element_type=jnp.float32)
    edge_tile = jnp.concatenate(
        [edges[0].astype(jnp.float32), jnp.zeros((BAND, LANES - NH), jnp.float32)], axis=1
    )
    left_half = lax.broadcasted_iota(jnp.int32, (BAND, LANES), 1) < HALF
    for colour in range(COLORS):
        taps[...] = jnp.zeros_like(taps)
        taps[2:4, : 2 * KC + 1] = col_taps[0, colour].astype(jnp.float32)
        taps[4:6, : 2 * KR + 1] = row_taps[0, colour].astype(jnp.float32)
        turned = pltpu.roll(taps[0:8], HALF, 1)
        taps[0:2] = turned[2:4]
        taps[4:6] = turned[4:6]
        tile = jnp.where(left_half, edge_tile, taps[...])
        out[colour, :, COLS:] = tile.astype(jnp.bfloat16)
    for spare in range(COLORS, LAYERS):
        out[spare] = jnp.zeros((BAND, HALO_W), jnp.bfloat16)
    copies[5].wait()
    for colour in range(COLORS):
        out[colour, :, :COLS] = (light[0, colour] * live_pix).astype(jnp.bfloat16)
    picked.wait()


def halo_kernel(own, in_chip, cross, far_even, far_odd):
    band = lax.axis_index("rows")
    core = band % 2
    odd = (band // 2) % 2
    last = BAND - KR
    for near, start in ((in_chip, (1 - core) * last), (cross, core * last)):
        near[0:BAND] = own[0, :, :HALO_W]
        near[BAND : 2 * BAND] = own[1, :, :HALO_W]
        near[2 * BAND : NEAR] = own[2, pl.ds(pl.multiple_of(start, KR), KR), :HALO_W]
    for far, start in ((far_even, (1 - odd) * last), (far_odd, odd * last)):
        far[...] = own[0, pl.ds(pl.multiple_of(start, KR), KR), :HALO_W]


def ordered(in_chip, cross, far_even, far_odd):
    band = lax.axis_index("rows")
    even_core = band % 2 == 0
    even_chip = (band // 2) % 2 == 0
    in_chip, cross = in_chip[...], cross[...]
    far_even, far_odd = far_even[...], far_odd[...]
    return (
        jnp.where(even_core, cross, in_chip),
        jnp.where(even_core, in_chip, cross),
        jnp.where(even_chip, far_odd, far_even),
        jnp.where(even_chip, far_even, far_odd),
    )


def tiles_below(value, height):
    return jnp.concatenate(
        [
            jnp.concatenate(
                [
                    value[:height, tile * LANES : (tile + 1) * LANES],
                    value[height:, tile * LANES : (tile + 1) * LANES],
                ],
                axis=1,
            )
            for tile in range(TILES)
        ],
        axis=0,
    )


def stereo_tiles(blocks, left_tab, right_tab):
    arranged = []
    for light in blocks:
        doubled = jnp.concatenate([light, light], axis=0)
        left = jnp.dot(left_tab[...], doubled, preferred_element_type=jnp.float32)
        arranged.append(tiles_below(left.astype(jnp.bfloat16), light.shape[0]))
    arranged = jnp.concatenate(arranged, axis=0) if len(arranged) > 1 else arranged[0]
    return jnp.dot(arranged, right_tab[...], preferred_element_type=jnp.float32)


def clear_pixels(edges):
    edge_pix = jnp.dot(edges, spread_matrix(), preferred_element_type=jnp.float32)
    within = (lax.broadcasted_iota(jnp.int32, (1, COLS), 1) % HS).astype(jnp.float32)
    return jnp.where(within < edge_pix, 1.0, 0.0)


def banded(line, count, shift):
    base = jnp.concatenate([line, jnp.zeros((1, LANES), jnp.float32)], axis=1)
    base = jnp.broadcast_to(base, (count, 2 * LANES))
    return pltpu.roll(base, shift, 1, stride=1, stride_axis=0)


def filters(tile, layer):
    turned = pltpu.roll(tile[0:8], HALF, 1)
    left_half = lax.broadcasted_iota(jnp.int32, (2, LANES), 1) < HALF
    col_taps = jnp.where(left_half, turned[0:2], tile[2:4])
    row_taps = jnp.where(left_half, turned[4:6], 0.0)
    row_re, row_im = row_taps[0:1], row_taps[1:2]
    height = block_height(layer)
    before = height + 2 * KR
    upper = banded(row_re, height, 0) - banded(row_im, height, before)
    lower = banded(row_im, height, 0) + banded(row_re, height, before)
    row_mat = jnp.concatenate([upper, lower], axis=0).astype(jnp.bfloat16)
    col_re = banded(col_taps[0:1], LANES, 1)
    col_im = banded(col_taps[1:2], LANES, 1)
    upper = jnp.concatenate([col_re, -col_im], axis=1)
    lower = jnp.concatenate([col_im, col_re], axis=1)
    col_mat = jnp.concatenate([upper, lower], axis=0).astype(jnp.bfloat16)
    return row_mat, col_mat


def propagated(u_re, u_im, row_mat, col_mat, layer):
    height = layer_height(layer)
    block = block_height(layer)
    reach = block + 2 * KR
    parts = []
    for start in range(0, height, block):
        stacked = jnp.concatenate(
            [u_re[start : start + reach], u_im[start : start + reach]], axis=0
        )
        parts.append(
            jnp.dot(row_mat[:, : 2 * reach], stacked, preferred_element_type=jnp.float32)
        )
    rowed = jnp.concatenate(
        [part[:block] for part in parts] + [part[block:] for part in parts], axis=0
    )
    rowed = jnp.concatenate([rowed, jnp.zeros((2 * height, LANES), jnp.float32)], axis=1)
    rowed = pltpu.roll(rowed, HALF, 1).astype(jnp.bfloat16)
    windows = jnp.concatenate(
        [
            jnp.concatenate(
                [
                    rowed[:height, tile * LANES : (tile + 2) * LANES],
                    rowed[height:, tile * LANES : (tile + 2) * LANES],
                ],
                axis=1,
            )
            for tile in range(TILES)
        ],
        axis=0,
    )
    return lax.dot_general(
        windows, col_mat, (((1,), (1,)), ((), ())), preferred_element_type=jnp.float32
    )


def prepare_kernel(
    own, incident, in_chip, cross, far_even, far_odd, left_tab, right_tab,
    first, stereo, clear, col_mats, *row_mats
):
    low_near, high_near, low_far, high_far = ordered(in_chip, cross, far_even, far_odd)
    extended = []
    for part in range(2):
        pieces = [low_far, low_near, incident[...], high_near, high_far]
        pieces = [piece[part * BAND : (part + 1) * BAND] for piece in pieces]
        extended.append(jnp.concatenate(pieces, axis=0))
    row_mat, col_mat = filters(own[0, 0:16, COLS:].astype(jnp.float32), 0)
    first[...] = propagated(extended[0], extended[1], row_mat, col_mat, 0)
    for layer in range(1, LAYERS):
        row_mat, col_mat = filters(own[layer, 0:16, COLS:].astype(jnp.float32), layer)
        row_mats[layer - 1][...] = row_mat
        col_mats[layer - 1] = col_mat
    packed = jnp.concatenate([own[layer, :, :HALO_W] for layer in range(LAYERS)], axis=0)
    clear[...] = clear_pixels(packed[:, COLS : COLS + NH])
    tiles = stereo_tiles([packed[:, :COLS]], left_tab, right_tab)
    for tile in range(TILES):
        for part in range(2):
            block = tiles[
                tile * LANES : (tile + 1) * LANES, part * LANES : (part + 1) * LANES
            ]
            stereo[part, :, tile * LANES : (tile + 1) * LANES] = block


def chain_kernel(
    in_chip, cross, far_even, far_odd, left_tab, right_tab, first, stereo, clear, col_mats, *rest
):
    row_mats, (out, field) = rest[: LAYERS - 1], rest[LAYERS - 1 :]
    low_near, high_near, low_far, high_far = ordered(in_chip, cross, far_even, far_odd)
    pieces = [
        low_far,
        low_near[0:BAND],
        high_near[0:BAND],
        high_far,
        low_near[BAND : 2 * BAND],
        high_near[BAND : 2 * BAND],
        low_near[2 * BAND : NEAR],
        high_near[2 * BAND : NEAR],
    ]
    halo = jnp.concatenate(pieces, axis=0)
    half = halo.shape[0] // 2
    halo_tiles = stereo_tiles(
        [halo[:half, :COLS], halo[half:, :COLS]], left_tab, right_tab
    )
    halo_clear = clear_pixels(halo[:, COLS : COLS + NH])
    begins = (0, half, half + 2 * BAND, 0)
    sides = (BAND + FAR, BAND, KR, 0)
    for layer in range(LAYERS):
        height = layer_height(layer)
        before = height + 2 * KR
        low, side = begins[layer], sides[layer]
        if layer == 0:
            columned = first
        else:
            columned = propagated(
                field[0, :before], field[1, :before], row_mats[layer - 1], col_mats[layer - 1], layer
            )
        band = slice(layer * BAND, (layer + 1) * BAND)
        pieces = [clear[band]]
        if side:
            pieces = [halo_clear[low : low + side], clear[band], halo_clear[low + side : low + 2 * side]]
        passing = jnp.concatenate(pieces, axis=0)
        for tile in range(TILES):
            span = slice(tile * height, (tile + 1) * height)
            lanes = slice(tile * LANES, (tile + 1) * LANES)
            row = (low // half * TILES + tile) * half + low % half
            for part in range(2):
                within = slice(part * LANES, (part + 1) * LANES)
                pieces = [stereo[part, band, lanes]]
                if side:
                    pieces = [
                        halo_tiles[row : row + side, within],
                        stereo[part, band, lanes],
                        halo_tiles[row + side : row + 2 * side, within],
                    ]
                added = jnp.concatenate(pieces, axis=0)
                value = passing[:, lanes] * columned[span, within] + added
                field[part, :height, lanes] = value.astype(jnp.bfloat16)
        for part in range(2):
            out[layer, part] = field[part, side : side + BAND]


def exchanged(value, axis, by, phase):
    count = lax.axis_size(axis)
    lower = [i for i in range(count - by) if (i // by) % 2 == phase]
    pairs = [(i, i + by) for i in lower] + [(i + by, i) for i in lower]
    return lax.ppermute(value, axis, pairs)


def neighbours(sent):
    in_chip, cross, far_even, far_odd = sent
    cross = exchanged(cross, "rows", 1, 1)
    far_even = exchanged(far_even, "rows", 2, 0)
    far_odd = exchanged(far_odd, "rows", 2, 1)
    in_chip = exchanged(in_chip, "rows", 1, 0)
    return in_chip, cross, far_even, far_odd


def call(kernel, out_shape, in_specs, scratch=(), flops=0, moved=10**6, limit=VMEM_LIMIT):
    vmem = pl.BlockSpec(memory_space=pltpu.VMEM)
    many = isinstance(out_shape, (tuple, list))
    return pl.pallas_call(
        kernel,
        out_shape=out_shape,
        in_specs=in_specs,
        out_specs=(vmem,) * len(out_shape) if many else vmem,
        scratch_shapes=scratch,
        compiler_params=pltpu.CompilerParams(vmem_limit_bytes=limit),
        cost_estimate=pl.CostEstimate(flops=flops, bytes_accessed=moved, transcendentals=0),
    )


def body(incident, row_taps, col_taps, hogel_light, silhouette, fill_counts, hogel_index):
    vmem = pl.BlockSpec(memory_space=pltpu.VMEM)
    hbm = pl.BlockSpec(memory_space=pltpu.HBM)
    bf16, f32 = jnp.bfloat16, jnp.float32
    shaped = jax.ShapeDtypeStruct
    held = [
        pltpu.VMEM(hogel_index.shape, jnp.int32),
        pltpu.SMEM(fill_counts.shape, jnp.int32),
        pltpu.VMEM(silhouette.shape, jnp.int32),
        pltpu.VMEM(row_taps.shape, bf16),
        pltpu.VMEM(col_taps.shape, bf16),
        pltpu.VMEM(hogel_light.shape, f32),
    ]
    payload, mine = call(
        pack_kernel,
        (shaped((LAYERS, BAND, HALO_W), bf16), shaped(incident.shape[1:], bf16)),
        [hbm] * 7,
        held + [pltpu.SemaphoreType.DMA((7,)), pltpu.VMEM((BAND, LANES), f32)],
        flops=10**7,
        limit=PACK_LIMIT,
    )(hogel_light, silhouette, fill_counts, hogel_index, row_taps, col_taps, incident)
    mine = mine.reshape(2 * BAND, COLS)
    own = lax.all_to_all(payload, "depth", 0, 0, tiled=True)
    arrived = neighbours((mine,) * 4)
    near = shaped((NEAR, HALO_W), bf16)
    far = shaped((FAR, HALO_W), bf16)
    halos = neighbours(call(halo_kernel, (near, near, far, far), [vmem])(own))
    right_tab = jnp.asarray(right_table())
    made = call(
        prepare_kernel,
        [
            shaped((TILES * layer_height(0), 2 * LANES), f32),
            shaped((2, LANES, COLS), f32),
            shaped((LANES, COLS), f32),
            shaped((LAYERS - 1, 2 * LANES, 4 * LANES), bf16),
        ]
        + [shaped((2 * block_height(layer), 2 * LANES), bf16) for layer in range(1, LAYERS)],
        [vmem] * 8,
        flops=10**9,
        moved=3 * 10**6,
    )(own, mine, *arrived, jnp.asarray(left_table(LANES)), right_tab)
    halo_rows = NEAR + FAR
    result = call(
        chain_kernel,
        shaped((LAYERS, 2, BAND, COLS), bf16),
        [vmem] * (6 + len(made)),
        [pltpu.VMEM((2, layer_height(0), COLS), bf16)],
        flops=2 * 10**9,
        moved=3 * 10**6,
    )(*halos, jnp.asarray(left_table(halo_rows)), right_tab, *made)
    gathered = lax.all_to_all(result, "depth", 0, 0, tiled=True)
    return gathered[None, :COLORS]


def solution(mesh):
    placed = (
        P(None, None, "rows", None),
        P("depth", None, None, None),
        P("depth", None, None, None),
        P("depth", None, "rows", None),
        P("depth", "rows", None),
        P("depth", "rows"),
        P("depth", "rows", None),
    )
    return jax.shard_map(
        body,
        mesh=mesh,
        in_specs=placed,
        out_specs=P("depth", None, None, "rows", None),
        check_vma=False,
    )
```

```python
import math

import jax
import jax.numpy as jnp
import numpy as np
from jax import lax
from jax.experimental import pallas as pl
from jax.experimental.pallas import tpu as pltpu
from jax.sharding import PartitionSpec as P

HS = 16
KR = 16
KC = 63
COLORS = 3
LAYERS = 4
BAND = 32
COLS = 1024
NH = COLS // HS
LANES = 128
TILES = COLS // LANES
HALO_W = COLS + LANES
HALF = LANES // 2
FULL_W = COLS + 2 * LANES
NEAR = 2 * BAND + KR
FAR = KR
VMEM_LIMIT = 48 * 1024 * 1024
PACK_LIMIT = 63 * 1024 * 1024


def split_table(table):
    high = table.astype(jnp.bfloat16)
    low = (table - high.astype(np.float64)).astype(jnp.bfloat16)
    return high, low


def dft_pair():
    counter = np.arange(HS)
    angles = (counter[:, None] * counter[None, :] % HS) * (2.0 * math.pi / HS)
    return np.cos(angles) / math.sqrt(HS), np.sin(angles) / math.sqrt(HS)


def left_table(height):
    cos_tab, sin_tab = dft_pair()
    eye = np.eye(height // HS)
    full = np.concatenate([np.kron(eye, cos_tab), np.kron(eye, -sin_tab)], axis=0)
    return np.concatenate(split_table(full), axis=1)


def right_table():
    cos_tab, sin_tab = dft_pair()
    eye = np.eye(LANES // HS)
    cos_big, sin_big = np.kron(eye, cos_tab), np.kron(eye, sin_tab)
    full = np.concatenate(
        [
            np.concatenate([cos_big, -sin_big], axis=1),
            np.concatenate([sin_big, cos_big], axis=1),
        ],
        axis=0,
    )
    return full.astype(jnp.bfloat16)


def layer_height(layer):
    return BAND + 2 * KR * (LAYERS - 1 - layer)


def block_height(layer):
    height = layer_height(layer)
    return height // 2 if 2 * (height + 2 * KR) > 2 * LANES else height


def spread_matrix():
    tile = lax.broadcasted_iota(jnp.int32, (NH, COLS), 0)
    column = lax.broadcasted_iota(jnp.int32, (NH, COLS), 1)
    return jnp.where(column // HS == tile, 1.0, 0.0).astype(jnp.bfloat16)


def own_colour():
    return jnp.minimum(lax.axis_index("depth"), COLORS - 1)


def pack_kernel(light, edges, counts, listed, row_taps, col_taps, incident, out, mine, *scratch):
    held, sems, taps = scratch[:6], scratch[6], scratch[7]
    picked = pltpu.make_async_copy(incident.at[own_colour()], mine, sems.at[6])
    sources = (listed, counts, edges, row_taps, col_taps, light)
    copies = [
        pltpu.make_async_copy(source, target, sems.at[place])
        for place, (source, target) in enumerate(zip(sources, held))
    ]
    for copy in reversed(copies):
        copy.start()
    picked.start()
    listed, counts, edges, row_taps, col_taps, light = held
    spread = spread_matrix()
    slot = lax.broadcasted_iota(jnp.int32, (NH, NH), 0)
    place = lax.broadcasted_iota(jnp.int32, (NH, NH), 1)
    for copy in copies[:5]:
        copy.wait()
    rows = []
    for group in range(BAND // HS):
        listing = jnp.broadcast_to(listed[0, group : group + 1, :], (NH, NH))
        column = jnp.sum(jnp.where(slot == place, listing, 0), axis=1, keepdims=True)
        named = (column == place) & (slot < counts[0, group])
        live = jnp.max(jnp.where(named, 1.0, 0.0), axis=0, keepdims=True)
        rows.append(jnp.broadcast_to(live, (HS, NH)))
    live_rows = jnp.concatenate(rows, axis=0).astype(jnp.bfloat16)
    live_pix = jnp.dot(live_rows, spread, preferred_element_type=jnp.float32)
    edge_tile = jnp.concatenate(
        [edges[0].astype(jnp.float32), jnp.zeros((BAND, LANES - NH), jnp.float32)], axis=1
    ).astype(jnp.bfloat16)
    for colour in range(COLORS):
        out[colour, :, COLS:HALO_W] = edge_tile
        taps[...] = jnp.zeros_like(taps)
        taps[0:2, : 2 * KC + 1] = col_taps[0, colour].astype(jnp.float32)
        taps[2:4, : 2 * KR + 1] = row_taps[0, colour].astype(jnp.float32)
        out[colour, :, HALO_W:] = taps[...].astype(jnp.bfloat16)
    for spare in range(COLORS, LAYERS):
        out[spare] = jnp.zeros((BAND, FULL_W), jnp.bfloat16)
    copies[5].wait()
    for colour in range(COLORS):
        out[colour, :, :COLS] = (light[0, colour] * live_pix).astype(jnp.bfloat16)
    picked.wait()


def halo_kernel(own, in_chip, cross, far_even, far_odd):
    band = lax.axis_index("rows")
    core = band % 2
    odd = (band // 2) % 2
    last = BAND - KR
    for near, start in ((in_chip, (1 - core) * last), (cross, core * last)):
        near[0:BAND] = own[0, :, :HALO_W]
        near[BAND : 2 * BAND] = own[1, :, :HALO_W]
        near[2 * BAND : NEAR] = own[2, pl.ds(pl.multiple_of(start, KR), KR), :HALO_W]
    for far, start in ((far_even, (1 - odd) * last), (far_odd, odd * last)):
        far[...] = own[0, pl.ds(pl.multiple_of(start, KR), KR), :HALO_W]


def ordered(in_chip, cross, far_even, far_odd):
    band = lax.axis_index("rows")
    count = lax.axis_size("rows")
    even_core = band % 2 == 0
    even_chip = (band // 2) % 2 == 0

    def received(value, by, phase):
        lower = (band // by) % 2 == phase
        paired = jnp.where(lower, band + by < count, band >= by)
        value = value[...]
        return jnp.where(paired, value, jnp.zeros_like(value))

    in_chip, cross = received(in_chip, 1, 0), received(cross, 1, 1)
    far_even, far_odd = received(far_even, 2, 0), received(far_odd, 2, 1)
    return (
        jnp.where(even_core, cross, in_chip),
        jnp.where(even_core, in_chip, cross),
        jnp.where(even_chip, far_odd, far_even),
        jnp.where(even_chip, far_even, far_odd),
    )


def tiles_below(value, height):
    return jnp.concatenate(
        [
            jnp.concatenate(
                [
                    value[:height, tile * LANES : (tile + 1) * LANES],
                    value[height:, tile * LANES : (tile + 1) * LANES],
                ],
                axis=1,
            )
            for tile in range(TILES)
        ],
        axis=0,
    )


def stereo_tiles(blocks, left_tab, right_tab):
    arranged = []
    for light in blocks:
        doubled = jnp.concatenate([light, light], axis=0)
        left = jnp.dot(left_tab[...], doubled, preferred_element_type=jnp.float32)
        arranged.append(tiles_below(left.astype(jnp.bfloat16), light.shape[0]))
    arranged = jnp.concatenate(arranged, axis=0) if len(arranged) > 1 else arranged[0]
    return jnp.dot(arranged, right_tab[...], preferred_element_type=jnp.float32)


def clear_pixels(edges):
    edge_pix = jnp.dot(edges, spread_matrix(), preferred_element_type=jnp.float32)
    within = (lax.broadcasted_iota(jnp.int32, (1, COLS), 1) % HS).astype(jnp.float32)
    return jnp.where(within < edge_pix, 1.0, 0.0)


def banded(line, count, shift):
    base = jnp.concatenate([line, jnp.zeros((1, LANES), jnp.float32)], axis=1)
    base = jnp.broadcast_to(base, (count, 2 * LANES))
    return pltpu.roll(base, shift, 1, stride=1, stride_axis=0)


def filters(taps, layer):
    row_re, row_im = taps[2:3], taps[3:4]
    height = block_height(layer)
    before = height + 2 * KR
    upper = banded(row_re, height, 0) - banded(row_im, height, before)
    lower = banded(row_im, height, 0) + banded(row_re, height, before)
    row_mat = jnp.concatenate([upper, lower], axis=0).astype(jnp.bfloat16)
    col_re = banded(taps[0:1], LANES, 1)
    col_im = banded(taps[1:2], LANES, 1)
    upper = jnp.concatenate([col_re, -col_im], axis=1)
    lower = jnp.concatenate([col_im, col_re], axis=1)
    col_mat = jnp.concatenate([upper, lower], axis=0).astype(jnp.bfloat16)
    return row_mat, col_mat


def propagated(u_re, u_im, row_mat, col_mat, layer):
    height = layer_height(layer)
    block = block_height(layer)
    reach = block + 2 * KR
    parts = []
    for start in range(0, height, block):
        stacked = jnp.concatenate(
            [u_re[start : start + reach], u_im[start : start + reach]], axis=0
        )
        parts.append(
            jnp.dot(row_mat[:, : 2 * reach], stacked, preferred_element_type=jnp.float32)
        )
    rowed = jnp.concatenate(
        [part[:block] for part in parts] + [part[block:] for part in parts], axis=0
    )
    rowed = jnp.concatenate([rowed, jnp.zeros((2 * height, LANES), jnp.float32)], axis=1)
    rowed = pltpu.roll(rowed, HALF, 1).astype(jnp.bfloat16)
    windows = jnp.concatenate(
        [
            jnp.concatenate(
                [
                    rowed[:height, tile * LANES : (tile + 2) * LANES],
                    rowed[height:, tile * LANES : (tile + 2) * LANES],
                ],
                axis=1,
            )
            for tile in range(TILES)
        ],
        axis=0,
    )
    return lax.dot_general(
        windows, col_mat, (((1,), (1,)), ((), ())), preferred_element_type=jnp.float32
    )


def prepare_kernel(
    own, incident, in_chip, cross, far_even, far_odd, left_tab, right_tab,
    first, stereo, clear, col_mats, *row_mats
):
    low_near, high_near, low_far, high_far = ordered(in_chip, cross, far_even, far_odd)
    extended = []
    for part in range(2):
        pieces = [low_far, low_near, incident[...], high_near, high_far]
        pieces = [piece[part * BAND : (part + 1) * BAND] for piece in pieces]
        extended.append(jnp.concatenate(pieces, axis=0))
    row_mat, col_mat = filters(own[0, 0:16, HALO_W:].astype(jnp.float32), 0)
    first[...] = propagated(extended[0], extended[1], row_mat, col_mat, 0)
    for layer in range(1, LAYERS):
        row_mat, col_mat = filters(own[layer, 0:16, HALO_W:].astype(jnp.float32), layer)
        row_mats[layer - 1][...] = row_mat
        col_mats[layer - 1] = col_mat
    packed = jnp.concatenate([own[layer, :, :HALO_W] for layer in range(LAYERS)], axis=0)
    clear[...] = clear_pixels(packed[:, COLS : COLS + NH])
    tiles = stereo_tiles([packed[:, :COLS]], left_tab, right_tab)
    for tile in range(TILES):
        for part in range(2):
            block = tiles[
                tile * LANES : (tile + 1) * LANES, part * LANES : (part + 1) * LANES
            ]
            stereo[part, :, tile * LANES : (tile + 1) * LANES] = block


def chain_kernel(
    in_chip, cross, far_even, far_odd, left_tab, right_tab, first, stereo, clear, col_mats, *rest
):
    row_mats, (out, field) = rest[: LAYERS - 1], rest[LAYERS - 1 :]
    low_near, high_near, low_far, high_far = ordered(in_chip, cross, far_even, far_odd)
    pieces = [
        low_far,
        low_near[0:BAND],
        high_near[0:BAND],
        high_far,
        low_near[BAND : 2 * BAND],
        high_near[BAND : 2 * BAND],
        low_near[2 * BAND : NEAR],
        high_near[2 * BAND : NEAR],
    ]
    halo = jnp.concatenate(pieces, axis=0)
    half = halo.shape[0] // 2
    halo_tiles = stereo_tiles(
        [halo[:half, :COLS], halo[half:, :COLS]], left_tab, right_tab
    )
    halo_clear = clear_pixels(halo[:, COLS : COLS + NH])
    begins = (0, half, half + 2 * BAND, 0)
    sides = (BAND + FAR, BAND, KR, 0)
    for layer in range(LAYERS):
        height = layer_height(layer)
        before = height + 2 * KR
        low, side = begins[layer], sides[layer]
        if layer == 0:
            columned = first
        else:
            columned = propagated(
                field[0, :before], field[1, :before], row_mats[layer - 1], col_mats[layer - 1], layer
            )
        band = slice(layer * BAND, (layer + 1) * BAND)
        pieces = [clear[band]]
        if side:
            pieces = [halo_clear[low : low + side], clear[band], halo_clear[low + side : low + 2 * side]]
        passing = jnp.concatenate(pieces, axis=0)
        for tile in range(TILES):
            span = slice(tile * height, (tile + 1) * height)
            lanes = slice(tile * LANES, (tile + 1) * LANES)
            row = (low // half * TILES + tile) * half + low % half
            for part in range(2):
                within = slice(part * LANES, (part + 1) * LANES)
                pieces = [stereo[part, band, lanes]]
                if side:
                    pieces = [
                        halo_tiles[row : row + side, within],
                        stereo[part, band, lanes],
                        halo_tiles[row + side : row + 2 * side, within],
                    ]
                added = jnp.concatenate(pieces, axis=0)
                value = passing[:, lanes] * columned[span, within] + added
                field[part, :height, lanes] = value.astype(jnp.bfloat16)
        for part in range(2):
            out[layer, part] = field[part, side : side + BAND]


def exchanged(value, by, phase):
    count, depths = lax.axis_size("rows"), lax.axis_size("depth")
    partner = {}
    for low in range(count - by):
        if (low // by) % 2 == phase:
            partner[low], partner[low + by] = low + by, low
    pairs = []
    for depth in range(depths):
        for band in range(count):
            if band in partner:
                to = (depth, partner[band])
            elif by > 1:
                to = (depth, band ^ 1)
            else:
                to = (depth ^ 1, band)
            pairs.append((depth * count + band, to[0] * count + to[1]))
    return lax.ppermute(value, ("depth", "rows"), pairs)


def neighbours(sent):
    in_chip, cross, far_even, far_odd = sent
    cross = exchanged(cross, 1, 1)
    far_even = exchanged(far_even, 2, 0)
    far_odd = exchanged(far_odd, 2, 1)
    in_chip = exchanged(in_chip, 1, 0)
    return in_chip, cross, far_even, far_odd


def call(kernel, out_shape, in_specs, scratch=(), flops=0, moved=10**6, limit=VMEM_LIMIT):
    vmem = pl.BlockSpec(memory_space=pltpu.VMEM)
    many = isinstance(out_shape, (tuple, list))
    return pl.pallas_call(
        kernel,
        out_shape=out_shape,
        in_specs=in_specs,
        out_specs=(vmem,) * len(out_shape) if many else vmem,
        scratch_shapes=scratch,
        compiler_params=pltpu.CompilerParams(vmem_limit_bytes=limit),
        cost_estimate=pl.CostEstimate(flops=flops, bytes_accessed=moved, transcendentals=0),
    )


def body(incident, row_taps, col_taps, hogel_light, silhouette, fill_counts, hogel_index):
    vmem = pl.BlockSpec(memory_space=pltpu.VMEM)
    hbm = pl.BlockSpec(memory_space=pltpu.HBM)
    bf16, f32 = jnp.bfloat16, jnp.float32
    shaped = jax.ShapeDtypeStruct
    held = [
        pltpu.VMEM(hogel_index.shape, jnp.int32),
        pltpu.SMEM(fill_counts.shape, jnp.int32),
        pltpu.VMEM(silhouette.shape, jnp.int32),
        pltpu.VMEM(row_taps.shape, bf16),
        pltpu.VMEM(col_taps.shape, bf16),
        pltpu.VMEM(hogel_light.shape, f32),
    ]
    payload, mine = call(
        pack_kernel,
        (shaped((LAYERS, BAND, FULL_W), bf16), shaped(incident.shape[1:], bf16)),
        [hbm] * 7,
        held + [pltpu.SemaphoreType.DMA((7,)), pltpu.VMEM((BAND, LANES), f32)],
        flops=10**7,
        limit=PACK_LIMIT,
    )(hogel_light, silhouette, fill_counts, hogel_index, row_taps, col_taps, incident)
    mine = mine.reshape(2 * BAND, COLS)
    own = lax.all_to_all(payload, "depth", 0, 0, tiled=True)
    arrived = neighbours((mine,) * 4)
    near = shaped((NEAR, HALO_W), bf16)
    far = shaped((FAR, HALO_W), bf16)
    halos = neighbours(call(halo_kernel, (near, near, far, far), [vmem])(own))
    right_tab = jnp.asarray(right_table())
    made = call(
        prepare_kernel,
        [
            shaped((TILES * layer_height(0), 2 * LANES), f32),
            shaped((2, LANES, COLS), f32),
            shaped((LANES, COLS), f32),
            shaped((LAYERS - 1, 2 * LANES, 4 * LANES), bf16),
        ]
        + [shaped((2 * block_height(layer), 2 * LANES), bf16) for layer in range(1, LAYERS)],
        [vmem] * 8,
        flops=10**9,
        moved=3 * 10**6,
    )(own, mine, *arrived, jnp.asarray(left_table(LANES)), right_tab)
    halo_rows = NEAR + FAR
    result = call(
        chain_kernel,
        shaped((LAYERS, 2, BAND, COLS), bf16),
        [vmem] * (6 + len(made)),
        [pltpu.VMEM((2, layer_height(0), COLS), bf16)],
        flops=2 * 10**9,
        moved=3 * 10**6,
    )(*halos, jnp.asarray(left_table(halo_rows)), right_tab, *made)
    gathered = lax.all_to_all(result, "depth", 0, 0, tiled=True)
    return gathered[None, :COLORS]


def solution(mesh):
    placed = (
        P(None, None, "rows", None),
        P("depth", None, None, None),
        P("depth", None, None, None),
        P("depth", None, "rows", None),
        P("depth", "rows", None),
        P("depth", "rows"),
        P("depth", "rows", None),
    )
    return jax.shard_map(
        body,
        mesh=mesh,
        in_specs=placed,
        out_specs=P("depth", None, None, "rows", None),
        check_vma=False,
    )
```

```python
import math

import jax
import jax.numpy as jnp
import numpy as np
from jax import lax
from jax.experimental import pallas as pl
from jax.experimental.pallas import tpu as pltpu
from jax.sharding import PartitionSpec as P

HS = 16
KR = 16
KC = 63
COLORS = 3
LAYERS = 4
BAND = 32
COLS = 1024
NH = COLS // HS
LANES = 128
TILES = COLS // LANES
HALO_W = COLS + LANES
HALF = LANES // 2
NEAR = 2 * BAND + KR
FAR = KR
VMEM_LIMIT = 48 * 1024 * 1024
PACK_LIMIT = 63 * 1024 * 1024


def split_table(table):
    high = table.astype(jnp.bfloat16)
    low = (table - high.astype(np.float64)).astype(jnp.bfloat16)
    return high, low


def dft_pair():
    counter = np.arange(HS)
    angles = (counter[:, None] * counter[None, :] % HS) * (2.0 * math.pi / HS)
    return np.cos(angles) / math.sqrt(HS), np.sin(angles) / math.sqrt(HS)


def left_table(height):
    cos_tab, sin_tab = dft_pair()
    eye = np.eye(height // HS)
    full = np.concatenate([np.kron(eye, cos_tab), np.kron(eye, -sin_tab)], axis=0)
    return np.concatenate(split_table(full), axis=1)


def right_table():
    cos_tab, sin_tab = dft_pair()
    eye = np.eye(LANES // HS)
    cos_big, sin_big = np.kron(eye, cos_tab), np.kron(eye, sin_tab)
    full = np.concatenate(
        [
            np.concatenate([cos_big, -sin_big], axis=1),
            np.concatenate([sin_big, cos_big], axis=1),
        ],
        axis=0,
    )
    return full.astype(jnp.bfloat16)


def layer_height(layer):
    return BAND + 2 * KR * (LAYERS - 1 - layer)


def block_height(layer):
    height = layer_height(layer)
    return height // 2 if 2 * (height + 2 * KR) > 2 * LANES else height


def spread_matrix():
    tile = lax.broadcasted_iota(jnp.int32, (NH, COLS), 0)
    column = lax.broadcasted_iota(jnp.int32, (NH, COLS), 1)
    return jnp.where(column // HS == tile, 1.0, 0.0).astype(jnp.bfloat16)


def own_colour():
    return jnp.minimum(lax.axis_index("depth"), COLORS - 1)


def pack_kernel(light, edges, counts, listed, row_taps, col_taps, incident, *rest):
    outs, mine, held, sems, taps = rest[:LAYERS], rest[LAYERS], rest[5:11], rest[11], rest[12]
    depth = lax.axis_index("depth")
    picked = pltpu.make_async_copy(incident.at[own_colour()], mine, sems.at[6])
    sources = (listed, counts, edges, row_taps, col_taps, light)
    copies = [
        pltpu.make_async_copy(source, target, sems.at[place])
        for place, (source, target) in enumerate(zip(sources, held))
    ]
    for copy in reversed(copies):
        copy.start()
    picked.start()
    listed, counts, edges, row_taps, col_taps, light = held
    spread = spread_matrix()
    slot = lax.broadcasted_iota(jnp.int32, (NH, NH), 0)
    place = lax.broadcasted_iota(jnp.int32, (NH, NH), 1)
    for copy in copies[:5]:
        copy.wait()
    rows = []
    for group in range(BAND // HS):
        listing = jnp.broadcast_to(listed[0, group : group + 1, :], (NH, NH))
        column = jnp.sum(jnp.where(slot == place, listing, 0), axis=1, keepdims=True)
        named = (column == place) & (slot < counts[0, group])
        live = jnp.max(jnp.where(named, 1.0, 0.0), axis=0, keepdims=True)
        rows.append(jnp.broadcast_to(live, (HS, NH)))
    live_rows = jnp.concatenate(rows, axis=0).astype(jnp.bfloat16)
    live_pix = jnp.dot(live_rows, spread, preferred_element_type=jnp.float32)
    edge_tile = jnp.concatenate(
        [edges[0].astype(jnp.float32), jnp.zeros((BAND, LANES - NH), jnp.float32)], axis=1
    )
    left_half = lax.broadcasted_iota(jnp.int32, (BAND, LANES), 1) < HALF
    colours = [jnp.minimum(depth ^ hop, COLORS - 1) for hop in range(LAYERS)]
    for colour, out in zip(colours, outs):
        taps[...] = jnp.zeros_like(taps)
        taps[2:4, : 2 * KC + 1] = col_taps[0, colour].astype(jnp.float32)
        taps[4:6, : 2 * KR + 1] = row_taps[0, colour].astype(jnp.float32)
        turned = pltpu.roll(taps[0:8], HALF, 1)
        taps[0:2] = turned[2:4]
        taps[4:6] = turned[4:6]
        tile = jnp.where(left_half, edge_tile, taps[...])
        out[:, COLS:] = tile.astype(jnp.bfloat16)
    copies[5].wait()
    for colour, out in zip(colours, outs):
        out[:, :COLS] = (light[0, colour] * live_pix).astype(jnp.bfloat16)
    picked.wait()


def halo_kernel(*refs):
    arrived, (own, in_chip, cross, far_even, far_odd) = refs[:LAYERS], refs[LAYERS:]
    depth = lax.axis_index("depth")
    for hop in range(LAYERS):
        own[depth ^ hop] = arrived[hop][...]
    band = lax.axis_index("rows")
    core = band % 2
    odd = (band // 2) % 2
    last = BAND - KR
    for near, start in ((in_chip, (1 - core) * last), (cross, core * last)):
        near[0:BAND] = own[0, :, :HALO_W]
        near[BAND : 2 * BAND] = own[1, :, :HALO_W]
        near[2 * BAND : NEAR] = own[2, pl.ds(pl.multiple_of(start, KR), KR), :HALO_W]
    for far, start in ((far_even, (1 - odd) * last), (far_odd, odd * last)):
        far[...] = own[0, pl.ds(pl.multiple_of(start, KR), KR), :HALO_W]


def ordered(in_chip, cross, far_even, far_odd):
    band = lax.axis_index("rows")
    count = lax.axis_size("rows")
    even_core = band % 2 == 0
    even_chip = (band // 2) % 2 == 0

    def received(value, by, phase):
        lower = (band // by) % 2 == phase
        paired = jnp.where(lower, band + by < count, band >= by)
        value = value[...]
        return jnp.where(paired, value, jnp.zeros_like(value))

    in_chip, cross = received(in_chip, 1, 0), received(cross, 1, 1)
    far_even, far_odd = received(far_even, 2, 0), received(far_odd, 2, 1)
    return (
        jnp.where(even_core, cross, in_chip),
        jnp.where(even_core, in_chip, cross),
        jnp.where(even_chip, far_odd, far_even),
        jnp.where(even_chip, far_even, far_odd),
    )


def tiles_below(value, height):
    return jnp.concatenate(
        [
            jnp.concatenate(
                [
                    value[:height, tile * LANES : (tile + 1) * LANES],
                    value[height:, tile * LANES : (tile + 1) * LANES],
                ],
                axis=1,
            )
            for tile in range(TILES)
        ],
        axis=0,
    )


def stereo_tiles(blocks, left_tab, right_tab):
    arranged = []
    for light in blocks:
        doubled = jnp.concatenate([light, light], axis=0)
        left = jnp.dot(left_tab[...], doubled, preferred_element_type=jnp.float32)
        arranged.append(tiles_below(left.astype(jnp.bfloat16), light.shape[0]))
    arranged = jnp.concatenate(arranged, axis=0) if len(arranged) > 1 else arranged[0]
    return jnp.dot(arranged, right_tab[...], preferred_element_type=jnp.float32)


def clear_pixels(edges):
    edge_pix = jnp.dot(edges, spread_matrix(), preferred_element_type=jnp.float32)
    within = (lax.broadcasted_iota(jnp.int32, (1, COLS), 1) % HS).astype(jnp.float32)
    return jnp.where(within < edge_pix, 1.0, 0.0)


def banded(line, count, shift):
    base = jnp.concatenate([line, jnp.zeros((1, LANES), jnp.float32)], axis=1)
    base = jnp.broadcast_to(base, (count, 2 * LANES))
    return pltpu.roll(base, shift, 1, stride=1, stride_axis=0)


def filters(tile, layer):
    turned = pltpu.roll(tile[0:8], HALF, 1)
    left_half = lax.broadcasted_iota(jnp.int32, (2, LANES), 1) < HALF
    col_taps = jnp.where(left_half, turned[0:2], tile[2:4])
    row_taps = jnp.where(left_half, turned[4:6], 0.0)
    row_re, row_im = row_taps[0:1], row_taps[1:2]
    height = block_height(layer)
    before = height + 2 * KR
    upper = banded(row_re, height, 0) - banded(row_im, height, before)
    lower = banded(row_im, height, 0) + banded(row_re, height, before)
    row_mat = jnp.concatenate([upper, lower], axis=0).astype(jnp.bfloat16)
    col_re = banded(col_taps[0:1], LANES, 1)
    col_im = banded(col_taps[1:2], LANES, 1)
    upper = jnp.concatenate([col_re, -col_im], axis=1)
    lower = jnp.concatenate([col_im, col_re], axis=1)
    col_mat = jnp.concatenate([upper, lower], axis=0).astype(jnp.bfloat16)
    return row_mat, col_mat


def propagated(u_re, u_im, row_mat, col_mat, layer):
    height = layer_height(layer)
    block = block_height(layer)
    reach = block + 2 * KR
    parts = []
    for start in range(0, height, block):
        stacked = jnp.concatenate(
            [u_re[start : start + reach], u_im[start : start + reach]], axis=0
        )
        parts.append(
            jnp.dot(row_mat[:, : 2 * reach], stacked, preferred_element_type=jnp.float32)
        )
    rowed = jnp.concatenate(
        [part[:block] for part in parts] + [part[block:] for part in parts], axis=0
    )
    rowed = jnp.concatenate([rowed, jnp.zeros((2 * height, LANES), jnp.float32)], axis=1)
    rowed = pltpu.roll(rowed, HALF, 1).astype(jnp.bfloat16)
    windows = jnp.concatenate(
        [
            jnp.concatenate(
                [
                    rowed[:height, tile * LANES : (tile + 2) * LANES],
                    rowed[height:, tile * LANES : (tile + 2) * LANES],
                ],
                axis=1,
            )
            for tile in range(TILES)
        ],
        axis=0,
    )
    return lax.dot_general(
        windows, col_mat, (((1,), (1,)), ((), ())), preferred_element_type=jnp.float32
    )


def prepare_kernel(
    own, incident, in_chip, cross, far_even, far_odd, left_tab, right_tab,
    first, stereo, clear, col_mats, *row_mats
):
    low_near, high_near, low_far, high_far = ordered(in_chip, cross, far_even, far_odd)
    extended = []
    for part in range(2):
        pieces = [low_far, low_near, incident[...], high_near, high_far]
        pieces = [piece[part * BAND : (part + 1) * BAND] for piece in pieces]
        extended.append(jnp.concatenate(pieces, axis=0))
    row_mat, col_mat = filters(own[0, 0:16, COLS:].astype(jnp.float32), 0)
    first[...] = propagated(extended[0], extended[1], row_mat, col_mat, 0)
    for layer in range(1, LAYERS):
        row_mat, col_mat = filters(own[layer, 0:16, COLS:].astype(jnp.float32), layer)
        row_mats[layer - 1][...] = row_mat
        col_mats[layer - 1] = col_mat
    packed = jnp.concatenate([own[layer, :, :HALO_W] for layer in range(LAYERS)], axis=0)
    clear[...] = clear_pixels(packed[:, COLS : COLS + NH])
    tiles = stereo_tiles([packed[:, :COLS]], left_tab, right_tab)
    for tile in range(TILES):
        for part in range(2):
            block = tiles[
                tile * LANES : (tile + 1) * LANES, part * LANES : (part + 1) * LANES
            ]
            stereo[part, :, tile * LANES : (tile + 1) * LANES] = block


def chain_kernel(
    in_chip, cross, far_even, far_odd, left_tab, right_tab, first, stereo, clear, col_mats, *rest
):
    row_mats, outs, field = rest[: LAYERS - 1], rest[LAYERS - 1 : -1], rest[-1]
    depth = lax.axis_index("depth")
    low_near, high_near, low_far, high_far = ordered(in_chip, cross, far_even, far_odd)
    pieces = [
        low_far,
        low_near[0:BAND],
        high_near[0:BAND],
        high_far,
        low_near[BAND : 2 * BAND],
        high_near[BAND : 2 * BAND],
        low_near[2 * BAND : NEAR],
        high_near[2 * BAND : NEAR],
    ]
    halo = jnp.concatenate(pieces, axis=0)
    half = halo.shape[0] // 2
    halo_tiles = stereo_tiles(
        [halo[:half, :COLS], halo[half:, :COLS]], left_tab, right_tab
    )
    halo_clear = clear_pixels(halo[:, COLS : COLS + NH])
    begins = (0, half, half + 2 * BAND, 0)
    sides = (BAND + FAR, BAND, KR, 0)
    for layer in range(LAYERS):
        height = layer_height(layer)
        before = height + 2 * KR
        low, side = begins[layer], sides[layer]
        if layer == 0:
            columned = first
        else:
            columned = propagated(
                field[0, :before], field[1, :before], row_mats[layer - 1], col_mats[layer - 1], layer
            )
        band = slice(layer * BAND, (layer + 1) * BAND)
        pieces = [clear[band]]
        if side:
            pieces = [halo_clear[low : low + side], clear[band], halo_clear[low + side : low + 2 * side]]
        passing = jnp.concatenate(pieces, axis=0)
        for tile in range(TILES):
            span = slice(tile * height, (tile + 1) * height)
            lanes = slice(tile * LANES, (tile + 1) * LANES)
            row = (low // half * TILES + tile) * half + low % half
            for part in range(2):
                within = slice(part * LANES, (part + 1) * LANES)
                pieces = [stereo[part, band, lanes]]
                if side:
                    pieces = [
                        halo_tiles[row : row + side, within],
                        stereo[part, band, lanes],
                        halo_tiles[row + side : row + 2 * side, within],
                    ]
                added = jnp.concatenate(pieces, axis=0)
                value = passing[:, lanes] * columned[span, within] + added
                field[part, :height, lanes] = value.astype(jnp.bfloat16)
        for hop, out in enumerate(outs):

            @pl.when((depth ^ hop) == layer)
            def keep(out=out, side=side):
                for part in range(2):
                    out[part] = field[part, side : side + BAND]


def home_kernel(*refs):
    arrived, out, sems = refs[:LAYERS], refs[LAYERS], refs[LAYERS + 1]
    depth = lax.axis_index("depth")
    for colour in range(COLORS):
        for hop in range(LAYERS):

            @pl.when((depth ^ hop) == colour)
            def begin(hop=hop, colour=colour):
                pltpu.make_async_copy(arrived[hop], out.at[0, colour], sems.at[colour]).start()

    for colour in range(COLORS):
        pltpu.make_async_copy(arrived[0], out.at[0, colour], sems.at[colour]).wait()


def over_depth(value, hop):
    return lax.ppermute(value, "depth", [(i, i ^ hop) for i in range(LAYERS)])


def exchanged(value, by, phase):
    count, depths = lax.axis_size("rows"), lax.axis_size("depth")
    partner = {}
    for low in range(count - by):
        if (low // by) % 2 == phase:
            partner[low], partner[low + by] = low + by, low
    pairs = []
    for depth in range(depths):
        for band in range(count):
            if band in partner:
                to = (depth, partner[band])
            elif by > 1:
                to = (depth, band ^ 1)
            else:
                to = (depth ^ 1, band)
            pairs.append((depth * count + band, to[0] * count + to[1]))
    return lax.ppermute(value, ("depth", "rows"), pairs)


def neighbours(sent):
    in_chip, cross, far_even, far_odd = sent
    cross = exchanged(cross, 1, 1)
    far_even = exchanged(far_even, 2, 0)
    far_odd = exchanged(far_odd, 2, 1)
    in_chip = exchanged(in_chip, 1, 0)
    return in_chip, cross, far_even, far_odd


def call(
    kernel, out_shape, in_specs, scratch=(), flops=0, moved=10**6, limit=VMEM_LIMIT,
    out_space=pltpu.VMEM,
):
    vmem = pl.BlockSpec(memory_space=out_space)
    many = isinstance(out_shape, (tuple, list))
    return pl.pallas_call(
        kernel,
        out_shape=out_shape,
        in_specs=in_specs,
        out_specs=(vmem,) * len(out_shape) if many else vmem,
        scratch_shapes=scratch,
        compiler_params=pltpu.CompilerParams(vmem_limit_bytes=limit),
        cost_estimate=pl.CostEstimate(flops=flops, bytes_accessed=moved, transcendentals=0),
    )


def body(incident, row_taps, col_taps, hogel_light, silhouette, fill_counts, hogel_index):
    vmem = pl.BlockSpec(memory_space=pltpu.VMEM)
    hbm = pl.BlockSpec(memory_space=pltpu.HBM)
    bf16, f32 = jnp.bfloat16, jnp.float32
    shaped = jax.ShapeDtypeStruct
    held = [
        pltpu.VMEM(hogel_index.shape, jnp.int32),
        pltpu.SMEM(fill_counts.shape, jnp.int32),
        pltpu.VMEM(silhouette.shape, jnp.int32),
        pltpu.VMEM(row_taps.shape, bf16),
        pltpu.VMEM(col_taps.shape, bf16),
        pltpu.VMEM(hogel_light.shape, f32),
    ]
    *messages, mine = call(
        pack_kernel,
        (shaped((BAND, HALO_W), bf16),) * LAYERS + (shaped(incident.shape[1:], bf16),),
        [hbm] * 7,
        held + [pltpu.SemaphoreType.DMA((7,)), pltpu.VMEM((BAND, LANES), f32)],
        flops=10**7,
        limit=PACK_LIMIT,
    )(hogel_light, silhouette, fill_counts, hogel_index, row_taps, col_taps, incident)
    mine = mine.reshape(2 * BAND, COLS)
    layers_in = messages[:1] + [over_depth(messages[hop], hop) for hop in range(1, LAYERS)]
    arrived = neighbours((mine,) * 4)
    near = shaped((NEAR, HALO_W), bf16)
    far = shaped((FAR, HALO_W), bf16)
    own, *sent = call(
        halo_kernel,
        (shaped((LAYERS, BAND, HALO_W), bf16), near, near, far, far),
        [vmem] * LAYERS,
    )(*layers_in)
    halos = neighbours(sent)
    right_tab = jnp.asarray(right_table())
    made = call(
        prepare_kernel,
        [
            shaped((TILES * layer_height(0), 2 * LANES), f32),
            shaped((2, LANES, COLS), f32),
            shaped((LANES, COLS), f32),
            shaped((LAYERS - 1, 2 * LANES, 4 * LANES), bf16),
        ]
        + [shaped((2 * block_height(layer), 2 * LANES), bf16) for layer in range(1, LAYERS)],
        [vmem] * 8,
        flops=10**9,
        moved=3 * 10**6,
    )(own, mine, *arrived, jnp.asarray(left_table(LANES)), right_tab)
    halo_rows = NEAR + FAR
    results = call(
        chain_kernel,
        [shaped((2, BAND, COLS), bf16)] * LAYERS,
        [vmem] * (6 + len(made)),
        [pltpu.VMEM((2, layer_height(0), COLS), bf16)],
        flops=2 * 10**9,
        moved=3 * 10**6,
    )(*halos, jnp.asarray(left_table(halo_rows)), right_tab, *made)
    returned = [results[0]] + [over_depth(results[hop], hop) for hop in range(1, LAYERS)]
    return call(
        home_kernel,
        shaped((1, COLORS, 2, BAND, COLS), bf16),
        [vmem] * LAYERS,
        [pltpu.SemaphoreType.DMA((COLORS,))],
        out_space=pltpu.HBM,
    )(*returned)


def solution(mesh):
    placed = (
        P(None, None, "rows", None),
        P("depth", None, None, None),
        P("depth", None, None, None),
        P("depth", None, "rows", None),
        P("depth", "rows", None),
        P("depth", "rows"),
        P("depth", "rows", None),
    )
    return jax.shard_map(
        body,
        mesh=mesh,
        in_specs=placed,
        out_specs=P("depth", None, None, "rows", None),
        check_vma=False,
    )
```

```python
import math

import jax
import jax.numpy as jnp
import numpy as np
from jax import lax
from jax.experimental import pallas as pl
from jax.experimental.pallas import tpu as pltpu
from jax.sharding import PartitionSpec as P

HS = 16
KR = 16
KC = 63
COLORS = 3
LAYERS = 4
BAND = 32
COLS = 1024
NH = COLS // HS
LANES = 128
TILES = COLS // LANES
HALO_W = COLS + LANES
HALF = LANES // 2
NEAR = 2 * BAND + KR
FAR = KR
VMEM_LIMIT = 40 * 1024 * 1024
PACK_LIMIT = 63 * 1024 * 1024


def split_table(table):
    high = table.astype(jnp.bfloat16)
    low = (table - high.astype(np.float64)).astype(jnp.bfloat16)
    return high, low


def dft_pair():
    counter = np.arange(HS)
    angles = (counter[:, None] * counter[None, :] % HS) * (2.0 * math.pi / HS)
    return np.cos(angles) / math.sqrt(HS), np.sin(angles) / math.sqrt(HS)


def left_table(height):
    cos_tab, sin_tab = dft_pair()
    eye = np.eye(height // HS)
    full = np.concatenate([np.kron(eye, cos_tab), np.kron(eye, -sin_tab)], axis=0)
    return np.concatenate(split_table(full), axis=1)


def right_table():
    cos_tab, sin_tab = dft_pair()
    eye = np.eye(LANES // HS)
    cos_big, sin_big = np.kron(eye, cos_tab), np.kron(eye, sin_tab)
    full = np.concatenate(
        [
            np.concatenate([cos_big, -sin_big], axis=1),
            np.concatenate([sin_big, cos_big], axis=1),
        ],
        axis=0,
    )
    return full.astype(jnp.bfloat16)


def layer_height(layer):
    return BAND + 2 * KR * (LAYERS - 1 - layer)


def block_height(layer):
    height = layer_height(layer)
    return height // 2 if 2 * (height + 2 * KR) > 2 * LANES else height


def spread_matrix():
    tile = lax.broadcasted_iota(jnp.int32, (NH, COLS), 0)
    column = lax.broadcasted_iota(jnp.int32, (NH, COLS), 1)
    return jnp.where(column // HS == tile, 1.0, 0.0).astype(jnp.bfloat16)


def own_colour():
    return jnp.minimum(lax.axis_index("depth"), COLORS - 1)


def pack_kernel(light, edges, counts, listed, row_taps, col_taps, incident, *rest):
    outs, mine, held, sems, taps = rest[:LAYERS], rest[LAYERS], rest[5:11], rest[11], rest[12]
    depth = lax.axis_index("depth")
    picked = pltpu.make_async_copy(incident.at[own_colour()], mine, sems.at[6])
    sources = (listed, counts, edges, row_taps, col_taps, light)
    copies = [
        pltpu.make_async_copy(source, target, sems.at[place])
        for place, (source, target) in enumerate(zip(sources, held))
    ]
    for copy in reversed(copies):
        copy.start()
    picked.start()
    listed, counts, edges, row_taps, col_taps, light = held
    spread = spread_matrix()
    slot = lax.broadcasted_iota(jnp.int32, (NH, NH), 0)
    place = lax.broadcasted_iota(jnp.int32, (NH, NH), 1)
    for copy in copies[:5]:
        copy.wait()
    rows = []
    for group in range(BAND // HS):
        listing = jnp.broadcast_to(listed[0, group : group + 1, :], (NH, NH))
        column = jnp.sum(jnp.where(slot == place, listing, 0), axis=1, keepdims=True)
        named = (column == place) & (slot < counts[0, group])
        live = jnp.max(jnp.where(named, 1.0, 0.0), axis=0, keepdims=True)
        rows.append(jnp.broadcast_to(live, (HS, NH)))
    live_rows = jnp.concatenate(rows, axis=0).astype(jnp.bfloat16)
    live_pix = jnp.dot(live_rows, spread, preferred_element_type=jnp.float32)
    edge_tile = jnp.concatenate(
        [edges[0].astype(jnp.float32), jnp.zeros((BAND, LANES - NH), jnp.float32)], axis=1
    )
    left_half = lax.broadcasted_iota(jnp.int32, (BAND, LANES), 1) < HALF
    colours = [jnp.minimum(depth ^ hop, COLORS - 1) for hop in range(LAYERS)]
    for colour, out in zip(colours, outs):
        taps[...] = jnp.zeros_like(taps)
        taps[2:4, : 2 * KC + 1] = col_taps[0, colour].astype(jnp.float32)
        taps[4:6, : 2 * KR + 1] = row_taps[0, colour].astype(jnp.float32)
        turned = pltpu.roll(taps[0:8], HALF, 1)
        taps[0:2] = turned[2:4]
        taps[4:6] = turned[4:6]
        tile = jnp.where(left_half, edge_tile, taps[...])
        out[:, COLS:] = tile.astype(jnp.bfloat16)
    copies[5].wait()
    for colour, out in zip(colours, outs):
        out[:, :COLS] = (light[0, colour] * live_pix).astype(jnp.bfloat16)
    picked.wait()


def halo_kernel(*refs):
    arrived, (own, in_chip, cross, far_even, far_odd) = refs[:LAYERS], refs[LAYERS:]
    depth = lax.axis_index("depth")
    for hop in range(LAYERS):
        own[depth ^ hop] = arrived[hop][...]
    band = lax.axis_index("rows")
    core = band % 2
    odd = (band // 2) % 2
    last = BAND - KR
    for near, start in ((in_chip, (1 - core) * last), (cross, core * last)):
        near[0:BAND] = own[0, :, :HALO_W]
        near[BAND : 2 * BAND] = own[1, :, :HALO_W]
        near[2 * BAND : NEAR] = own[2, pl.ds(pl.multiple_of(start, KR), KR), :HALO_W]
    for far, start in ((far_even, (1 - odd) * last), (far_odd, odd * last)):
        far[...] = own[0, pl.ds(pl.multiple_of(start, KR), KR), :HALO_W]


def received(value, by, phase):
    band, count = lax.axis_index("rows"), lax.axis_size("rows")
    lower = (band // by) % 2 == phase
    paired = jnp.where(lower, band + by < count, band >= by)
    value = value[...]
    return jnp.where(paired, value, jnp.zeros_like(value))


def near_sides(in_chip, cross):
    even_core = lax.axis_index("rows") % 2 == 0
    in_chip, cross = received(in_chip, 1, 0), received(cross, 1, 1)
    return jnp.where(even_core, cross, in_chip), jnp.where(even_core, in_chip, cross)


def far_sides(far_even, far_odd):
    even_chip = (lax.axis_index("rows") // 2) % 2 == 0
    far_even, far_odd = received(far_even, 2, 0), received(far_odd, 2, 1)
    return jnp.where(even_chip, far_odd, far_even), jnp.where(even_chip, far_even, far_odd)


def tiles_below(value, height):
    return jnp.concatenate(
        [
            jnp.concatenate(
                [
                    value[:height, tile * LANES : (tile + 1) * LANES],
                    value[height:, tile * LANES : (tile + 1) * LANES],
                ],
                axis=1,
            )
            for tile in range(TILES)
        ],
        axis=0,
    )


def stereo_tiles(blocks, left_tab, right_tab):
    arranged = []
    for light in blocks:
        doubled = jnp.concatenate([light, light], axis=0)
        left = jnp.dot(left_tab[...], doubled, preferred_element_type=jnp.float32)
        arranged.append(tiles_below(left.astype(jnp.bfloat16), light.shape[0]))
    arranged = jnp.concatenate(arranged, axis=0) if len(arranged) > 1 else arranged[0]
    return jnp.dot(arranged, right_tab[...], preferred_element_type=jnp.float32)


def clear_pixels(edges):
    edge_pix = jnp.dot(edges, spread_matrix(), preferred_element_type=jnp.float32)
    within = (lax.broadcasted_iota(jnp.int32, (1, COLS), 1) % HS).astype(jnp.float32)
    return jnp.where(within < edge_pix, 1.0, 0.0)


def banded(line, count, shift):
    base = jnp.concatenate([line, jnp.zeros((1, LANES), jnp.float32)], axis=1)
    base = jnp.broadcast_to(base, (count, 2 * LANES))
    return pltpu.roll(base, shift, 1, stride=1, stride_axis=0)


def filters(tile, layer):
    turned = pltpu.roll(tile[0:8], HALF, 1)
    left_half = lax.broadcasted_iota(jnp.int32, (2, LANES), 1) < HALF
    col_taps = jnp.where(left_half, turned[0:2], tile[2:4])
    row_taps = jnp.where(left_half, turned[4:6], 0.0)
    row_re, row_im = row_taps[0:1], row_taps[1:2]
    height = block_height(layer)
    before = height + 2 * KR
    upper = banded(row_re, height, 0) - banded(row_im, height, before)
    lower = banded(row_im, height, 0) + banded(row_re, height, before)
    row_mat = jnp.concatenate([upper, lower], axis=0).astype(jnp.bfloat16)
    col_re = banded(col_taps[0:1], LANES, 1)
    col_im = banded(col_taps[1:2], LANES, 1)
    upper = jnp.concatenate([col_re, -col_im], axis=1)
    lower = jnp.concatenate([col_im, col_re], axis=1)
    col_mat = jnp.concatenate([upper, lower], axis=0).astype(jnp.bfloat16)
    return row_mat, col_mat


def propagated(u_re, u_im, row_mat, col_mat, layer):
    height = layer_height(layer)
    block = block_height(layer)
    reach = block + 2 * KR
    parts = []
    for start in range(0, height, block):
        stacked = jnp.concatenate(
            [u_re[start : start + reach], u_im[start : start + reach]], axis=0
        )
        parts.append(
            jnp.dot(row_mat[:, : 2 * reach], stacked, preferred_element_type=jnp.float32)
        )
    rowed = jnp.concatenate(
        [part[:block] for part in parts] + [part[block:] for part in parts], axis=0
    )
    rowed = jnp.concatenate([rowed, jnp.zeros((2 * height, LANES), jnp.float32)], axis=1)
    rowed = pltpu.roll(rowed, HALF, 1).astype(jnp.bfloat16)
    windows = jnp.concatenate(
        [
            jnp.concatenate(
                [
                    rowed[:height, tile * LANES : (tile + 2) * LANES],
                    rowed[height:, tile * LANES : (tile + 2) * LANES],
                ],
                axis=1,
            )
            for tile in range(TILES)
        ],
        axis=0,
    )
    return lax.dot_general(
        windows, col_mat, (((1,), (1,)), ((), ())), preferred_element_type=jnp.float32
    )


def prepare_kernel(
    own, incident, in_chip, cross, far_even, far_odd, left_tab, right_tab,
    first, stereo, clear, col_mats, *row_mats
):
    low_near, high_near = near_sides(in_chip, cross)
    low_far, high_far = far_sides(far_even, far_odd)
    colour = own_colour()
    extended = []
    for part in range(2):
        low_rows, near_rows, high_rows, top_rows = (
            side[part * BAND : (part + 1) * BAND]
            for side in (low_far, low_near, high_near, high_far)
        )
        pieces = [low_rows, near_rows, incident[colour, part], high_rows, top_rows]
        extended.append(jnp.concatenate(pieces, axis=0))
    row_mat, col_mat = filters(own[0, 0:16, COLS:].astype(jnp.float32), 0)
    first[...] = propagated(extended[0], extended[1], row_mat, col_mat, 0)
    for layer in range(1, LAYERS):
        row_mat, col_mat = filters(own[layer, 0:16, COLS:].astype(jnp.float32), layer)
        row_mats[layer - 1][...] = row_mat
        col_mats[layer - 1] = col_mat
    packed = jnp.concatenate([own[layer, :, :HALO_W] for layer in range(LAYERS)], axis=0)
    clear[...] = clear_pixels(packed[:, COLS : COLS + NH])
    tiles = stereo_tiles([packed[:, :COLS]], left_tab, right_tab)
    for tile in range(TILES):
        for part in range(2):
            block = tiles[
                tile * LANES : (tile + 1) * LANES, part * LANES : (part + 1) * LANES
            ]
            stereo[part, :, tile * LANES : (tile + 1) * LANES] = block


def near_kernel(light_in_chip, light_cross, near_tab, right_tab, near_tiles, near_clear):
    low, high = near_sides(light_in_chip, light_cross)
    blocks = [
        jnp.concatenate([low[0:BAND], high[0:BAND], low[2 * BAND :]], axis=0),
        jnp.concatenate(
            [low[BAND : 2 * BAND], high[BAND : 2 * BAND], high[2 * BAND :]], axis=0
        ),
    ]
    near_tiles[...] = stereo_tiles([block[:, :COLS] for block in blocks], near_tab, right_tab)
    edges = jnp.concatenate([block[:, COLS : COLS + NH] for block in blocks], axis=0)
    near_clear[...] = clear_pixels(edges)


def chain_kernel(
    far_even, far_odd, left_tab, right_tab,
    near_tiles, near_clear, first, stereo, clear, col_mats, *rest
):
    row_mats, outs, field = rest[: LAYERS - 1], rest[LAYERS - 1 : -1], rest[-1]
    depth = lax.axis_index("depth")
    far = jnp.concatenate(far_sides(far_even, far_odd), axis=0)
    far_tiles = stereo_tiles([far[:, :COLS]], left_tab, right_tab)
    far_clear = clear_pixels(far[:, COLS : COLS + NH])

    spots = (
        ((0, BAND), (BAND, BAND)),
        ((NEAR, BAND), (NEAR + BAND, BAND)),
        ((2 * BAND, KR), (NEAR + 2 * BAND, KR)),
        None,
    )
    for layer in range(LAYERS):
        height = layer_height(layer)
        before = height + 2 * KR
        side = (height - BAND) // 2
        if layer == 0:
            columned = first
        else:
            columned = propagated(
                field[0, :before], field[1, :before], row_mats[layer - 1], col_mats[layer - 1], layer
            )
        band = slice(layer * BAND, (layer + 1) * BAND)
        pieces = [clear[band]]
        if side:
            (low, count), (high, _) = spots[layer]
            pieces = [near_clear[low : low + count], clear[band], near_clear[high : high + count]]
        if layer == 0:
            pieces = [far_clear[:FAR]] + pieces + [far_clear[FAR:]]
        passing = jnp.concatenate(pieces, axis=0)
        for tile in range(TILES):
            span = slice(tile * height, (tile + 1) * height)
            lanes = slice(tile * LANES, (tile + 1) * LANES)
            for part in range(2):
                within = slice(part * LANES, (part + 1) * LANES)
                pieces = [stereo[part, band, lanes]]
                if side:
                    rows = [
                        (start // NEAR * TILES + tile) * NEAR + start % NEAR for start in (low, high)
                    ]
                    pieces = [
                        near_tiles[rows[0] : rows[0] + count, within],
                        stereo[part, band, lanes],
                        near_tiles[rows[1] : rows[1] + count, within],
                    ]
                if layer == 0:
                    row = tile * 2 * FAR
                    pieces = (
                        [far_tiles[row : row + FAR, within]]
                        + pieces
                        + [far_tiles[row + FAR : row + 2 * FAR, within]]
                    )
                added = jnp.concatenate(pieces, axis=0)
                value = passing[:, lanes] * columned[span, within] + added
                field[part, :height, lanes] = value.astype(jnp.bfloat16)
        for hop, out in enumerate(outs):

            @pl.when((depth ^ hop) == layer)
            def keep(out=out, side=side):
                for part in range(2):
                    out[part] = field[part, side : side + BAND]


def home_kernel(*refs):
    arrived, out, sems = refs[:LAYERS], refs[LAYERS], refs[LAYERS + 1]
    depth = lax.axis_index("depth")
    for colour in range(COLORS):
        for hop in range(LAYERS):

            @pl.when((depth ^ hop) == colour)
            def begin(hop=hop, colour=colour):
                pltpu.make_async_copy(arrived[hop], out.at[0, colour], sems.at[colour]).start()

    for colour in range(COLORS):
        pltpu.make_async_copy(arrived[0], out.at[0, colour], sems.at[colour]).wait()


def all_depths(values):
    arrived = list(values)
    for hop in (3, 1, 2):
        arrived[hop] = lax.ppermute(values[hop], "depth", [(i, i ^ hop) for i in range(LAYERS)])
    return arrived


def exchanged(value, by, phase):
    count, depths = lax.axis_size("rows"), lax.axis_size("depth")
    partner = {}
    for low in range(count - by):
        if (low // by) % 2 == phase:
            partner[low], partner[low + by] = low + by, low
    pairs = []
    for depth in range(depths):
        for band in range(count):
            if band in partner:
                to = (depth, partner[band])
            elif by > 1:
                to = (depth, band ^ 1)
            else:
                to = (depth ^ 1, band)
            pairs.append((depth * count + band, to[0] * count + to[1]))
    return lax.ppermute(value, ("depth", "rows"), pairs)


def neighbours(sent):
    in_chip, cross, far_even, far_odd = sent
    cross = exchanged(cross, 1, 1)
    far_even = exchanged(far_even, 2, 0)
    far_odd = exchanged(far_odd, 2, 1)
    in_chip = exchanged(in_chip, 1, 0)
    return in_chip, cross, far_even, far_odd


def call(
    kernel, out_shape, in_specs, scratch=(), flops=0, moved=10**6, limit=VMEM_LIMIT,
    out_space=pltpu.VMEM,
):
    vmem = pl.BlockSpec(memory_space=out_space)
    many = isinstance(out_shape, (tuple, list))
    return pl.pallas_call(
        kernel,
        out_shape=out_shape,
        in_specs=in_specs,
        out_specs=(vmem,) * len(out_shape) if many else vmem,
        scratch_shapes=scratch,
        compiler_params=pltpu.CompilerParams(vmem_limit_bytes=limit),
        cost_estimate=pl.CostEstimate(flops=flops, bytes_accessed=moved, transcendentals=0),
    )


def body(incident, row_taps, col_taps, hogel_light, silhouette, fill_counts, hogel_index):
    vmem = pl.BlockSpec(memory_space=pltpu.VMEM)
    hbm = pl.BlockSpec(memory_space=pltpu.HBM)
    bf16, f32 = jnp.bfloat16, jnp.float32
    shaped = jax.ShapeDtypeStruct
    held = [
        pltpu.VMEM(hogel_index.shape, jnp.int32),
        pltpu.SMEM(fill_counts.shape, jnp.int32),
        pltpu.VMEM(silhouette.shape, jnp.int32),
        pltpu.VMEM(row_taps.shape, bf16),
        pltpu.VMEM(col_taps.shape, bf16),
        pltpu.VMEM(hogel_light.shape, f32),
    ]
    *messages, mine = call(
        pack_kernel,
        (shaped((BAND, HALO_W), bf16),) * LAYERS + (shaped(incident.shape[1:], bf16),),
        [hbm] * 7,
        held + [pltpu.SemaphoreType.DMA((7,)), pltpu.VMEM((BAND, LANES), f32)],
        flops=10**7,
        limit=PACK_LIMIT,
    )(hogel_light, silhouette, fill_counts, hogel_index, row_taps, col_taps, incident)
    mine = mine.reshape(2 * BAND, COLS)
    layers_in = all_depths(messages)
    arrived = neighbours((mine,) * 4)
    near = shaped((NEAR, HALO_W), bf16)
    far = shaped((FAR, HALO_W), bf16)
    own, *sent = call(
        halo_kernel,
        (shaped((LAYERS, BAND, HALO_W), bf16), near, near, far, far),
        [vmem] * LAYERS,
    )(*layers_in)
    halos = neighbours(sent)
    right_tab = jnp.asarray(right_table())
    made = call(
        prepare_kernel,
        [
            shaped((TILES * layer_height(0), 2 * LANES), f32),
            shaped((2, LANES, COLS), f32),
            shaped((LANES, COLS), f32),
            shaped((LAYERS - 1, 2 * LANES, 4 * LANES), bf16),
        ]
        + [shaped((2 * block_height(layer), 2 * LANES), bf16) for layer in range(1, LAYERS)],
        [vmem] * 8,
        flops=10**9,
        moved=3 * 10**6,
    )(own, incident, *arrived, jnp.asarray(left_table(LANES)), right_tab)
    side_made = call(
        near_kernel,
        [shaped((2 * NEAR * TILES, 2 * LANES), f32), shaped((2 * NEAR, COLS), f32)],
        [vmem] * 4,
        flops=5 * 10**8,
        moved=2 * 10**6,
    )(*halos[:2], jnp.asarray(left_table(NEAR)), right_tab)
    results = call(
        chain_kernel,
        [shaped((2, BAND, COLS), bf16)] * LAYERS,
        [vmem] * (6 + len(made)),
        [pltpu.VMEM((2, layer_height(0), COLS), bf16)],
        flops=2 * 10**9,
        moved=3 * 10**6,
    )(*halos[2:], jnp.asarray(left_table(2 * FAR)), right_tab, *side_made, *made)
    returned = all_depths(results)
    return call(
        home_kernel,
        shaped((1, COLORS, 2, BAND, COLS), bf16),
        [vmem] * LAYERS,
        [pltpu.SemaphoreType.DMA((COLORS,))],
        out_space=pltpu.HBM,
    )(*returned)


def solution(mesh):
    placed = (
        P(None, None, "rows", None),
        P("depth", None, None, None),
        P("depth", None, None, None),
        P("depth", None, "rows", None),
        P("depth", "rows", None),
        P("depth", "rows"),
        P("depth", "rows", None),
    )
    return jax.shard_map(
        body,
        mesh=mesh,
        in_specs=placed,
        out_specs=P("depth", None, None, "rows", None),
        check_vma=False,
    )
```

```python
import math

import jax
import jax.numpy as jnp
import numpy as np
from jax import lax
from jax.experimental import pallas as pl
from jax.experimental.pallas import tpu as pltpu
from jax.sharding import PartitionSpec as P

HS = 16
KR = 16
KC = 63
COLORS = 3
LAYERS = 4
BAND = 32
COLS = 1024
NH = COLS // HS
LANES = 128
TILES = COLS // LANES
HALO_W = COLS + LANES
HALF = LANES // 2
NEAR = 2 * BAND + KR
FAR = KR
VMEM_LIMIT = 48 * 1024 * 1024
PACK_LIMIT = 63 * 1024 * 1024


def split_table(table):
    high = table.astype(jnp.bfloat16)
    low = (table - high.astype(np.float64)).astype(jnp.bfloat16)
    return high, low


def dft_pair():
    counter = np.arange(HS)
    angles = (counter[:, None] * counter[None, :] % HS) * (2.0 * math.pi / HS)
    return np.cos(angles) / math.sqrt(HS), np.sin(angles) / math.sqrt(HS)


def left_table(height):
    cos_tab, sin_tab = dft_pair()
    eye = np.eye(height // HS)
    full = np.concatenate([np.kron(eye, cos_tab), np.kron(eye, -sin_tab)], axis=0)
    return np.concatenate(split_table(full), axis=1)


def right_table():
    cos_tab, sin_tab = dft_pair()
    eye = np.eye(LANES // HS)
    cos_big, sin_big = np.kron(eye, cos_tab), np.kron(eye, sin_tab)
    full = np.concatenate(
        [
            np.concatenate([cos_big, -sin_big], axis=1),
            np.concatenate([sin_big, cos_big], axis=1),
        ],
        axis=0,
    )
    return full.astype(jnp.bfloat16)


def layer_height(layer):
    return BAND + 2 * KR * (LAYERS - 1 - layer)


def block_height(layer):
    height = layer_height(layer)
    return height // 2 if 2 * (height + 2 * KR) > 2 * LANES else height


def spread_matrix():
    tile = lax.broadcasted_iota(jnp.int32, (NH, COLS), 0)
    column = lax.broadcasted_iota(jnp.int32, (NH, COLS), 1)
    return jnp.where(column // HS == tile, 1.0, 0.0).astype(jnp.bfloat16)


def own_colour():
    return jnp.minimum(lax.axis_index("depth"), COLORS - 1)


def pack_kernel(light, edges, counts, listed, row_taps, col_taps, incident, *rest):
    outs, mine, held, sems, taps = rest[:LAYERS], rest[LAYERS], rest[5:11], rest[11], rest[12]
    depth = lax.axis_index("depth")
    picked = pltpu.make_async_copy(incident.at[own_colour()], mine, sems.at[6])
    sources = (listed, counts, edges, row_taps, col_taps, light)
    copies = [
        pltpu.make_async_copy(source, target, sems.at[place])
        for place, (source, target) in enumerate(zip(sources, held))
    ]
    for copy in reversed(copies):
        copy.start()
    picked.start()
    listed, counts, edges, row_taps, col_taps, light = held
    spread = spread_matrix()
    slot = lax.broadcasted_iota(jnp.int32, (NH, NH), 0)
    place = lax.broadcasted_iota(jnp.int32, (NH, NH), 1)
    for copy in copies[:5]:
        copy.wait()
    rows = []
    for group in range(BAND // HS):
        listing = jnp.broadcast_to(listed[0, group : group + 1, :], (NH, NH))
        column = jnp.sum(jnp.where(slot == place, listing, 0), axis=1, keepdims=True)
        named = (column == place) & (slot < counts[0, group])
        live = jnp.max(jnp.where(named, 1.0, 0.0), axis=0, keepdims=True)
        rows.append(jnp.broadcast_to(live, (HS, NH)))
    live_rows = jnp.concatenate(rows, axis=0).astype(jnp.bfloat16)
    live_pix = jnp.dot(live_rows, spread, preferred_element_type=jnp.float32)
    edge_tile = jnp.concatenate(
        [edges[0].astype(jnp.float32), jnp.zeros((BAND, LANES - NH), jnp.float32)], axis=1
    )
    left_half = lax.broadcasted_iota(jnp.int32, (BAND, LANES), 1) < HALF
    colours = [jnp.minimum(depth ^ hop, COLORS - 1) for hop in range(LAYERS)]
    for colour, out in zip(colours, outs):
        taps[...] = jnp.zeros_like(taps)
        taps[2:4, : 2 * KC + 1] = col_taps[0, colour].astype(jnp.float32)
        taps[4:6, : 2 * KR + 1] = row_taps[0, colour].astype(jnp.float32)
        turned = pltpu.roll(taps[0:8], HALF, 1)
        taps[0:2] = turned[2:4]
        taps[4:6] = turned[4:6]
        tile = jnp.where(left_half, edge_tile, taps[...])
        out[:, COLS:] = tile.astype(jnp.bfloat16)
    copies[5].wait()
    for colour, out in zip(colours, outs):
        out[:, :COLS] = (light[0, colour] * live_pix).astype(jnp.bfloat16)
    picked.wait()


def halo_kernel(*refs):
    arrived, (own, in_chip, cross, far_even, far_odd) = refs[:LAYERS], refs[LAYERS:]
    depth = lax.axis_index("depth")
    for hop in range(LAYERS):
        own[depth ^ hop] = arrived[hop][...]
    band = lax.axis_index("rows")
    core = band % 2
    odd = (band // 2) % 2
    last = BAND - KR
    for near, start in ((in_chip, (1 - core) * last), (cross, core * last)):
        near[0:BAND] = own[0, :, :HALO_W]
        near[BAND : 2 * BAND] = own[1, :, :HALO_W]
        near[2 * BAND : NEAR] = own[2, pl.ds(pl.multiple_of(start, KR), KR), :HALO_W]
    for far, start in ((far_even, (1 - odd) * last), (far_odd, odd * last)):
        far[...] = own[0, pl.ds(pl.multiple_of(start, KR), KR), :HALO_W]


def ordered(in_chip, cross, far_even, far_odd):
    band = lax.axis_index("rows")
    count = lax.axis_size("rows")
    even_core = band % 2 == 0
    even_chip = (band // 2) % 2 == 0

    def received(value, by, phase):
        lower = (band // by) % 2 == phase
        paired = jnp.where(lower, band + by < count, band >= by)
        value = value[...]
        return jnp.where(paired, value, jnp.zeros_like(value))

    in_chip, cross = received(in_chip, 1, 0), received(cross, 1, 1)
    far_even, far_odd = received(far_even, 2, 0), received(far_odd, 2, 1)
    return (
        jnp.where(even_core, cross, in_chip),
        jnp.where(even_core, in_chip, cross),
        jnp.where(even_chip, far_odd, far_even),
        jnp.where(even_chip, far_even, far_odd),
    )


def tiles_below(value, height):
    return jnp.concatenate(
        [
            jnp.concatenate(
                [
                    value[:height, tile * LANES : (tile + 1) * LANES],
                    value[height:, tile * LANES : (tile + 1) * LANES],
                ],
                axis=1,
            )
            for tile in range(TILES)
        ],
        axis=0,
    )


def stereo_tiles(blocks, left_tab, right_tab):
    arranged = []
    for light in blocks:
        doubled = jnp.concatenate([light, light], axis=0)
        left = jnp.dot(left_tab[...], doubled, preferred_element_type=jnp.float32)
        arranged.append(tiles_below(left.astype(jnp.bfloat16), light.shape[0]))
    arranged = jnp.concatenate(arranged, axis=0) if len(arranged) > 1 else arranged[0]
    return jnp.dot(arranged, right_tab[...], preferred_element_type=jnp.float32)


def clear_pixels(edges):
    edge_pix = jnp.dot(edges, spread_matrix(), preferred_element_type=jnp.float32)
    within = (lax.broadcasted_iota(jnp.int32, (1, COLS), 1) % HS).astype(jnp.float32)
    return jnp.where(within < edge_pix, 1.0, 0.0)


def banded(line, count, shift):
    base = jnp.concatenate([line, jnp.zeros((1, LANES), jnp.float32)], axis=1)
    base = jnp.broadcast_to(base, (count, 2 * LANES))
    return pltpu.roll(base, shift, 1, stride=1, stride_axis=0)


def filters(tile, layer):
    turned = pltpu.roll(tile[0:8], HALF, 1)
    left_half = lax.broadcasted_iota(jnp.int32, (2, LANES), 1) < HALF
    col_taps = jnp.where(left_half, turned[0:2], tile[2:4])
    row_taps = jnp.where(left_half, turned[4:6], 0.0)
    row_re, row_im = row_taps[0:1], row_taps[1:2]
    height = block_height(layer)
    before = height + 2 * KR
    upper = banded(row_re, height, 0) - banded(row_im, height, before)
    lower = banded(row_im, height, 0) + banded(row_re, height, before)
    row_mat = jnp.concatenate([upper, lower], axis=0).astype(jnp.bfloat16)
    col_re = banded(col_taps[0:1], LANES, 1)
    col_im = banded(col_taps[1:2], LANES, 1)
    upper = jnp.concatenate([col_re, -col_im], axis=1)
    lower = jnp.concatenate([col_im, col_re], axis=1)
    col_mat = jnp.concatenate([upper, lower], axis=0).astype(jnp.bfloat16)
    return row_mat, col_mat


def propagated(u_re, u_im, row_mat, col_mat, layer):
    height = layer_height(layer)
    block = block_height(layer)
    reach = block + 2 * KR
    parts = []
    for start in range(0, height, block):
        stacked = jnp.concatenate(
            [u_re[start : start + reach], u_im[start : start + reach]], axis=0
        )
        parts.append(
            jnp.dot(row_mat[:, : 2 * reach], stacked, preferred_element_type=jnp.float32)
        )
    rowed = jnp.concatenate(
        [part[:block] for part in parts] + [part[block:] for part in parts], axis=0
    )
    rowed = jnp.concatenate([rowed, jnp.zeros((2 * height, LANES), jnp.float32)], axis=1)
    rowed = pltpu.roll(rowed, HALF, 1).astype(jnp.bfloat16)
    windows = jnp.concatenate(
        [
            jnp.concatenate(
                [
                    rowed[:height, tile * LANES : (tile + 2) * LANES],
                    rowed[height:, tile * LANES : (tile + 2) * LANES],
                ],
                axis=1,
            )
            for tile in range(TILES)
        ],
        axis=0,
    )
    return lax.dot_general(
        windows, col_mat, (((1,), (1,)), ((), ())), preferred_element_type=jnp.float32
    )


def prepare_kernel(
    own, incident, cross, far_even, far_odd, in_chip, left_tab, right_tab,
    first, stereo, clear, col_mats, *row_mats
):
    low_near, high_near, low_far, high_far = ordered(in_chip, cross, far_even, far_odd)
    extended = []
    for part in range(2):
        pieces = [low_far, low_near, incident[...], high_near, high_far]
        pieces = [piece[part * BAND : (part + 1) * BAND] for piece in pieces]
        extended.append(jnp.concatenate(pieces, axis=0))
    row_mat, col_mat = filters(own[0, 0:16, COLS:].astype(jnp.float32), 0)
    first[...] = propagated(extended[0], extended[1], row_mat, col_mat, 0)
    for layer in range(1, LAYERS):
        row_mat, col_mat = filters(own[layer, 0:16, COLS:].astype(jnp.float32), layer)
        row_mats[layer - 1][...] = row_mat
        col_mats[layer - 1] = col_mat
    packed = jnp.concatenate([own[layer, :, :HALO_W] for layer in range(LAYERS)], axis=0)
    clear[...] = clear_pixels(packed[:, COLS : COLS + NH])
    tiles = stereo_tiles([packed[:, :COLS]], left_tab, right_tab)
    for tile in range(TILES):
        for part in range(2):
            block = tiles[
                tile * LANES : (tile + 1) * LANES, part * LANES : (part + 1) * LANES
            ]
            stereo[part, :, tile * LANES : (tile + 1) * LANES] = block


def chain_kernel(
    in_chip, cross, far_even, far_odd, left_tab, right_tab, first, stereo, clear, col_mats, *rest
):
    row_mats, outs, field = rest[: LAYERS - 1], rest[LAYERS - 1 : -1], rest[-1]
    depth = lax.axis_index("depth")
    low_near, high_near, low_far, high_far = ordered(in_chip, cross, far_even, far_odd)
    pieces = [
        low_far,
        low_near[0:BAND],
        high_near[0:BAND],
        high_far,
        low_near[BAND : 2 * BAND],
        high_near[BAND : 2 * BAND],
        low_near[2 * BAND : NEAR],
        high_near[2 * BAND : NEAR],
    ]
    halo = jnp.concatenate(pieces, axis=0)
    half = halo.shape[0] // 2
    halo_tiles = stereo_tiles(
        [halo[:half, :COLS], halo[half:, :COLS]], left_tab, right_tab
    )
    halo_clear = clear_pixels(halo[:, COLS : COLS + NH])
    begins = (0, half, half + 2 * BAND, 0)
    sides = (BAND + FAR, BAND, KR, 0)
    for layer in range(LAYERS):
        height = layer_height(layer)
        before = height + 2 * KR
        low, side = begins[layer], sides[layer]
        if layer == 0:
            columned = first
        else:
            columned = propagated(
                field[layer - 1, 0, :before],
                field[layer - 1, 1, :before],
                row_mats[layer - 1],
                col_mats[layer - 1],
                layer,
            )
        band = slice(layer * BAND, (layer + 1) * BAND)
        pieces = [clear[band]]
        if side:
            pieces = [halo_clear[low : low + side], clear[band], halo_clear[low + side : low + 2 * side]]
        passing = jnp.concatenate(pieces, axis=0)
        for tile in range(TILES):
            span = slice(tile * height, (tile + 1) * height)
            lanes = slice(tile * LANES, (tile + 1) * LANES)
            row = (low // half * TILES + tile) * half + low % half
            for part in range(2):
                within = slice(part * LANES, (part + 1) * LANES)
                pieces = [stereo[part, band, lanes]]
                if side:
                    pieces = [
                        halo_tiles[row : row + side, within],
                        stereo[part, band, lanes],
                        halo_tiles[row + side : row + 2 * side, within],
                    ]
                added = jnp.concatenate(pieces, axis=0)
                value = passing[:, lanes] * columned[span, within] + added
                field[layer, part, :height, lanes] = value.astype(jnp.bfloat16)
    for hop, out in enumerate(outs):
        layer = depth ^ hop
        start = pl.multiple_of((LAYERS - 1 - layer) * KR, KR)
        for part in range(2):
            out[part] = field[layer, part, pl.ds(start, BAND)]


def home_kernel(*refs):
    arrived, out, sems = refs[:LAYERS], refs[LAYERS], refs[LAYERS + 1]
    depth = lax.axis_index("depth")
    for colour in range(COLORS):
        for hop in range(LAYERS):

            @pl.when((depth ^ hop) == colour)
            def begin(hop=hop, colour=colour):
                pltpu.make_async_copy(arrived[hop], out.at[0, colour], sems.at[colour]).start()

    for colour in range(COLORS):
        pltpu.make_async_copy(arrived[0], out.at[0, colour], sems.at[colour]).wait()


def over_depth(value, hop):
    return lax.ppermute(value, "depth", [(i, i ^ hop) for i in range(LAYERS)])


def exchanged(value, by, phase):
    count, depths = lax.axis_size("rows"), lax.axis_size("depth")
    partner = {}
    for low in range(count - by):
        if (low // by) % 2 == phase:
            partner[low], partner[low + by] = low + by, low
    pairs = []
    for depth in range(depths):
        for band in range(count):
            if band in partner:
                to = (depth, partner[band])
            elif by > 1:
                to = (depth, band ^ 1)
            else:
                to = (depth ^ 1, band)
            pairs.append((depth * count + band, to[0] * count + to[1]))
    return lax.ppermute(value, ("depth", "rows"), pairs)


def neighbours(sent):
    in_chip, cross, far_even, far_odd = sent
    cross = exchanged(cross, 1, 1)
    far_even = exchanged(far_even, 2, 0)
    far_odd = exchanged(far_odd, 2, 1)
    in_chip = exchanged(in_chip, 1, 0)
    return in_chip, cross, far_even, far_odd


def call(
    kernel, out_shape, in_specs, scratch=(), flops=0, moved=10**6, limit=VMEM_LIMIT,
    out_space=pltpu.VMEM,
):
    vmem = pl.BlockSpec(memory_space=out_space)
    many = isinstance(out_shape, (tuple, list))
    return pl.pallas_call(
        kernel,
        out_shape=out_shape,
        in_specs=in_specs,
        out_specs=(vmem,) * len(out_shape) if many else vmem,
        scratch_shapes=scratch,
        compiler_params=pltpu.CompilerParams(vmem_limit_bytes=limit),
        cost_estimate=pl.CostEstimate(flops=flops, bytes_accessed=moved, transcendentals=0),
    )


def body(incident, row_taps, col_taps, hogel_light, silhouette, fill_counts, hogel_index):
    vmem = pl.BlockSpec(memory_space=pltpu.VMEM)
    hbm = pl.BlockSpec(memory_space=pltpu.HBM)
    bf16, f32 = jnp.bfloat16, jnp.float32
    shaped = jax.ShapeDtypeStruct
    held = [
        pltpu.VMEM(hogel_index.shape, jnp.int32),
        pltpu.SMEM(fill_counts.shape, jnp.int32),
        pltpu.VMEM(silhouette.shape, jnp.int32),
        pltpu.VMEM(row_taps.shape, bf16),
        pltpu.VMEM(col_taps.shape, bf16),
        pltpu.VMEM(hogel_light.shape, f32),
    ]
    *messages, mine = call(
        pack_kernel,
        (shaped((BAND, HALO_W), bf16),) * LAYERS + (shaped(incident.shape[1:], bf16),),
        [hbm] * 7,
        held + [pltpu.SemaphoreType.DMA((7,)), pltpu.VMEM((BAND, LANES), f32)],
        flops=10**7,
        limit=PACK_LIMIT,
    )(hogel_light, silhouette, fill_counts, hogel_index, row_taps, col_taps, incident)
    mine = mine.reshape(2 * BAND, COLS)
    layers_in = messages[:1] + [over_depth(messages[hop], hop) for hop in range(1, LAYERS)]
    in_chip, *arrived = neighbours((mine,) * 4)
    near = shaped((NEAR, HALO_W), bf16)
    far = shaped((FAR, HALO_W), bf16)
    own, *sent = call(
        halo_kernel,
        (shaped((LAYERS, BAND, HALO_W), bf16), near, near, far, far),
        [vmem] * LAYERS,
    )(*layers_in)
    halos = neighbours(sent)
    right_tab = jnp.asarray(right_table())
    made = call(
        prepare_kernel,
        [
            shaped((TILES * layer_height(0), 2 * LANES), f32),
            shaped((2, LANES, COLS), f32),
            shaped((LANES, COLS), f32),
            shaped((LAYERS - 1, 2 * LANES, 4 * LANES), bf16),
        ]
        + [shaped((2 * block_height(layer), 2 * LANES), bf16) for layer in range(1, LAYERS)],
        [vmem] * 8,
        flops=10**9,
        moved=3 * 10**6,
    )(own, mine, *arrived, in_chip, jnp.asarray(left_table(LANES)), right_tab)
    halo_rows = NEAR + FAR
    results = call(
        chain_kernel,
        [shaped((2, BAND, COLS), bf16)] * LAYERS,
        [vmem] * (6 + len(made)),
        [pltpu.VMEM((LAYERS, 2, layer_height(0), COLS), bf16)],
        flops=2 * 10**9,
        moved=3 * 10**6,
    )(*halos, jnp.asarray(left_table(halo_rows)), right_tab, *made)
    returned = [results[0]] + [over_depth(results[hop], hop) for hop in range(1, LAYERS)]
    return call(
        home_kernel,
        shaped((1, COLORS, 2, BAND, COLS), bf16),
        [vmem] * LAYERS,
        [pltpu.SemaphoreType.DMA((COLORS,))],
        out_space=pltpu.HBM,
    )(*returned)


def solution(mesh):
    placed = (
        P(None, None, "rows", None),
        P("depth", None, None, None),
        P("depth", None, None, None),
        P("depth", None, "rows", None),
        P("depth", "rows", None),
        P("depth", "rows"),
        P("depth", "rows", None),
    )
    return jax.shard_map(
        body,
        mesh=mesh,
        in_specs=placed,
        out_specs=P("depth", None, None, "rows", None),
        check_vma=False,
    )
```

```python
import math

import jax
import jax.numpy as jnp
import numpy as np
from jax import lax
from jax.experimental import pallas as pl
from jax.experimental.pallas import tpu as pltpu
from jax.sharding import PartitionSpec as P

HS = 16
KR = 16
KC = 63
COLORS = 3
LAYERS = 4
BAND = 32
COLS = 1024
NH = COLS // HS
LANES = 128
TILES = COLS // LANES
HALO_W = COLS + LANES
HALF = LANES // 2
NEAR = 2 * BAND + KR
FAR = KR
VMEM_LIMIT = 48 * 1024 * 1024
PACK_LIMIT = 63 * 1024 * 1024


def split_table(table):
    high = table.astype(jnp.bfloat16)
    low = (table - high.astype(np.float64)).astype(jnp.bfloat16)
    return high, low


def dft_pair():
    counter = np.arange(HS)
    angles = (counter[:, None] * counter[None, :] % HS) * (2.0 * math.pi / HS)
    return np.cos(angles) / math.sqrt(HS), np.sin(angles) / math.sqrt(HS)


def left_table(height):
    cos_tab, sin_tab = dft_pair()
    eye = np.eye(height // HS)
    full = np.concatenate([np.kron(eye, cos_tab), np.kron(eye, -sin_tab)], axis=0)
    return np.concatenate(split_table(full), axis=1)


def right_table():
    cos_tab, sin_tab = dft_pair()
    eye = np.eye(LANES // HS)
    cos_big, sin_big = np.kron(eye, cos_tab), np.kron(eye, sin_tab)
    full = np.concatenate(
        [
            np.concatenate([cos_big, -sin_big], axis=1),
            np.concatenate([sin_big, cos_big], axis=1),
        ],
        axis=0,
    )
    return full.astype(jnp.bfloat16)


def layer_height(layer):
    return BAND + 2 * KR * (LAYERS - 1 - layer)


def block_height(layer):
    height = layer_height(layer)
    return height // 2 if 2 * (height + 2 * KR) > 2 * LANES else height


def spread_matrix():
    tile = lax.broadcasted_iota(jnp.int32, (NH, COLS), 0)
    column = lax.broadcasted_iota(jnp.int32, (NH, COLS), 1)
    return jnp.where(column // HS == tile, 1.0, 0.0).astype(jnp.bfloat16)


def own_colour():
    return jnp.minimum(lax.axis_index("depth"), COLORS - 1)


def pack_kernel(light, edges, counts, listed, row_taps, col_taps, incident, *rest):
    outs, mine, held, sems, taps = rest[:LAYERS], rest[LAYERS], rest[5:11], rest[11], rest[12]
    depth = lax.axis_index("depth")
    picked = pltpu.make_async_copy(incident.at[own_colour()], mine, sems.at[6])
    sources = (listed, counts, edges, row_taps, col_taps, light)
    copies = [
        pltpu.make_async_copy(source, target, sems.at[place])
        for place, (source, target) in enumerate(zip(sources, held))
    ]
    for copy in reversed(copies):
        copy.start()
    picked.start()
    listed, counts, edges, row_taps, col_taps, light = held
    spread = spread_matrix()
    slot = lax.broadcasted_iota(jnp.int32, (NH, NH), 0)
    place = lax.broadcasted_iota(jnp.int32, (NH, NH), 1)
    for copy in copies[:5]:
        copy.wait()
    rows = []
    for group in range(BAND // HS):
        listing = jnp.broadcast_to(listed[0, group : group + 1, :], (NH, NH))
        column = jnp.sum(jnp.where(slot == place, listing, 0), axis=1, keepdims=True)
        named = (column == place) & (slot < counts[0, group])
        live = jnp.max(jnp.where(named, 1.0, 0.0), axis=0, keepdims=True)
        rows.append(jnp.broadcast_to(live, (HS, NH)))
    live_rows = jnp.concatenate(rows, axis=0).astype(jnp.bfloat16)
    live_pix = jnp.dot(live_rows, spread, preferred_element_type=jnp.float32)
    edge_tile = jnp.concatenate(
        [edges[0].astype(jnp.float32), jnp.zeros((BAND, LANES - NH), jnp.float32)], axis=1
    )
    left_half = lax.broadcasted_iota(jnp.int32, (BAND, LANES), 1) < HALF
    colours = [jnp.minimum(depth ^ hop, COLORS - 1) for hop in range(LAYERS)]
    for colour, out in zip(colours, outs):
        taps[...] = jnp.zeros_like(taps)
        taps[2:4, : 2 * KC + 1] = col_taps[0, colour].astype(jnp.float32)
        taps[4:6, : 2 * KR + 1] = row_taps[0, colour].astype(jnp.float32)
        turned = pltpu.roll(taps[0:8], HALF, 1)
        taps[0:2] = turned[2:4]
        taps[4:6] = turned[4:6]
        tile = jnp.where(left_half, edge_tile, taps[...])
        out[:, COLS:] = tile.astype(jnp.bfloat16)
    copies[5].wait()
    for colour, out in zip(colours, outs):
        out[:, :COLS] = (light[0, colour] * live_pix).astype(jnp.bfloat16)
    picked.wait()


def halo_kernel(*refs):
    arrived, (own, in_chip, cross, far_even, far_odd) = refs[:LAYERS], refs[LAYERS:]
    depth = lax.axis_index("depth")
    for hop in range(LAYERS):
        own[depth ^ hop] = arrived[hop][...]
    band = lax.axis_index("rows")
    core = band % 2
    odd = (band // 2) % 2
    last = BAND - KR
    for near, start in ((in_chip, (1 - core) * last), (cross, core * last)):
        near[0:BAND] = own[0, :, :HALO_W]
        near[BAND : 2 * BAND] = own[1, :, :HALO_W]
        near[2 * BAND : NEAR] = own[2, pl.ds(pl.multiple_of(start, KR), KR), :HALO_W]
    for far, start in ((far_even, (1 - odd) * last), (far_odd, odd * last)):
        far[...] = own[0, pl.ds(pl.multiple_of(start, KR), KR), :HALO_W]


def ordered(in_chip, cross, far_even, far_odd):
    band = lax.axis_index("rows")
    count = lax.axis_size("rows")
    even_core = band % 2 == 0
    even_chip = (band // 2) % 2 == 0

    def received(value, by, phase):
        lower = (band // by) % 2 == phase
        paired = jnp.where(lower, band + by < count, band >= by)
        value = value[...]
        return jnp.where(paired, value, jnp.zeros_like(value))

    in_chip, cross = received(in_chip, 1, 0), received(cross, 1, 1)
    far_even, far_odd = received(far_even, 2, 0), received(far_odd, 2, 1)
    return (
        jnp.where(even_core, cross, in_chip),
        jnp.where(even_core, in_chip, cross),
        jnp.where(even_chip, far_odd, far_even),
        jnp.where(even_chip, far_even, far_odd),
    )


def tiles_below(value, height):
    return jnp.concatenate(
        [
            jnp.concatenate(
                [
                    value[:height, tile * LANES : (tile + 1) * LANES],
                    value[height:, tile * LANES : (tile + 1) * LANES],
                ],
                axis=1,
            )
            for tile in range(TILES)
        ],
        axis=0,
    )


def stereo_tiles(blocks, left_tab, right_tab):
    arranged = []
    for light in blocks:
        doubled = jnp.concatenate([light, light], axis=0)
        left = jnp.dot(left_tab[...], doubled, preferred_element_type=jnp.float32)
        arranged.append(tiles_below(left.astype(jnp.bfloat16), light.shape[0]))
    arranged = jnp.concatenate(arranged, axis=0) if len(arranged) > 1 else arranged[0]
    return jnp.dot(arranged, right_tab[...], preferred_element_type=jnp.float32)


def clear_pixels(edges):
    edge_pix = jnp.dot(edges, spread_matrix(), preferred_element_type=jnp.float32)
    within = (lax.broadcasted_iota(jnp.int32, (1, COLS), 1) % HS).astype(jnp.float32)
    return jnp.where(within < edge_pix, 1.0, 0.0)


def banded(line, count, shift):
    base = jnp.concatenate([line, jnp.zeros((1, LANES), jnp.float32)], axis=1)
    base = jnp.broadcast_to(base, (count, 2 * LANES))
    return pltpu.roll(base, shift, 1, stride=1, stride_axis=0)


def filters(tile, layer):
    turned = pltpu.roll(tile[0:8], HALF, 1)
    left_half = lax.broadcasted_iota(jnp.int32, (2, LANES), 1) < HALF
    col_taps = jnp.where(left_half, turned[0:2], tile[2:4])
    row_taps = jnp.where(left_half, turned[4:6], 0.0)
    row_re, row_im = row_taps[0:1], row_taps[1:2]
    height = block_height(layer)
    before = height + 2 * KR
    upper = banded(row_re, height, 0) - banded(row_im, height, before)
    lower = banded(row_im, height, 0) + banded(row_re, height, before)
    row_mat = jnp.concatenate([upper, lower], axis=0).astype(jnp.bfloat16)
    col_re = banded(col_taps[0:1], LANES, 1)
    col_im = banded(col_taps[1:2], LANES, 1)
    upper = jnp.concatenate([col_re, -col_im], axis=1)
    lower = jnp.concatenate([col_im, col_re], axis=1)
    col_mat = jnp.concatenate([upper, lower], axis=0).astype(jnp.bfloat16)
    return row_mat, col_mat


def propagated(u_re, u_im, row_mat, col_mat, layer):
    height = layer_height(layer)
    block = block_height(layer)
    reach = block + 2 * KR
    parts = []
    for start in range(0, height, block):
        stacked = jnp.concatenate(
            [u_re[start : start + reach], u_im[start : start + reach]], axis=0
        )
        parts.append(
            jnp.dot(row_mat[:, : 2 * reach], stacked, preferred_element_type=jnp.float32)
        )
    rowed = jnp.concatenate(
        [part[:block] for part in parts] + [part[block:] for part in parts], axis=0
    )
    rowed = jnp.concatenate([rowed, jnp.zeros((2 * height, LANES), jnp.float32)], axis=1)
    rowed = pltpu.roll(rowed, HALF, 1).astype(jnp.bfloat16)
    windows = jnp.concatenate(
        [
            jnp.concatenate(
                [
                    rowed[:height, tile * LANES : (tile + 2) * LANES],
                    rowed[height:, tile * LANES : (tile + 2) * LANES],
                ],
                axis=1,
            )
            for tile in range(TILES)
        ],
        axis=0,
    )
    return lax.dot_general(
        windows, col_mat, (((1,), (1,)), ((), ())), preferred_element_type=jnp.float32
    )


def prepare_kernel(
    own, incident, far_odd, far_even, cross, in_chip, left_tab, right_tab,
    first, stereo, clear, col_mats, *row_mats
):
    low_near, high_near, low_far, high_far = ordered(in_chip, cross, far_even, far_odd)
    extended = []
    for part in range(2):
        pieces = [low_far, low_near, incident[...], high_near, high_far]
        pieces = [piece[part * BAND : (part + 1) * BAND] for piece in pieces]
        extended.append(jnp.concatenate(pieces, axis=0))
    row_mat, col_mat = filters(own[0, 0:16, COLS:].astype(jnp.float32), 0)
    first[...] = propagated(extended[0], extended[1], row_mat, col_mat, 0)
    for layer in range(1, LAYERS):
        row_mat, col_mat = filters(own[layer, 0:16, COLS:].astype(jnp.float32), layer)
        row_mats[layer - 1][...] = row_mat
        col_mats[layer - 1] = col_mat
    packed = jnp.concatenate([own[layer, :, :HALO_W] for layer in range(LAYERS)], axis=0)
    clear[...] = clear_pixels(packed[:, COLS : COLS + NH])
    tiles = stereo_tiles([packed[:, :COLS]], left_tab, right_tab)
    for tile in range(TILES):
        for part in range(2):
            block = tiles[
                tile * LANES : (tile + 1) * LANES, part * LANES : (part + 1) * LANES
            ]
            stereo[part, :, tile * LANES : (tile + 1) * LANES] = block


def chain_kernel(
    in_chip, cross, far_even, far_odd, left_tab, right_tab, first, stereo, clear, col_mats, *rest
):
    row_mats, outs, field = rest[: LAYERS - 1], rest[LAYERS - 1 : -1], rest[-1]
    depth = lax.axis_index("depth")
    low_near, high_near, low_far, high_far = ordered(in_chip, cross, far_even, far_odd)
    pieces = [
        low_far,
        low_near[0:BAND],
        high_near[0:BAND],
        high_far,
        low_near[BAND : 2 * BAND],
        high_near[BAND : 2 * BAND],
        low_near[2 * BAND : NEAR],
        high_near[2 * BAND : NEAR],
    ]
    halo = jnp.concatenate(pieces, axis=0)
    half = halo.shape[0] // 2
    halo_tiles = stereo_tiles(
        [halo[:half, :COLS], halo[half:, :COLS]], left_tab, right_tab
    )
    halo_clear = clear_pixels(halo[:, COLS : COLS + NH])
    begins = (0, half, half + 2 * BAND, 0)
    sides = (BAND + FAR, BAND, KR, 0)
    for layer in range(LAYERS):
        height = layer_height(layer)
        before = height + 2 * KR
        low, side = begins[layer], sides[layer]
        if layer == 0:
            columned = first
        else:
            columned = propagated(
                field[layer - 1, 0, :before],
                field[layer - 1, 1, :before],
                row_mats[layer - 1],
                col_mats[layer - 1],
                layer,
            )
        band = slice(layer * BAND, (layer + 1) * BAND)
        pieces = [clear[band]]
        if side:
            pieces = [halo_clear[low : low + side], clear[band], halo_clear[low + side : low + 2 * side]]
        passing = jnp.concatenate(pieces, axis=0)
        for tile in range(TILES):
            span = slice(tile * height, (tile + 1) * height)
            lanes = slice(tile * LANES, (tile + 1) * LANES)
            row = (low // half * TILES + tile) * half + low % half
            for part in range(2):
                within = slice(part * LANES, (part + 1) * LANES)
                pieces = [stereo[part, band, lanes]]
                if side:
                    pieces = [
                        halo_tiles[row : row + side, within],
                        stereo[part, band, lanes],
                        halo_tiles[row + side : row + 2 * side, within],
                    ]
                added = jnp.concatenate(pieces, axis=0)
                value = passing[:, lanes] * columned[span, within] + added
                field[layer, part, :height, lanes] = value.astype(jnp.bfloat16)
    for hop, out in enumerate(outs):
        layer = depth ^ hop
        start = pl.multiple_of((LAYERS - 1 - layer) * KR, KR)
        for part in range(2):
            out[part] = field[layer, part, pl.ds(start, BAND)]


def home_kernel(*refs):
    arrived, out, sems = refs[:LAYERS], refs[LAYERS], refs[LAYERS + 1]
    depth = lax.axis_index("depth")
    for colour in range(COLORS):
        for hop in range(LAYERS):

            @pl.when((depth ^ hop) == colour)
            def begin(hop=hop, colour=colour):
                pltpu.make_async_copy(arrived[hop], out.at[0, colour], sems.at[colour]).start()

    for colour in range(COLORS):
        pltpu.make_async_copy(arrived[0], out.at[0, colour], sems.at[colour]).wait()


def over_depth(value, hop):
    return lax.ppermute(value, "depth", [(i, i ^ hop) for i in range(LAYERS)])


def exchanged(value, by, phase):
    count, depths = lax.axis_size("rows"), lax.axis_size("depth")
    partner = {}
    for low in range(count - by):
        if (low // by) % 2 == phase:
            partner[low], partner[low + by] = low + by, low
    pairs = []
    for depth in range(depths):
        for band in range(count):
            if band in partner:
                to = (depth, partner[band])
            elif by > 1:
                to = (depth, band ^ 1)
            else:
                to = (depth ^ 1, band)
            pairs.append((depth * count + band, to[0] * count + to[1]))
    return lax.ppermute(value, ("depth", "rows"), pairs)


def neighbours(sent):
    in_chip, cross, far_even, far_odd = sent
    far_odd = exchanged(far_odd, 2, 1)
    far_even = exchanged(far_even, 2, 0)
    cross = exchanged(cross, 1, 1)
    in_chip = exchanged(in_chip, 1, 0)
    return in_chip, cross, far_even, far_odd


def call(
    kernel, out_shape, in_specs, scratch=(), flops=0, moved=10**6, limit=VMEM_LIMIT,
    out_space=pltpu.VMEM,
):
    vmem = pl.BlockSpec(memory_space=out_space)
    many = isinstance(out_shape, (tuple, list))
    return pl.pallas_call(
        kernel,
        out_shape=out_shape,
        in_specs=in_specs,
        out_specs=(vmem,) * len(out_shape) if many else vmem,
        scratch_shapes=scratch,
        compiler_params=pltpu.CompilerParams(vmem_limit_bytes=limit),
        cost_estimate=pl.CostEstimate(flops=flops, bytes_accessed=moved, transcendentals=0),
    )


def body(incident, row_taps, col_taps, hogel_light, silhouette, fill_counts, hogel_index):
    vmem = pl.BlockSpec(memory_space=pltpu.VMEM)
    hbm = pl.BlockSpec(memory_space=pltpu.HBM)
    bf16, f32 = jnp.bfloat16, jnp.float32
    shaped = jax.ShapeDtypeStruct
    held = [
        pltpu.VMEM(hogel_index.shape, jnp.int32),
        pltpu.SMEM(fill_counts.shape, jnp.int32),
        pltpu.VMEM(silhouette.shape, jnp.int32),
        pltpu.VMEM(row_taps.shape, bf16),
        pltpu.VMEM(col_taps.shape, bf16),
        pltpu.VMEM(hogel_light.shape, f32),
    ]
    *messages, mine = call(
        pack_kernel,
        (shaped((BAND, HALO_W), bf16),) * LAYERS + (shaped(incident.shape[1:], bf16),),
        [hbm] * 7,
        held + [pltpu.SemaphoreType.DMA((7,)), pltpu.VMEM((BAND, LANES), f32)],
        flops=10**7,
        limit=PACK_LIMIT,
    )(hogel_light, silhouette, fill_counts, hogel_index, row_taps, col_taps, incident)
    mine = mine.reshape(2 * BAND, COLS)
    layers_in = messages[:1] + [over_depth(messages[hop], hop) for hop in range(1, LAYERS)]
    arrived = neighbours((mine,) * 4)[::-1]
    near = shaped((NEAR, HALO_W), bf16)
    far = shaped((FAR, HALO_W), bf16)
    own, *sent = call(
        halo_kernel,
        (shaped((LAYERS, BAND, HALO_W), bf16), near, near, far, far),
        [vmem] * LAYERS,
    )(*layers_in)
    halos = neighbours(sent)
    right_tab = jnp.asarray(right_table())
    made = call(
        prepare_kernel,
        [
            shaped((TILES * layer_height(0), 2 * LANES), f32),
            shaped((2, LANES, COLS), f32),
            shaped((LANES, COLS), f32),
            shaped((LAYERS - 1, 2 * LANES, 4 * LANES), bf16),
        ]
        + [shaped((2 * block_height(layer), 2 * LANES), bf16) for layer in range(1, LAYERS)],
        [vmem] * 8,
        flops=10**9,
        moved=3 * 10**6,
    )(own, mine, *arrived, jnp.asarray(left_table(LANES)), right_tab)
    halo_rows = NEAR + FAR
    results = call(
        chain_kernel,
        [shaped((2, BAND, COLS), bf16)] * LAYERS,
        [vmem] * (6 + len(made)),
        [pltpu.VMEM((LAYERS, 2, layer_height(0), COLS), bf16)],
        flops=2 * 10**9,
        moved=3 * 10**6,
    )(*halos, jnp.asarray(left_table(halo_rows)), right_tab, *made)
    returned = [results[0]] + [over_depth(results[hop], hop) for hop in range(1, LAYERS)]
    return call(
        home_kernel,
        shaped((1, COLORS, 2, BAND, COLS), bf16),
        [vmem] * LAYERS,
        [pltpu.SemaphoreType.DMA((COLORS,))],
        out_space=pltpu.HBM,
    )(*returned)


def solution(mesh):
    placed = (
        P(None, None, "rows", None),
        P("depth", None, None, None),
        P("depth", None, None, None),
        P("depth", None, "rows", None),
        P("depth", "rows", None),
        P("depth", "rows"),
        P("depth", "rows", None),
    )
    return jax.shard_map(
        body,
        mesh=mesh,
        in_specs=placed,
        out_specs=P("depth", None, None, "rows", None),
        check_vma=False,
    )
```

```python
import math

import jax
import jax.numpy as jnp
import numpy as np
from jax import lax
from jax.experimental import pallas as pl
from jax.experimental.pallas import tpu as pltpu
from jax.sharding import PartitionSpec as P

HS = 16
KR = 16
KC = 63
COLORS = 3
LAYERS = 4
BAND = 32
COLS = 1024
NH = COLS // HS
LANES = 128
TILES = COLS // LANES
HALO_W = COLS + LANES
HALF = LANES // 2
NEAR = 2 * BAND + KR
FAR = KR
VMEM_LIMIT = 48 * 1024 * 1024
PACK_LIMIT = 63 * 1024 * 1024


def split_table(table):
    high = table.astype(jnp.bfloat16)
    low = (table - high.astype(np.float64)).astype(jnp.bfloat16)
    return high, low


def dft_pair():
    counter = np.arange(HS)
    angles = (counter[:, None] * counter[None, :] % HS) * (2.0 * math.pi / HS)
    return np.cos(angles) / math.sqrt(HS), np.sin(angles) / math.sqrt(HS)


def left_table(height):
    cos_tab, sin_tab = dft_pair()
    eye = np.eye(height // HS)
    full = np.concatenate([np.kron(eye, cos_tab), np.kron(eye, -sin_tab)], axis=0)
    return np.concatenate(split_table(full), axis=1)


def right_table():
    cos_tab, sin_tab = dft_pair()
    eye = np.eye(LANES // HS)
    cos_big, sin_big = np.kron(eye, cos_tab), np.kron(eye, sin_tab)
    full = np.concatenate(
        [
            np.concatenate([cos_big, -sin_big], axis=1),
            np.concatenate([sin_big, cos_big], axis=1),
        ],
        axis=0,
    )
    return full.astype(jnp.bfloat16)


def layer_height(layer):
    return BAND + 2 * KR * (LAYERS - 1 - layer)


def block_height(layer):
    height = layer_height(layer)
    return height // 2 if 2 * (height + 2 * KR) > 2 * LANES else height


def spread_matrix():
    tile = lax.broadcasted_iota(jnp.int32, (NH, COLS), 0)
    column = lax.broadcasted_iota(jnp.int32, (NH, COLS), 1)
    return jnp.where(column // HS == tile, 1.0, 0.0).astype(jnp.bfloat16)


def own_colour():
    return jnp.minimum(lax.axis_index("depth"), COLORS - 1)


def pack_kernel(light, edges, counts, listed, row_taps, col_taps, incident, *rest):
    outs, mine, held, sems, taps = rest[:LAYERS], rest[LAYERS], rest[5:11], rest[11], rest[12]
    depth = lax.axis_index("depth")
    picked = pltpu.make_async_copy(incident.at[own_colour()], mine, sems.at[6])
    sources = (listed, counts, edges, row_taps, col_taps, light)
    copies = [
        pltpu.make_async_copy(source, target, sems.at[place])
        for place, (source, target) in enumerate(zip(sources, held))
    ]
    for copy in reversed(copies):
        copy.start()
    picked.start()
    listed, counts, edges, row_taps, col_taps, light = held
    spread = spread_matrix()
    slot = lax.broadcasted_iota(jnp.int32, (NH, NH), 0)
    place = lax.broadcasted_iota(jnp.int32, (NH, NH), 1)
    for copy in copies[:5]:
        copy.wait()
    rows = []
    for group in range(BAND // HS):
        listing = jnp.broadcast_to(listed[0, group : group + 1, :], (NH, NH))
        column = jnp.sum(jnp.where(slot == place, listing, 0), axis=1, keepdims=True)
        named = (column == place) & (slot < counts[0, group])
        live = jnp.max(jnp.where(named, 1.0, 0.0), axis=0, keepdims=True)
        rows.append(jnp.broadcast_to(live, (HS, NH)))
    live_rows = jnp.concatenate(rows, axis=0).astype(jnp.bfloat16)
    live_pix = jnp.dot(live_rows, spread, preferred_element_type=jnp.float32)
    edge_tile = jnp.concatenate(
        [edges[0].astype(jnp.float32), jnp.zeros((BAND, LANES - NH), jnp.float32)], axis=1
    )
    left_half = lax.broadcasted_iota(jnp.int32, (BAND, LANES), 1) < HALF
    colours = [jnp.minimum(depth ^ hop, COLORS - 1) for hop in range(LAYERS)]
    for colour, out in zip(colours, outs):
        taps[...] = jnp.zeros_like(taps)
        taps[2:4, : 2 * KC + 1] = col_taps[0, colour].astype(jnp.float32)
        taps[4:6, : 2 * KR + 1] = row_taps[0, colour].astype(jnp.float32)
        turned = pltpu.roll(taps[0:8], HALF, 1)
        taps[0:2] = turned[2:4]
        taps[4:6] = turned[4:6]
        tile = jnp.where(left_half, edge_tile, taps[...])
        out[:, COLS:] = tile.astype(jnp.bfloat16)
    copies[5].wait()
    for colour, out in zip(colours, outs):
        out[:, :COLS] = (light[0, colour] * live_pix).astype(jnp.bfloat16)
    picked.wait()


def stay_kernel(message, here):
    here[...] = message[...]


def halo_kernel(*refs):
    arrived, (own, in_chip, cross, far_even, far_odd) = refs[:LAYERS], refs[LAYERS:]
    depth = lax.axis_index("depth")
    for hop in range(LAYERS):
        own[depth ^ hop] = arrived[hop][...]
    band = lax.axis_index("rows")
    core = band % 2
    odd = (band // 2) % 2
    last = BAND - KR
    for near, start in ((in_chip, (1 - core) * last), (cross, core * last)):
        near[0:BAND] = own[0, :, :HALO_W]
        near[BAND : 2 * BAND] = own[1, :, :HALO_W]
        near[2 * BAND : NEAR] = own[2, pl.ds(pl.multiple_of(start, KR), KR), :HALO_W]
    for far, start in ((far_even, (1 - odd) * last), (far_odd, odd * last)):
        far[...] = own[0, pl.ds(pl.multiple_of(start, KR), KR), :HALO_W]


def ordered(in_chip, cross, far_even, far_odd):
    band = lax.axis_index("rows")
    count = lax.axis_size("rows")
    even_core = band % 2 == 0
    even_chip = (band // 2) % 2 == 0

    def received(value, by, phase):
        lower = (band // by) % 2 == phase
        paired = jnp.where(lower, band + by < count, band >= by)
        value = value[...]
        return jnp.where(paired, value, jnp.zeros_like(value))

    in_chip, cross = received(in_chip, 1, 0), received(cross, 1, 1)
    far_even, far_odd = received(far_even, 2, 0), received(far_odd, 2, 1)
    return (
        jnp.where(even_core, cross, in_chip),
        jnp.where(even_core, in_chip, cross),
        jnp.where(even_chip, far_odd, far_even),
        jnp.where(even_chip, far_even, far_odd),
    )


def tiles_below(value, height):
    return jnp.concatenate(
        [
            jnp.concatenate(
                [
                    value[:height, tile * LANES : (tile + 1) * LANES],
                    value[height:, tile * LANES : (tile + 1) * LANES],
                ],
                axis=1,
            )
            for tile in range(TILES)
        ],
        axis=0,
    )


def stereo_tiles(blocks, left_tab, right_tab):
    arranged = []
    for light in blocks:
        doubled = jnp.concatenate([light, light], axis=0)
        left = jnp.dot(left_tab[...], doubled, preferred_element_type=jnp.float32)
        arranged.append(tiles_below(left.astype(jnp.bfloat16), light.shape[0]))
    arranged = jnp.concatenate(arranged, axis=0) if len(arranged) > 1 else arranged[0]
    return jnp.dot(arranged, right_tab[...], preferred_element_type=jnp.float32)


def clear_pixels(edges):
    edge_pix = jnp.dot(edges, spread_matrix(), preferred_element_type=jnp.float32)
    within = (lax.broadcasted_iota(jnp.int32, (1, COLS), 1) % HS).astype(jnp.float32)
    return jnp.where(within < edge_pix, 1.0, 0.0)


def banded(line, count, shift):
    base = jnp.concatenate([line, jnp.zeros((1, LANES), jnp.float32)], axis=1)
    base = jnp.broadcast_to(base, (count, 2 * LANES))
    return pltpu.roll(base, shift, 1, stride=1, stride_axis=0)


def filters(tile, layer):
    turned = pltpu.roll(tile[0:8], HALF, 1)
    left_half = lax.broadcasted_iota(jnp.int32, (2, LANES), 1) < HALF
    col_taps = jnp.where(left_half, turned[0:2], tile[2:4])
    row_taps = jnp.where(left_half, turned[4:6], 0.0)
    row_re, row_im = row_taps[0:1], row_taps[1:2]
    height = block_height(layer)
    before = height + 2 * KR
    upper = banded(row_re, height, 0) - banded(row_im, height, before)
    lower = banded(row_im, height, 0) + banded(row_re, height, before)
    row_mat = jnp.concatenate([upper, lower], axis=0).astype(jnp.bfloat16)
    col_re = banded(col_taps[0:1], LANES, 1)
    col_im = banded(col_taps[1:2], LANES, 1)
    upper = jnp.concatenate([col_re, -col_im], axis=1)
    lower = jnp.concatenate([col_im, col_re], axis=1)
    col_mat = jnp.concatenate([upper, lower], axis=0).astype(jnp.bfloat16)
    return row_mat, col_mat


def propagated(u_re, u_im, row_mat, col_mat, layer):
    height = layer_height(layer)
    block = block_height(layer)
    reach = block + 2 * KR
    parts = []
    for start in range(0, height, block):
        stacked = jnp.concatenate(
            [u_re[start : start + reach], u_im[start : start + reach]], axis=0
        )
        parts.append(
            jnp.dot(row_mat[:, : 2 * reach], stacked, preferred_element_type=jnp.float32)
        )
    rowed = jnp.concatenate(
        [part[:block] for part in parts] + [part[block:] for part in parts], axis=0
    )
    rowed = jnp.concatenate([rowed, jnp.zeros((2 * height, LANES), jnp.float32)], axis=1)
    rowed = pltpu.roll(rowed, HALF, 1).astype(jnp.bfloat16)
    windows = jnp.concatenate(
        [
            jnp.concatenate(
                [
                    rowed[:height, tile * LANES : (tile + 2) * LANES],
                    rowed[height:, tile * LANES : (tile + 2) * LANES],
                ],
                axis=1,
            )
            for tile in range(TILES)
        ],
        axis=0,
    )
    return lax.dot_general(
        windows, col_mat, (((1,), (1,)), ((), ())), preferred_element_type=jnp.float32
    )


def prepare_kernel(
    own, incident, far_odd, far_even, cross, in_chip, left_tab, right_tab,
    first, stereo, clear, col_mats, *row_mats
):
    low_near, high_near, low_far, high_far = ordered(in_chip, cross, far_even, far_odd)
    extended = []
    for part in range(2):
        pieces = [low_far, low_near, incident[...], high_near, high_far]
        pieces = [piece[part * BAND : (part + 1) * BAND] for piece in pieces]
        extended.append(jnp.concatenate(pieces, axis=0))
    row_mat, col_mat = filters(own[0, 0:16, COLS:].astype(jnp.float32), 0)
    first[...] = propagated(extended[0], extended[1], row_mat, col_mat, 0)
    for layer in range(1, LAYERS):
        row_mat, col_mat = filters(own[layer, 0:16, COLS:].astype(jnp.float32), layer)
        row_mats[layer - 1][...] = row_mat
        col_mats[layer - 1] = col_mat
    packed = jnp.concatenate([own[layer, :, :HALO_W] for layer in range(LAYERS)], axis=0)
    clear[...] = clear_pixels(packed[:, COLS : COLS + NH])
    tiles = stereo_tiles([packed[:, :COLS]], left_tab, right_tab)
    for tile in range(TILES):
        for part in range(2):
            block = tiles[
                tile * LANES : (tile + 1) * LANES, part * LANES : (part + 1) * LANES
            ]
            stereo[part, :, tile * LANES : (tile + 1) * LANES] = block


def chain_kernel(
    in_chip, cross, far_even, far_odd, left_tab, right_tab, first, stereo, clear, col_mats, *rest
):
    row_mats, outs, field = rest[: LAYERS - 1], rest[LAYERS - 1 : -1], rest[-1]
    depth = lax.axis_index("depth")
    low_near, high_near, low_far, high_far = ordered(in_chip, cross, far_even, far_odd)
    pieces = [
        low_far,
        low_near[0:BAND],
        high_near[0:BAND],
        high_far,
        low_near[BAND : 2 * BAND],
        high_near[BAND : 2 * BAND],
        low_near[2 * BAND : NEAR],
        high_near[2 * BAND : NEAR],
    ]
    halo = jnp.concatenate(pieces, axis=0)
    half = halo.shape[0] // 2
    halo_tiles = stereo_tiles(
        [halo[:half, :COLS], halo[half:, :COLS]], left_tab, right_tab
    )
    halo_clear = clear_pixels(halo[:, COLS : COLS + NH])
    begins = (0, half, half + 2 * BAND, 0)
    sides = (BAND + FAR, BAND, KR, 0)
    for layer in range(LAYERS):
        height = layer_height(layer)
        before = height + 2 * KR
        low, side = begins[layer], sides[layer]
        if layer == 0:
            columned = first
        else:
            columned = propagated(
                field[layer - 1, 0, :before],
                field[layer - 1, 1, :before],
                row_mats[layer - 1],
                col_mats[layer - 1],
                layer,
            )
        band = slice(layer * BAND, (layer + 1) * BAND)
        pieces = [clear[band]]
        if side:
            pieces = [halo_clear[low : low + side], clear[band], halo_clear[low + side : low + 2 * side]]
        passing = jnp.concatenate(pieces, axis=0)
        for tile in range(TILES):
            span = slice(tile * height, (tile + 1) * height)
            lanes = slice(tile * LANES, (tile + 1) * LANES)
            row = (low // half * TILES + tile) * half + low % half
            for part in range(2):
                within = slice(part * LANES, (part + 1) * LANES)
                pieces = [stereo[part, band, lanes]]
                if side:
                    pieces = [
                        halo_tiles[row : row + side, within],
                        stereo[part, band, lanes],
                        halo_tiles[row + side : row + 2 * side, within],
                    ]
                added = jnp.concatenate(pieces, axis=0)
                value = passing[:, lanes] * columned[span, within] + added
                field[layer, part, :height, lanes] = value.astype(jnp.bfloat16)
    for hop, out in enumerate(outs):
        layer = depth ^ hop
        start = pl.multiple_of((LAYERS - 1 - layer) * KR, KR)
        for part in range(2):
            out[part] = field[layer, part, pl.ds(start, BAND)]


def home_kernel(*refs):
    arrived, out, sems = refs[:LAYERS], refs[LAYERS], refs[LAYERS + 1]
    depth = lax.axis_index("depth")
    for colour in range(COLORS):
        for hop in range(LAYERS):

            @pl.when((depth ^ hop) == colour)
            def begin(hop=hop, colour=colour):
                pltpu.make_async_copy(arrived[hop], out.at[0, colour], sems.at[colour]).start()

    for colour in range(COLORS):
        pltpu.make_async_copy(arrived[0], out.at[0, colour], sems.at[colour]).wait()


def over_depth(value, hop):
    return lax.ppermute(value, "depth", [(i, i ^ hop) for i in range(LAYERS)])


def exchanged(value, by, phase):
    count, depths = lax.axis_size("rows"), lax.axis_size("depth")
    partner = {}
    for low in range(count - by):
        if (low // by) % 2 == phase:
            partner[low], partner[low + by] = low + by, low
    pairs = []
    for depth in range(depths):
        for band in range(count):
            if band in partner:
                to = (depth, partner[band])
            elif by > 1:
                to = (depth, band ^ 1)
            else:
                to = (depth ^ 1, band)
            pairs.append((depth * count + band, to[0] * count + to[1]))
    return lax.ppermute(value, ("depth", "rows"), pairs)


def neighbours(sent):
    in_chip, cross, far_even, far_odd = sent
    far_odd = exchanged(far_odd, 2, 1)
    far_even = exchanged(far_even, 2, 0)
    cross = exchanged(cross, 1, 1)
    in_chip = exchanged(in_chip, 1, 0)
    return in_chip, cross, far_even, far_odd


def call(
    kernel, out_shape, in_specs, scratch=(), flops=0, moved=10**6, limit=VMEM_LIMIT,
    out_space=pltpu.VMEM,
):
    vmem = pl.BlockSpec(memory_space=out_space)
    many = isinstance(out_shape, (tuple, list))
    return pl.pallas_call(
        kernel,
        out_shape=out_shape,
        in_specs=in_specs,
        out_specs=(vmem,) * len(out_shape) if many else vmem,
        scratch_shapes=scratch,
        compiler_params=pltpu.CompilerParams(vmem_limit_bytes=limit),
        cost_estimate=pl.CostEstimate(flops=flops, bytes_accessed=moved, transcendentals=0),
    )


def body(incident, row_taps, col_taps, hogel_light, silhouette, fill_counts, hogel_index):
    vmem = pl.BlockSpec(memory_space=pltpu.VMEM)
    hbm = pl.BlockSpec(memory_space=pltpu.HBM)
    bf16, f32 = jnp.bfloat16, jnp.float32
    shaped = jax.ShapeDtypeStruct
    held = [
        pltpu.VMEM(hogel_index.shape, jnp.int32),
        pltpu.SMEM(fill_counts.shape, jnp.int32),
        pltpu.VMEM(silhouette.shape, jnp.int32),
        pltpu.VMEM(row_taps.shape, bf16),
        pltpu.VMEM(col_taps.shape, bf16),
        pltpu.VMEM(hogel_light.shape, f32),
    ]
    *messages, mine = call(
        pack_kernel,
        (shaped((BAND, HALO_W), bf16),) * LAYERS + (shaped(incident.shape[1:], bf16),),
        [hbm] * 7,
        held + [pltpu.SemaphoreType.DMA((7,)), pltpu.VMEM((BAND, LANES), f32)],
        flops=10**7,
        limit=PACK_LIMIT,
    )(hogel_light, silhouette, fill_counts, hogel_index, row_taps, col_taps, incident)
    mine = mine.reshape(2 * BAND, COLS)
    kept = call(stay_kernel, shaped((BAND, HALO_W), bf16), [vmem], moved=10**5)(messages[0])
    layers_in = [kept] + [over_depth(messages[hop], hop) for hop in range(1, LAYERS)]
    arrived = neighbours((mine,) * 4)[::-1]
    near = shaped((NEAR, HALO_W), bf16)
    far = shaped((FAR, HALO_W), bf16)
    own, *sent = call(
        halo_kernel,
        (shaped((LAYERS, BAND, HALO_W), bf16), near, near, far, far),
        [vmem] * LAYERS,
    )(*layers_in)
    halos = neighbours(sent)
    right_tab = jnp.asarray(right_table())
    made = call(
        prepare_kernel,
        [
            shaped((TILES * layer_height(0), 2 * LANES), f32),
            shaped((2, LANES, COLS), f32),
            shaped((LANES, COLS), f32),
            shaped((LAYERS - 1, 2 * LANES, 4 * LANES), bf16),
        ]
        + [shaped((2 * block_height(layer), 2 * LANES), bf16) for layer in range(1, LAYERS)],
        [vmem] * 8,
        flops=10**9,
        moved=3 * 10**6,
    )(own, mine, *arrived, jnp.asarray(left_table(LANES)), right_tab)
    halo_rows = NEAR + FAR
    results = call(
        chain_kernel,
        [shaped((2, BAND, COLS), bf16)] * LAYERS,
        [vmem] * (6 + len(made)),
        [pltpu.VMEM((LAYERS, 2, layer_height(0), COLS), bf16)],
        flops=2 * 10**9,
        moved=3 * 10**6,
    )(*halos, jnp.asarray(left_table(halo_rows)), right_tab, *made)
    returned = [results[0]] + [over_depth(results[hop], hop) for hop in range(1, LAYERS)]
    return call(
        home_kernel,
        shaped((1, COLORS, 2, BAND, COLS), bf16),
        [vmem] * LAYERS,
        [pltpu.SemaphoreType.DMA((COLORS,))],
        out_space=pltpu.HBM,
    )(*returned)


def solution(mesh):
    placed = (
        P(None, None, "rows", None),
        P("depth", None, None, None),
        P("depth", None, None, None),
        P("depth", None, "rows", None),
        P("depth", "rows", None),
        P("depth", "rows"),
        P("depth", "rows", None),
    )
    return jax.shard_map(
        body,
        mesh=mesh,
        in_specs=placed,
        out_specs=P("depth", None, None, "rows", None),
        check_vma=False,
    )
```

```python
import math

import jax
import jax.numpy as jnp
import numpy as np
from jax import lax
from jax.experimental import pallas as pl
from jax.experimental.pallas import tpu as pltpu
from jax.sharding import PartitionSpec as P

HS = 16
KR = 16
KC = 63
COLORS = 3
LAYERS = 4
BAND = 32
COLS = 1024
NH = COLS // HS
LANES = 128
TILES = COLS // LANES
HALO_W = COLS + LANES
HALF = LANES // 2
NEAR = 2 * BAND + KR
FAR = KR
VMEM_LIMIT = 48 * 1024 * 1024
PACK_LIMIT = 63 * 1024 * 1024


def split_table(table):
    high = table.astype(jnp.bfloat16)
    low = (table - high.astype(np.float64)).astype(jnp.bfloat16)
    return high, low


def dft_pair():
    counter = np.arange(HS)
    angles = (counter[:, None] * counter[None, :] % HS) * (2.0 * math.pi / HS)
    return np.cos(angles) / math.sqrt(HS), np.sin(angles) / math.sqrt(HS)


def left_table(height):
    cos_tab, sin_tab = dft_pair()
    eye = np.eye(height // HS)
    full = np.concatenate([np.kron(eye, cos_tab), np.kron(eye, -sin_tab)], axis=0)
    return np.concatenate(split_table(full), axis=1)


def right_table():
    cos_tab, sin_tab = dft_pair()
    eye = np.eye(LANES // HS)
    cos_big, sin_big = np.kron(eye, cos_tab), np.kron(eye, sin_tab)
    full = np.concatenate(
        [
            np.concatenate([cos_big, -sin_big], axis=1),
            np.concatenate([sin_big, cos_big], axis=1),
        ],
        axis=0,
    )
    return full.astype(jnp.bfloat16)


def layer_height(layer):
    return BAND + 2 * KR * (LAYERS - 1 - layer)


def block_height(layer):
    height = layer_height(layer)
    return height // 2 if 2 * (height + 2 * KR) > 2 * LANES else height


def spread_matrix():
    tile = lax.broadcasted_iota(jnp.int32, (NH, COLS), 0)
    column = lax.broadcasted_iota(jnp.int32, (NH, COLS), 1)
    return jnp.where(column // HS == tile, 1.0, 0.0).astype(jnp.bfloat16)


def own_colour():
    return jnp.minimum(lax.axis_index("depth"), COLORS - 1)


def pack_kernel(light, edges, counts, listed, row_taps, col_taps, incident, *rest):
    outs, mine, held, sems, taps = rest[:LAYERS], rest[LAYERS], rest[5:11], rest[11], rest[12]
    depth = lax.axis_index("depth")
    picked = pltpu.make_async_copy(incident.at[own_colour()], mine, sems.at[6])
    sources = (listed, counts, edges, row_taps, col_taps, light)
    copies = [
        pltpu.make_async_copy(source, target, sems.at[place])
        for place, (source, target) in enumerate(zip(sources, held))
    ]
    for copy in reversed(copies):
        copy.start()
    picked.start()
    listed, counts, edges, row_taps, col_taps, light = held
    spread = spread_matrix()
    slot = lax.broadcasted_iota(jnp.int32, (NH, NH), 0)
    place = lax.broadcasted_iota(jnp.int32, (NH, NH), 1)
    for copy in copies[:5]:
        copy.wait()
    rows = []
    for group in range(BAND // HS):
        listing = jnp.broadcast_to(listed[0, group : group + 1, :], (NH, NH))
        column = jnp.sum(jnp.where(slot == place, listing, 0), axis=1, keepdims=True)
        named = (column == place) & (slot < counts[0, group])
        live = jnp.max(jnp.where(named, 1.0, 0.0), axis=0, keepdims=True)
        rows.append(jnp.broadcast_to(live, (HS, NH)))
    live_rows = jnp.concatenate(rows, axis=0).astype(jnp.bfloat16)
    live_pix = jnp.dot(live_rows, spread, preferred_element_type=jnp.float32)
    edge_tile = jnp.concatenate(
        [edges[0].astype(jnp.float32), jnp.zeros((BAND, LANES - NH), jnp.float32)], axis=1
    )
    left_half = lax.broadcasted_iota(jnp.int32, (BAND, LANES), 1) < HALF
    colours = [jnp.minimum(depth ^ hop, COLORS - 1) for hop in range(LAYERS)]
    for colour, out in zip(colours, outs):
        taps[...] = jnp.zeros_like(taps)
        taps[2:4, : 2 * KC + 1] = col_taps[0, colour].astype(jnp.float32)
        taps[4:6, : 2 * KR + 1] = row_taps[0, colour].astype(jnp.float32)
        turned = pltpu.roll(taps[0:8], HALF, 1)
        taps[0:2] = turned[2:4]
        taps[4:6] = turned[4:6]
        tile = jnp.where(left_half, edge_tile, taps[...])
        out[:, COLS:] = tile.astype(jnp.bfloat16)
    copies[5].wait()
    for colour, out in zip(colours, outs):
        out[:, :COLS] = (light[0, colour] * live_pix).astype(jnp.bfloat16)
    picked.wait()


def stay_kernel(message, here):
    here[...] = message[...]


def halo_kernel(*refs):
    arrived, (own, in_chip, cross, far_even, far_odd) = refs[:LAYERS], refs[LAYERS:]
    depth = lax.axis_index("depth")
    for place, hop in enumerate((0, 3, 1, 2)):
        own[depth ^ hop] = arrived[place][...]
    band = lax.axis_index("rows")
    core = band % 2
    odd = (band // 2) % 2
    last = BAND - KR
    for near, start in ((in_chip, (1 - core) * last), (cross, core * last)):
        near[0:BAND] = own[0, :, :HALO_W]
        near[BAND : 2 * BAND] = own[1, :, :HALO_W]
        near[2 * BAND : NEAR] = own[2, pl.ds(pl.multiple_of(start, KR), KR), :HALO_W]
    for far, start in ((far_even, (1 - odd) * last), (far_odd, odd * last)):
        far[...] = own[0, pl.ds(pl.multiple_of(start, KR), KR), :HALO_W]


def ordered(in_chip, cross, far_even, far_odd):
    band = lax.axis_index("rows")
    count = lax.axis_size("rows")
    even_core = band % 2 == 0
    even_chip = (band // 2) % 2 == 0

    def received(value, by, phase):
        lower = (band // by) % 2 == phase
        paired = jnp.where(lower, band + by < count, band >= by)
        value = value[...]
        return jnp.where(paired, value, jnp.zeros_like(value))

    in_chip, cross = received(in_chip, 1, 0), received(cross, 1, 1)
    far_even, far_odd = received(far_even, 2, 0), received(far_odd, 2, 1)
    return (
        jnp.where(even_core, cross, in_chip),
        jnp.where(even_core, in_chip, cross),
        jnp.where(even_chip, far_odd, far_even),
        jnp.where(even_chip, far_even, far_odd),
    )


def tiles_below(value, height):
    return jnp.concatenate(
        [
            jnp.concatenate(
                [
                    value[:height, tile * LANES : (tile + 1) * LANES],
                    value[height:, tile * LANES : (tile + 1) * LANES],
                ],
                axis=1,
            )
            for tile in range(TILES)
        ],
        axis=0,
    )


def stereo_tiles(blocks, left_tab, right_tab):
    arranged = []
    for light in blocks:
        doubled = jnp.concatenate([light, light], axis=0)
        left = jnp.dot(left_tab[...], doubled, preferred_element_type=jnp.float32)
        arranged.append(tiles_below(left.astype(jnp.bfloat16), light.shape[0]))
    arranged = jnp.concatenate(arranged, axis=0) if len(arranged) > 1 else arranged[0]
    return jnp.dot(arranged, right_tab[...], preferred_element_type=jnp.float32)


def clear_pixels(edges):
    edge_pix = jnp.dot(edges, spread_matrix(), preferred_element_type=jnp.float32)
    within = (lax.broadcasted_iota(jnp.int32, (1, COLS), 1) % HS).astype(jnp.float32)
    return jnp.where(within < edge_pix, 1.0, 0.0)


def banded(line, count, shift):
    base = jnp.concatenate([line, jnp.zeros((1, LANES), jnp.float32)], axis=1)
    base = jnp.broadcast_to(base, (count, 2 * LANES))
    return pltpu.roll(base, shift, 1, stride=1, stride_axis=0)


def filters(tile, layer):
    turned = pltpu.roll(tile[0:8], HALF, 1)
    left_half = lax.broadcasted_iota(jnp.int32, (2, LANES), 1) < HALF
    col_taps = jnp.where(left_half, turned[0:2], tile[2:4])
    row_taps = jnp.where(left_half, turned[4:6], 0.0)
    row_re, row_im = row_taps[0:1], row_taps[1:2]
    height = block_height(layer)
    before = height + 2 * KR
    upper = banded(row_re, height, 0) - banded(row_im, height, before)
    lower = banded(row_im, height, 0) + banded(row_re, height, before)
    row_mat = jnp.concatenate([upper, lower], axis=0).astype(jnp.bfloat16)
    col_re = banded(col_taps[0:1], LANES, 1)
    col_im = banded(col_taps[1:2], LANES, 1)
    upper = jnp.concatenate([col_re, -col_im], axis=1)
    lower = jnp.concatenate([col_im, col_re], axis=1)
    col_mat = jnp.concatenate([upper, lower], axis=0).astype(jnp.bfloat16)
    return row_mat, col_mat


def propagated(u_re, u_im, row_mat, col_mat, layer):
    height = layer_height(layer)
    block = block_height(layer)
    reach = block + 2 * KR
    parts = []
    for start in range(0, height, block):
        stacked = jnp.concatenate(
            [u_re[start : start + reach], u_im[start : start + reach]], axis=0
        )
        parts.append(
            jnp.dot(row_mat[:, : 2 * reach], stacked, preferred_element_type=jnp.float32)
        )
    rowed = jnp.concatenate(
        [part[:block] for part in parts] + [part[block:] for part in parts], axis=0
    )
    rowed = jnp.concatenate([rowed, jnp.zeros((2 * height, LANES), jnp.float32)], axis=1)
    rowed = pltpu.roll(rowed, HALF, 1).astype(jnp.bfloat16)
    windows = jnp.concatenate(
        [
            jnp.concatenate(
                [
                    rowed[:height, tile * LANES : (tile + 2) * LANES],
                    rowed[height:, tile * LANES : (tile + 2) * LANES],
                ],
                axis=1,
            )
            for tile in range(TILES)
        ],
        axis=0,
    )
    return lax.dot_general(
        windows, col_mat, (((1,), (1,)), ((), ())), preferred_element_type=jnp.float32
    )


def prepare_kernel(
    own, incident, far_odd, far_even, cross, in_chip, left_tab, right_tab,
    first, stereo, clear, col_mats, *row_mats
):
    low_near, high_near, low_far, high_far = ordered(in_chip, cross, far_even, far_odd)
    extended = []
    for part in range(2):
        pieces = [low_far, low_near, incident[...], high_near, high_far]
        pieces = [piece[part * BAND : (part + 1) * BAND] for piece in pieces]
        extended.append(jnp.concatenate(pieces, axis=0))
    row_mat, col_mat = filters(own[0, 0:16, COLS:].astype(jnp.float32), 0)
    first[...] = propagated(extended[0], extended[1], row_mat, col_mat, 0)
    for layer in range(1, LAYERS):
        row_mat, col_mat = filters(own[layer, 0:16, COLS:].astype(jnp.float32), layer)
        row_mats[layer - 1][...] = row_mat
        col_mats[layer - 1] = col_mat
    packed = jnp.concatenate([own[layer, :, :HALO_W] for layer in range(LAYERS)], axis=0)
    clear[...] = clear_pixels(packed[:, COLS : COLS + NH])
    tiles = stereo_tiles([packed[:, :COLS]], left_tab, right_tab)
    for tile in range(TILES):
        for part in range(2):
            block = tiles[
                tile * LANES : (tile + 1) * LANES, part * LANES : (part + 1) * LANES
            ]
            stereo[part, :, tile * LANES : (tile + 1) * LANES] = block


def chain_kernel(
    in_chip, cross, far_even, far_odd, left_tab, right_tab, first, stereo, clear, col_mats, *rest
):
    row_mats, outs, field = rest[: LAYERS - 1], rest[LAYERS - 1 : -1], rest[-1]
    depth = lax.axis_index("depth")
    low_near, high_near, low_far, high_far = ordered(in_chip, cross, far_even, far_odd)
    pieces = [
        low_far,
        low_near[0:BAND],
        high_near[0:BAND],
        high_far,
        low_near[BAND : 2 * BAND],
        high_near[BAND : 2 * BAND],
        low_near[2 * BAND : NEAR],
        high_near[2 * BAND : NEAR],
    ]
    halo = jnp.concatenate(pieces, axis=0)
    half = halo.shape[0] // 2
    halo_tiles = stereo_tiles(
        [halo[:half, :COLS], halo[half:, :COLS]], left_tab, right_tab
    )
    halo_clear = clear_pixels(halo[:, COLS : COLS + NH])
    begins = (0, half, half + 2 * BAND, 0)
    sides = (BAND + FAR, BAND, KR, 0)
    for layer in range(LAYERS):
        height = layer_height(layer)
        before = height + 2 * KR
        low, side = begins[layer], sides[layer]
        if layer == 0:
            columned = first
        else:
            columned = propagated(
                field[layer - 1, 0, :before],
                field[layer - 1, 1, :before],
                row_mats[layer - 1],
                col_mats[layer - 1],
                layer,
            )
        band = slice(layer * BAND, (layer + 1) * BAND)
        pieces = [clear[band]]
        if side:
            pieces = [halo_clear[low : low + side], clear[band], halo_clear[low + side : low + 2 * side]]
        passing = jnp.concatenate(pieces, axis=0)
        for tile in range(TILES):
            span = slice(tile * height, (tile + 1) * height)
            lanes = slice(tile * LANES, (tile + 1) * LANES)
            row = (low // half * TILES + tile) * half + low % half
            for part in range(2):
                within = slice(part * LANES, (part + 1) * LANES)
                pieces = [stereo[part, band, lanes]]
                if side:
                    pieces = [
                        halo_tiles[row : row + side, within],
                        stereo[part, band, lanes],
                        halo_tiles[row + side : row + 2 * side, within],
                    ]
                added = jnp.concatenate(pieces, axis=0)
                value = passing[:, lanes] * columned[span, within] + added
                field[layer, part, :height, lanes] = value.astype(jnp.bfloat16)
    for hop, out in enumerate(outs):
        layer = depth ^ hop
        start = pl.multiple_of((LAYERS - 1 - layer) * KR, KR)
        for part in range(2):
            out[part] = field[layer, part, pl.ds(start, BAND)]


def home_kernel(*refs):
    arrived, out, sems = refs[:LAYERS], refs[LAYERS], refs[LAYERS + 1]
    depth = lax.axis_index("depth")
    for colour in range(COLORS):
        for hop in range(LAYERS):

            @pl.when((depth ^ hop) == colour)
            def begin(hop=hop, colour=colour):
                pltpu.make_async_copy(arrived[hop], out.at[0, colour], sems.at[colour]).start()

    for colour in range(COLORS):
        pltpu.make_async_copy(arrived[0], out.at[0, colour], sems.at[colour]).wait()


def over_depth(value, hop):
    return lax.ppermute(value, "depth", [(i, i ^ hop) for i in range(LAYERS)])


def exchanged(value, by, phase):
    count, depths = lax.axis_size("rows"), lax.axis_size("depth")
    partner = {}
    for low in range(count - by):
        if (low // by) % 2 == phase:
            partner[low], partner[low + by] = low + by, low
    pairs = []
    for depth in range(depths):
        for band in range(count):
            if band in partner:
                to = (depth, partner[band])
            elif by > 1:
                to = (depth, band ^ 1)
            else:
                to = (depth ^ 1, band)
            pairs.append((depth * count + band, to[0] * count + to[1]))
    return lax.ppermute(value, ("depth", "rows"), pairs)


def neighbours(sent):
    in_chip, cross, far_even, far_odd = sent
    far_odd = exchanged(far_odd, 2, 1)
    far_even = exchanged(far_even, 2, 0)
    cross = exchanged(cross, 1, 1)
    in_chip = exchanged(in_chip, 1, 0)
    return in_chip, cross, far_even, far_odd


def call(
    kernel, out_shape, in_specs, scratch=(), flops=0, moved=10**6, limit=VMEM_LIMIT,
    out_space=pltpu.VMEM,
):
    vmem = pl.BlockSpec(memory_space=out_space)
    many = isinstance(out_shape, (tuple, list))
    return pl.pallas_call(
        kernel,
        out_shape=out_shape,
        in_specs=in_specs,
        out_specs=(vmem,) * len(out_shape) if many else vmem,
        scratch_shapes=scratch,
        compiler_params=pltpu.CompilerParams(vmem_limit_bytes=limit),
        cost_estimate=pl.CostEstimate(flops=flops, bytes_accessed=moved, transcendentals=0),
    )


def body(incident, row_taps, col_taps, hogel_light, silhouette, fill_counts, hogel_index):
    vmem = pl.BlockSpec(memory_space=pltpu.VMEM)
    hbm = pl.BlockSpec(memory_space=pltpu.HBM)
    bf16, f32 = jnp.bfloat16, jnp.float32
    shaped = jax.ShapeDtypeStruct
    held = [
        pltpu.VMEM(hogel_index.shape, jnp.int32),
        pltpu.SMEM(fill_counts.shape, jnp.int32),
        pltpu.VMEM(silhouette.shape, jnp.int32),
        pltpu.VMEM(row_taps.shape, bf16),
        pltpu.VMEM(col_taps.shape, bf16),
        pltpu.VMEM(hogel_light.shape, f32),
    ]
    *messages, mine = call(
        pack_kernel,
        (shaped((BAND, HALO_W), bf16),) * LAYERS + (shaped(incident.shape[1:], bf16),),
        [hbm] * 7,
        held + [pltpu.SemaphoreType.DMA((7,)), pltpu.VMEM((BAND, LANES), f32)],
        flops=10**7,
        limit=PACK_LIMIT,
    )(hogel_light, silhouette, fill_counts, hogel_index, row_taps, col_taps, incident)
    mine = mine.reshape(2 * BAND, COLS)
    kept = call(stay_kernel, shaped((BAND, HALO_W), bf16), [vmem], moved=10**5)(messages[0])
    diagonal = over_depth(messages[3], 3)
    layers_in = [kept, over_depth(messages[1], 1), over_depth(messages[2], 2), diagonal]
    arrived = neighbours((mine,) * 4)[::-1]
    near = shaped((NEAR, HALO_W), bf16)
    far = shaped((FAR, HALO_W), bf16)
    own, *sent = call(
        halo_kernel,
        (shaped((LAYERS, BAND, HALO_W), bf16), near, near, far, far),
        [vmem] * LAYERS,
    )(layers_in[0], layers_in[3], layers_in[1], layers_in[2])
    halos = neighbours(sent)
    right_tab = jnp.asarray(right_table())
    made = call(
        prepare_kernel,
        [
            shaped((TILES * layer_height(0), 2 * LANES), f32),
            shaped((2, LANES, COLS), f32),
            shaped((LANES, COLS), f32),
            shaped((LAYERS - 1, 2 * LANES, 4 * LANES), bf16),
        ]
        + [shaped((2 * block_height(layer), 2 * LANES), bf16) for layer in range(1, LAYERS)],
        [vmem] * 8,
        flops=10**9,
        moved=3 * 10**6,
    )(own, mine, *arrived, jnp.asarray(left_table(LANES)), right_tab)
    halo_rows = NEAR + FAR
    results = call(
        chain_kernel,
        [shaped((2, BAND, COLS), bf16)] * LAYERS,
        [vmem] * (6 + len(made)),
        [pltpu.VMEM((LAYERS, 2, layer_height(0), COLS), bf16)],
        flops=2 * 10**9,
        moved=3 * 10**6,
    )(*halos, jnp.asarray(left_table(halo_rows)), right_tab, *made)
    returned = [results[0]] + [over_depth(results[hop], hop) for hop in range(1, LAYERS)]
    return call(
        home_kernel,
        shaped((1, COLORS, 2, BAND, COLS), bf16),
        [vmem] * LAYERS,
        [pltpu.SemaphoreType.DMA((COLORS,))],
        out_space=pltpu.HBM,
    )(*returned)


def solution(mesh):
    placed = (
        P(None, None, "rows", None),
        P("depth", None, None, None),
        P("depth", None, None, None),
        P("depth", None, "rows", None),
        P("depth", "rows", None),
        P("depth", "rows"),
        P("depth", "rows", None),
    )
    return jax.shard_map(
        body,
        mesh=mesh,
        in_specs=placed,
        out_specs=P("depth", None, None, "rows", None),
        check_vma=False,
    )
```

```python
import math

import jax
import jax.numpy as jnp
import numpy as np
from jax import lax
from jax.experimental import pallas as pl
from jax.experimental.pallas import tpu as pltpu
from jax.sharding import PartitionSpec as P

HS = 16
KR = 16
KC = 63
COLORS = 3
LAYERS = 4
BAND = 32
COLS = 1024
NH = COLS // HS
LANES = 128
TILES = COLS // LANES
HALO_W = COLS + LANES
HALF = LANES // 2
NEAR = 2 * BAND + KR
FAR = KR
VMEM_LIMIT = 48 * 1024 * 1024
PACK_LIMIT = 63 * 1024 * 1024


def split_table(table):
    high = table.astype(jnp.bfloat16)
    low = (table - high.astype(np.float64)).astype(jnp.bfloat16)
    return high, low


def dft_pair():
    counter = np.arange(HS)
    angles = (counter[:, None] * counter[None, :] % HS) * (2.0 * math.pi / HS)
    return np.cos(angles) / math.sqrt(HS), np.sin(angles) / math.sqrt(HS)


def left_table(height):
    cos_tab, sin_tab = dft_pair()
    eye = np.eye(height // HS)
    full = np.concatenate([np.kron(eye, cos_tab), np.kron(eye, -sin_tab)], axis=0)
    return np.concatenate(split_table(full), axis=1)


def right_table():
    cos_tab, sin_tab = dft_pair()
    eye = np.eye(LANES // HS)
    cos_big, sin_big = np.kron(eye, cos_tab), np.kron(eye, sin_tab)
    full = np.concatenate(
        [
            np.concatenate([cos_big, -sin_big], axis=1),
            np.concatenate([sin_big, cos_big], axis=1),
        ],
        axis=0,
    )
    return full.astype(jnp.bfloat16)


def layer_height(layer):
    return BAND + 2 * KR * (LAYERS - 1 - layer)


def block_height(layer):
    height = layer_height(layer)
    return height // 2 if 2 * (height + 2 * KR) > 2 * LANES else height


def spread_matrix():
    tile = lax.broadcasted_iota(jnp.int32, (NH, COLS), 0)
    column = lax.broadcasted_iota(jnp.int32, (NH, COLS), 1)
    return jnp.where(column // HS == tile, 1.0, 0.0).astype(jnp.bfloat16)


def own_colour():
    return jnp.minimum(lax.axis_index("depth"), COLORS - 1)


def pack_kernel(light, edges, counts, listed, row_taps, col_taps, incident, *rest):
    outs, mine, held, sems, taps = rest[:LAYERS], rest[LAYERS], rest[5:11], rest[11], rest[12]
    depth = lax.axis_index("depth")
    picked = pltpu.make_async_copy(incident.at[own_colour()], mine, sems.at[6])
    sources = (listed, counts, edges, row_taps, col_taps, light)
    copies = [
        pltpu.make_async_copy(source, target, sems.at[place])
        for place, (source, target) in enumerate(zip(sources, held))
    ]
    for copy in reversed(copies):
        copy.start()
    picked.start()
    listed, counts, edges, row_taps, col_taps, light = held
    spread = spread_matrix()
    slot = lax.broadcasted_iota(jnp.int32, (NH, NH), 0)
    place = lax.broadcasted_iota(jnp.int32, (NH, NH), 1)
    for copy in copies[:5]:
        copy.wait()
    rows = []
    for group in range(BAND // HS):
        listing = jnp.broadcast_to(listed[0, group : group + 1, :], (NH, NH))
        column = jnp.sum(jnp.where(slot == place, listing, 0), axis=1, keepdims=True)
        named = (column == place) & (slot < counts[0, group])
        live = jnp.max(jnp.where(named, 1.0, 0.0), axis=0, keepdims=True)
        rows.append(jnp.broadcast_to(live, (HS, NH)))
    live_rows = jnp.concatenate(rows, axis=0).astype(jnp.bfloat16)
    live_pix = jnp.dot(live_rows, spread, preferred_element_type=jnp.float32)
    edge_tile = jnp.concatenate(
        [edges[0].astype(jnp.float32), jnp.zeros((BAND, LANES - NH), jnp.float32)], axis=1
    )
    left_half = lax.broadcasted_iota(jnp.int32, (BAND, LANES), 1) < HALF
    colours = [jnp.minimum(depth ^ hop, COLORS - 1) for hop in range(LAYERS)]
    for colour, out in zip(colours, outs):
        taps[...] = jnp.zeros_like(taps)
        taps[2:4, : 2 * KC + 1] = col_taps[0, colour].astype(jnp.float32)
        taps[4:6, : 2 * KR + 1] = row_taps[0, colour].astype(jnp.float32)
        turned = pltpu.roll(taps[0:8], HALF, 1)
        taps[0:2] = turned[2:4]
        taps[4:6] = turned[4:6]
        tile = jnp.where(left_half, edge_tile, taps[...])
        out[:, COLS:] = tile.astype(jnp.bfloat16)
    copies[5].wait()
    for colour, out in zip(colours, outs):
        out[:, :COLS] = (light[0, colour] * live_pix).astype(jnp.bfloat16)
    picked.wait()


def stay_kernel(message, here):
    here[...] = message[...]


def halo_kernel(*refs):
    arrived, (own, in_chip, cross, far_even, far_odd) = refs[:LAYERS], refs[LAYERS:]
    depth = lax.axis_index("depth")
    for hop in range(LAYERS):
        own[depth ^ hop] = arrived[hop][...]
    band = lax.axis_index("rows")
    core = band % 2
    odd = (band // 2) % 2
    last = BAND - KR
    for near, start in ((in_chip, (1 - core) * last), (cross, core * last)):
        near[0:BAND] = own[0, :, :HALO_W]
        near[BAND : 2 * BAND] = own[1, :, :HALO_W]
        near[2 * BAND : NEAR] = own[2, pl.ds(pl.multiple_of(start, KR), KR), :HALO_W]
    for far, start in ((far_even, (1 - odd) * last), (far_odd, odd * last)):
        far[...] = own[0, pl.ds(pl.multiple_of(start, KR), KR), :HALO_W]


def ordered(in_chip, cross, far_even, far_odd):
    band = lax.axis_index("rows")
    count = lax.axis_size("rows")
    even_core = band % 2 == 0
    even_chip = (band // 2) % 2 == 0

    def received(value, by, phase):
        lower = (band // by) % 2 == phase
        paired = jnp.where(lower, band + by < count, band >= by)
        value = value[...]
        return jnp.where(paired, value, jnp.zeros_like(value))

    in_chip, cross = received(in_chip, 1, 0), received(cross, 1, 1)
    far_even, far_odd = received(far_even, 2, 0), received(far_odd, 2, 1)
    return (
        jnp.where(even_core, cross, in_chip),
        jnp.where(even_core, in_chip, cross),
        jnp.where(even_chip, far_odd, far_even),
        jnp.where(even_chip, far_even, far_odd),
    )


def tiles_below(value, height):
    return jnp.concatenate(
        [
            jnp.concatenate(
                [
                    value[:height, tile * LANES : (tile + 1) * LANES],
                    value[height:, tile * LANES : (tile + 1) * LANES],
                ],
                axis=1,
            )
            for tile in range(TILES)
        ],
        axis=0,
    )


def stereo_tiles(blocks, left_tab, right_tab):
    arranged = []
    for light in blocks:
        doubled = jnp.concatenate([light, light], axis=0)
        left = jnp.dot(left_tab[...], doubled, preferred_element_type=jnp.float32)
        arranged.append(tiles_below(left.astype(jnp.bfloat16), light.shape[0]))
    arranged = jnp.concatenate(arranged, axis=0) if len(arranged) > 1 else arranged[0]
    return jnp.dot(arranged, right_tab[...], preferred_element_type=jnp.float32)


def clear_pixels(edges):
    edge_pix = jnp.dot(edges, spread_matrix(), preferred_element_type=jnp.float32)
    within = (lax.broadcasted_iota(jnp.int32, (1, COLS), 1) % HS).astype(jnp.float32)
    return jnp.where(within < edge_pix, 1.0, 0.0)


def banded(line, count, shift):
    base = jnp.concatenate([line, jnp.zeros((1, LANES), jnp.float32)], axis=1)
    base = jnp.broadcast_to(base, (count, 2 * LANES))
    return pltpu.roll(base, shift, 1, stride=1, stride_axis=0)


def filters(tile, layer):
    turned = pltpu.roll(tile[0:8], HALF, 1)
    left_half = lax.broadcasted_iota(jnp.int32, (2, LANES), 1) < HALF
    col_taps = jnp.where(left_half, turned[0:2], tile[2:4])
    row_taps = jnp.where(left_half, turned[4:6], 0.0)
    row_re, row_im = row_taps[0:1], row_taps[1:2]
    height = block_height(layer)
    before = height + 2 * KR
    upper = banded(row_re, height, 0) - banded(row_im, height, before)
    lower = banded(row_im, height, 0) + banded(row_re, height, before)
    row_mat = jnp.concatenate([upper, lower], axis=0).astype(jnp.bfloat16)
    col_re = banded(col_taps[0:1], LANES, 1)
    col_im = banded(col_taps[1:2], LANES, 1)
    upper = jnp.concatenate([col_re, -col_im], axis=1)
    lower = jnp.concatenate([col_im, col_re], axis=1)
    col_mat = jnp.concatenate([upper, lower], axis=0).astype(jnp.bfloat16)
    return row_mat, col_mat


def propagated(u_re, u_im, row_mat, col_mat, layer):
    height = layer_height(layer)
    block = block_height(layer)
    reach = block + 2 * KR
    parts = []
    for start in range(0, height, block):
        stacked = jnp.concatenate(
            [u_re[start : start + reach], u_im[start : start + reach]], axis=0
        )
        parts.append(
            jnp.dot(row_mat[:, : 2 * reach], stacked, preferred_element_type=jnp.float32)
        )
    rowed = jnp.concatenate(
        [part[:block] for part in parts] + [part[block:] for part in parts], axis=0
    )
    rowed = jnp.concatenate([rowed, jnp.zeros((2 * height, LANES), jnp.float32)], axis=1)
    rowed = pltpu.roll(rowed, HALF, 1).astype(jnp.bfloat16)
    windows = jnp.concatenate(
        [
            jnp.concatenate(
                [
                    rowed[:height, tile * LANES : (tile + 2) * LANES],
                    rowed[height:, tile * LANES : (tile + 2) * LANES],
                ],
                axis=1,
            )
            for tile in range(TILES)
        ],
        axis=0,
    )
    return lax.dot_general(
        windows, col_mat, (((1,), (1,)), ((), ())), preferred_element_type=jnp.float32
    )


def prepare_kernel(
    own, incident, far_odd, far_even, cross, in_chip, left_tab, right_tab,
    first, stereo, clear, col_mats, *row_mats
):
    low_near, high_near, low_far, high_far = ordered(in_chip, cross, far_even, far_odd)
    extended = []
    for part in range(2):
        pieces = [low_far, low_near, incident[...], high_near, high_far]
        pieces = [piece[part * BAND : (part + 1) * BAND] for piece in pieces]
        extended.append(jnp.concatenate(pieces, axis=0))
    row_mat, col_mat = filters(own[0, 0:16, COLS:].astype(jnp.float32), 0)
    first[...] = propagated(extended[0], extended[1], row_mat, col_mat, 0)
    for layer in range(1, LAYERS):
        row_mat, col_mat = filters(own[layer, 0:16, COLS:].astype(jnp.float32), layer)
        row_mats[layer - 1][...] = row_mat
        col_mats[layer - 1] = col_mat
    packed = jnp.concatenate([own[layer, :, :HALO_W] for layer in range(LAYERS)], axis=0)
    clear[...] = clear_pixels(packed[:, COLS : COLS + NH])
    tiles = stereo_tiles([packed[:, :COLS]], left_tab, right_tab)
    for tile in range(TILES):
        for part in range(2):
            block = tiles[
                tile * LANES : (tile + 1) * LANES, part * LANES : (part + 1) * LANES
            ]
            stereo[part, :, tile * LANES : (tile + 1) * LANES] = block


def chain_kernel(
    in_chip, cross, far_even, far_odd, left_tab, right_tab, first, stereo, clear, col_mats, *rest
):
    row_mats, outs, field = rest[: LAYERS - 1], rest[LAYERS - 1 : -1], rest[-1]
    depth = lax.axis_index("depth")
    low_near, high_near, low_far, high_far = ordered(in_chip, cross, far_even, far_odd)
    pieces = [
        low_far,
        low_near[0:BAND],
        high_near[0:BAND],
        high_far,
        low_near[BAND : 2 * BAND],
        high_near[BAND : 2 * BAND],
        low_near[2 * BAND : NEAR],
        high_near[2 * BAND : NEAR],
    ]
    halo = jnp.concatenate(pieces, axis=0)
    half = halo.shape[0] // 2
    halo_tiles = stereo_tiles(
        [halo[:half, :COLS], halo[half:, :COLS]], left_tab, right_tab
    )
    halo_clear = clear_pixels(halo[:, COLS : COLS + NH])
    begins = (0, half, half + 2 * BAND, 0)
    sides = (BAND + FAR, BAND, KR, 0)
    for layer in range(LAYERS):
        height = layer_height(layer)
        before = height + 2 * KR
        low, side = begins[layer], sides[layer]
        if layer == 0:
            columned = first
        else:
            columned = propagated(
                field[layer - 1, 0, :before],
                field[layer - 1, 1, :before],
                row_mats[layer - 1],
                col_mats[layer - 1],
                layer,
            )
        band = slice(layer * BAND, (layer + 1) * BAND)
        pieces = [clear[band]]
        if side:
            pieces = [halo_clear[low : low + side], clear[band], halo_clear[low + side : low + 2 * side]]
        passing = jnp.concatenate(pieces, axis=0)
        for tile in range(TILES):
            span = slice(tile * height, (tile + 1) * height)
            lanes = slice(tile * LANES, (tile + 1) * LANES)
            row = (low // half * TILES + tile) * half + low % half
            for part in range(2):
                within = slice(part * LANES, (part + 1) * LANES)
                pieces = [stereo[part, band, lanes]]
                if side:
                    pieces = [
                        halo_tiles[row : row + side, within],
                        stereo[part, band, lanes],
                        halo_tiles[row + side : row + 2 * side, within],
                    ]
                added = jnp.concatenate(pieces, axis=0)
                value = passing[:, lanes] * columned[span, within] + added
                field[layer, part, :height, lanes] = value.astype(jnp.bfloat16)
    for hop, out in enumerate(outs):
        layer = depth ^ hop
        start = pl.multiple_of((LAYERS - 1 - layer) * KR, KR)
        for part in range(2):
            out[part] = field[layer, part, pl.ds(start, BAND)]


def home_kernel(*refs):
    arrived, out, sems = refs[:LAYERS], refs[LAYERS], refs[LAYERS + 1]
    depth = lax.axis_index("depth")
    for colour in range(COLORS):
        for hop in range(LAYERS):

            @pl.when((depth ^ hop) == colour)
            def begin(hop=hop, colour=colour):
                pltpu.make_async_copy(arrived[hop], out.at[0, colour], sems.at[colour]).start()

    for colour in range(COLORS):
        pltpu.make_async_copy(arrived[0], out.at[0, colour], sems.at[colour]).wait()


def over_depth(value, hop):
    return lax.ppermute(value, "depth", [(i, i ^ hop) for i in range(LAYERS)])


def exchanged(value, by, phase):
    count, depths = lax.axis_size("rows"), lax.axis_size("depth")
    partner = {}
    for low in range(count - by):
        if (low // by) % 2 == phase:
            partner[low], partner[low + by] = low + by, low
    pairs = []
    for depth in range(depths):
        for band in range(count):
            if band in partner:
                to = (depth, partner[band])
            elif by > 1:
                to = (depth, band ^ 1)
            else:
                to = (depth ^ 2, band)
            pairs.append((depth * count + band, to[0] * count + to[1]))
    return lax.ppermute(value, ("depth", "rows"), pairs)


def neighbours(sent):
    in_chip, cross, far_even, far_odd = sent
    far_odd = exchanged(far_odd, 2, 1)
    far_even = exchanged(far_even, 2, 0)
    cross = exchanged(cross, 1, 1)
    in_chip = exchanged(in_chip, 1, 0)
    return in_chip, cross, far_even, far_odd


def call(
    kernel, out_shape, in_specs, scratch=(), flops=0, moved=10**6, limit=VMEM_LIMIT,
    out_space=pltpu.VMEM,
):
    vmem = pl.BlockSpec(memory_space=out_space)
    many = isinstance(out_shape, (tuple, list))
    return pl.pallas_call(
        kernel,
        out_shape=out_shape,
        in_specs=in_specs,
        out_specs=(vmem,) * len(out_shape) if many else vmem,
        scratch_shapes=scratch,
        compiler_params=pltpu.CompilerParams(vmem_limit_bytes=limit),
        cost_estimate=pl.CostEstimate(flops=flops, bytes_accessed=moved, transcendentals=0),
    )


def body(incident, row_taps, col_taps, hogel_light, silhouette, fill_counts, hogel_index):
    vmem = pl.BlockSpec(memory_space=pltpu.VMEM)
    hbm = pl.BlockSpec(memory_space=pltpu.HBM)
    bf16, f32 = jnp.bfloat16, jnp.float32
    shaped = jax.ShapeDtypeStruct
    held = [
        pltpu.VMEM(hogel_index.shape, jnp.int32),
        pltpu.SMEM(fill_counts.shape, jnp.int32),
        pltpu.VMEM(silhouette.shape, jnp.int32),
        pltpu.VMEM(row_taps.shape, bf16),
        pltpu.VMEM(col_taps.shape, bf16),
        pltpu.VMEM(hogel_light.shape, f32),
    ]
    *messages, mine = call(
        pack_kernel,
        (shaped((BAND, HALO_W), bf16),) * LAYERS + (shaped(incident.shape[1:], bf16),),
        [hbm] * 7,
        held + [pltpu.SemaphoreType.DMA((7,)), pltpu.VMEM((BAND, LANES), f32)],
        flops=10**7,
        limit=PACK_LIMIT,
    )(hogel_light, silhouette, fill_counts, hogel_index, row_taps, col_taps, incident)
    mine = mine.reshape(2 * BAND, COLS)
    kept = call(stay_kernel, shaped((BAND, HALO_W), bf16), [vmem], moved=10**5)(messages[0])
    layers_in = [kept] + [over_depth(messages[hop], hop) for hop in range(1, LAYERS)]
    arrived = neighbours((mine,) * 4)[::-1]
    near = shaped((NEAR, HALO_W), bf16)
    far = shaped((FAR, HALO_W), bf16)
    own, *sent = call(
        halo_kernel,
        (shaped((LAYERS, BAND, HALO_W), bf16), near, near, far, far),
        [vmem] * LAYERS,
    )(*layers_in)
    halos = neighbours(sent)
    right_tab = jnp.asarray(right_table())
    made = call(
        prepare_kernel,
        [
            shaped((TILES * layer_height(0), 2 * LANES), f32),
            shaped((2, LANES, COLS), f32),
            shaped((LANES, COLS), f32),
            shaped((LAYERS - 1, 2 * LANES, 4 * LANES), bf16),
        ]
        + [shaped((2 * block_height(layer), 2 * LANES), bf16) for layer in range(1, LAYERS)],
        [vmem] * 8,
        flops=10**9,
        moved=3 * 10**6,
    )(own, mine, *arrived, jnp.asarray(left_table(LANES)), right_tab)
    halo_rows = NEAR + FAR
    results = call(
        chain_kernel,
        [shaped((2, BAND, COLS), bf16)] * LAYERS,
        [vmem] * (6 + len(made)),
        [pltpu.VMEM((LAYERS, 2, layer_height(0), COLS), bf16)],
        flops=2 * 10**9,
        moved=3 * 10**6,
    )(*halos, jnp.asarray(left_table(halo_rows)), right_tab, *made)
    returned = [results[0]] + [over_depth(results[hop], hop) for hop in range(1, LAYERS)]
    return call(
        home_kernel,
        shaped((1, COLORS, 2, BAND, COLS), bf16),
        [vmem] * LAYERS,
        [pltpu.SemaphoreType.DMA((COLORS,))],
        out_space=pltpu.HBM,
    )(*returned)


def solution(mesh):
    placed = (
        P(None, None, "rows", None),
        P("depth", None, None, None),
        P("depth", None, None, None),
        P("depth", None, "rows", None),
        P("depth", "rows", None),
        P("depth", "rows"),
        P("depth", "rows", None),
    )
    return jax.shard_map(
        body,
        mesh=mesh,
        in_specs=placed,
        out_specs=P("depth", None, None, "rows", None),
        check_vma=False,
    )
```

```python
import functools
import math

import jax
import jax.numpy as jnp
import numpy as np
from jax import lax
from jax.experimental import pallas as pl
from jax.experimental.pallas import tpu as pltpu
from jax.sharding import PartitionSpec as P

HS = 16
KR = 16
KC = 63
COLORS = 3
LAYERS = 4
BAND = 32
COLS = 1024
NH = COLS // HS
LANES = 128
TILES = COLS // LANES
HALO_W = COLS + LANES
HALF = LANES // 2
NEAR = 2 * BAND + KR
FAR = KR
VMEM_LIMIT = 48 * 1024 * 1024
PACK_LIMIT = 63 * 1024 * 1024


def split_table(table):
    high = table.astype(jnp.bfloat16)
    low = (table - high.astype(np.float64)).astype(jnp.bfloat16)
    return high, low


def dft_pair():
    counter = np.arange(HS)
    angles = (counter[:, None] * counter[None, :] % HS) * (2.0 * math.pi / HS)
    return np.cos(angles) / math.sqrt(HS), np.sin(angles) / math.sqrt(HS)


def left_table(height):
    cos_tab, sin_tab = dft_pair()
    eye = np.eye(height // HS)
    full = np.concatenate([np.kron(eye, cos_tab), np.kron(eye, -sin_tab)], axis=0)
    return np.concatenate(split_table(full), axis=1)


def right_table():
    cos_tab, sin_tab = dft_pair()
    eye = np.eye(LANES // HS)
    cos_big, sin_big = np.kron(eye, cos_tab), np.kron(eye, sin_tab)
    full = np.concatenate(
        [
            np.concatenate([cos_big, -sin_big], axis=1),
            np.concatenate([sin_big, cos_big], axis=1),
        ],
        axis=0,
    )
    return full.astype(jnp.bfloat16)


def layer_height(layer):
    return BAND + 2 * KR * (LAYERS - 1 - layer)


def block_height(layer):
    height = layer_height(layer)
    return height // 2 if 2 * (height + 2 * KR) > 2 * LANES else height


def spread_matrix():
    tile = lax.broadcasted_iota(jnp.int32, (NH, COLS), 0)
    column = lax.broadcasted_iota(jnp.int32, (NH, COLS), 1)
    return jnp.where(column // HS == tile, 1.0, 0.0).astype(jnp.bfloat16)


def own_colour():
    return jnp.minimum(lax.axis_index("depth"), COLORS - 1)


def pack_kernel(light, edges, counts, listed, row_taps, col_taps, incident, *rest):
    outs, mine, held, sems, taps = rest[:LAYERS], rest[LAYERS], rest[5:11], rest[11], rest[12]
    depth = lax.axis_index("depth")
    picked = pltpu.make_async_copy(incident.at[own_colour()], mine, sems.at[6])
    sources = (listed, counts, edges, row_taps, col_taps, light)
    copies = [
        pltpu.make_async_copy(source, target, sems.at[place])
        for place, (source, target) in enumerate(zip(sources, held))
    ]
    for copy in reversed(copies):
        copy.start()
    picked.start()
    listed, counts, edges, row_taps, col_taps, light = held
    spread = spread_matrix()
    slot = lax.broadcasted_iota(jnp.int32, (NH, NH), 0)
    place = lax.broadcasted_iota(jnp.int32, (NH, NH), 1)
    for copy in copies[:5]:
        copy.wait()
    rows = []
    for group in range(BAND // HS):
        listing = jnp.broadcast_to(listed[0, group : group + 1, :], (NH, NH))
        column = jnp.sum(jnp.where(slot == place, listing, 0), axis=1, keepdims=True)
        named = (column == place) & (slot < counts[0, group])
        live = jnp.max(jnp.where(named, 1.0, 0.0), axis=0, keepdims=True)
        rows.append(jnp.broadcast_to(live, (HS, NH)))
    live_rows = jnp.concatenate(rows, axis=0).astype(jnp.bfloat16)
    live_pix = jnp.dot(live_rows, spread, preferred_element_type=jnp.float32)
    edge_tile = jnp.concatenate(
        [edges[0].astype(jnp.float32), jnp.zeros((BAND, LANES - NH), jnp.float32)], axis=1
    )
    left_half = lax.broadcasted_iota(jnp.int32, (BAND, LANES), 1) < HALF
    colours = [jnp.minimum(depth ^ hop, COLORS - 1) for hop in range(LAYERS)]
    for colour, out in zip(colours, outs):
        taps[...] = jnp.zeros_like(taps)
        taps[2:4, : 2 * KC + 1] = col_taps[0, colour].astype(jnp.float32)
        taps[4:6, : 2 * KR + 1] = row_taps[0, colour].astype(jnp.float32)
        turned = pltpu.roll(taps[0:8], HALF, 1)
        taps[0:2] = turned[2:4]
        taps[4:6] = turned[4:6]
        tile = jnp.where(left_half, edge_tile, taps[...])
        out[:, COLS:] = tile.astype(jnp.bfloat16)
    copies[5].wait()
    for colour, out in zip(colours, outs):
        out[:, :COLS] = (light[0, colour] * live_pix).astype(jnp.bfloat16)
    picked.wait()


def stay_kernel(message, here):
    here[...] = message[...]


def halo_kernel(*refs):
    arrived, (own, in_chip, cross, far_even, far_odd) = refs[:LAYERS], refs[LAYERS:]
    depth = lax.axis_index("depth")
    for hop in range(LAYERS):
        own[depth ^ hop] = arrived[hop][...]
    band = lax.axis_index("rows")
    core = band % 2
    odd = (band // 2) % 2
    last = BAND - KR
    for near, start in ((in_chip, (1 - core) * last), (cross, core * last)):
        near[0:BAND] = own[0, :, :HALO_W]
        near[BAND : 2 * BAND] = own[1, :, :HALO_W]
        near[2 * BAND : NEAR] = own[2, pl.ds(pl.multiple_of(start, KR), KR), :HALO_W]
    for far, start in ((far_even, (1 - odd) * last), (far_odd, odd * last)):
        far[...] = own[0, pl.ds(pl.multiple_of(start, KR), KR), :HALO_W]


def ordered(in_chip, cross, far_even, far_odd):
    band = lax.axis_index("rows")
    count = lax.axis_size("rows")
    even_core = band % 2 == 0
    even_chip = (band // 2) % 2 == 0

    def received(value, by, phase):
        lower = (band // by) % 2 == phase
        paired = jnp.where(lower, band + by < count, band >= by)
        value = value[...]
        return jnp.where(paired, value, jnp.zeros_like(value))

    in_chip, cross = received(in_chip, 1, 0), received(cross, 1, 1)
    far_even, far_odd = received(far_even, 2, 0), received(far_odd, 2, 1)
    return (
        jnp.where(even_core, cross, in_chip),
        jnp.where(even_core, in_chip, cross),
        jnp.where(even_chip, far_odd, far_even),
        jnp.where(even_chip, far_even, far_odd),
    )


def tiles_below(value, height):
    return jnp.concatenate(
        [
            jnp.concatenate(
                [
                    value[:height, tile * LANES : (tile + 1) * LANES],
                    value[height:, tile * LANES : (tile + 1) * LANES],
                ],
                axis=1,
            )
            for tile in range(TILES)
        ],
        axis=0,
    )


def stereo_tiles(blocks, left_tab, right_tab):
    arranged = []
    for light in blocks:
        doubled = jnp.concatenate([light, light], axis=0)
        left = jnp.dot(left_tab[...], doubled, preferred_element_type=jnp.float32)
        arranged.append(tiles_below(left.astype(jnp.bfloat16), light.shape[0]))
    arranged = jnp.concatenate(arranged, axis=0) if len(arranged) > 1 else arranged[0]
    return jnp.dot(arranged, right_tab[...], preferred_element_type=jnp.float32)


def clear_pixels(edges):
    edge_pix = jnp.dot(edges, spread_matrix(), preferred_element_type=jnp.float32)
    within = (lax.broadcasted_iota(jnp.int32, (1, COLS), 1) % HS).astype(jnp.float32)
    return jnp.where(within < edge_pix, 1.0, 0.0)


def banded(line, count, shift):
    base = jnp.concatenate([line, jnp.zeros((1, LANES), jnp.float32)], axis=1)
    base = jnp.broadcast_to(base, (count, 2 * LANES))
    return pltpu.roll(base, shift, 1, stride=1, stride_axis=0)


def filters(tile, layer):
    turned = pltpu.roll(tile[0:8], HALF, 1)
    left_half = lax.broadcasted_iota(jnp.int32, (2, LANES), 1) < HALF
    col_taps = jnp.where(left_half, turned[0:2], tile[2:4])
    row_taps = jnp.where(left_half, turned[4:6], 0.0)
    row_re, row_im = row_taps[0:1], row_taps[1:2]
    height = block_height(layer)
    before = height + 2 * KR
    upper = banded(row_re, height, 0) - banded(row_im, height, before)
    lower = banded(row_im, height, 0) + banded(row_re, height, before)
    row_mat = jnp.concatenate([upper, lower], axis=0).astype(jnp.bfloat16)
    col_re = banded(col_taps[0:1], LANES, 1)
    col_im = banded(col_taps[1:2], LANES, 1)
    upper = jnp.concatenate([col_re, -col_im], axis=1)
    lower = jnp.concatenate([col_im, col_re], axis=1)
    col_mat = jnp.concatenate([upper, lower], axis=0).astype(jnp.bfloat16)
    return row_mat, col_mat


def propagated(u_re, u_im, row_mat, col_mat, layer):
    height = layer_height(layer)
    block = block_height(layer)
    reach = block + 2 * KR
    parts = []
    for start in range(0, height, block):
        stacked = jnp.concatenate(
            [u_re[start : start + reach], u_im[start : start + reach]], axis=0
        )
        parts.append(
            jnp.dot(row_mat[:, : 2 * reach], stacked, preferred_element_type=jnp.float32)
        )
    rowed = jnp.concatenate(
        [part[:block] for part in parts] + [part[block:] for part in parts], axis=0
    )
    rowed = jnp.concatenate([rowed, jnp.zeros((2 * height, LANES), jnp.float32)], axis=1)
    rowed = pltpu.roll(rowed, HALF, 1).astype(jnp.bfloat16)
    windows = jnp.concatenate(
        [
            jnp.concatenate(
                [
                    rowed[:height, tile * LANES : (tile + 2) * LANES],
                    rowed[height:, tile * LANES : (tile + 2) * LANES],
                ],
                axis=1,
            )
            for tile in range(TILES)
        ],
        axis=0,
    )
    return lax.dot_general(
        windows, col_mat, (((1,), (1,)), ((), ())), preferred_element_type=jnp.float32
    )


def prepare_kernel(
    own, incident, far_odd, far_even, cross, in_chip, left_tab, right_tab,
    first, stereo, clear, col_mats, *row_mats
):
    low_near, high_near, low_far, high_far = ordered(in_chip, cross, far_even, far_odd)
    extended = []
    for part in range(2):
        pieces = [low_far, low_near, incident[...], high_near, high_far]
        pieces = [piece[part * BAND : (part + 1) * BAND] for piece in pieces]
        extended.append(jnp.concatenate(pieces, axis=0))
    row_mat, col_mat = filters(own[0, 0:16, COLS:].astype(jnp.float32), 0)
    first[...] = propagated(extended[0], extended[1], row_mat, col_mat, 0)
    for layer in range(1, LAYERS):
        row_mat, col_mat = filters(own[layer, 0:16, COLS:].astype(jnp.float32), layer)
        row_mats[layer - 1][...] = row_mat
        col_mats[layer - 1] = col_mat
    packed = jnp.concatenate([own[layer, :, :HALO_W] for layer in range(LAYERS)], axis=0)
    clear[...] = clear_pixels(packed[:, COLS : COLS + NH])
    tiles = stereo_tiles([packed[:, :COLS]], left_tab, right_tab)
    for tile in range(TILES):
        for part in range(2):
            block = tiles[
                tile * LANES : (tile + 1) * LANES, part * LANES : (part + 1) * LANES
            ]
            stereo[part, :, tile * LANES : (tile + 1) * LANES] = block


def chain_kernel(
    in_chip, cross, far_even, far_odd, left_tab, right_tab, first, stereo, clear, col_mats, *rest
):
    row_mats, outs, field = rest[: LAYERS - 1], rest[LAYERS - 1 : -1], rest[-1]
    depth = lax.axis_index("depth")
    low_near, high_near, low_far, high_far = ordered(in_chip, cross, far_even, far_odd)
    pieces = [
        low_far,
        low_near[0:BAND],
        high_near[0:BAND],
        high_far,
        low_near[BAND : 2 * BAND],
        high_near[BAND : 2 * BAND],
        low_near[2 * BAND : NEAR],
        high_near[2 * BAND : NEAR],
    ]
    halo = jnp.concatenate(pieces, axis=0)
    half = halo.shape[0] // 2
    halo_tiles = stereo_tiles(
        [halo[:half, :COLS], halo[half:, :COLS]], left_tab, right_tab
    )
    halo_clear = clear_pixels(halo[:, COLS : COLS + NH])
    begins = (0, half, half + 2 * BAND, 0)
    sides = (BAND + FAR, BAND, KR, 0)
    for layer in range(LAYERS):
        height = layer_height(layer)
        before = height + 2 * KR
        low, side = begins[layer], sides[layer]
        if layer == 0:
            columned = first
        else:
            columned = propagated(
                field[layer - 1, 0, :before],
                field[layer - 1, 1, :before],
                row_mats[layer - 1],
                col_mats[layer - 1],
                layer,
            )
        band = slice(layer * BAND, (layer + 1) * BAND)
        pieces = [clear[band]]
        if side:
            pieces = [halo_clear[low : low + side], clear[band], halo_clear[low + side : low + 2 * side]]
        passing = jnp.concatenate(pieces, axis=0)
        for tile in range(TILES):
            span = slice(tile * height, (tile + 1) * height)
            lanes = slice(tile * LANES, (tile + 1) * LANES)
            row = (low // half * TILES + tile) * half + low % half
            for part in range(2):
                within = slice(part * LANES, (part + 1) * LANES)
                pieces = [stereo[part, band, lanes]]
                if side:
                    pieces = [
                        halo_tiles[row : row + side, within],
                        stereo[part, band, lanes],
                        halo_tiles[row + side : row + 2 * side, within],
                    ]
                added = jnp.concatenate(pieces, axis=0)
                value = passing[:, lanes] * columned[span, within] + added
                field[layer, part, :height, lanes] = value.astype(jnp.bfloat16)
    for hop, out in enumerate(outs):
        layer = depth ^ hop
        start = pl.multiple_of((LAYERS - 1 - layer) * KR, KR)
        for part in range(2):
            out[part] = field[layer, part, pl.ds(start, BAND)]


def home_kernel(hops, *refs):
    arrived, out, sems = refs[: len(hops)], refs[-2], refs[-1]
    depth = lax.axis_index("depth")
    for finish in (False, True):
        for place, hop in enumerate(hops):

            @pl.when((depth ^ hop) < COLORS)
            def write(place=place, hop=hop):
                copy = pltpu.make_async_copy(
                    arrived[place], out.at[0, depth ^ hop], sems.at[place]
                )
                if finish:
                    copy.wait()
                else:
                    copy.start()


def over_depth(value, hop):
    return lax.ppermute(value, "depth", [(i, i ^ hop) for i in range(LAYERS)])


def exchanged(value, by, phase):
    count, depths = lax.axis_size("rows"), lax.axis_size("depth")
    partner = {}
    for low in range(count - by):
        if (low // by) % 2 == phase:
            partner[low], partner[low + by] = low + by, low
    pairs = []
    for depth in range(depths):
        for band in range(count):
            if band in partner:
                to = (depth, partner[band])
            elif by > 1:
                to = (depth, band ^ 1)
            else:
                to = (depth ^ 1, band)
            pairs.append((depth * count + band, to[0] * count + to[1]))
    return lax.ppermute(value, ("depth", "rows"), pairs)


def neighbours(sent):
    in_chip, cross, far_even, far_odd = sent
    far_odd = exchanged(far_odd, 2, 1)
    far_even = exchanged(far_even, 2, 0)
    cross = exchanged(cross, 1, 1)
    in_chip = exchanged(in_chip, 1, 0)
    return in_chip, cross, far_even, far_odd


def call(
    kernel, out_shape, in_specs, scratch=(), flops=0, moved=10**6, limit=VMEM_LIMIT,
    out_space=pltpu.VMEM, aliases=None,
):
    vmem = pl.BlockSpec(memory_space=out_space)
    many = isinstance(out_shape, (tuple, list))
    return pl.pallas_call(
        kernel,
        out_shape=out_shape,
        in_specs=in_specs,
        out_specs=(vmem,) * len(out_shape) if many else vmem,
        scratch_shapes=scratch,
        input_output_aliases=aliases or {},
        compiler_params=pltpu.CompilerParams(vmem_limit_bytes=limit),
        cost_estimate=pl.CostEstimate(flops=flops, bytes_accessed=moved, transcendentals=0),
    )


def body(incident, row_taps, col_taps, hogel_light, silhouette, fill_counts, hogel_index):
    vmem = pl.BlockSpec(memory_space=pltpu.VMEM)
    hbm = pl.BlockSpec(memory_space=pltpu.HBM)
    bf16, f32 = jnp.bfloat16, jnp.float32
    shaped = jax.ShapeDtypeStruct
    held = [
        pltpu.VMEM(hogel_index.shape, jnp.int32),
        pltpu.SMEM(fill_counts.shape, jnp.int32),
        pltpu.VMEM(silhouette.shape, jnp.int32),
        pltpu.VMEM(row_taps.shape, bf16),
        pltpu.VMEM(col_taps.shape, bf16),
        pltpu.VMEM(hogel_light.shape, f32),
    ]
    *messages, mine = call(
        pack_kernel,
        (shaped((BAND, HALO_W), bf16),) * LAYERS + (shaped(incident.shape[1:], bf16),),
        [hbm] * 7,
        held + [pltpu.SemaphoreType.DMA((7,)), pltpu.VMEM((BAND, LANES), f32)],
        flops=10**7,
        limit=PACK_LIMIT,
    )(hogel_light, silhouette, fill_counts, hogel_index, row_taps, col_taps, incident)
    mine = mine.reshape(2 * BAND, COLS)
    kept = call(stay_kernel, shaped((BAND, HALO_W), bf16), [vmem], moved=10**5)(messages[0])
    layers_in = [kept] + [over_depth(messages[hop], hop) for hop in range(1, LAYERS)]
    arrived = neighbours((mine,) * 4)[::-1]
    near = shaped((NEAR, HALO_W), bf16)
    far = shaped((FAR, HALO_W), bf16)
    own, *sent = call(
        halo_kernel,
        (shaped((LAYERS, BAND, HALO_W), bf16), near, near, far, far),
        [vmem] * LAYERS,
    )(*layers_in)
    halos = neighbours(sent)
    right_tab = jnp.asarray(right_table())
    made = call(
        prepare_kernel,
        [
            shaped((TILES * layer_height(0), 2 * LANES), f32),
            shaped((2, LANES, COLS), f32),
            shaped((LANES, COLS), f32),
            shaped((LAYERS - 1, 2 * LANES, 4 * LANES), bf16),
        ]
        + [shaped((2 * block_height(layer), 2 * LANES), bf16) for layer in range(1, LAYERS)],
        [vmem] * 8,
        flops=10**9,
        moved=3 * 10**6,
    )(own, mine, *arrived, jnp.asarray(left_table(LANES)), right_tab)
    halo_rows = NEAR + FAR
    results = call(
        chain_kernel,
        [shaped((2, BAND, COLS), bf16)] * LAYERS,
        [vmem] * (6 + len(made)),
        [pltpu.VMEM((LAYERS, 2, layer_height(0), COLS), bf16)],
        flops=2 * 10**9,
        moved=3 * 10**6,
    )(*halos, jnp.asarray(left_table(halo_rows)), right_tab, *made)
    returned = [results[0]] + [over_depth(results[hop], hop) for hop in range(1, LAYERS)]
    home = shaped((1, COLORS, 2, BAND, COLS), bf16)
    early = (0, 1, 2)
    partly = call(
        functools.partial(home_kernel, early),
        home,
        [vmem] * len(early),
        [pltpu.SemaphoreType.DMA((len(early),))],
        out_space=pltpu.HBM,
    )(*(returned[hop] for hop in early))
    return call(
        functools.partial(home_kernel, (3,)),
        home,
        [vmem, hbm],
        [pltpu.SemaphoreType.DMA((1,))],
        out_space=pltpu.HBM,
        aliases={1: 0},
    )(returned[3], partly)


def solution(mesh):
    placed = (
        P(None, None, "rows", None),
        P("depth", None, None, None),
        P("depth", None, None, None),
        P("depth", None, "rows", None),
        P("depth", "rows", None),
        P("depth", "rows"),
        P("depth", "rows", None),
    )
    return jax.shard_map(
        body,
        mesh=mesh,
        in_specs=placed,
        out_specs=P("depth", None, None, "rows", None),
        check_vma=False,
    )
```

```python
import functools
import math

import jax
import jax.numpy as jnp
import numpy as np
from jax import lax
from jax.experimental import pallas as pl
from jax.experimental.pallas import tpu as pltpu
from jax.sharding import PartitionSpec as P

HS = 16
KR = 16
KC = 63
COLORS = 3
LAYERS = 4
BAND = 32
COLS = 1024
NH = COLS // HS
LANES = 128
TILES = COLS // LANES
HALO_W = COLS + LANES
HALF = LANES // 2
NEAR = 2 * BAND + KR
FAR = KR
VMEM_LIMIT = 48 * 1024 * 1024
PACK_LIMIT = 63 * 1024 * 1024


def split_table(table):
    high = table.astype(jnp.bfloat16)
    low = (table - high.astype(np.float64)).astype(jnp.bfloat16)
    return high, low


def dft_pair():
    counter = np.arange(HS)
    angles = (counter[:, None] * counter[None, :] % HS) * (2.0 * math.pi / HS)
    return np.cos(angles) / math.sqrt(HS), np.sin(angles) / math.sqrt(HS)


def left_table(height):
    cos_tab, sin_tab = dft_pair()
    eye = np.eye(height // HS)
    full = np.concatenate([np.kron(eye, cos_tab), np.kron(eye, -sin_tab)], axis=0)
    return np.concatenate(split_table(full), axis=1)


def right_table():
    cos_tab, sin_tab = dft_pair()
    eye = np.eye(LANES // HS)
    cos_big, sin_big = np.kron(eye, cos_tab), np.kron(eye, sin_tab)
    full = np.concatenate(
        [
            np.concatenate([cos_big, -sin_big], axis=1),
            np.concatenate([sin_big, cos_big], axis=1),
        ],
        axis=0,
    )
    return full.astype(jnp.bfloat16)


def layer_height(layer):
    return BAND + 2 * KR * (LAYERS - 1 - layer)


def block_height(layer):
    height = layer_height(layer)
    return height // 2 if 2 * (height + 2 * KR) > 2 * LANES else height


def spread_matrix():
    tile = lax.broadcasted_iota(jnp.int32, (NH, COLS), 0)
    column = lax.broadcasted_iota(jnp.int32, (NH, COLS), 1)
    return jnp.where(column // HS == tile, 1.0, 0.0).astype(jnp.bfloat16)


def own_colour():
    return jnp.minimum(lax.axis_index("depth"), COLORS - 1)


def pack_kernel(light, edges, counts, listed, row_taps, col_taps, incident, *rest):
    outs, mine, held, sems, taps = rest[:LAYERS], rest[LAYERS], rest[5:11], rest[11], rest[12]
    depth = lax.axis_index("depth")
    picked = pltpu.make_async_copy(incident.at[own_colour()], mine, sems.at[6])
    sources = (listed, counts, edges, row_taps, col_taps, light)
    copies = [
        pltpu.make_async_copy(source, target, sems.at[place])
        for place, (source, target) in enumerate(zip(sources, held))
    ]
    for copy in reversed(copies):
        copy.start()
    picked.start()
    listed, counts, edges, row_taps, col_taps, light = held
    spread = spread_matrix()
    slot = lax.broadcasted_iota(jnp.int32, (NH, NH), 0)
    place = lax.broadcasted_iota(jnp.int32, (NH, NH), 1)
    for copy in copies[:5]:
        copy.wait()
    rows = []
    for group in range(BAND // HS):
        listing = jnp.broadcast_to(listed[0, group : group + 1, :], (NH, NH))
        column = jnp.sum(jnp.where(slot == place, listing, 0), axis=1, keepdims=True)
        named = (column == place) & (slot < counts[0, group])
        live = jnp.max(jnp.where(named, 1.0, 0.0), axis=0, keepdims=True)
        rows.append(jnp.broadcast_to(live, (HS, NH)))
    live_rows = jnp.concatenate(rows, axis=0).astype(jnp.bfloat16)
    live_pix = jnp.dot(live_rows, spread, preferred_element_type=jnp.float32)
    edge_tile = jnp.concatenate(
        [edges[0].astype(jnp.float32), jnp.zeros((BAND, LANES - NH), jnp.float32)], axis=1
    )
    left_half = lax.broadcasted_iota(jnp.int32, (BAND, LANES), 1) < HALF
    colours = [jnp.minimum(depth ^ hop, COLORS - 1) for hop in range(LAYERS)]
    taps[...] = jnp.zeros_like(taps)
    for hop, colour in enumerate(colours):
        col = col_taps[0, colour].astype(jnp.float32)
        taps[8 * hop : 8 * hop + 2, : 2 * KC + 1] = col
        taps[8 * hop + 2 : 8 * hop + 4, : 2 * KC + 1] = col
        taps[8 * hop + 4 : 8 * hop + 6, : 2 * KR + 1] = row_taps[0, colour].astype(jnp.float32)
    stays = lax.broadcasted_iota(jnp.int32, (BAND, LANES), 0) % 8 // 2 == 1
    turned = jnp.where(stays, taps[...], pltpu.roll(taps[...], HALF, 1))
    below = jnp.zeros((BAND - 8, LANES), jnp.float32)
    for hop, out in enumerate(outs):
        tile = jnp.concatenate([turned[8 * hop : 8 * hop + 8], below], axis=0)
        out[:, COLS:] = jnp.where(left_half, edge_tile, tile).astype(jnp.bfloat16)
    copies[5].wait()
    for colour, out in zip(colours, outs):
        out[:, :COLS] = (light[0, colour] * live_pix).astype(jnp.bfloat16)
    picked.wait()


def stay_kernel(message, here):
    here[...] = message[...]


def halo_kernel(*refs):
    arrived, (own, in_chip, cross, far_even, far_odd) = refs[:LAYERS], refs[LAYERS:]
    depth = lax.axis_index("depth")
    for hop in range(LAYERS):
        own[depth ^ hop] = arrived[hop][...]
    band = lax.axis_index("rows")
    core = band % 2
    odd = (band // 2) % 2
    last = BAND - KR
    for near, start in ((in_chip, (1 - core) * last), (cross, core * last)):
        near[0:BAND] = own[0, :, :HALO_W]
        near[BAND : 2 * BAND] = own[1, :, :HALO_W]
        near[2 * BAND : NEAR] = own[2, pl.ds(pl.multiple_of(start, KR), KR), :HALO_W]
    for far, start in ((far_even, (1 - odd) * last), (far_odd, odd * last)):
        far[...] = own[0, pl.ds(pl.multiple_of(start, KR), KR), :HALO_W]


def ordered(in_chip, cross, far_even, far_odd):
    band = lax.axis_index("rows")
    count = lax.axis_size("rows")
    even_core = band % 2 == 0
    even_chip = (band // 2) % 2 == 0

    def received(value, by, phase):
        lower = (band // by) % 2 == phase
        paired = jnp.where(lower, band + by < count, band >= by)
        value = value[...]
        return jnp.where(paired, value, jnp.zeros_like(value))

    in_chip, cross = received(in_chip, 1, 0), received(cross, 1, 1)
    far_even, far_odd = received(far_even, 2, 0), received(far_odd, 2, 1)
    return (
        jnp.where(even_core, cross, in_chip),
        jnp.where(even_core, in_chip, cross),
        jnp.where(even_chip, far_odd, far_even),
        jnp.where(even_chip, far_even, far_odd),
    )


def tiles_below(value, height):
    return jnp.concatenate(
        [
            jnp.concatenate(
                [
                    value[:height, tile * LANES : (tile + 1) * LANES],
                    value[height:, tile * LANES : (tile + 1) * LANES],
                ],
                axis=1,
            )
            for tile in range(TILES)
        ],
        axis=0,
    )


def stereo_tiles(blocks, left_tab, right_tab):
    arranged = []
    for light in blocks:
        doubled = jnp.concatenate([light, light], axis=0)
        left = jnp.dot(left_tab[...], doubled, preferred_element_type=jnp.float32)
        arranged.append(tiles_below(left.astype(jnp.bfloat16), light.shape[0]))
    arranged = jnp.concatenate(arranged, axis=0) if len(arranged) > 1 else arranged[0]
    return jnp.dot(arranged, right_tab[...], preferred_element_type=jnp.float32)


def clear_pixels(edges):
    edge_pix = jnp.dot(edges, spread_matrix(), preferred_element_type=jnp.float32)
    within = (lax.broadcasted_iota(jnp.int32, (1, COLS), 1) % HS).astype(jnp.float32)
    return jnp.where(within < edge_pix, 1.0, 0.0)


def banded(line, count, shift):
    base = jnp.concatenate([line, jnp.zeros((1, LANES), jnp.float32)], axis=1)
    base = jnp.broadcast_to(base, (count, 2 * LANES))
    return pltpu.roll(base, shift, 1, stride=1, stride_axis=0)


def filters(tile, layer):
    turned = pltpu.roll(tile[0:8], HALF, 1)
    left_half = lax.broadcasted_iota(jnp.int32, (2, LANES), 1) < HALF
    col_taps = jnp.where(left_half, turned[0:2], tile[2:4])
    row_taps = jnp.where(left_half, turned[4:6], 0.0)
    row_re, row_im = row_taps[0:1], row_taps[1:2]
    height = block_height(layer)
    before = height + 2 * KR
    upper = banded(row_re, height, 0) - banded(row_im, height, before)
    lower = banded(row_im, height, 0) + banded(row_re, height, before)
    row_mat = jnp.concatenate([upper, lower], axis=0).astype(jnp.bfloat16)
    col_re = banded(col_taps[0:1], LANES, 1)
    col_im = banded(col_taps[1:2], LANES, 1)
    upper = jnp.concatenate([col_re, -col_im], axis=1)
    lower = jnp.concatenate([col_im, col_re], axis=1)
    col_mat = jnp.concatenate([upper, lower], axis=0).astype(jnp.bfloat16)
    return row_mat, col_mat


def propagated(u_re, u_im, row_mat, col_mat, layer):
    height = layer_height(layer)
    block = block_height(layer)
    reach = block + 2 * KR
    parts = []
    for start in range(0, height, block):
        stacked = jnp.concatenate(
            [u_re[start : start + reach], u_im[start : start + reach]], axis=0
        )
        parts.append(
            jnp.dot(row_mat[:, : 2 * reach], stacked, preferred_element_type=jnp.float32)
        )
    rowed = jnp.concatenate(
        [part[:block] for part in parts] + [part[block:] for part in parts], axis=0
    )
    rowed = jnp.concatenate([rowed, jnp.zeros((2 * height, LANES), jnp.float32)], axis=1)
    rowed = pltpu.roll(rowed, HALF, 1).astype(jnp.bfloat16)
    windows = jnp.concatenate(
        [
            jnp.concatenate(
                [
                    rowed[:height, tile * LANES : (tile + 2) * LANES],
                    rowed[height:, tile * LANES : (tile + 2) * LANES],
                ],
                axis=1,
            )
            for tile in range(TILES)
        ],
        axis=0,
    )
    return lax.dot_general(
        windows, col_mat, (((1,), (1,)), ((), ())), preferred_element_type=jnp.float32
    )


def prepare_kernel(
    own, incident, far_odd, far_even, cross, in_chip, left_tab, right_tab,
    first, stereo, clear, col_mats, *row_mats
):
    low_near, high_near, low_far, high_far = ordered(in_chip, cross, far_even, far_odd)
    extended = []
    for part in range(2):
        pieces = [low_far, low_near, incident[...], high_near, high_far]
        pieces = [piece[part * BAND : (part + 1) * BAND] for piece in pieces]
        extended.append(jnp.concatenate(pieces, axis=0))
    row_mat, col_mat = filters(own[0, 0:16, COLS:].astype(jnp.float32), 0)
    first[...] = propagated(extended[0], extended[1], row_mat, col_mat, 0)
    for layer in range(1, LAYERS):
        row_mat, col_mat = filters(own[layer, 0:16, COLS:].astype(jnp.float32), layer)
        row_mats[layer - 1][...] = row_mat
        col_mats[layer - 1] = col_mat
    packed = jnp.concatenate([own[layer, :, :HALO_W] for layer in range(LAYERS)], axis=0)
    clear[...] = clear_pixels(packed[:, COLS : COLS + NH])
    tiles = stereo_tiles([packed[:, :COLS]], left_tab, right_tab)
    for tile in range(TILES):
        for part in range(2):
            block = tiles[
                tile * LANES : (tile + 1) * LANES, part * LANES : (part + 1) * LANES
            ]
            stereo[part, :, tile * LANES : (tile + 1) * LANES] = block


def chain_kernel(
    in_chip, cross, far_even, far_odd, left_tab, right_tab, first, stereo, clear, col_mats, *rest
):
    row_mats, outs, field = rest[: LAYERS - 1], rest[LAYERS - 1 : -1], rest[-1]
    depth = lax.axis_index("depth")
    low_near, high_near, low_far, high_far = ordered(in_chip, cross, far_even, far_odd)
    pieces = [
        low_far,
        low_near[0:BAND],
        high_near[0:BAND],
        high_far,
        low_near[BAND : 2 * BAND],
        high_near[BAND : 2 * BAND],
        low_near[2 * BAND : NEAR],
        high_near[2 * BAND : NEAR],
    ]
    halo = jnp.concatenate(pieces, axis=0)
    half = halo.shape[0] // 2
    halo_tiles = stereo_tiles(
        [halo[:half, :COLS], halo[half:, :COLS]], left_tab, right_tab
    )
    halo_clear = clear_pixels(halo[:, COLS : COLS + NH])
    begins = (0, half, half + 2 * BAND, 0)
    sides = (BAND + FAR, BAND, KR, 0)
    for layer in range(LAYERS):
        height = layer_height(layer)
        before = height + 2 * KR
        low, side = begins[layer], sides[layer]
        if layer == 0:
            columned = first
        else:
            columned = propagated(
                field[layer - 1, 0, :before],
                field[layer - 1, 1, :before],
                row_mats[layer - 1],
                col_mats[layer - 1],
                layer,
            )
        band = slice(layer * BAND, (layer + 1) * BAND)
        pieces = [clear[band]]
        if side:
            pieces = [halo_clear[low : low + side], clear[band], halo_clear[low + side : low + 2 * side]]
        passing = jnp.concatenate(pieces, axis=0)
        for tile in range(TILES):
            span = slice(tile * height, (tile + 1) * height)
            lanes = slice(tile * LANES, (tile + 1) * LANES)
            row = (low // half * TILES + tile) * half + low % half
            for part in range(2):
                within = slice(part * LANES, (part + 1) * LANES)
                pieces = [stereo[part, band, lanes]]
                if side:
                    pieces = [
                        halo_tiles[row : row + side, within],
                        stereo[part, band, lanes],
                        halo_tiles[row + side : row + 2 * side, within],
                    ]
                added = jnp.concatenate(pieces, axis=0)
                value = passing[:, lanes] * columned[span, within] + added
                field[layer, part, :height, lanes] = value.astype(jnp.bfloat16)
    for hop, out in enumerate(outs):
        layer = depth ^ hop
        start = pl.multiple_of((LAYERS - 1 - layer) * KR, KR)
        for part in range(2):
            out[part] = field[layer, part, pl.ds(start, BAND)]


def home_kernel(hops, *refs):
    arrived, out, sems = refs[: len(hops)], refs[-2], refs[-1]
    depth = lax.axis_index("depth")
    for finish in (False, True):
        for place, hop in enumerate(hops):

            @pl.when((depth ^ hop) < COLORS)
            def write(place=place, hop=hop):
                copy = pltpu.make_async_copy(
                    arrived[place], out.at[0, depth ^ hop], sems.at[place]
                )
                if finish:
                    copy.wait()
                else:
                    copy.start()


def over_depth(value, hop):
    return lax.ppermute(value, "depth", [(i, i ^ hop) for i in range(LAYERS)])


def exchanged(value, by, phase):
    count, depths = lax.axis_size("rows"), lax.axis_size("depth")
    partner = {}
    for low in range(count - by):
        if (low // by) % 2 == phase:
            partner[low], partner[low + by] = low + by, low
    pairs = []
    for depth in range(depths):
        for band in range(count):
            if band in partner:
                to = (depth, partner[band])
            elif by > 1:
                to = (depth, band ^ 1)
            else:
                to = (depth ^ 1, band)
            pairs.append((depth * count + band, to[0] * count + to[1]))
    return lax.ppermute(value, ("depth", "rows"), pairs)


def neighbours(sent):
    in_chip, cross, far_even, far_odd = sent
    far_odd = exchanged(far_odd, 2, 1)
    far_even = exchanged(far_even, 2, 0)
    cross = exchanged(cross, 1, 1)
    in_chip = exchanged(in_chip, 1, 0)
    return in_chip, cross, far_even, far_odd


def call(
    kernel, out_shape, in_specs, scratch=(), flops=0, moved=10**6, limit=VMEM_LIMIT,
    out_space=pltpu.VMEM, aliases=None,
):
    vmem = pl.BlockSpec(memory_space=out_space)
    many = isinstance(out_shape, (tuple, list))
    return pl.pallas_call(
        kernel,
        out_shape=out_shape,
        in_specs=in_specs,
        out_specs=(vmem,) * len(out_shape) if many else vmem,
        scratch_shapes=scratch,
        input_output_aliases=aliases or {},
        compiler_params=pltpu.CompilerParams(vmem_limit_bytes=limit),
        cost_estimate=pl.CostEstimate(flops=flops, bytes_accessed=moved, transcendentals=0),
    )


def body(incident, row_taps, col_taps, hogel_light, silhouette, fill_counts, hogel_index):
    vmem = pl.BlockSpec(memory_space=pltpu.VMEM)
    hbm = pl.BlockSpec(memory_space=pltpu.HBM)
    bf16, f32 = jnp.bfloat16, jnp.float32
    shaped = jax.ShapeDtypeStruct
    held = [
        pltpu.VMEM(hogel_index.shape, jnp.int32),
        pltpu.SMEM(fill_counts.shape, jnp.int32),
        pltpu.VMEM(silhouette.shape, jnp.int32),
        pltpu.VMEM(row_taps.shape, bf16),
        pltpu.VMEM(col_taps.shape, bf16),
        pltpu.VMEM(hogel_light.shape, f32),
    ]
    *messages, mine = call(
        pack_kernel,
        (shaped((BAND, HALO_W), bf16),) * LAYERS + (shaped(incident.shape[1:], bf16),),
        [hbm] * 7,
        held + [pltpu.SemaphoreType.DMA((7,)), pltpu.VMEM((BAND, LANES), f32)],
        flops=10**7,
        limit=PACK_LIMIT,
    )(hogel_light, silhouette, fill_counts, hogel_index, row_taps, col_taps, incident)
    mine = mine.reshape(2 * BAND, COLS)
    kept = call(stay_kernel, shaped((BAND, HALO_W), bf16), [vmem], moved=10**5)(messages[0])
    layers_in = [kept] + [over_depth(messages[hop], hop) for hop in range(1, LAYERS)]
    arrived = neighbours((mine,) * 4)[::-1]
    near = shaped((NEAR, HALO_W), bf16)
    far = shaped((FAR, HALO_W), bf16)
    own, *sent = call(
        halo_kernel,
        (shaped((LAYERS, BAND, HALO_W), bf16), near, near, far, far),
        [vmem] * LAYERS,
    )(*layers_in)
    halos = neighbours(sent)
    right_tab = jnp.asarray(right_table())
    made = call(
        prepare_kernel,
        [
            shaped((TILES * layer_height(0), 2 * LANES), f32),
            shaped((2, LANES, COLS), f32),
            shaped((LANES, COLS), f32),
            shaped((LAYERS - 1, 2 * LANES, 4 * LANES), bf16),
        ]
        + [shaped((2 * block_height(layer), 2 * LANES), bf16) for layer in range(1, LAYERS)],
        [vmem] * 8,
        flops=10**9,
        moved=3 * 10**6,
    )(own, mine, *arrived, jnp.asarray(left_table(LANES)), right_tab)
    halo_rows = NEAR + FAR
    results = call(
        chain_kernel,
        [shaped((2, BAND, COLS), bf16)] * LAYERS,
        [vmem] * (6 + len(made)),
        [pltpu.VMEM((LAYERS, 2, layer_height(0), COLS), bf16)],
        flops=2 * 10**9,
        moved=3 * 10**6,
    )(*halos, jnp.asarray(left_table(halo_rows)), right_tab, *made)
    returned = [results[0]] + [over_depth(results[hop], hop) for hop in range(1, LAYERS)]
    home = shaped((1, COLORS, 2, BAND, COLS), bf16)
    early = (0, 1, 2)
    partly = call(
        functools.partial(home_kernel, early),
        home,
        [vmem] * len(early),
        [pltpu.SemaphoreType.DMA((len(early),))],
        out_space=pltpu.HBM,
    )(*(returned[hop] for hop in early))
    return call(
        functools.partial(home_kernel, (3,)),
        home,
        [vmem, hbm],
        [pltpu.SemaphoreType.DMA((1,))],
        out_space=pltpu.HBM,
        aliases={1: 0},
    )(returned[3], partly)


def solution(mesh):
    placed = (
        P(None, None, "rows", None),
        P("depth", None, None, None),
        P("depth", None, None, None),
        P("depth", None, "rows", None),
        P("depth", "rows", None),
        P("depth", "rows"),
        P("depth", "rows", None),
    )
    return jax.shard_map(
        body,
        mesh=mesh,
        in_specs=placed,
        out_specs=P("depth", None, None, "rows", None),
        check_vma=False,
    )
```

```python
import functools
import math

import jax
import jax.numpy as jnp
import numpy as np
from jax import lax
from jax.experimental import pallas as pl
from jax.experimental.pallas import tpu as pltpu
from jax.sharding import PartitionSpec as P

HS = 16
KR = 16
KC = 63
COLORS = 3
LAYERS = 4
BAND = 32
COLS = 1024
NH = COLS // HS
LANES = 128
TILES = COLS // LANES
HALO_W = COLS + LANES
HALF = LANES // 2
NEAR = 2 * BAND + KR
FAR = KR
VMEM_LIMIT = 48 * 1024 * 1024
PACK_LIMIT = 63 * 1024 * 1024


def split_table(table):
    high = table.astype(jnp.bfloat16)
    low = (table - high.astype(np.float64)).astype(jnp.bfloat16)
    return high, low


def dft_pair():
    counter = np.arange(HS)
    angles = (counter[:, None] * counter[None, :] % HS) * (2.0 * math.pi / HS)
    return np.cos(angles) / math.sqrt(HS), np.sin(angles) / math.sqrt(HS)


def left_table(height):
    cos_tab, sin_tab = dft_pair()
    eye = np.eye(height // HS)
    full = np.concatenate([np.kron(eye, cos_tab), np.kron(eye, -sin_tab)], axis=0)
    return np.concatenate(split_table(full), axis=1)


def right_table():
    cos_tab, sin_tab = dft_pair()
    eye = np.eye(LANES // HS)
    cos_big, sin_big = np.kron(eye, cos_tab), np.kron(eye, sin_tab)
    full = np.concatenate(
        [
            np.concatenate([cos_big, -sin_big], axis=1),
            np.concatenate([sin_big, cos_big], axis=1),
        ],
        axis=0,
    )
    return full.astype(jnp.bfloat16)


def layer_height(layer):
    return BAND + 2 * KR * (LAYERS - 1 - layer)


def block_height(layer):
    height = layer_height(layer)
    return height // 2 if 2 * (height + 2 * KR) > 2 * LANES else height


def spread_matrix():
    tile = lax.broadcasted_iota(jnp.int32, (NH, COLS), 0)
    column = lax.broadcasted_iota(jnp.int32, (NH, COLS), 1)
    return jnp.where(column // HS == tile, 1.0, 0.0).astype(jnp.bfloat16)


def own_colour():
    return jnp.minimum(lax.axis_index("depth"), COLORS - 1)


def pack_kernel(light, edges, counts, listed, row_taps, col_taps, incident, *rest):
    outs, mine, held, sems, taps = rest[:LAYERS], rest[LAYERS], rest[5:11], rest[11], rest[12]
    depth = lax.axis_index("depth")
    picked = pltpu.make_async_copy(incident.at[own_colour()], mine, sems.at[6])
    sources = (listed, counts, edges, row_taps, col_taps, light)
    copies = [
        pltpu.make_async_copy(source, target, sems.at[place])
        for place, (source, target) in enumerate(zip(sources, held))
    ]
    for copy in reversed(copies):
        copy.start()
    picked.start()
    listed, counts, edges, row_taps, col_taps, light = held
    spread = spread_matrix()
    slot = lax.broadcasted_iota(jnp.int32, (NH, NH), 0)
    place = lax.broadcasted_iota(jnp.int32, (NH, NH), 1)
    for copy in copies[:5]:
        copy.wait()
    rows = []
    for group in range(BAND // HS):
        listing = jnp.broadcast_to(listed[0, group : group + 1, :], (NH, NH))
        column = jnp.sum(jnp.where(slot == place, listing, 0), axis=1, keepdims=True)
        named = (column == place) & (slot < counts[0, group])
        live = jnp.max(jnp.where(named, 1.0, 0.0), axis=0, keepdims=True)
        rows.append(jnp.broadcast_to(live, (HS, NH)))
    live_rows = jnp.concatenate(rows, axis=0).astype(jnp.bfloat16)
    live_pix = jnp.dot(live_rows, spread, preferred_element_type=jnp.float32)
    edge_tile = jnp.concatenate(
        [edges[0].astype(jnp.float32), jnp.zeros((BAND, LANES - NH), jnp.float32)], axis=1
    )
    left_half = lax.broadcasted_iota(jnp.int32, (BAND, LANES), 1) < HALF
    colours = [jnp.minimum(depth ^ hop, COLORS - 1) for hop in range(LAYERS)]
    taps[...] = jnp.zeros_like(taps)
    for hop, colour in enumerate(colours):
        col = col_taps[0, colour].astype(jnp.float32)
        taps[8 * hop : 8 * hop + 2, : 2 * KC + 1] = col
        taps[8 * hop + 2 : 8 * hop + 4, : 2 * KC + 1] = col
        taps[8 * hop + 4 : 8 * hop + 6, : 2 * KR + 1] = row_taps[0, colour].astype(jnp.float32)
    stays = lax.broadcasted_iota(jnp.int32, (BAND, LANES), 0) % 8 // 2 == 1
    turned = jnp.where(stays, taps[...], pltpu.roll(taps[...], HALF, 1))
    below = jnp.zeros((BAND - 8, LANES), jnp.float32)
    for hop, out in enumerate(outs):
        tile = jnp.concatenate([turned[8 * hop : 8 * hop + 8], below], axis=0)
        out[:, COLS:] = jnp.where(left_half, edge_tile, tile).astype(jnp.bfloat16)
    copies[5].wait()
    for colour, out in zip(colours, outs):
        out[:, :COLS] = (light[0, colour] * live_pix).astype(jnp.bfloat16)
    picked.wait()


def stay_kernel(message, here):
    here[...] = message[...]


def halo_kernel(*refs):
    arrived, (own, in_chip, cross, far_even, far_odd) = refs[:LAYERS], refs[LAYERS:]
    depth = lax.axis_index("depth")
    for hop in range(LAYERS):
        own[depth ^ hop] = arrived[hop][...]
    band = lax.axis_index("rows")
    core = band % 2
    odd = (band // 2) % 2
    last = BAND - KR
    for near, start in ((in_chip, (1 - core) * last), (cross, core * last)):
        near[0:BAND] = own[0, :, :HALO_W]
        near[BAND : 2 * BAND] = own[1, :, :HALO_W]
        near[2 * BAND : NEAR] = own[2, pl.ds(pl.multiple_of(start, KR), KR), :HALO_W]
    for far, start in ((far_even, (1 - odd) * last), (far_odd, odd * last)):
        far[...] = own[0, pl.ds(pl.multiple_of(start, KR), KR), :HALO_W]


def ordered(in_chip, cross, far_even, far_odd):
    band = lax.axis_index("rows")
    count = lax.axis_size("rows")
    even_core = band % 2 == 0
    even_chip = (band // 2) % 2 == 0

    def received(value, by, phase):
        lower = (band // by) % 2 == phase
        paired = jnp.where(lower, band + by < count, band >= by)
        value = value[...]
        return jnp.where(paired, value, jnp.zeros_like(value))

    in_chip, cross = received(in_chip, 1, 0), received(cross, 1, 1)
    far_even, far_odd = received(far_even, 2, 0), received(far_odd, 2, 1)
    return (
        jnp.where(even_core, cross, in_chip),
        jnp.where(even_core, in_chip, cross),
        jnp.where(even_chip, far_odd, far_even),
        jnp.where(even_chip, far_even, far_odd),
    )


def tiles_below(value, height):
    return jnp.concatenate(
        [
            jnp.concatenate(
                [
                    value[:height, tile * LANES : (tile + 1) * LANES],
                    value[height:, tile * LANES : (tile + 1) * LANES],
                ],
                axis=1,
            )
            for tile in range(TILES)
        ],
        axis=0,
    )


def stereo_tiles(blocks, left_tab, right_tab):
    arranged = []
    for light in blocks:
        doubled = jnp.concatenate([light, light], axis=0)
        left = jnp.dot(left_tab[...], doubled, preferred_element_type=jnp.float32)
        arranged.append(tiles_below(left.astype(jnp.bfloat16), light.shape[0]))
    arranged = jnp.concatenate(arranged, axis=0) if len(arranged) > 1 else arranged[0]
    return jnp.dot(arranged, right_tab[...], preferred_element_type=jnp.float32)


def clear_pixels(edges, spread):
    edge_pix = jnp.dot(edges, spread, preferred_element_type=jnp.float32)
    within = (lax.broadcasted_iota(jnp.int32, (1, COLS), 1) % HS).astype(jnp.float32)
    return jnp.where(within < edge_pix, 1.0, 0.0)


def banded(line, count, shift):
    base = jnp.concatenate([line, jnp.zeros((1, LANES), jnp.float32)], axis=1)
    base = jnp.broadcast_to(base, (count, 2 * LANES))
    return pltpu.roll(base, shift, 1, stride=1, stride_axis=0)


def filters(tile, layer):
    turned = pltpu.roll(tile[0:8], HALF, 1)
    left_half = lax.broadcasted_iota(jnp.int32, (2, LANES), 1) < HALF
    col_taps = jnp.where(left_half, turned[0:2], tile[2:4])
    row_taps = jnp.where(left_half, turned[4:6], 0.0)
    row_re, row_im = row_taps[0:1], row_taps[1:2]
    height = block_height(layer)
    before = height + 2 * KR
    upper = banded(row_re, height, 0) - banded(row_im, height, before)
    lower = banded(row_im, height, 0) + banded(row_re, height, before)
    row_mat = jnp.concatenate([upper, lower], axis=0).astype(jnp.bfloat16)
    col_re = banded(col_taps[0:1], LANES, 1)
    col_im = banded(col_taps[1:2], LANES, 1)
    upper = jnp.concatenate([col_re, -col_im], axis=1)
    lower = jnp.concatenate([col_im, col_re], axis=1)
    col_mat = jnp.concatenate([upper, lower], axis=0).astype(jnp.bfloat16)
    return row_mat, col_mat


def propagated(u_re, u_im, row_mat, col_mat, layer):
    height = layer_height(layer)
    block = block_height(layer)
    reach = block + 2 * KR
    parts = []
    for start in range(0, height, block):
        stacked = jnp.concatenate(
            [u_re[start : start + reach], u_im[start : start + reach]], axis=0
        )
        parts.append(
            jnp.dot(row_mat[:, : 2 * reach], stacked, preferred_element_type=jnp.float32)
        )
    rowed = jnp.concatenate(
        [part[:block] for part in parts] + [part[block:] for part in parts], axis=0
    )
    rowed = jnp.concatenate([rowed, jnp.zeros((2 * height, LANES), jnp.float32)], axis=1)
    rowed = pltpu.roll(rowed, HALF, 1).astype(jnp.bfloat16)
    windows = jnp.concatenate(
        [
            jnp.concatenate(
                [
                    rowed[:height, tile * LANES : (tile + 2) * LANES],
                    rowed[height:, tile * LANES : (tile + 2) * LANES],
                ],
                axis=1,
            )
            for tile in range(TILES)
        ],
        axis=0,
    )
    return lax.dot_general(
        windows, col_mat, (((1,), (1,)), ((), ())), preferred_element_type=jnp.float32
    )


def prepare_kernel(
    own, incident, far_odd, far_even, cross, in_chip, left_tab, right_tab,
    first, stereo, clear, col_mats, spread, *row_mats
):
    low_near, high_near, low_far, high_far = ordered(in_chip, cross, far_even, far_odd)
    extended = []
    for part in range(2):
        pieces = [low_far, low_near, incident[...], high_near, high_far]
        pieces = [piece[part * BAND : (part + 1) * BAND] for piece in pieces]
        extended.append(jnp.concatenate(pieces, axis=0))
    row_mat, col_mat = filters(own[0, 0:16, COLS:].astype(jnp.float32), 0)
    first[...] = propagated(extended[0], extended[1], row_mat, col_mat, 0)
    for layer in range(1, LAYERS):
        row_mat, col_mat = filters(own[layer, 0:16, COLS:].astype(jnp.float32), layer)
        row_mats[layer - 1][...] = row_mat
        col_mats[layer - 1] = col_mat
    packed = jnp.concatenate([own[layer, :, :HALO_W] for layer in range(LAYERS)], axis=0)
    spread[...] = spread_matrix()
    clear[...] = clear_pixels(packed[:, COLS : COLS + NH], spread[...])
    tiles = stereo_tiles([packed[:, :COLS]], left_tab, right_tab)
    for tile in range(TILES):
        for part in range(2):
            block = tiles[
                tile * LANES : (tile + 1) * LANES, part * LANES : (part + 1) * LANES
            ]
            stereo[part, :, tile * LANES : (tile + 1) * LANES] = block


def chain_kernel(
    in_chip, cross, far_even, far_odd, left_tab, right_tab, first, stereo, clear, col_mats, spread, *rest
):
    row_mats, outs, field = rest[: LAYERS - 1], rest[LAYERS - 1 : -1], rest[-1]
    depth = lax.axis_index("depth")
    low_near, high_near, low_far, high_far = ordered(in_chip, cross, far_even, far_odd)
    pieces = [
        low_far,
        low_near[0:BAND],
        high_near[0:BAND],
        high_far,
        low_near[BAND : 2 * BAND],
        high_near[BAND : 2 * BAND],
        low_near[2 * BAND : NEAR],
        high_near[2 * BAND : NEAR],
    ]
    halo = jnp.concatenate(pieces, axis=0)
    half = halo.shape[0] // 2
    halo_tiles = stereo_tiles(
        [halo[:half, :COLS], halo[half:, :COLS]], left_tab, right_tab
    )
    halo_clear = clear_pixels(halo[:, COLS : COLS + NH], spread[...])
    begins = (0, half, half + 2 * BAND, 0)
    sides = (BAND + FAR, BAND, KR, 0)
    for layer in range(LAYERS):
        height = layer_height(layer)
        before = height + 2 * KR
        low, side = begins[layer], sides[layer]
        if layer == 0:
            columned = first
        else:
            columned = propagated(
                field[layer - 1, 0, :before],
                field[layer - 1, 1, :before],
                row_mats[layer - 1],
                col_mats[layer - 1],
                layer,
            )
        band = slice(layer * BAND, (layer + 1) * BAND)
        pieces = [clear[band]]
        if side:
            pieces = [halo_clear[low : low + side], clear[band], halo_clear[low + side : low + 2 * side]]
        passing = jnp.concatenate(pieces, axis=0)
        for tile in range(TILES):
            span = slice(tile * height, (tile + 1) * height)
            lanes = slice(tile * LANES, (tile + 1) * LANES)
            row = (low // half * TILES + tile) * half + low % half
            for part in range(2):
                within = slice(part * LANES, (part + 1) * LANES)
                pieces = [stereo[part, band, lanes]]
                if side:
                    pieces = [
                        halo_tiles[row : row + side, within],
                        stereo[part, band, lanes],
                        halo_tiles[row + side : row + 2 * side, within],
                    ]
                added = jnp.concatenate(pieces, axis=0)
                value = passing[:, lanes] * columned[span, within] + added
                field[layer, part, :height, lanes] = value.astype(jnp.bfloat16)
    for hop, out in enumerate(outs):
        layer = depth ^ hop
        start = pl.multiple_of((LAYERS - 1 - layer) * KR, KR)
        for part in range(2):
            out[part] = field[layer, part, pl.ds(start, BAND)]


def home_kernel(hops, *refs):
    arrived, out, sems = refs[: len(hops)], refs[-2], refs[-1]
    depth = lax.axis_index("depth")
    for finish in (False, True):
        for place, hop in enumerate(hops):

            @pl.when((depth ^ hop) < COLORS)
            def write(place=place, hop=hop):
                copy = pltpu.make_async_copy(
                    arrived[place], out.at[0, depth ^ hop], sems.at[place]
                )
                if finish:
                    copy.wait()
                else:
                    copy.start()


def over_depth(value, hop):
    return lax.ppermute(value, "depth", [(i, i ^ hop) for i in range(LAYERS)])


def exchanged(value, by, phase):
    count, depths = lax.axis_size("rows"), lax.axis_size("depth")
    partner = {}
    for low in range(count - by):
        if (low // by) % 2 == phase:
            partner[low], partner[low + by] = low + by, low
    pairs = []
    for depth in range(depths):
        for band in range(count):
            if band in partner:
                to = (depth, partner[band])
            elif by > 1:
                to = (depth, band ^ 1)
            else:
                to = (depth ^ 1, band)
            pairs.append((depth * count + band, to[0] * count + to[1]))
    return lax.ppermute(value, ("depth", "rows"), pairs)


def neighbours(sent):
    in_chip, cross, far_even, far_odd = sent
    far_odd = exchanged(far_odd, 2, 1)
    far_even = exchanged(far_even, 2, 0)
    cross = exchanged(cross, 1, 1)
    in_chip = exchanged(in_chip, 1, 0)
    return in_chip, cross, far_even, far_odd


def call(
    kernel, out_shape, in_specs, scratch=(), flops=0, moved=10**6, limit=VMEM_LIMIT,
    out_space=pltpu.VMEM, aliases=None,
):
    vmem = pl.BlockSpec(memory_space=out_space)
    many = isinstance(out_shape, (tuple, list))
    return pl.pallas_call(
        kernel,
        out_shape=out_shape,
        in_specs=in_specs,
        out_specs=(vmem,) * len(out_shape) if many else vmem,
        scratch_shapes=scratch,
        input_output_aliases=aliases or {},
        compiler_params=pltpu.CompilerParams(vmem_limit_bytes=limit),
        cost_estimate=pl.CostEstimate(flops=flops, bytes_accessed=moved, transcendentals=0),
    )


def body(incident, row_taps, col_taps, hogel_light, silhouette, fill_counts, hogel_index):
    vmem = pl.BlockSpec(memory_space=pltpu.VMEM)
    hbm = pl.BlockSpec(memory_space=pltpu.HBM)
    bf16, f32 = jnp.bfloat16, jnp.float32
    shaped = jax.ShapeDtypeStruct
    held = [
        pltpu.VMEM(hogel_index.shape, jnp.int32),
        pltpu.SMEM(fill_counts.shape, jnp.int32),
        pltpu.VMEM(silhouette.shape, jnp.int32),
        pltpu.VMEM(row_taps.shape, bf16),
        pltpu.VMEM(col_taps.shape, bf16),
        pltpu.VMEM(hogel_light.shape, f32),
    ]
    *messages, mine = call(
        pack_kernel,
        (shaped((BAND, HALO_W), bf16),) * LAYERS + (shaped(incident.shape[1:], bf16),),
        [hbm] * 7,
        held + [pltpu.SemaphoreType.DMA((7,)), pltpu.VMEM((BAND, LANES), f32)],
        flops=10**7,
        limit=PACK_LIMIT,
    )(hogel_light, silhouette, fill_counts, hogel_index, row_taps, col_taps, incident)
    mine = mine.reshape(2 * BAND, COLS)
    kept = call(stay_kernel, shaped((BAND, HALO_W), bf16), [vmem], moved=10**5)(messages[0])
    layers_in = [kept] + [over_depth(messages[hop], hop) for hop in range(1, LAYERS)]
    arrived = neighbours((mine,) * 4)[::-1]
    near = shaped((NEAR, HALO_W), bf16)
    far = shaped((FAR, HALO_W), bf16)
    own, *sent = call(
        halo_kernel,
        (shaped((LAYERS, BAND, HALO_W), bf16), near, near, far, far),
        [vmem] * LAYERS,
    )(*layers_in)
    halos = neighbours(sent)
    right_tab = jnp.asarray(right_table())
    made = call(
        prepare_kernel,
        [
            shaped((TILES * layer_height(0), 2 * LANES), f32),
            shaped((2, LANES, COLS), f32),
            shaped((LANES, COLS), f32),
            shaped((LAYERS - 1, 2 * LANES, 4 * LANES), bf16),
            shaped((NH, COLS), bf16),
        ]
        + [shaped((2 * block_height(layer), 2 * LANES), bf16) for layer in range(1, LAYERS)],
        [vmem] * 8,
        flops=10**9,
        moved=3 * 10**6,
    )(own, mine, *arrived, jnp.asarray(left_table(LANES)), right_tab)
    halo_rows = NEAR + FAR
    results = call(
        chain_kernel,
        [shaped((2, BAND, COLS), bf16)] * LAYERS,
        [vmem] * (6 + len(made)),
        [pltpu.VMEM((LAYERS, 2, layer_height(0), COLS), bf16)],
        flops=2 * 10**9,
        moved=3 * 10**6,
    )(*halos, jnp.asarray(left_table(halo_rows)), right_tab, *made)
    returned = [results[0]] + [over_depth(results[hop], hop) for hop in range(1, LAYERS)]
    home = shaped((1, COLORS, 2, BAND, COLS), bf16)
    early = (0, 1, 2)
    partly = call(
        functools.partial(home_kernel, early),
        home,
        [vmem] * len(early),
        [pltpu.SemaphoreType.DMA((len(early),))],
        out_space=pltpu.HBM,
    )(*(returned[hop] for hop in early))
    return call(
        functools.partial(home_kernel, (3,)),
        home,
        [vmem, hbm],
        [pltpu.SemaphoreType.DMA((1,))],
        out_space=pltpu.HBM,
        aliases={1: 0},
    )(returned[3], partly)


def solution(mesh):
    placed = (
        P(None, None, "rows", None),
        P("depth", None, None, None),
        P("depth", None, None, None),
        P("depth", None, "rows", None),
        P("depth", "rows", None),
        P("depth", "rows"),
        P("depth", "rows", None),
    )
    return jax.shard_map(
        body,
        mesh=mesh,
        in_specs=placed,
        out_specs=P("depth", None, None, "rows", None),
        check_vma=False,
    )
```

```python
import functools
import math

import jax
import jax.numpy as jnp
import numpy as np
from jax import lax
from jax.experimental import pallas as pl
from jax.experimental.pallas import tpu as pltpu
from jax.sharding import PartitionSpec as P

HS = 16
KR = 16
KC = 63
COLORS = 3
LAYERS = 4
BAND = 32
COLS = 1024
NH = COLS // HS
LANES = 128
TILES = COLS // LANES
HALO_W = COLS + LANES
HALF = LANES // 2
NEAR = 2 * BAND + KR
FAR = KR
VMEM_LIMIT = 48 * 1024 * 1024
PACK_LIMIT = 63 * 1024 * 1024


def split_table(table):
    high = table.astype(jnp.bfloat16)
    low = (table - high.astype(np.float64)).astype(jnp.bfloat16)
    return high, low


def dft_pair():
    counter = np.arange(HS)
    angles = (counter[:, None] * counter[None, :] % HS) * (2.0 * math.pi / HS)
    return np.cos(angles) / math.sqrt(HS), np.sin(angles) / math.sqrt(HS)


def left_table(height):
    cos_tab, sin_tab = dft_pair()
    eye = np.eye(height // HS)
    full = np.concatenate([np.kron(eye, cos_tab), np.kron(eye, -sin_tab)], axis=0)
    return np.concatenate(split_table(full), axis=1)


def right_table():
    cos_tab, sin_tab = dft_pair()
    eye = np.eye(LANES // HS)
    cos_big, sin_big = np.kron(eye, cos_tab), np.kron(eye, sin_tab)
    full = np.concatenate(
        [
            np.concatenate([cos_big, -sin_big], axis=1),
            np.concatenate([sin_big, cos_big], axis=1),
        ],
        axis=0,
    )
    return full.astype(jnp.bfloat16)


def layer_height(layer):
    return BAND + 2 * KR * (LAYERS - 1 - layer)


def block_height(layer):
    height = layer_height(layer)
    return height // 2 if 2 * (height + 2 * KR) > 2 * LANES else height


def spread_matrix():
    tile = lax.broadcasted_iota(jnp.int32, (NH, COLS), 0)
    column = lax.broadcasted_iota(jnp.int32, (NH, COLS), 1)
    return jnp.where(column // HS == tile, 1.0, 0.0).astype(jnp.bfloat16)


def own_colour():
    return jnp.minimum(lax.axis_index("depth"), COLORS - 1)


def pack_kernel(light, edges, counts, listed, row_taps, col_taps, incident, *rest):
    outs, mine, held, sems, taps = rest[:LAYERS], rest[LAYERS], rest[5:11], rest[11], rest[12]
    depth = lax.axis_index("depth")
    picked = pltpu.make_async_copy(incident.at[own_colour()], mine, sems.at[6])
    sources = (listed, counts, edges, row_taps, col_taps, light)
    copies = [
        pltpu.make_async_copy(source, target, sems.at[place])
        for place, (source, target) in enumerate(zip(sources, held))
    ]
    for copy in reversed(copies):
        copy.start()
    picked.start()
    listed, counts, edges, row_taps, col_taps, light = held
    spread = spread_matrix()
    slot = lax.broadcasted_iota(jnp.int32, (NH, NH), 0)
    place = lax.broadcasted_iota(jnp.int32, (NH, NH), 1)
    for copy in copies[:5]:
        copy.wait()
    rows = []
    for group in range(BAND // HS):
        listing = jnp.broadcast_to(listed[0, group : group + 1, :], (NH, NH))
        column = jnp.sum(jnp.where(slot == place, listing, 0), axis=1, keepdims=True)
        named = (column == place) & (slot < counts[0, group])
        live = jnp.max(jnp.where(named, 1.0, 0.0), axis=0, keepdims=True)
        rows.append(jnp.broadcast_to(live, (HS, NH)))
    live_rows = jnp.concatenate(rows, axis=0).astype(jnp.bfloat16)
    live_pix = jnp.dot(live_rows, spread, preferred_element_type=jnp.float32)
    edge_tile = jnp.concatenate(
        [edges[0].astype(jnp.float32), jnp.zeros((BAND, LANES - NH), jnp.float32)], axis=1
    )
    left_half = lax.broadcasted_iota(jnp.int32, (BAND, LANES), 1) < HALF
    colours = [jnp.minimum(depth ^ hop, COLORS - 1) for hop in range(LAYERS)]
    taps[...] = jnp.zeros_like(taps)
    for hop, colour in enumerate(colours):
        col = col_taps[0, colour].astype(jnp.float32)
        taps[8 * hop : 8 * hop + 2, : 2 * KC + 1] = col
        taps[8 * hop + 2 : 8 * hop + 4, : 2 * KC + 1] = col
        taps[8 * hop + 4 : 8 * hop + 6, : 2 * KR + 1] = row_taps[0, colour].astype(jnp.float32)
    stays = lax.broadcasted_iota(jnp.int32, (BAND, LANES), 0) % 8 // 2 == 1
    turned = jnp.where(stays, taps[...], pltpu.roll(taps[...], HALF, 1))
    below = jnp.zeros((BAND - 8, LANES), jnp.float32)
    for hop, out in enumerate(outs):
        tile = jnp.concatenate([turned[8 * hop : 8 * hop + 8], below], axis=0)
        out[:, COLS:] = jnp.where(left_half, edge_tile, tile).astype(jnp.bfloat16)
    copies[5].wait()
    for colour, out in zip(colours, outs):
        out[:, :COLS] = (light[0, colour] * live_pix).astype(jnp.bfloat16)
    picked.wait()


def stay_kernel(message, here):
    here[...] = message[...]


def halo_kernel(*refs):
    arrived, (own, in_chip, cross, far_even, far_odd) = refs[:LAYERS], refs[LAYERS:]
    depth = lax.axis_index("depth")
    for hop in range(LAYERS):
        own[depth ^ hop] = arrived[hop][...]
    band = lax.axis_index("rows")
    core = band % 2
    odd = (band // 2) % 2
    last = BAND - KR
    for near, start in ((in_chip, (1 - core) * last), (cross, core * last)):
        near[0:BAND] = own[0, :, :HALO_W]
        near[BAND : 2 * BAND] = own[1, :, :HALO_W]
        near[2 * BAND : NEAR] = own[2, pl.ds(pl.multiple_of(start, KR), KR), :HALO_W]
    for far, start in ((far_even, (1 - odd) * last), (far_odd, odd * last)):
        far[...] = own[0, pl.ds(pl.multiple_of(start, KR), KR), :HALO_W]


def ordered(in_chip, cross, far_even, far_odd):
    band = lax.axis_index("rows")
    count = lax.axis_size("rows")
    even_core = band % 2 == 0
    even_chip = (band // 2) % 2 == 0

    def received(value, by, phase):
        lower = (band // by) % 2 == phase
        paired = jnp.where(lower, band + by < count, band >= by)
        value = value[...]
        return jnp.where(paired, value, jnp.zeros_like(value))

    in_chip, cross = received(in_chip, 1, 0), received(cross, 1, 1)
    far_even, far_odd = received(far_even, 2, 0), received(far_odd, 2, 1)
    return (
        jnp.where(even_core, cross, in_chip),
        jnp.where(even_core, in_chip, cross),
        jnp.where(even_chip, far_odd, far_even),
        jnp.where(even_chip, far_even, far_odd),
    )


def tiles_below(value, height):
    return jnp.concatenate(
        [
            jnp.concatenate(
                [
                    value[:height, tile * LANES : (tile + 1) * LANES],
                    value[height:, tile * LANES : (tile + 1) * LANES],
                ],
                axis=1,
            )
            for tile in range(TILES)
        ],
        axis=0,
    )


def stereo_tiles(blocks, left_tab, right_tab):
    arranged = []
    for light in blocks:
        doubled = jnp.concatenate([light, light], axis=0)
        left = jnp.dot(left_tab[...], doubled, preferred_element_type=jnp.float32)
        arranged.append(tiles_below(left.astype(jnp.bfloat16), light.shape[0]))
    arranged = jnp.concatenate(arranged, axis=0) if len(arranged) > 1 else arranged[0]
    return jnp.dot(arranged, right_tab[...], preferred_element_type=jnp.float32)


def clear_pixels(edges, spread):
    edge_pix = jnp.dot(edges, spread, preferred_element_type=jnp.float32)
    within = (lax.broadcasted_iota(jnp.int32, (1, COLS), 1) % HS).astype(jnp.float32)
    return jnp.where(within < edge_pix, 1.0, 0.0)


def banded(line, count, shift):
    base = jnp.concatenate([line, jnp.zeros((1, LANES), jnp.float32)], axis=1)
    base = jnp.broadcast_to(base, (count, 2 * LANES))
    return pltpu.roll(base, shift, 1, stride=1, stride_axis=0)


def filters(tile, layer):
    turned = pltpu.roll(tile[0:8], HALF, 1)
    left_half = lax.broadcasted_iota(jnp.int32, (2, LANES), 1) < HALF
    col_taps = jnp.where(left_half, turned[0:2], tile[2:4])
    row_taps = jnp.where(left_half, turned[4:6], 0.0)
    row_re, row_im = row_taps[0:1], row_taps[1:2]
    height = block_height(layer)
    before = height + 2 * KR
    upper = banded(row_re, height, 0) - banded(row_im, height, before)
    lower = banded(row_im, height, 0) + banded(row_re, height, before)
    row_mat = jnp.concatenate([upper, lower], axis=0).astype(jnp.bfloat16)
    col_re = banded(col_taps[0:1], LANES, 1)
    col_im = banded(col_taps[1:2], LANES, 1)
    upper = jnp.concatenate([col_re, -col_im], axis=1)
    lower = jnp.concatenate([col_im, col_re], axis=1)
    col_mat = jnp.concatenate([upper, lower], axis=0).astype(jnp.bfloat16)
    return row_mat, col_mat


def propagated(u_re, u_im, row_mat, col_mat, layer):
    height = layer_height(layer)
    block = block_height(layer)
    reach = block + 2 * KR
    parts = []
    for start in range(0, height, block):
        stacked = jnp.concatenate(
            [u_re[start : start + reach], u_im[start : start + reach]], axis=0
        )
        parts.append(
            jnp.dot(row_mat[:, : 2 * reach], stacked, preferred_element_type=jnp.float32)
        )
    rowed = jnp.concatenate(
        [part[:block] for part in parts] + [part[block:] for part in parts], axis=0
    )
    rowed = jnp.concatenate([rowed, jnp.zeros((2 * height, LANES), jnp.float32)], axis=1)
    rowed = pltpu.roll(rowed, HALF, 1).astype(jnp.bfloat16)
    windows = jnp.concatenate(
        [
            jnp.concatenate(
                [
                    rowed[:height, tile * LANES : (tile + 2) * LANES],
                    rowed[height:, tile * LANES : (tile + 2) * LANES],
                ],
                axis=1,
            )
            for tile in range(TILES)
        ],
        axis=0,
    )
    return lax.dot_general(
        windows, col_mat, (((1,), (1,)), ((), ())), preferred_element_type=jnp.float32
    )


def prepare_kernel(
    own, incident, far_odd, far_even, cross, in_chip, left_tab, right_tab,
    first, stereo, clear, col_mats, spread, *row_mats
):
    low_near, high_near, low_far, high_far = ordered(in_chip, cross, far_even, far_odd)
    extended = []
    for part in range(2):
        pieces = [low_far, low_near, incident[...], high_near, high_far]
        pieces = [piece[part * BAND : (part + 1) * BAND] for piece in pieces]
        extended.append(jnp.concatenate(pieces, axis=0))
    row_mat, col_mat = filters(own[0, 0:16, COLS:].astype(jnp.float32), 0)
    first[...] = propagated(extended[0], extended[1], row_mat, col_mat, 0)
    for layer in range(1, LAYERS):
        row_mat, col_mat = filters(own[layer, 0:16, COLS:].astype(jnp.float32), layer)
        row_mats[layer - 1][...] = row_mat
        col_mats[layer - 1] = col_mat
    packed = jnp.concatenate([own[layer, :, :HALO_W] for layer in range(LAYERS)], axis=0)
    spread[...] = spread_matrix()
    clear[...] = clear_pixels(packed[:, COLS : COLS + NH], spread[...])
    tiles = stereo_tiles([packed[:, :COLS]], left_tab, right_tab)
    for tile in range(TILES):
        for part in range(2):
            block = tiles[
                tile * LANES : (tile + 1) * LANES, part * LANES : (part + 1) * LANES
            ]
            stereo[part, :, tile * LANES : (tile + 1) * LANES] = block


def chain_kernel(
    in_chip, cross, far_even, far_odd, left_tab, right_tab, first, stereo, clear, col_mats, spread, *rest
):
    row_mats, outs, field = rest[: LAYERS - 1], rest[LAYERS - 1 : -1], rest[-1]
    depth = lax.axis_index("depth")
    low_near, high_near, low_far, high_far = ordered(in_chip, cross, far_even, far_odd)
    pieces = [
        low_far,
        low_near[0:BAND],
        high_near[0:BAND],
        high_far,
        low_near[BAND : 2 * BAND],
        high_near[BAND : 2 * BAND],
        low_near[2 * BAND : NEAR],
        high_near[2 * BAND : NEAR],
    ]
    halo = jnp.concatenate(pieces, axis=0)
    half = halo.shape[0] // 2
    halo_tiles = stereo_tiles(
        [halo[:half, :COLS], halo[half:, :COLS]], left_tab, right_tab
    )
    halo_clear = clear_pixels(halo[:, COLS : COLS + NH], spread[...])
    begins = (0, half, half + 2 * BAND, 0)
    sides = (BAND + FAR, BAND, KR, 0)
    for layer in range(LAYERS):
        height = layer_height(layer)
        before = height + 2 * KR
        low, side = begins[layer], sides[layer]
        if layer == 0:
            columned = first
        else:
            columned = propagated(
                field[layer - 1, 0, :before],
                field[layer - 1, 1, :before],
                row_mats[layer - 1],
                col_mats[layer - 1],
                layer,
            )
        band = slice(layer * BAND, (layer + 1) * BAND)
        pieces = [clear[band]]
        if side:
            pieces = [halo_clear[low : low + side], clear[band], halo_clear[low + side : low + 2 * side]]
        passing = jnp.concatenate(pieces, axis=0)
        for tile in range(TILES):
            span = slice(tile * height, (tile + 1) * height)
            lanes = slice(tile * LANES, (tile + 1) * LANES)
            row = (low // half * TILES + tile) * half + low % half
            for part in range(2):
                within = slice(part * LANES, (part + 1) * LANES)
                pieces = [stereo[part, band, lanes]]
                if side:
                    pieces = [
                        halo_tiles[row : row + side, within],
                        stereo[part, band, lanes],
                        halo_tiles[row + side : row + 2 * side, within],
                    ]
                added = jnp.concatenate(pieces, axis=0)
                value = passing[:, lanes] * columned[span, within] + added
                field[layer, part, :height, lanes] = value.astype(jnp.bfloat16)
    for hop, out in enumerate(outs):
        layer = depth ^ hop
        start = pl.multiple_of((LAYERS - 1 - layer) * KR, KR)
        for part in range(2):
            out[part] = field[layer, part, pl.ds(start, BAND)]


def home_kernel(hops, *refs):
    arrived, out, sems = refs[: len(hops)], refs[-2], refs[-1]
    depth = lax.axis_index("depth")
    for finish in (False, True):
        for place, hop in enumerate(hops):

            @pl.when((depth ^ hop) < COLORS)
            def write(place=place, hop=hop):
                copy = pltpu.make_async_copy(
                    arrived[place], out.at[0, depth ^ hop], sems.at[place]
                )
                if finish:
                    copy.wait()
                else:
                    copy.start()


def over_depth(value, hop):
    return lax.ppermute(value, "depth", [(i, i ^ hop) for i in range(LAYERS)])


def exchanged(value, by, phase):
    count, depths = lax.axis_size("rows"), lax.axis_size("depth")
    partner = {}
    for low in range(count - by):
        if (low // by) % 2 == phase:
            partner[low], partner[low + by] = low + by, low
    pairs = []
    for depth in range(depths):
        for band in range(count):
            if band in partner:
                to = (depth, partner[band])
            elif by > 1:
                to = (depth, band ^ 1)
            else:
                to = (depth ^ 2, band)
            pairs.append((depth * count + band, to[0] * count + to[1]))
    return lax.ppermute(value, ("depth", "rows"), pairs)


def neighbours(sent):
    in_chip, cross, far_even, far_odd = sent
    far_odd = exchanged(far_odd, 2, 1)
    far_even = exchanged(far_even, 2, 0)
    cross = exchanged(cross, 1, 1)
    in_chip = exchanged(in_chip, 1, 0)
    return in_chip, cross, far_even, far_odd


def call(
    kernel, out_shape, in_specs, scratch=(), flops=0, moved=10**6, limit=VMEM_LIMIT,
    out_space=pltpu.VMEM, aliases=None,
):
    vmem = pl.BlockSpec(memory_space=out_space)
    many = isinstance(out_shape, (tuple, list))
    return pl.pallas_call(
        kernel,
        out_shape=out_shape,
        in_specs=in_specs,
        out_specs=(vmem,) * len(out_shape) if many else vmem,
        scratch_shapes=scratch,
        input_output_aliases=aliases or {},
        compiler_params=pltpu.CompilerParams(vmem_limit_bytes=limit),
        cost_estimate=pl.CostEstimate(flops=flops, bytes_accessed=moved, transcendentals=0),
    )


def body(incident, row_taps, col_taps, hogel_light, silhouette, fill_counts, hogel_index):
    vmem = pl.BlockSpec(memory_space=pltpu.VMEM)
    hbm = pl.BlockSpec(memory_space=pltpu.HBM)
    bf16, f32 = jnp.bfloat16, jnp.float32
    shaped = jax.ShapeDtypeStruct
    held = [
        pltpu.VMEM(hogel_index.shape, jnp.int32),
        pltpu.SMEM(fill_counts.shape, jnp.int32),
        pltpu.VMEM(silhouette.shape, jnp.int32),
        pltpu.VMEM(row_taps.shape, bf16),
        pltpu.VMEM(col_taps.shape, bf16),
        pltpu.VMEM(hogel_light.shape, f32),
    ]
    *messages, mine = call(
        pack_kernel,
        (shaped((BAND, HALO_W), bf16),) * LAYERS + (shaped(incident.shape[1:], bf16),),
        [hbm] * 7,
        held + [pltpu.SemaphoreType.DMA((7,)), pltpu.VMEM((BAND, LANES), f32)],
        flops=10**7,
        limit=PACK_LIMIT,
    )(hogel_light, silhouette, fill_counts, hogel_index, row_taps, col_taps, incident)
    mine = mine.reshape(2 * BAND, COLS)
    kept = call(stay_kernel, shaped((BAND, HALO_W), bf16), [vmem], moved=10**5)(messages[0])
    layers_in = [kept] + [over_depth(messages[hop], hop) for hop in range(1, LAYERS)]
    arrived = neighbours((mine,) * 4)[::-1]
    near = shaped((NEAR, HALO_W), bf16)
    far = shaped((FAR, HALO_W), bf16)
    own, *sent = call(
        halo_kernel,
        (shaped((LAYERS, BAND, HALO_W), bf16), near, near, far, far),
        [vmem] * LAYERS,
    )(*layers_in)
    halos = neighbours(sent)
    right_tab = jnp.asarray(right_table())
    made = call(
        prepare_kernel,
        [
            shaped((TILES * layer_height(0), 2 * LANES), f32),
            shaped((2, LANES, COLS), f32),
            shaped((LANES, COLS), f32),
            shaped((LAYERS - 1, 2 * LANES, 4 * LANES), bf16),
            shaped((NH, COLS), bf16),
        ]
        + [shaped((2 * block_height(layer), 2 * LANES), bf16) for layer in range(1, LAYERS)],
        [vmem] * 8,
        flops=10**9,
        moved=3 * 10**6,
    )(own, mine, *arrived, jnp.asarray(left_table(LANES)), right_tab)
    halo_rows = NEAR + FAR
    results = call(
        chain_kernel,
        [shaped((2, BAND, COLS), bf16)] * LAYERS,
        [vmem] * (6 + len(made)),
        [pltpu.VMEM((LAYERS, 2, layer_height(0), COLS), bf16)],
        flops=2 * 10**9,
        moved=3 * 10**6,
    )(*halos, jnp.asarray(left_table(halo_rows)), right_tab, *made)
    returned = [results[0]] + [over_depth(results[hop], hop) for hop in range(1, LAYERS)]
    home = shaped((1, COLORS, 2, BAND, COLS), bf16)
    early = (0, 1, 2)
    partly = call(
        functools.partial(home_kernel, early),
        home,
        [vmem] * len(early),
        [pltpu.SemaphoreType.DMA((len(early),))],
        out_space=pltpu.HBM,
    )(*(returned[hop] for hop in early))
    return call(
        functools.partial(home_kernel, (3,)),
        home,
        [vmem, hbm],
        [pltpu.SemaphoreType.DMA((1,))],
        out_space=pltpu.HBM,
        aliases={1: 0},
    )(returned[3], partly)


def solution(mesh):
    placed = (
        P(None, None, "rows", None),
        P("depth", None, None, None),
        P("depth", None, None, None),
        P("depth", None, "rows", None),
        P("depth", "rows", None),
        P("depth", "rows"),
        P("depth", "rows", None),
    )
    return jax.shard_map(
        body,
        mesh=mesh,
        in_specs=placed,
        out_specs=P("depth", None, None, "rows", None),
        check_vma=False,
    )
```
